128 devices in a mesh: row: 16 (over z, y_lo, core), col: 8 (over y_hi, x).
Axes of the slice: x: 4, y: 4 (y_hi: 2, y_lo: 2; y = y_hi * 2 + y_lo), z: 4, core: 2. Of those that a mesh axis runs over, the one named last changes fastest.
Arguments:
- tokens: bfloat16 [16384, 1536], P(('row', 'col')), may hold values from -6 to 6
- segments: int32 [16384], P(('row', 'col')), may hold values from 0 to 2, as said below
- routes: int32 [16384, 6], P(('row', 'col')), may hold values from 0 to 63, all different within a row; in each aligned block of 128 rows (0 to 127, 128 to 255, ...) at most 24 rows name the same one
- norm1_gain: bfloat16 [1536], P(('row', 'col')), may hold values from 0.5 to 1.5
- w_query: bfloat16 [1536, 1536], P(('row', 'col')), may hold values from -0.15625 to 0.15625
- key_value_weight: bfloat16 [1536, 1024], P(('row', 'col')), may hold values from -0.15625 to 0.15625
- w_output: bfloat16 [1536, 1536], P(None, ('row', 'col')), may hold values from -0.625 to 0.625
- norm2_gain: bfloat16 [1536], P(('row', 'col')), may hold values from 0.5 to 1.5
- w_router: bfloat16 [1536, 64], P(('row', 'col')), may hold values from -0.078125 to 0.078125
- w_shgate: bfloat16 [1536, 1024], P(('row', 'col')), may hold values from -0.15625 to 0.15625
- w_shup: bfloat16 [1536, 1024], P(('row', 'col')), may hold values from -0.15625 to 0.15625
- w_shdown: bfloat16 [1024, 1536], P(None, ('row', 'col')), may hold values from -0.1875 to 0.1875
- w_exgate: bfloat16 [128, 1536, 256], P(('row', 'col')), may hold values from -0.15625 to 0.15625
- w_exup: bfloat16 [128, 1536, 256], P(('row', 'col')), may hold values from -0.15625 to 0.15625
- w_exdown: bfloat16 [128, 256, 1536], P(('row', 'col')), may hold values from -0.5 to 0.5
- cotangent: bfloat16 [16384, 1536], P(('row', 'col')), may hold values from -24 to 24
Outputs:
- block_out: bfloat16 [16384, 1536], P(('row', 'col'))
- grad_tokens: float32 [16384, 1536], P(('row', 'col'))
- grad_norm1_gain: float32 [1536], P(('row', 'col'))
- grad_w_query: float32 [1536, 1536], P(('row', 'col'))
- grad_w_keyval: float32 [1536, 1024], P(('row', 'col'))
- grad_w_output: float32 [1536, 1536], P(None, ('row', 'col'))
- grad_norm2_gain: float32 [1536], P(('row', 'col'))
- grad_w_router: float32 [1536, 64], P(('row', 'col'))
- grad_w_shgate: float32 [1536, 1024], P(('row', 'col'))
- grad_w_shup: float32 [1536, 1024], P(('row', 'col'))
- grad_w_shdown: float32 [1024, 1536], P(None, ('row', 'col'))
- grad_w_exgate: float32 [128, 1536, 256], P(('row', 'col'))
- grad_w_exup: float32 [128, 1536, 256], P(('row', 'col'))
- grad_w_exdown: float32 [128, 256, 1536], P(('row', 'col'))
The draws below stay inside these ranges and needn't reach their ends.
Inputs may be any that keep to these rules, and one draw needn't show every extreme that they name: `routes`: each row names 6 different experts. Among the rows of one device no expert is named more than 24 times, and in every draw some expert is named exactly 24 times by the rows of some device. `segments`: each sequence of 1024 tokens holds three documents numbered 0, 1, 2 in order: the first and the last of 96 to 127 tokens each, the middle one all tokens between them, so that it holds tokens of every index of col.
All inputs are finite; a program needn't handle non-finite values.
Results may differ from the reference program's by a relative error of at most 0.02.
Values may be sent and summed in bfloat16 or wider, within the bound.
A program may use at most 320 MiB of HBM per device.

```python
import math
import jax
import jax.numpy as jnp
import numpy as np
from jax import lax

MODEL_WIDTH = 1536
QUERY_HEADS = 12
KEY_VALUE_HEADS = 4
HEAD_SIZE = 128
EXPERTS = 64
TOPK = 6
EH = 512
SH = 1024
TOK_DEV = 128
TOKENS = 16384
SEQUENCE_TOKENS = 1024
CAP = 24
UNITS = 128


def draw_segments(key, part):
    key = jax.random.fold_in(key, 7)
    sequence_batch = TOKENS // SEQUENCE_TOKENS
    key_head, key_tail = jax.random.split(key, 2)
    shortest = 3 * TOK_DEV // 4
    head_length = jax.random.randint(key_head, (sequence_batch, 1), shortest, TOK_DEV)
    tail_length = jax.random.randint(key_tail, (sequence_batch, 1), shortest, TOK_DEV)
    tail_start = SEQUENCE_TOKENS - tail_length
    position = jnp.arange(SEQUENCE_TOKENS, dtype=jnp.int32)[None, :]
    number = (position >= head_length).astype(jnp.int32) + (position >= tail_start).astype(jnp.int32)
    return number.reshape(TOKENS)


def raised(result, own_key, source, target, blocks, factor):
    def block_of(dim):
        return (jnp.arange(result.shape[dim]) // (result.shape[dim] // blocks)).reshape((-1,) + (1,) * (result.ndim - 1 - dim))

    one_side = jax.random.permutation(own_key, blocks)[block_of(target)]
    far = (block_of(target) + blocks // 2) % blocks
    return jnp.where((block_of(source) == one_side) | (block_of(source) == far), factor * result, result)


def level_of(own_key, dims, shards, least, top_value):
    gain = 1.0
    for dim, shards_of in shards:
        heights = jax.random.uniform(jax.random.fold_in(jax.random.fold_in(own_key, 6), dim), (shards_of,), jnp.float32, least / len(shards), top_value / len(shards))
        gain = gain * jnp.repeat(jnp.exp(heights), dims[dim] // shards_of).reshape((-1,) + (1,) * (len(dims) - 1 - dim))
    return gain


def deal_out(stream_key, own, number, rows, count, top, most, lean):
    sequence = jax.random.permutation(stream_key, count)
    packed, common = load_shares(count, rows * top, most, lean, True), load_shares(count, rows * top, most, lean, False)
    places = jnp.arange(count)

    def named(tallies, turn):
        used = int((tallies > 0).sum())
        fixed = max(1, used // 4)
        moved = fixed + (places - fixed + turn * (used - fixed)) % max(1, count - fixed)
        return jnp.zeros((count,), jnp.int32).at[sequence[jnp.where(places < fixed, places, moved)]].set(jnp.asarray(tallies, jnp.int32))

    tallies = jnp.where(number % 4 == 0, named(packed, number // 4), named(common, number - number // 4 - 1))
    mixed = jax.random.permutation(jax.random.fold_in(own, 3), count)
    donor, receiver = mixed[0:count // 2 * 2:2], mixed[1:count // 2 * 2:2]
    slack = jnp.minimum(tallies[donor] - 1, most - tallies[receiver]) // 2
    slack = jnp.where((donor == sequence[0]) | (receiver == sequence[0]) | (tallies[receiver] == 0), 0, jnp.maximum(slack, 0))
    moved = jax.random.randint(jax.random.fold_in(own, 4), (count // 2,), 0, 1 << 20) % (slack + 1)
    tallies = tallies.at[donor].add(-moved).at[receiver].add(moved)
    items = jnp.searchsorted(jnp.cumsum(tallies), jnp.arange(rows * top), side="right").astype(jnp.int32)
    grid = items.reshape(top, rows).T
    grid = grid[jax.random.permutation(jax.random.fold_in(own, 1), rows)]
    turn = jax.random.randint(jax.random.fold_in(own, 2), (rows, 1), 0, top)
    return jnp.take_along_axis(grid, (jnp.arange(top)[None, :] + turn) % top, axis=1)


def load_shares(number_of, total, reach, lean, full):
    loads = [(1 << 20) // math.isqrt(grade ** lean) + 1 for grade in range(1, number_of + 1)]
    largest = reach if full else min(reach, max(-(-total // number_of), total * loads[0] // sum(loads)))
    least = 1 if total - largest >= number_of - 1 else 0
    counts, rest = [largest] + [least] * (number_of - 1), total - largest - least * (number_of - 1)
    while rest > 0:
        candidates = [i for i in range(1, number_of) if counts[i] < largest] or [i for i in range(1, number_of) if counts[i] < reach]
        whole, left = sum([loads[i] for i in candidates]), rest
        for i in candidates:
            addition = min(reach - counts[i], max(1, left * loads[i] // whole), rest)
            counts[i] = counts[i] + addition
            rest = rest - addition
    return np.array(counts)


def normal_values(stream_key, dims, scale, most, cuts=(), kind=jnp.bfloat16):
    drawn = jax.random.normal(stream_key, dims, jnp.float32) * scale
    if len(cuts) > 0:
        drawn = level_of(stream_key, dims, cuts, -0.22, 0.18) * drawn
    return jnp.clip(drawn, min=-most, max=most).astype(kind)


def gaussian_with(own_key, extent, deviation, limit, shards, heavy, kind=jnp.bfloat16):
    result = deviation * jax.random.normal(own_key, extent, jnp.float32)
    if shards:
        result = result * level_of(own_key, extent, shards, -0.22, 0.18)
    return jnp.clip(raised(result, jax.random.fold_in(own_key, 3), *heavy), -limit, limit).astype(kind)


def setup_inputs(seed: int = 0) -> dict:
    key_list = jax.random.split(jax.random.key(seed), 17)
    tokens = normal_values(key_list[0], (TOKENS, MODEL_WIDTH), 1.0, 6.0, ((0, 128),))
    segments = draw_segments(jax.random.fold_in(key_list[16], 71), 0)
    routes_keys = jax.random.split(jax.random.fold_in(key_list[2], 1), TOKENS // TOK_DEV)
    routes_turns = jax.random.permutation(jax.random.fold_in(key_list[2], 3), TOKENS // TOK_DEV)
    routes = jax.vmap(lambda own, number: deal_out(jax.random.fold_in(key_list[2], 2), own, number, TOK_DEV, EXPERTS, TOPK, CAP, 1))(routes_keys, routes_turns).reshape((TOKENS, TOPK))
    norm1_gain = jnp.clip(1.0 + 0.1 * jax.random.normal(key_list[3], (MODEL_WIDTH,), jnp.float32), 0.5, 1.5).astype(jnp.bfloat16)
    w_query = normal_values(key_list[4], (MODEL_WIDTH, QUERY_HEADS * HEAD_SIZE), MODEL_WIDTH ** -0.5, 0.15625, ((0, 128),))
    key_value_weight = normal_values(key_list[5], (MODEL_WIDTH, 2 * KEY_VALUE_HEADS * HEAD_SIZE), MODEL_WIDTH ** -0.5, 0.15625, ((0, 128),))
    w_output = normal_values(key_list[6], (QUERY_HEADS * HEAD_SIZE, MODEL_WIDTH), (QUERY_HEADS * HEAD_SIZE // 16) ** -0.5, 0.625, ((1, 128),))
    norm2_gain = jnp.clip(1.0 + 0.1 * jax.random.normal(key_list[7], (MODEL_WIDTH,), jnp.float32), 0.5, 1.5).astype(jnp.bfloat16)
    w_router = normal_values(key_list[8], (MODEL_WIDTH, EXPERTS), (4 * MODEL_WIDTH) ** -0.5, 0.078125, ((0, 128),))
    w_shgate = normal_values(key_list[9], (MODEL_WIDTH, SH), MODEL_WIDTH ** -0.5, 0.15625, ((0, 128),))
    w_shup = normal_values(key_list[10], (MODEL_WIDTH, SH), MODEL_WIDTH ** -0.5, 0.15625, ((0, 128),))
    w_shdown = normal_values(key_list[11], (SH, MODEL_WIDTH), SH ** -0.5, 0.1875, ((1, 128),))
    w_exgate = normal_values(key_list[12], (UNITS, MODEL_WIDTH, EH // 2), MODEL_WIDTH ** -0.5, 0.15625, ((0, 128),))
    w_exup = normal_values(key_list[13], (UNITS, MODEL_WIDTH, EH // 2), MODEL_WIDTH ** -0.5, 0.15625, ((0, 128),))
    w_exdown = normal_values(key_list[14], (UNITS, EH // 2, MODEL_WIDTH), (EH // 4) ** -0.5, 0.5, ((0, 128),))
    cotangent = gaussian_with(key_list[15], (TOKENS, MODEL_WIDTH), 1.0, 24.0, ((0, 128),), (0, 1, 128, 5.5))
    return {"tokens": tokens, "segments": segments, "routes": routes, "norm1_gain": norm1_gain, "w_query": w_query, "key_value_weight": key_value_weight, "w_output": w_output, "norm2_gain": norm2_gain, "w_router": w_router, "w_shgate": w_shgate, "w_shup": w_shup, "w_shdown": w_shdown, "w_exgate": w_exgate, "w_exup": w_exup, "w_exdown": w_exdown, "cotangent": cotangent}


@jax.custom_vjp
def low(v):
    return lax.optimization_barrier(v.astype(jnp.bfloat16)).astype(jnp.float32)

@jax.custom_vjp
def low_back(v):
    return v

def low_keep(v):
    return (low(v), None)

def low_pass(kept, grad):
    return (grad,)

def back_keep(v):
    return (v, None)

def back_low(kept, grad):
    return (low(grad),)
low.defvjp(low_keep, low_pass)
low_back.defvjp(back_keep, back_low)
EPSILON = 1e-05

def product(left_side, right_side):
    return jnp.dot(left_side, right_side, precision=lax.Precision.HIGHEST, preferred_element_type=jnp.float32)

def normalize(residual, gain_row):
    return residual * lax.rsqrt(lax.optimization_barrier(jnp.mean(residual * residual, axis=-1, keepdims=True)) + EPSILON) * gain_row

def softmax_rows(entries):
    shifted = jnp.exp(entries - lax.optimization_barrier(jnp.max(entries, axis=-1, keepdims=True)))
    return shifted / lax.optimization_barrier(jnp.sum(shifted, axis=-1, keepdims=True))

def attend_heads(pieces):
    query_rows, key_value_rows, segment_ids = pieces
    heads_per_group = QUERY_HEADS // KEY_VALUE_HEADS
    query_head_count = query_rows.reshape(SEQUENCE_TOKENS, KEY_VALUE_HEADS, heads_per_group, HEAD_SIZE)
    key_matrix = key_value_rows[:, :KEY_VALUE_HEADS * HEAD_SIZE].reshape(SEQUENCE_TOKENS, KEY_VALUE_HEADS, HEAD_SIZE)
    value_matrix = key_value_rows[:, KEY_VALUE_HEADS * HEAD_SIZE:].reshape(SEQUENCE_TOKENS, KEY_VALUE_HEADS, HEAD_SIZE)
    scores = low_back(jnp.einsum('tkgd,skd->kgts', query_head_count, key_matrix, precision=lax.Precision.HIGHEST) * HEAD_SIZE ** (-0.5))
    position = jnp.arange(SEQUENCE_TOKENS, dtype=jnp.int32)
    allowed = (position[None, :] <= position[:, None]) & (segment_ids[None, :] == segment_ids[:, None])
    attention_weights = softmax_rows(jnp.where(allowed, scores, -1e+30))
    combined = jnp.einsum('kgts,skd->tkgd', low(attention_weights), value_matrix, precision=lax.Precision.HIGHEST)
    return combined.reshape(SEQUENCE_TOKENS, QUERY_HEADS * HEAD_SIZE)

def slot_table(routes):
    blocks = TOKENS // TOK_DEV
    flat_routes = routes.reshape(blocks, TOK_DEV * TOPK)
    onehot = (flat_routes[:, :, None] == jnp.arange(EXPERTS, dtype=jnp.int32)[None, None, :]).astype(jnp.int32)
    slot_rank = lax.optimization_barrier(jnp.sum((jnp.cumsum(onehot, axis=1) - 1) * onehot, axis=2))
    column = jnp.arange(blocks, dtype=jnp.int32)[:, None] * CAP + slot_rank
    route_ids = jnp.arange(TOKENS * TOPK, dtype=jnp.int32).reshape(blocks, TOK_DEV * TOPK)
    route_table = jnp.full((EXPERTS, blocks * CAP), TOKENS * TOPK, jnp.int32)
    return route_table.at[flat_routes.reshape(-1), column.reshape(-1)].set(route_ids.reshape(-1))

def expert_term(pieces, rows_padded, gates_padded):
    route_ids, gate_halves, up_halves, down_halves = pieces
    token_ids = route_ids // TOPK
    inputs = rows_padded[token_ids]
    summed = jnp.zeros((route_ids.shape[0], MODEL_WIDTH), jnp.float32)
    for which_half in range(2):
        entries = low_back(inputs)
        gate_pre = low_back(product(entries, gate_halves[which_half]))
        up_pre = low_back(product(entries, up_halves[which_half]))
        hidden = low(jax.nn.silu(gate_pre) * up_pre)
        summed = summed + low(product(hidden, down_halves[which_half]))
    expert_out = low_back(summed)
    weighted = expert_out * gates_padded[route_ids][:, None]
    return jnp.zeros((TOKENS + 1, MODEL_WIDTH), jnp.float32).at[token_ids].add(weighted)[:TOKENS]

def reference(tokens, segments, routes, norm1_gain, w_query, key_value_weight, w_output, norm2_gain, w_router, w_shgate, w_shup, w_shdown, w_exgate, w_exup, w_exdown, cotangent):
    route_table = slot_table(routes)
    sequence_batch = TOKENS // SEQUENCE_TOKENS

    def forward(tokens_in, gain_one, query_w, keyval_w, output_w, gain_two, router_w, shgate_w, shup_w, shdown_w, exgate_w, exup_w, exdown_w):
        first_normed = low(normalize(tokens_in, gain_one))
        query_rows = low_back(low(product(first_normed, query_w)))
        key_value_rows = low_back(low(product(first_normed, keyval_w)))
        attended_rows = lax.map(jax.checkpoint(attend_heads), (query_rows.reshape(sequence_batch, SEQUENCE_TOKENS, QUERY_HEADS * HEAD_SIZE), key_value_rows.reshape(sequence_batch, SEQUENCE_TOKENS, 2 * KEY_VALUE_HEADS * HEAD_SIZE), segments.reshape(sequence_batch, SEQUENCE_TOKENS)))
        attended_rows = low_back(low(attended_rows.reshape(TOKENS, QUERY_HEADS * HEAD_SIZE)))
        residual1 = tokens_in + low_back(product(attended_rows, output_w))
        second_normed = low(normalize(residual1, gain_two))
        logits = low_back(product(second_normed, router_w))
        gate_probs = softmax_rows(jnp.take_along_axis(logits, routes, axis=1))
        shared_gate = low_back(product(second_normed, shgate_w))
        shared_up = low_back(product(second_normed, shup_w))
        shared_out = low_back(product(low(jax.nn.silu(shared_gate) * shared_up), shdown_w))
        rows_padded = jnp.concatenate([second_normed, jnp.zeros((1, MODEL_WIDTH), jnp.float32)], axis=0)
        gates_padded = jnp.concatenate([gate_probs.reshape(-1), jnp.zeros((1,), jnp.float32)], axis=0)

        def accumulate(carried, pieces):
            return (carried + jax.checkpoint(expert_term)(pieces, rows_padded, gates_padded), None)
        stacked = (route_table, exgate_w.reshape(EXPERTS, 2, MODEL_WIDTH, EH // 2), exup_w.reshape(EXPERTS, 2, MODEL_WIDTH, EH // 2), exdown_w.reshape(EXPERTS, 2, EH // 2, MODEL_WIDTH))
        experts_out, unused = lax.scan(accumulate, jnp.zeros((TOKENS, MODEL_WIDTH), jnp.float32), stacked)
        return residual1 + shared_out + experts_out
    block_out, pullback = jax.vjp(forward, tokens.astype(jnp.float32), norm1_gain.astype(jnp.float32), w_query.astype(jnp.float32), key_value_weight.astype(jnp.float32), w_output.astype(jnp.float32), norm2_gain.astype(jnp.float32), w_router.astype(jnp.float32), w_shgate.astype(jnp.float32), w_shup.astype(jnp.float32), w_shdown.astype(jnp.float32), w_exgate.astype(jnp.float32), w_exup.astype(jnp.float32), w_exdown.astype(jnp.float32))
    gradients = pullback(cotangent.astype(jnp.float32))
    return (block_out.astype(jnp.bfloat16), gradients[0], gradients[1], gradients[2], gradients[3], gradients[4], gradients[5], gradients[6], gradients[7], gradients[8], gradients[9], gradients[10], gradients[11], gradients[12])
```

```python
import functools

import jax
import jax.numpy as jnp
from jax import lax
from jax.experimental import pallas as pl
from jax.experimental.pallas import tpu as pltpu
from jax.sharding import Mesh
from jax.sharding import PartitionSpec as P

QUERY_HEADS = 12
KEY_VALUE_HEADS = 4
HEAD_SIZE = 128
EXPERTS = 64
TOPK = 6
CAP = 24
EPSILON = 1e-05

F32 = jnp.float32
BF16 = jnp.bfloat16
MESH_ID = pl.DeviceIdType.MESH
AXES = ("z", "yl", "core", "yh", "xh", "xl")
SIZES = (4, 2, 2, 2, 2, 2)
EXPERT_AXES = ("z", "yl", "core", "yh", "xh")
COL_AXES = ("yh", "xh", "xl")

PARTS = (
    ("qkv", 2560, "yz"),
    ("outt", 1536, "yzx"),
    ("shgu", 2048, "zy"),
    ("shdt", 1024, "zy"),
    ("misc", 128, "yz"),
)
TOTAL = sum(part[1] for part in PARTS)


def rem(value, size):
    return lax.rem(value, jnp.int32(size))


def place():
    at = {name: lax.axis_index(name) for name in AXES}
    return {
        "x": at["xh"] * 2 + at["xl"],
        "y": at["yh"] * 2 + at["yl"],
        "z": at["z"],
        "core": at["core"],
    }


def device(axis, value):
    if axis == "x":
        return {"xh": value // 2, "xl": rem(value, 2)}
    if axis == "y":
        return {"yh": value // 2, "yl": rem(value, 2)}
    return {axis: value}


def greet(targets):
    barrier = pltpu.get_barrier_semaphore()
    for target in targets:
        pl.semaphore_signal(barrier, inc=1, device_id=target, device_id_type=MESH_ID)
    pl.semaphore_wait(barrier, len(targets))


class Wires:
    def __init__(self, send_sems, recv_sems, local_sems):
        self.send, self.recv, self.local = send_sems, recv_sems, local_sems
        self.used, self.used_local, self.started, self.kept = 0, 0, [], []

    def remote(self, source, target, where):
        copy = pltpu.make_async_remote_copy(
            src_ref=source,
            dst_ref=target,
            send_sem=self.send.at[self.used],
            recv_sem=self.recv.at[self.used],
            device_id=where,
            device_id_type=MESH_ID,
        )
        self.used += 1
        copy.start()
        self.started.append(copy)
        return copy

    def copy(self, source, target):
        copy = pltpu.make_async_copy(source, target, self.local.at[self.used_local])
        self.used_local += 1
        copy.start()
        return copy

    def finish(self):
        for copy in self.started:
            copy.wait_send()


def halves(width):
    first = width // 256 * 128 if width > 128 else width
    return first, width - first


def spread_rows(shape, swap):
    dense = lax.broadcasted_iota(jnp.int32, shape, 1 if swap else 0)
    padded = lax.broadcasted_iota(jnp.int32, shape, 0 if swap else 1)
    shift = jnp.zeros(shape, jnp.int32)
    for edge in (12, 24, 36):
        shift = shift + jnp.where(dense >= edge, 4, 0)
    return dense + shift == padded


def block_ref(ref, axes, me, axis, value, columns):
    spot = dict(me)
    spot[axis] = value
    z = slice(None) if "z" in axes else spot["z"]
    yl = slice(None) if "y" in axes else rem(spot["y"], 2)
    yh = slice(None) if "y" in axes else spot["y"] // 2
    return ref.at[z, yl, me["core"], yh, :, columns]


def gather_kernel(shard_ref, *rest):
    count = len(PARTS)
    outs = rest[:count]
    landed = rest[count]
    stages = rest[count + 1 : count + 1 + count]
    send_sems, recv_sems, local_sems = rest[count + 1 + count :]
    me = place()
    nxt = {axis: rem(me[axis] + 1, 4) for axis in "xyz"}
    opp = {axis: rem(me[axis] + 2, 4) for axis in "xyz"}
    prv = {axis: rem(me[axis] + 3, 4) for axis in "xyz"}
    sibling = {"core": 1 - me["core"]}
    greet(
        [device("x", nxt["x"]), device("x", opp["x"]), device("x", prv["x"])]
        + [device("y", nxt["y"]), device("y", prv["y"])]
        + [device("z", nxt["z"]), device("z", prv["z"]), sibling]
    )
    wires = Wires(send_sems, recv_sems, local_sems)
    first = [
        wires.remote(shard_ref, landed.at[me["x"]], device("x", where["x"]))
        for where in (nxt, prv, opp)
    ]
    own = wires.copy(shard_ref, landed.at[me["x"]])
    own.wait()
    for copy in first:
        copy.wait_recv()
    pick = spread_rows((48, 64), False).astype(BF16)
    runs, start = [], 0
    for index, (name, width, order) in enumerate(PARTS):
        for left in range(0, width, 512):
            size = min(512, width - left)
            piece = landed[:, :, start + left : start + left + size].reshape(64, size)
            stages[index][:, left : left + size] = jnp.dot(
                pick, piece, preferred_element_type=F32
            ).astype(BF16)
        start += width
        if len(order) == 3:
            quarter = width // 4
            columns = pl.ds(pl.multiple_of(me["x"] * quarter, 128), quarter)
        else:
            quarter, columns = width, pl.ds(0, width)
        runs.append(
            {
                "out": outs[index],
                "order": order,
                "width": quarter,
                "base": me["x"] * quarter if len(order) == 3 else 0,
                "columns": columns,
                "done": "",
                "stage": stages[index],
                "index": index,
            }
        )
        runs[-1]["own"] = wires.copy(
            stages[index].at[:, columns],
            outs[index].at[me["z"], rem(me["y"], 2), me["core"], me["y"] // 2, :, columns],
        )

    def part_columns(run, axis, value, which):
        if axis == "x":
            base = value * run["width"]
        else:
            base = run["base"]
        left, size = 0, run["width"]
        if which is not None:
            first_half, second_half = halves(run["width"])
            left, size = (0, first_half) if which == 0 else (first_half, second_half)
        if isinstance(base, int):
            return pl.ds(base + left, size)
        return pl.ds(pl.multiple_of(base + left, 128), size)

    def blocks(run, axis, value, which=None):
        columns = part_columns(run, axis, value, which)
        return block_ref(run["out"], run["done"], me, axis, value, columns)

    def begin(run, axis):
        target = blocks(run, axis, me[axis])
        run["forth"] = wires.remote(target, target, device(axis, nxt[axis]))
        run["back"] = wires.remote(target, target, device(axis, prv[axis]))

    def forward(run, axis):
        run["forth"].wait_recv()
        source = blocks(run, axis, prv[axis], 0)
        run["more"] = [wires.remote(source, source, device(axis, nxt[axis]))]
        run["back"].wait_recv()
        if halves(run["width"])[1] > 0:
            source = blocks(run, axis, nxt[axis], 1)
            run["more"].append(wires.remote(source, source, device(axis, prv[axis])))

    def share(run, axis, value):
        source = blocks(run, axis, value)
        run["shared"].append(wires.remote(source, source, sibling))

    for run in runs:
        run["own"].wait()
        begin(run, run["order"][0])
    most = max(len(run["order"]) for run in runs)
    for step in range(most):
        active = [run for run in runs if step < len(run["order"])]
        for run in active:
            forward(run, run["order"][step])
            if step == len(run["order"]) - 1:
                axis = run["order"][step]
                share(run, axis, prv[axis])
                share(run, axis, nxt[axis])
        for run in active:
            axis = run["order"][step]
            for copy in run["more"]:
                copy.wait_recv()
            if step < len(run["order"]) - 1:
                run["done"] = run["done"] + axis
                following = run["order"][step + 1]
                begin(run, following)
                if step + 1 == len(run["order"]) - 1:
                    run["shared"] = []
                    share(run, following, me[following])
            else:
                share(run, axis, opp[axis])
    for run in runs:
        for copy in run["shared"]:
            copy.wait_recv()
    wires.finish()


def gather_weights(shard):
    shapes = [jax.ShapeDtypeStruct((4, 2, 2, 2, 48, width), BF16) for _, width, _ in PARTS]
    copies = 160
    return pl.pallas_call(
        gather_kernel,
        out_shape=shapes,
        in_specs=[pl.BlockSpec(memory_space=pltpu.VMEM)],
        out_specs=[pl.BlockSpec(memory_space=pl.ANY)] * len(PARTS),
        scratch_shapes=[pltpu.VMEM((4, 16, TOTAL), BF16)]
        + [pltpu.VMEM((48, width), BF16) for _, width, _ in PARTS]
        + [
            pltpu.SemaphoreType.DMA((copies,)),
            pltpu.SemaphoreType.DMA((copies,)),
            pltpu.SemaphoreType.DMA((16,)),
        ],
        compiler_params=pltpu.CompilerParams(
            collective_id=0, has_side_effects=True, vmem_limit_bytes=16 * 1024 * 1024
        ),
    )(shard)


def sum_kernel(*refs):
    count = len(PARTS)
    grads = refs[:count]
    outs = refs[count : 2 * count]
    rest = refs[2 * count :]
    own = rest[:count]
    theirs = rest[count : 2 * count]
    near1 = rest[2 * count : 3 * count]
    near2 = rest[3 * count : 4 * count]
    ends = rest[4 * count : 5 * count]
    arrived = rest[5 * count : 6 * count]
    send_sems, recv_sems, local_sems = rest[6 * count :]
    me = place()
    core = me["core"]
    nxt = {axis: rem(me[axis] + 1, 4) for axis in "xyz"}
    opp = {axis: rem(me[axis] + 2, 4) for axis in "xyz"}
    prv = {axis: rem(me[axis] + 3, 4) for axis in "xyz"}
    sibling = {"core": 1 - core}
    greet(
        [device("x", nxt["x"]), device("x", opp["x"]), device("x", prv["x"])]
        + [device("y", nxt["y"]), device("y", prv["y"])]
        + [device("z", nxt["z"]), device("z", prv["z"]), sibling]
    )
    wires = Wires(send_sems, recv_sems, local_sems)

    def spot(left_axes, axis, value, with_core):
        at = dict(me)
        if axis is not None:
            at[axis] = value
        whole = [name for name in left_axes if name != axis]
        z = slice(None) if "z" in whole else at["z"]
        yl = slice(None) if "y" in whole else rem(at["y"], 2)
        yh = slice(None) if "y" in whole else at["y"] // 2
        return (z, yl) + (() if with_core is None else (with_core,)) + (yh,)

    def lead(left_axes, axis):
        dims = []
        for name in ("z", "y"):
            if name in left_axes and name != axis:
                dims += [4] if name == "z" else [2, 2]
        return dims

    def loop_over(dims, body):
        total = 1
        for size in dims:
            total *= size

        def step(flat, carry):
            index, rest_flat = [], flat
            for size in reversed(dims):
                index.append(rem(rest_flat, size))
                rest_flat = rest_flat // size
            body(tuple(reversed(index)))
            return carry

        if total == 1:
            body(())
        else:
            lax.fori_loop(0, total, step, 0)

    def add_into(target, sources, dims):
        def body(index):
            for row in range(0, 48, 16):
                at = index + (pl.ds(row, 16),)
                value = target[at].astype(F32)
                for source in sources:
                    value = value + source[at].astype(F32)
                target[at] = value.astype(target.dtype)

        loop_over(dims, body)

    runs = []
    for index, (name, width, order) in enumerate(PARTS):
        quarter = width // 4 if len(order) == 3 else width
        runs.append(
            {
                "index": index,
                "name": name,
                "order": order[::-1],
                "width": quarter,
                "full": width,
                "left": "zy",
                "turn": 0,
            }
        )

    def columns_of(run, axis, value, which):
        if len(run["order"]) == 3:
            base = (value if axis == "x" else me["x"]) * run["width"]
        else:
            base = 0
        left, size = 0, run["width"]
        if which is not None:
            first_half, second_half = halves(run["width"])
            left, size = (0, first_half) if which == 0 else (first_half, second_half)
        if isinstance(base, int):
            return pl.ds(base + left, size)
        return pl.ds(pl.multiple_of(base + left, 128), size)

    def chunk(run, axis, value, which=None, ref=None, with_core=None):
        ref = own[run["index"]] if ref is None else ref
        columns = columns_of(run, axis, value, which)
        return ref.at[spot(run["left"], axis, value, with_core) + (slice(None), columns)]

    def pair(run, axis, value):
        index = run["index"]
        give = wires.remote(
            chunk(run, axis, value, None, grads[index], 1 - core),
            chunk(run, axis, value, None, theirs[index]),
            sibling,
        )
        keep = wires.copy(
            chunk(run, axis, value, None, grads[index], core), chunk(run, axis, value)
        )
        return give, keep

    def join(run, axis, value, copies):
        copies[0].wait_recv()
        copies[1].wait()
        add_into(
            chunk(run, axis, value),
            [chunk(run, axis, value, None, theirs[run["index"]])],
            lead(run["left"], axis),
        )

    def slots(run, axis):
        dims = lead(run["left"], axis)
        phase = run["turn"]
        ref = (near1 if phase == 0 else near2)[run["index"]]
        if phase == 2:
            ref = ends[run["index"]]
        if not dims:
            ref = ref.at[:, pl.ds(0, 48)]
        return ref.at[0], ref.at[1], ref.at[2], dims

    def part(ref, run, which, dims):
        first_half, second_half = halves(run["width"])
        columns = pl.ds(0, first_half) if which == 0 else pl.ds(first_half, second_half)
        return ref.at[(slice(None),) * len(dims) + (slice(None), columns)]

    def ring_open(run, axis):
        from_prv, from_nxt, passing, dims = slots(run, axis)
        run["passing"] = [
            wires.remote(
                chunk(run, axis, opp[axis], 0), part(passing, run, 0, dims), device(axis, nxt[axis])
            )
        ]
        if halves(run["width"])[1]:
            run["passing"].append(
                wires.remote(
                    chunk(run, axis, opp[axis], 1),
                    part(passing, run, 1, dims),
                    device(axis, prv[axis]),
                )
            )

    def ring_near(run, axis):
        from_prv, from_nxt, passing, dims = slots(run, axis)
        run["near"] = []
        if halves(run["width"])[1]:
            run["near"].append(
                wires.remote(
                    chunk(run, axis, nxt[axis], 1),
                    part(from_prv, run, 1, dims),
                    device(axis, nxt[axis]),
                )
            )
        run["near"].append(
            wires.remote(
                chunk(run, axis, prv[axis], 0), part(from_nxt, run, 0, dims), device(axis, prv[axis])
            )
        )

    def ring_pass(run, axis):
        from_prv, from_nxt, passing, dims = slots(run, axis)
        run["passing"][0].wait_recv()
        add_into(chunk(run, axis, nxt[axis], 0), [part(passing, run, 0, dims)], dims)
        run["near"].append(
            wires.remote(
                chunk(run, axis, nxt[axis], 0), part(from_prv, run, 0, dims), device(axis, nxt[axis])
            )
        )
        if halves(run["width"])[1]:
            run["passing"][1].wait_recv()
            add_into(chunk(run, axis, prv[axis], 1), [part(passing, run, 1, dims)], dims)
            run["near"].append(
                wires.remote(
                    chunk(run, axis, prv[axis], 1),
                    part(from_nxt, run, 1, dims),
                    device(axis, prv[axis]),
                )
            )

    def ring_close(run, axis):
        from_prv, from_nxt, passing, dims = slots(run, axis)
        for copy in run["near"]:
            copy.wait_recv()
        if halves(run["width"])[1]:
            add_into(chunk(run, axis, me[axis]), [from_prv, from_nxt], dims)
        else:
            add_into(chunk(run, axis, me[axis]), [from_prv, from_nxt], dims)
        run["left"] = run["left"].replace(axis, "")
        run["turn"] += 1

    begun = []
    for where in (opp, nxt, prv, me):
        begun.append([pair(run, run["order"][0], where[run["order"][0]]) for run in runs])
    for run, copies in zip(runs, begun[0]):
        axis = run["order"][0]
        join(run, axis, opp[axis], copies)
        ring_open(run, axis)
    for run, nexts, prevs in zip(runs, begun[1], begun[2]):
        axis = run["order"][0]
        join(run, axis, nxt[axis], nexts)
        join(run, axis, prv[axis], prevs)
        ring_near(run, axis)
    for run, copies in zip(runs, begun[3]):
        axis = run["order"][0]
        join(run, axis, me[axis], copies)
    for run in runs:
        ring_pass(run, run["order"][0])
    for run in runs:
        ring_close(run, run["order"][0])
        following = run["order"][1]
        ring_open(run, following)
        ring_near(run, following)
    for run in runs:
        ring_pass(run, run["order"][1])
    for run in runs:
        ring_close(run, run["order"][1])
        if len(run["order"]) == 3:
            following = run["order"][2]
            ring_open(run, following)
            ring_near(run, following)
    for run in runs:
        if len(run["order"]) == 3:
            ring_pass(run, run["order"][2])
            ring_close(run, run["order"][2])
    lasts = []
    for run in runs:
        index, width = run["index"], run["width"]
        summed = own[index].at[me["z"], rem(me["y"], 2), me["y"] // 2]
        exact = lax.Precision.HIGHEST if summed.dtype == F32 else None
        pick = spread_rows((64, 48), True).astype(summed.dtype)
        target = arrived[index]
        staging = ends[index].at[3] if len(run["order"]) == 3 else near2[index].at[3]
        base = me["x"] * width if len(run["order"]) == 3 else 0
        for left in range(0, width, 512):
            size = min(512, width - left)
            if isinstance(base, int):
                columns = pl.ds(left, size)
            else:
                columns = pl.ds(pl.multiple_of(base + left, 128), size)
            staging[:, left : left + size] = jnp.dot(
                pick, summed[:, columns], preferred_element_type=F32, precision=exact
            ).astype(staging.dtype)
        if len(run["order"]) == 3:
            columns = pl.ds(pl.multiple_of(base, 128), width)
            lands = target.at[:, columns]
        else:
            lands = target.at[me["x"]]
        run["copies"] = []
        for where in (nxt, opp, prv):
            row = pl.ds(pl.multiple_of(where["x"] * 16, 16), 16)
            run["copies"].append(
                wires.remote(staging.at[row], lands, device("x", where["x"]))
            )
        row = pl.ds(pl.multiple_of(me["x"] * 16, 16), 16)
        run["keep"] = wires.copy(staging.at[row], lands)
    for run in runs:
        index = run["index"]
        run["keep"].wait()
        for copy in run["copies"]:
            copy.wait_recv()
        if len(run["order"]) == 3:
            outs[index][...] = arrived[index][...].astype(F32)
        else:
            value = arrived[index][0].astype(F32)
            for place_x in range(1, 4):
                value = value + arrived[index][place_x].astype(F32)
            outs[index][...] = value
    wires.finish()


def sum_gradients(grads):
    scratch_own, scratch_theirs, near1, near2, ends, arrived = [], [], [], [], [], []
    for name, width, order in PARTS:
        kind = F32 if name == "misc" else BF16
        scratch_own.append(pltpu.VMEM((4, 2, 2, 48, width), kind))
        scratch_theirs.append(pltpu.VMEM((4, 2, 2, 48, width), kind))
        if order == "yz":
            near1.append(pltpu.VMEM((3, 2, 2, 48, width), kind))
            near2.append(pltpu.VMEM((4, 64, width), kind))
        elif order == "zy":
            near1.append(pltpu.VMEM((3, 4, 48, width), kind))
            near2.append(pltpu.VMEM((4, 64, width), kind))
        else:
            quarter = width // 4
            near1.append(pltpu.VMEM((3, 4, 2, 2, 48, quarter), kind))
            near2.append(pltpu.VMEM((3, 2, 2, 48, quarter), kind))
        ends.append(pltpu.VMEM((4, 64, width // 4 if len(order) == 3 else 128), kind))
        arrived.append(pltpu.VMEM((16, width) if len(order) == 3 else (4, 16, width), kind))
    copies = 160
    return pl.pallas_call(
        sum_kernel,
        out_shape=[jax.ShapeDtypeStruct((16, width), F32) for _, width, _ in PARTS],
        in_specs=[pl.BlockSpec(memory_space=pl.ANY)] * len(PARTS),
        out_specs=[pl.BlockSpec(memory_space=pltpu.VMEM)] * len(PARTS),
        scratch_shapes=scratch_own
        + scratch_theirs
        + near1
        + near2
        + ends
        + arrived
        + [
            pltpu.SemaphoreType.DMA((copies,)),
            pltpu.SemaphoreType.DMA((copies,)),
            pltpu.SemaphoreType.DMA((48,)),
        ],
        compiler_params=pltpu.CompilerParams(
            collective_id=1, has_side_effects=True, vmem_limit_bytes=56 * 1024 * 1024
        ),
    )(*grads)


def col_device(col):
    return {"yh": col // 4, "xh": rem(col // 2, 2), "xl": rem(col, 2)}


def col_index():
    return lax.axis_index("yh") * 4 + lax.axis_index("xh") * 2 + lax.axis_index("xl")


def later_kernel(own_ref, out_ref, send_sems, recv_sems, local_sem):
    me = col_index()
    greet([col_device(rem(me + far, 8)) for far in range(1, 8)])

    def copy(far):
        return pltpu.make_async_remote_copy(
            src_ref=own_ref,
            dst_ref=out_ref.at[me],
            send_sem=send_sems.at[far],
            recv_sem=recv_sems.at[far],
            device_id=col_device(rem(me + far, 8)),
            device_id_type=MESH_ID,
        )

    for far in range(7, 0, -1):

        @pl.when(me + far < 8)
        def _():
            copy(far).start()

    keep = pltpu.make_async_copy(own_ref, out_ref.at[me], local_sem)
    keep.start()
    for far in range(1, 8):

        @pl.when(me + far < 8)
        def _():
            out_ref[me + far] = jnp.zeros(own_ref.shape, own_ref.dtype)

    keep.wait()
    for far in range(1, 8):

        @pl.when(me >= far)
        def _():
            copy(far).wait_recv()

        @pl.when(me + far < 8)
        def _():
            copy(far).wait_send()


def to_later(rows):
    return pl.pallas_call(
        later_kernel,
        out_shape=jax.ShapeDtypeStruct((8,) + rows.shape, rows.dtype),
        in_specs=[pl.BlockSpec(memory_space=pltpu.VMEM)],
        out_specs=pl.BlockSpec(memory_space=pltpu.VMEM),
        scratch_shapes=[
            pltpu.SemaphoreType.DMA((8,)),
            pltpu.SemaphoreType.DMA((8,)),
            pltpu.SemaphoreType.DMA,
        ],
        compiler_params=pltpu.CompilerParams(
            collective_id=2, has_side_effects=True, vmem_limit_bytes=16 * 1024 * 1024
        ),
    )(rows)


def earlier_kernel(blocks_ref, out_ref, landed, send_sems, recv_sems):
    me = col_index()
    greet([col_device(rem(me + far, 8)) for far in range(1, 8)])

    def copy(far):
        return pltpu.make_async_remote_copy(
            src_ref=blocks_ref.at[rem(me + 8 - far, 8)],
            dst_ref=landed.at[far],
            send_sem=send_sems.at[far],
            recv_sem=recv_sems.at[far],
            device_id=col_device(rem(me + 8 - far, 8)),
            device_id_type=MESH_ID,
        )

    for far in range(7, 0, -1):

        @pl.when(me >= far)
        def _():
            copy(far).start()

    for far in range(1, 8):

        @pl.when(me + far < 8)
        def _():
            copy(far).wait_recv()

        @pl.when(me + far >= 8)
        def _():
            landed[far] = jnp.zeros(landed.shape[1:], landed.dtype)

    rows = out_ref.shape[0]
    for row in range(0, rows, 16):
        at = pl.ds(row, 16)
        value = blocks_ref[me, at].astype(F32)
        for far in range(1, 8):
            value = value + landed[far, at].astype(F32)
        out_ref[at] = value.astype(out_ref.dtype)
    for far in range(1, 8):

        @pl.when(me >= far)
        def _():
            copy(far).wait_send()


def sum_earlier(blocks):
    return pl.pallas_call(
        earlier_kernel,
        out_shape=jax.ShapeDtypeStruct(blocks.shape[1:], blocks.dtype),
        in_specs=[pl.BlockSpec(memory_space=pltpu.VMEM)],
        out_specs=pl.BlockSpec(memory_space=pltpu.VMEM),
        scratch_shapes=[
            pltpu.VMEM(blocks.shape, blocks.dtype),
            pltpu.SemaphoreType.DMA((8,)),
            pltpu.SemaphoreType.DMA((8,)),
        ],
        compiler_params=pltpu.CompilerParams(
            collective_id=3, has_side_effects=True, vmem_limit_bytes=16 * 1024 * 1024
        ),
    )(blocks)


def inverse_rms(residual):
    return lax.rsqrt(jnp.mean(residual * residual, axis=-1, keepdims=True) + EPSILON)


def contract(left_side, right_side, left_dim, right_dim):
    return lax.dot_general(
        left_side,
        right_side,
        (((left_dim,), (right_dim,)), ((), ())),
        preferred_element_type=F32,
    )


def gated_unit(gate_pre, up_pre):
    return jax.nn.silu(gate_pre) * up_pre


def norm_backward(residual, norm_scale, gain_row, grad_normed):
    weighted = grad_normed * gain_row
    inner_sum = jnp.mean(weighted * residual, axis=-1, keepdims=True)
    grad_residual = (
        norm_scale * weighted - residual * norm_scale * norm_scale * norm_scale * inner_sum
    )
    grad_gain = jnp.sum(grad_normed * residual * norm_scale, axis=0)
    return (grad_residual, grad_gain)


def to_experts(rows):
    return lax.all_to_all(rows, EXPERT_AXES, split_axis=0, concat_axis=0, tiled=True)


def swap_halves(block):
    return lax.ppermute(block, "xl", [(0, 1), (1, 0)])


def shards(
    tokens,
    segments,
    routes,
    norm1_gain,
    w_query,
    key_value_weight,
    w_output,
    norm2_gain,
    w_router,
    w_shgate,
    w_shup,
    w_shdown,
    w_exgate,
    w_exup,
    w_exdown,
    cotangent,
):
    local_rows, feature_count = tokens.shape
    sequence_length = local_rows * 8
    heads_per_group = QUERY_HEADS // KEY_VALUE_HEADS
    key_value_width = KEY_VALUE_HEADS * HEAD_SIZE
    score_scale = HEAD_SIZE ** (-0.5)

    own_gate, own_up, own_down = w_exgate[0], w_exup[0], w_exdown[0]
    other_gate, other_up, other_down = (
        swap_halves(own_gate),
        swap_halves(own_up),
        swap_halves(own_down),
    )

    shard = jnp.concatenate(
        [
            w_query,
            key_value_weight,
            w_output.T,
            w_shgate,
            w_shup,
            w_shdown.T,
            w_router,
            norm1_gain[:, None],
            norm2_gain[:, None],
            jnp.zeros((12, 62), BF16),
        ],
        axis=1,
    )
    shard = jnp.concatenate([shard, jnp.zeros((4, TOTAL), BF16)], axis=0)
    qkv_w, outt_w, shgu_w, shdt_w, misc_w = [
        gathered.reshape(feature_count, gathered.shape[-1]) for gathered in gather_weights(shard)
    ]
    router_w = misc_w[:, :EXPERTS]
    gain_first = misc_w[:, EXPERTS].astype(F32)
    gain_second = misc_w[:, EXPERTS + 1].astype(F32)

    residual0 = tokens.astype(F32)
    scale_first = inverse_rms(residual0)
    first_normed = (residual0 * scale_first * gain_first).astype(BF16)
    qkv_rows = jnp.dot(first_normed, qkv_w, preferred_element_type=F32).astype(BF16)
    query_rows = qkv_rows[:, : QUERY_HEADS * HEAD_SIZE]
    own_segments = segments.astype(BF16)
    key_value_rows = jnp.concatenate(
        [
            qkv_rows[:, QUERY_HEADS * HEAD_SIZE :],
            jnp.broadcast_to(own_segments[:, None], (local_rows, 128)),
        ],
        axis=1,
    )
    every = to_later(key_value_rows).reshape(sequence_length, 2 * key_value_width + 128)
    all_segments = every[:, 2 * key_value_width]
    key_matrix = every[:, :key_value_width].reshape(sequence_length, KEY_VALUE_HEADS, HEAD_SIZE)
    value_matrix = every[:, key_value_width : 2 * key_value_width].reshape(
        sequence_length, KEY_VALUE_HEADS, HEAD_SIZE
    )
    query_head_count = query_rows.reshape(local_rows, KEY_VALUE_HEADS, heads_per_group, HEAD_SIZE)
    query_place = col_index() * local_rows + jnp.arange(local_rows, dtype=jnp.int32)
    key_place = jnp.arange(sequence_length, dtype=jnp.int32)
    allowed = (key_place[None, :] <= query_place[:, None]) & (
        all_segments[None, :] == own_segments[:, None]
    )

    def masked_scores():
        raw_scores = (
            jnp.einsum("tkgd,skd->kgts", query_head_count, key_matrix, preferred_element_type=F32)
            * score_scale
        )
        return jnp.where(allowed, raw_scores, -1e30)

    scores = masked_scores()
    row_max = jnp.max(scores, axis=-1, keepdims=True)
    shifted = jnp.exp(scores - row_max)
    row_total = jnp.sum(shifted, axis=-1, keepdims=True)
    log_total = row_max + jnp.log(row_total)
    weights_low = (shifted / row_total).astype(BF16)
    attended_rows = jnp.einsum(
        "kgts,skd->tkgd", weights_low, value_matrix, preferred_element_type=F32
    )
    attended_rows = attended_rows.reshape(local_rows, QUERY_HEADS * HEAD_SIZE).astype(BF16)
    residual1 = residual0 + contract(attended_rows, outt_w, 1, 1)
    scale_second = inverse_rms(residual1)
    second_normed = (residual1 * scale_second * gain_second).astype(BF16)

    logits = jnp.dot(second_normed, router_w, preferred_element_type=F32)
    expert_ids = jnp.arange(EXPERTS, dtype=jnp.int32)
    named = jnp.any(routes[:, :, None] == expert_ids[None, None, :], axis=1)
    named_low = named.astype(BF16)
    chosen = jnp.where(named, logits, -jnp.inf)
    chosen_exp = jnp.where(named, jnp.exp(chosen - jnp.max(chosen, axis=1, keepdims=True)), 0.0)
    gates = chosen_exp / jnp.sum(chosen_exp, axis=1, keepdims=True)
    token_ids = jnp.arange(local_rows, dtype=jnp.int32)
    before = (token_ids[None, :] <= token_ids[:, None]).astype(BF16)
    rank = jnp.dot(before, named_low, preferred_element_type=F32) * named.astype(F32)
    slot_count = EXPERTS * CAP
    slot_ids = jnp.arange(slot_count, dtype=jnp.int32)
    widen = (slot_ids[None, :] // CAP == expert_ids[:, None]).astype(BF16)
    rank_wide = jnp.dot(rank.astype(BF16), widen, preferred_element_type=F32)
    slots = rank_wide == (slot_ids % CAP + 1).astype(F32)[None, :]
    slots_low = slots.astype(BF16)
    gates_wide = jnp.dot(
        gates, widen.astype(F32), precision=lax.Precision.HIGHEST, preferred_element_type=F32
    )
    slot_gates = jnp.where(slots, gates_wide, 0.0)

    def dispatch(rows):
        return rows.reshape(EXPERTS, CAP, feature_count)

    received = to_experts(dispatch(contract(slots_low, second_normed, 0, 0).astype(BF16)))
    gate_column = jnp.sum(slot_gates, axis=0)[:, None]
    sent_grads = (gate_column * contract(slots_low, cotangent, 0, 0)).astype(BF16)
    grad_received = to_experts(dispatch(sent_grads))
    received = received.reshape(slot_count, feature_count)
    grad_received = grad_received.reshape(slot_count, feature_count)

    shared_pre = jnp.dot(second_normed, shgu_w, preferred_element_type=F32)
    shared_gate, shared_up = shared_pre[:, :1024], shared_pre[:, 1024:]
    shared_hidden = gated_unit(shared_gate, shared_up).astype(BF16)
    shared_out = contract(shared_hidden, shdt_w, 1, 1)
    grad_shdt = contract(cotangent, shared_hidden, 0, 0).astype(BF16)
    grad_shared_hidden = jnp.dot(cotangent, shdt_w, preferred_element_type=F32)
    unused_shared, pull_shared = jax.vjp(gated_unit, shared_gate, shared_up)
    grad_shared_gate, grad_shared_up = pull_shared(grad_shared_hidden)
    grad_shared = jnp.concatenate(
        [grad_shared_gate.astype(BF16), grad_shared_up.astype(BF16)], axis=1
    )
    grad_shgu = contract(second_normed, grad_shared, 0, 0).astype(BF16)
    grad_second = contract(grad_shared, shgu_w, 1, 1)

    def units(first, second):
        left = jnp.dot(received, first, preferred_element_type=F32)
        right = jnp.dot(received, second, preferred_element_type=F32)
        return left, right

    sums = []
    half_out = None
    grad_rows = None
    for gate_w, up_w, down_w in (
        (own_gate, own_up, own_down),
        (other_gate, other_up, other_down),
    ):
        gate_units, up_units = units(gate_w, up_w)
        hidden = gated_unit(gate_units, up_units).astype(BF16)
        part_out = jnp.dot(hidden, down_w, preferred_element_type=F32)
        half_out = part_out if half_out is None else half_out + part_out
        grad_hidden = contract(grad_received, down_w, 1, 1)
        unused_units, pull_units = jax.vjp(gated_unit, gate_units, up_units)
        grad_gate_units, grad_up_units = pull_units(grad_hidden)
        grad_gate_low = grad_gate_units.astype(BF16)
        grad_up_low = grad_up_units.astype(BF16)
        part_rows = contract(grad_gate_low, gate_w, 1, 1) + contract(grad_up_low, up_w, 1, 1)
        grad_rows = part_rows if grad_rows is None else grad_rows + part_rows
        sums.append(
            (
                contract(received, grad_gate_low, 0, 0),
                contract(received, grad_up_low, 0, 0),
                contract(hidden, grad_received, 0, 0),
            )
        )
    returned = to_experts(dispatch(half_out.astype(BF16))).reshape(slot_count, feature_count)
    grad_returned = to_experts(dispatch(grad_rows.astype(BF16))).reshape(slot_count, feature_count)
    grad_exgate, grad_exup, grad_exdown = [
        (mine + swap_halves(theirs.astype(BF16)).astype(F32))[None]
        for mine, theirs in zip(sums[0], sums[1])
    ]

    gates_high = slot_gates.astype(BF16)
    gates_rest = (slot_gates - gates_high.astype(F32)).astype(BF16)
    expert_mix = jnp.dot(gates_high, returned, preferred_element_type=F32) + jnp.dot(
        gates_rest, returned, preferred_element_type=F32
    )
    block_out = (residual1 + shared_out + expert_mix).astype(BF16)
    along = jnp.where(slots, contract(cotangent, returned, 1, 1), 0.0)
    grad_gates = jnp.dot(
        along, widen.T.astype(F32), precision=lax.Precision.HIGHEST, preferred_element_type=F32
    )
    grad_logits = (
        gates * (grad_gates - jnp.sum(gates * grad_gates, axis=1, keepdims=True))
    ).astype(BF16)
    grad_router = contract(second_normed, grad_logits, 0, 0)
    grad_second = grad_second + contract(grad_logits, router_w, 1, 1)
    grad_second = grad_second + jnp.dot(slots_low, grad_returned, preferred_element_type=F32)
    grad_norm_second, grad_gain_second = norm_backward(
        residual1, scale_second, gain_second, grad_second
    )
    grad_residual1 = cotangent.astype(F32) + grad_norm_second
    grad_attn_low = grad_residual1.astype(BF16)
    grad_outt = contract(grad_attn_low, attended_rows, 0, 0).astype(BF16)
    attended_gradient = jnp.dot(grad_attn_low, outt_w, preferred_element_type=F32).astype(BF16)
    weights_again = jnp.exp(masked_scores() - log_total)
    heads_gradient = attended_gradient.reshape(
        local_rows, KEY_VALUE_HEADS, heads_per_group, HEAD_SIZE
    )
    grad_weights = jnp.einsum(
        "tkgd,skd->kgts", heads_gradient, value_matrix, preferred_element_type=F32
    )
    inner_sum = jnp.sum(weights_again * grad_weights, axis=-1, keepdims=True)
    grad_scores = (weights_again * (grad_weights - inner_sum)).astype(BF16)
    grad_queries = (
        jnp.einsum("kgts,skd->tkgd", grad_scores, key_matrix, preferred_element_type=F32)
        * score_scale
    )
    grad_queries = grad_queries.reshape(local_rows, QUERY_HEADS * HEAD_SIZE).astype(BF16)
    grad_keys = (
        jnp.einsum("kgts,tkgd->skd", grad_scores, query_head_count, preferred_element_type=F32)
        * score_scale
    )
    grad_values = jnp.einsum(
        "kgts,tkgd->skd",
        weights_again.astype(BF16),
        heads_gradient,
        preferred_element_type=F32,
    )
    partial_keyvals = jnp.concatenate(
        [
            grad_keys.reshape(sequence_length, key_value_width),
            grad_values.reshape(sequence_length, key_value_width),
        ],
        axis=1,
    ).astype(BF16)
    grad_keyvals = sum_earlier(partial_keyvals.reshape(8, local_rows, 2 * key_value_width))
    grad_qkv_rows = jnp.concatenate([grad_queries, grad_keyvals], axis=1)
    grad_qkv = contract(first_normed, grad_qkv_rows, 0, 0).astype(BF16)
    grad_first = contract(grad_qkv_rows, qkv_w, 1, 1)
    grad_norm_first, grad_gain_first = norm_backward(residual0, scale_first, gain_first, grad_first)
    grad_tokens = grad_residual1 + grad_norm_first
    grad_misc = jnp.concatenate(
        [
            grad_router,
            grad_gain_first[:, None],
            grad_gain_second[:, None],
            jnp.zeros((feature_count, 62), F32),
        ],
        axis=1,
    )
    summed = sum_gradients(
        [
            grad.reshape(4, 2, 2, 2, 48, grad.shape[-1])
            for grad in (grad_qkv, grad_outt, grad_shgu, grad_shdt, grad_misc)
        ]
    )
    sum_qkv, sum_outt, sum_shgu, sum_shdt, sum_misc = [piece[:12] for piece in summed]
    return (
        block_out,
        grad_tokens,
        sum_misc[:, EXPERTS],
        sum_qkv[:, :1536],
        sum_qkv[:, 1536:],
        sum_outt.T,
        sum_misc[:, EXPERTS + 1],
        sum_misc[:, :EXPERTS],
        sum_shgu[:, :1024],
        sum_shgu[:, 1024:],
        sum_shdt.T,
        grad_exgate,
        grad_exup,
        grad_exdown,
    )


def solution(mesh):
    fine = Mesh(mesh.devices.reshape(SIZES), AXES)
    rows = P(AXES, None)
    columns = P(None, AXES)
    flat = P(AXES)
    blocks = P(AXES, None, None)
    in_specs = (
        rows,
        flat,
        rows,
        flat,
        rows,
        rows,
        columns,
        flat,
        rows,
        rows,
        rows,
        columns,
        blocks,
        blocks,
        blocks,
        rows,
    )
    out_specs = (
        rows,
        rows,
        flat,
        rows,
        rows,
        columns,
        flat,
        rows,
        rows,
        rows,
        columns,
        blocks,
        blocks,
        blocks,
    )
    return jax.shard_map(shards, mesh=fine, in_specs=in_specs, out_specs=out_specs, check_vma=False)
```

```python
import functools

import jax
import jax.numpy as jnp
from jax import lax
from jax.experimental import pallas as pl
from jax.experimental.pallas import tpu as pltpu
from jax.sharding import Mesh
from jax.sharding import PartitionSpec as P

QUERY_HEADS = 12
KEY_VALUE_HEADS = 4
HEAD_SIZE = 128
EXPERTS = 64
TOPK = 6
CAP = 24
EPSILON = 1e-05

F32 = jnp.float32
BF16 = jnp.bfloat16
MESH_ID = pl.DeviceIdType.MESH
AXES = ("z", "yl", "core", "yh", "xh", "xl")
SIZES = (4, 2, 2, 2, 2, 2)
EXPERT_AXES = ("z", "yl", "yh", "xh", "xl")
COL_AXES = ("yh", "xh", "xl")

PARTS = (
    ("outt", 1536, "yzx"),
    ("misc", 128, "yz"),
    ("qkv", 2560, "yz"),
    ("shgu", 2048, "zy"),
    ("shdt", 1024, "zy"),
)
HALF = 256
EXPERT_SEM = 156
TOTAL = sum(part[1] for part in PARTS)


def rem(value, size):
    return lax.rem(value, jnp.int32(size))


def place():
    at = {name: lax.axis_index(name) for name in AXES}
    return {
        "x": at["xh"] * 2 + at["xl"],
        "y": at["yh"] * 2 + at["yl"],
        "z": at["z"],
        "core": at["core"],
    }


def device(axis, value):
    if axis == "x":
        return {"xh": value // 2, "xl": rem(value, 2)}
    if axis == "y":
        return {"yh": value // 2, "yl": rem(value, 2)}
    return {axis: value}


def greet(targets):
    barrier = pltpu.get_barrier_semaphore()
    for target in targets:
        pl.semaphore_signal(barrier, inc=1, device_id=target, device_id_type=MESH_ID)
    pl.semaphore_wait(barrier, len(targets))


class Wires:
    def __init__(self, send_sems, recv_sems, local_sems):
        self.send, self.recv, self.local = send_sems, recv_sems, local_sems
        self.used, self.used_local, self.started, self.kept = 0, 0, [], []

    def remote(self, source, target, where):
        copy = pltpu.make_async_remote_copy(
            src_ref=source,
            dst_ref=target,
            send_sem=self.send.at[self.used],
            recv_sem=self.recv.at[self.used],
            device_id=where,
            device_id_type=MESH_ID,
        )
        self.used += 1
        copy.start()
        self.started.append(copy)
        return copy

    def copy(self, source, target):
        copy = pltpu.make_async_copy(source, target, self.local.at[self.used_local])
        self.used_local += 1
        copy.start()
        return copy

    def finish(self):
        for copy in self.started:
            copy.wait_send()


def balanced_offsets():
    left = [(x, y, z) for x in range(4) for y in range(4) for z in range(4) if x + y + z > 0]
    load, order = [0] * 6, []

    def uses(offset):
        used = [0] * 6
        for axis, hops in enumerate(offset):
            used[2 * axis] += hops in (1, 2)
            used[2 * axis + 1] += hops in (2, 3)
        return used

    def cost(offset):
        used = uses(offset)
        after = [a + b for a, b in zip(load, used)]
        mean = sum(after) / 6
        return (max(after), sum((a - mean) ** 2 for a in after), -sum(used))

    while left:
        best = min(left, key=cost)
        load = [a + b for a, b in zip(load, uses(best))]
        left.remove(best)
        order.append(best)
    return order


OFFSETS = balanced_offsets()


def chip_at(me, offset, sign=1):
    x, y, z = [rem(me[axis] + (sign * hops) % 4, 4) for axis, hops in zip("xyz", offset)]
    where = {"z": z, "yh": y // 2, "yl": rem(y, 2), "xh": x // 2, "xl": rem(x, 2)}
    return where, z * 16 + rem(y, 2) * 8 + (y // 2) * 4 + x


def halves(width):
    first = width // 256 * 128 if width > 128 else width
    return first, width - first


def spread_rows(shape, swap):
    dense = lax.broadcasted_iota(jnp.int32, shape, 1 if swap else 0)
    padded = lax.broadcasted_iota(jnp.int32, shape, 0 if swap else 1)
    shift = jnp.zeros(shape, jnp.int32)
    for edge in (12, 24, 36):
        shift = shift + jnp.where(dense >= edge, 4, 0)
    return dense + shift == padded


def block_ref(ref, axes, me, axis, value, columns):
    spot = dict(me)
    spot[axis] = value
    z = slice(None) if "z" in axes else spot["z"]
    yl = slice(None) if "y" in axes else rem(spot["y"], 2)
    yh = slice(None) if "y" in axes else spot["y"] // 2
    return ref.at[z, yl, me["core"], yh, :, columns]


def gather_kernel(shard_ref, gate_ref, up_ref, down_ref, *rest):
    count = len(PARTS)
    outs = rest[:count]
    expert_in, expert_out, landed = rest[count : count + 3]
    stages = rest[count + 3 : 2 * count + 3]
    send_sems, recv_sems, local_sems = rest[2 * count + 3 :]
    me = place()
    nxt = {axis: rem(me[axis] + 1, 4) for axis in "xyz"}
    opp = {axis: rem(me[axis] + 2, 4) for axis in "xyz"}
    prv = {axis: rem(me[axis] + 3, 4) for axis in "xyz"}
    sibling = {"core": 1 - me["core"]}
    partner = {"core": 1 - me["core"], "xl": 1 - lax.axis_index("xl")}
    crossed = me["core"] != lax.axis_index("xl")
    greet(
        [device("x", nxt["x"]), device("x", opp["x"]), device("x", prv["x"])]
        + [device("y", nxt["y"]), device("y", prv["y"])]
        + [device("z", nxt["z"]), device("z", prv["z"]), sibling, partner]
    )
    wires = Wires(send_sems, recv_sems, local_sems)
    runs, start = [], 0
    for index, (name, width, order) in enumerate(PARTS):
        last_x = len(order) == 3
        quarter = width // 4 if last_x else width
        run = {
            "out": outs[index],
            "order": order,
            "width": quarter,
            "done": "",
            "stage": stages[index],
            "start": start,
            "landed": landed.at[:, :, pl.ds(start, quarter)],
            "base": me["x"] * quarter if last_x else 0,
            "first": [],
            "shared": [],
        }

        def piece(x):
            if last_x:
                return shard_ref.at[:, pl.ds(pl.multiple_of(start + x * quarter, 128), quarter)]
            return shard_ref.at[:, pl.ds(start, quarter)]

        for where in (nxt, prv, opp):
            run["first"].append(
                wires.remote(piece(where["x"]), run["landed"].at[me["x"]], device("x", where["x"]))
            )
        run["bring"] = wires.copy(piece(me["x"]), run["landed"].at[me["x"]])
        runs.append(run)
        start += width

    whole = [
        (gate_ref, expert_in.at[:, pl.ds(0, HALF)]),
        (up_ref, expert_in.at[:, pl.ds(HALF, HALF)]),
        (down_ref, expert_out.at[pl.ds(0, HALF)]),
    ]

    def moved(slot):
        source, target = whole[slot]
        return pltpu.make_async_remote_copy(
            src_ref=source,
            dst_ref=target,
            send_sem=send_sems.at[EXPERT_SEM + slot],
            recv_sem=recv_sems.at[EXPERT_SEM + slot],
            device_id=partner,
            device_id_type=MESH_ID,
        )

    def kept(slot):
        source, target = whole[slot]
        return pltpu.make_async_copy(source, target, local_sems.at[20 + slot])

    @pl.when(crossed)
    def _():
        for slot in range(3):
            moved(slot).start()

    @pl.when(jnp.logical_not(crossed))
    def _():
        for slot in range(3):
            kept(slot).start()

    def part_columns(run, axis, value, which):
        base = value * run["width"] if axis == "x" else run["base"]
        left, size = 0, run["width"]
        if which is not None:
            first_half, second_half = halves(run["width"])
            left, size = (0, first_half) if which == 0 else (first_half, second_half)
        if isinstance(base, int):
            return pl.ds(base + left, size)
        return pl.ds(pl.multiple_of(base + left, 128), size)

    def blocks(run, axis, value, which=None):
        columns = part_columns(run, axis, value, which)
        return block_ref(run["out"], run["done"], me, axis, value, columns)

    def begin(run, axis, source=None):
        target = blocks(run, axis, me[axis])
        source = target if source is None else source
        run["forth"] = wires.remote(source, target, device(axis, nxt[axis]))
        run["back"] = wires.remote(source, target, device(axis, prv[axis]))

    pick = spread_rows((48, 64), False).astype(BF16)
    for run in runs:
        run["bring"].wait()
        for copy in run["first"]:
            copy.wait_recv()
        for left in range(0, run["width"], 512):
            size = min(512, run["width"] - left)
            left_in = run["start"] + left
            piece_rows = landed[:, :, left_in : left_in + size].reshape(64, size)
            run["stage"][:, left : left + size] = jnp.dot(
                pick, piece_rows, preferred_element_type=F32
            ).astype(BF16)
        axis = run["order"][0]
        begin(run, axis, run["stage"])
        run["own"] = wires.copy(run["stage"], blocks(run, axis, me[axis]))

    def forward(run, axis):
        run["forth"].wait_recv()
        source = blocks(run, axis, prv[axis], 0)
        run["more"] = [wires.remote(source, source, device(axis, nxt[axis]))]
        run["back"].wait_recv()
        if halves(run["width"])[1] > 0:
            source = blocks(run, axis, nxt[axis], 1)
            run["more"].append(wires.remote(source, source, device(axis, prv[axis])))

    def share(run, axis, value):
        source = blocks(run, axis, value)
        run["shared"].append(wires.remote(source, source, sibling))

    def advance(run, step):
        axis = run["order"][step]
        for copy in run["more"]:
            copy.wait_recv()
        if step == len(run["order"]) - 1:
            share(run, axis, opp[axis])
            return
        if step == 0:
            run["own"].wait()
        run["done"] = run["done"] + axis
        following = run["order"][step + 1]
        begin(run, following)
        if step + 1 == len(run["order"]) - 1:
            share(run, following, me[following])

    def last_forward(run):
        axis = run["order"][-1]
        forward(run, axis)
        share(run, axis, prv[axis])
        share(run, axis, nxt[axis])

    threes = [run for run in runs if len(run["order"]) == 3]
    twos = [run for run in runs if len(run["order"]) == 2]
    for run in runs:
        forward(run, run["order"][0])
    for run in runs:
        advance(run, 0)
    for run in threes:
        forward(run, run["order"][1])
    for run in threes:
        advance(run, 1)
    for run in twos:
        last_forward(run)
    for run in threes:
        last_forward(run)

    @pl.when(crossed)
    def _():
        for slot in range(3):
            moved(slot).wait_recv()

    @pl.when(jnp.logical_not(crossed))
    def _():
        for slot in range(3):
            kept(slot).wait()

    handed = [
        wires.remote(
            expert_in.at[:, pl.ds(0, 2 * HALF)], expert_in.at[:, pl.ds(2 * HALF, 2 * HALF)], sibling
        ),
        wires.remote(expert_out.at[pl.ds(0, HALF)], expert_out.at[pl.ds(HALF, HALF)], sibling),
    ]
    for run in twos + threes:
        advance(run, len(run["order"]) - 1)
    for run in runs:
        for copy in run["shared"]:
            copy.wait_recv()
    for copy in handed:
        copy.wait_recv()
    wires.finish()

    @pl.when(crossed)
    def _():
        for slot in range(3):
            moved(slot).wait_send()


def gather_weights(shard, gate_w, up_w, down_w):
    shapes = [jax.ShapeDtypeStruct((4, 2, 2, 2, 48, width), BF16) for _, width, _ in PARTS]
    shapes += [
        jax.ShapeDtypeStruct((gate_w.shape[0], 4 * HALF), BF16),
        jax.ShapeDtypeStruct((2 * HALF, down_w.shape[1]), BF16),
    ]
    copies = 160
    anywhere = pl.BlockSpec(memory_space=pl.ANY)
    return pl.pallas_call(
        gather_kernel,
        out_shape=shapes,
        in_specs=[pl.BlockSpec(memory_space=pltpu.VMEM)] + [anywhere] * 3,
        out_specs=[anywhere] * (len(PARTS) + 2),
        scratch_shapes=[pltpu.VMEM((4, 16, TOTAL), BF16)]
        + [
            pltpu.VMEM((48, width // 4 if len(order) == 3 else width), BF16)
            for _, width, order in PARTS
        ]
        + [
            pltpu.SemaphoreType.DMA((copies,)),
            pltpu.SemaphoreType.DMA((copies,)),
            pltpu.SemaphoreType.DMA((24,)),
        ],
        compiler_params=pltpu.CompilerParams(
            collective_id=0, has_side_effects=True, vmem_limit_bytes=16 * 1024 * 1024
        ),
        cost_estimate=pl.CostEstimate(flops=0, bytes_accessed=200_000_000, transcendentals=0),
    )(shard, gate_w, up_w, down_w)


def sum_kernel(*refs):
    count = len(PARTS)
    grads = refs[:count]
    expert_from = refs[count : count + 2]
    outs = refs[count + 2 : 2 * count + 2]
    expert_to = refs[2 * count + 2 : 2 * count + 4]
    rest = refs[2 * count + 4 :]
    own = rest[:count]
    theirs = rest[count : 2 * count]
    near1 = rest[2 * count : 3 * count]
    near2 = rest[3 * count : 4 * count]
    ends = rest[4 * count : 5 * count]
    arrived = rest[5 * count : 6 * count]
    send_sems, recv_sems, local_sems = rest[6 * count :]
    me = place()
    core = me["core"]
    nxt = {axis: rem(me[axis] + 1, 4) for axis in "xyz"}
    opp = {axis: rem(me[axis] + 2, 4) for axis in "xyz"}
    prv = {axis: rem(me[axis] + 3, 4) for axis in "xyz"}
    sibling = {"core": 1 - core}
    partner = {"core": 1 - core, "xl": 1 - lax.axis_index("xl")}
    crossed = core != lax.axis_index("xl")
    greet(
        [device("x", nxt["x"]), device("x", opp["x"]), device("x", prv["x"])]
        + [device("y", nxt["y"]), device("y", prv["y"])]
        + [device("z", nxt["z"]), device("z", prv["z"]), sibling, partner]
    )

    def moved(slot):
        return pltpu.make_async_remote_copy(
            src_ref=expert_from[slot],
            dst_ref=expert_to[slot],
            send_sem=send_sems.at[EXPERT_SEM + slot],
            recv_sem=recv_sems.at[EXPERT_SEM + slot],
            device_id=partner,
            device_id_type=MESH_ID,
        )

    def kept(slot):
        return pltpu.make_async_copy(
            expert_from[slot], expert_to[slot], local_sems.at[44 + slot]
        )

    wires = Wires(send_sems, recv_sems, local_sems)

    def spot(left_axes, axis, value, with_core):
        at = dict(me)
        if axis is not None:
            at[axis] = value
        whole = [name for name in left_axes if name != axis]
        z = slice(None) if "z" in whole else at["z"]
        yl = slice(None) if "y" in whole else rem(at["y"], 2)
        yh = slice(None) if "y" in whole else at["y"] // 2
        return (z, yl) + (() if with_core is None else (with_core,)) + (yh,)

    def lead(left_axes, axis):
        dims = []
        for name in ("z", "y"):
            if name in left_axes and name != axis:
                dims += [4] if name == "z" else [2, 2]
        return dims

    def loop_over(dims, body):
        total = 1
        for size in dims:
            total *= size

        def step(flat, carry):
            index, rest_flat = [], flat
            for size in reversed(dims):
                index.append(rem(rest_flat, size))
                rest_flat = rest_flat // size
            body(tuple(reversed(index)))
            return carry

        if total == 1:
            body(())
        else:
            lax.fori_loop(0, total, step, 0)

    def add_into(target, sources, dims):
        def body(index):
            for row in range(0, 48, 16):
                at = index + (pl.ds(row, 16),)
                value = target[at].astype(F32)
                for source in sources:
                    value = value + source[at].astype(F32)
                target[at] = value.astype(target.dtype)

        loop_over(dims, body)

    runs = []
    for index, (name, width, order) in enumerate(PARTS):
        quarter = width // 4 if len(order) == 3 else width
        runs.append(
            {
                "index": index,
                "name": name,
                "order": order[::-1],
                "width": quarter,
                "full": width,
                "left": "zy",
                "turn": 0,
            }
        )

    def columns_of(run, axis, value, which):
        if len(run["order"]) == 3:
            base = (value if axis == "x" else me["x"]) * run["width"]
        else:
            base = 0
        left, size = 0, run["width"]
        if which is not None:
            first_half, second_half = halves(run["width"])
            left, size = (0, first_half) if which == 0 else (first_half, second_half)
        if isinstance(base, int):
            return pl.ds(base + left, size)
        return pl.ds(pl.multiple_of(base + left, 128), size)

    def chunk(run, axis, value, which=None, ref=None, with_core=None):
        ref = own[run["index"]] if ref is None else ref
        columns = columns_of(run, axis, value, which)
        return ref.at[spot(run["left"], axis, value, with_core) + (slice(None), columns)]

    def pair(run, axis, value):
        index = run["index"]
        give = wires.remote(
            chunk(run, axis, value, None, grads[index], 1 - core),
            chunk(run, axis, value, None, theirs[index]),
            sibling,
        )
        keep = wires.copy(
            chunk(run, axis, value, None, grads[index], core), chunk(run, axis, value)
        )
        return give, keep

    def join(run, axis, value, copies):
        copies[0].wait_recv()
        copies[1].wait()
        add_into(
            chunk(run, axis, value),
            [chunk(run, axis, value, None, theirs[run["index"]])],
            lead(run["left"], axis),
        )

    def slots(run, axis):
        dims = lead(run["left"], axis)
        phase = run["turn"]
        ref = (near1 if phase == 0 else near2)[run["index"]]
        if phase == 2:
            ref = ends[run["index"]]
        if not dims:
            ref = ref.at[:, pl.ds(0, 48)]
        return ref.at[0], ref.at[1], ref.at[2], dims

    def part(ref, run, which, dims):
        first_half, second_half = halves(run["width"])
        columns = pl.ds(0, first_half) if which == 0 else pl.ds(first_half, second_half)
        return ref.at[(slice(None),) * len(dims) + (slice(None), columns)]

    def ring_open(run, axis):
        from_prv, from_nxt, passing, dims = slots(run, axis)
        run["passing"] = [
            wires.remote(
                chunk(run, axis, opp[axis], 0), part(passing, run, 0, dims), device(axis, nxt[axis])
            )
        ]
        if halves(run["width"])[1]:
            run["passing"].append(
                wires.remote(
                    chunk(run, axis, opp[axis], 1),
                    part(passing, run, 1, dims),
                    device(axis, prv[axis]),
                )
            )

    def ring_near(run, axis):
        from_prv, from_nxt, passing, dims = slots(run, axis)
        run["near"] = []
        if halves(run["width"])[1]:
            run["near"].append(
                wires.remote(
                    chunk(run, axis, nxt[axis], 1),
                    part(from_prv, run, 1, dims),
                    device(axis, nxt[axis]),
                )
            )
        run["near"].append(
            wires.remote(
                chunk(run, axis, prv[axis], 0), part(from_nxt, run, 0, dims), device(axis, prv[axis])
            )
        )

    def ring_pass(run, axis):
        from_prv, from_nxt, passing, dims = slots(run, axis)
        run["passing"][0].wait_recv()
        add_into(chunk(run, axis, nxt[axis], 0), [part(passing, run, 0, dims)], dims)
        run["near"].append(
            wires.remote(
                chunk(run, axis, nxt[axis], 0), part(from_prv, run, 0, dims), device(axis, nxt[axis])
            )
        )
        if halves(run["width"])[1]:
            run["passing"][1].wait_recv()
            add_into(chunk(run, axis, prv[axis], 1), [part(passing, run, 1, dims)], dims)
            run["near"].append(
                wires.remote(
                    chunk(run, axis, prv[axis], 1),
                    part(from_nxt, run, 1, dims),
                    device(axis, prv[axis]),
                )
            )

    def ring_close(run, axis):
        from_prv, from_nxt, passing, dims = slots(run, axis)
        for copy in run["near"]:
            copy.wait_recv()
        if halves(run["width"])[1]:
            add_into(chunk(run, axis, me[axis]), [from_prv, from_nxt], dims)
        else:
            add_into(chunk(run, axis, me[axis]), [from_prv, from_nxt], dims)
        run["left"] = run["left"].replace(axis, "")
        run["turn"] += 1

    threes = [run for run in runs if len(run["order"]) == 3]
    twos = [run for run in runs if len(run["order"]) == 2]
    begun = []
    for where in (opp, nxt, prv, me):
        begun.append([pair(run, run["order"][0], where[run["order"][0]]) for run in runs])

    @pl.when(crossed)
    def _():
        for slot in range(2):
            moved(slot).start()

    @pl.when(jnp.logical_not(crossed))
    def _():
        for slot in range(2):
            kept(slot).start()

    for run, copies in zip(runs, begun[0]):
        axis = run["order"][0]
        join(run, axis, opp[axis], copies)
        ring_open(run, axis)
    for run, nexts, prevs in zip(runs, begun[1], begun[2]):
        axis = run["order"][0]
        join(run, axis, nxt[axis], nexts)
        join(run, axis, prv[axis], prevs)
        ring_near(run, axis)
    for run in threes:
        ring_pass(run, run["order"][0])
    for run, copies in zip(runs, begun[3]):
        axis = run["order"][0]
        join(run, axis, me[axis], copies)
    for run in twos:
        ring_pass(run, run["order"][0])

    def turn(run):
        ring_close(run, run["order"][run["turn"]])
        following = run["order"][run["turn"]]
        ring_open(run, following)
        ring_near(run, following)

    for run in threes:
        turn(run)
    for run in threes:
        ring_pass(run, run["order"][1])
    for run in twos:
        turn(run)
    for run in threes:
        turn(run)
    for run in twos:
        ring_pass(run, run["order"][1])
    for run in threes:
        ring_pass(run, run["order"][2])
    for run in twos:
        ring_close(run, run["order"][1])
    for run in threes:
        ring_close(run, run["order"][2])
    lasts = []
    for run in runs:
        index, width = run["index"], run["width"]
        summed = own[index].at[me["z"], rem(me["y"], 2), me["y"] // 2]
        exact = lax.Precision.HIGHEST if summed.dtype == F32 else None
        pick = spread_rows((64, 48), True).astype(summed.dtype)
        target = arrived[index]
        staging = ends[index].at[3] if len(run["order"]) == 3 else near2[index].at[3]
        base = me["x"] * width if len(run["order"]) == 3 else 0
        for left in range(0, width, 512):
            size = min(512, width - left)
            if isinstance(base, int):
                columns = pl.ds(left, size)
            else:
                columns = pl.ds(pl.multiple_of(base + left, 128), size)
            staging[:, left : left + size] = jnp.dot(
                pick, summed[:, columns], preferred_element_type=F32, precision=exact
            ).astype(staging.dtype)
        if len(run["order"]) == 3:
            columns = pl.ds(pl.multiple_of(base, 128), width)
            lands = target.at[:, columns]
        else:
            lands = target.at[me["x"]]
        run["copies"] = []
        for where in (nxt, opp, prv):
            row = pl.ds(pl.multiple_of(where["x"] * 16, 16), 16)
            run["copies"].append(
                wires.remote(staging.at[row], lands, device("x", where["x"]))
            )
        row = pl.ds(pl.multiple_of(me["x"] * 16, 16), 16)
        run["keep"] = wires.copy(staging.at[row], lands)
    for run in runs:
        index = run["index"]
        run["keep"].wait()
        for copy in run["copies"]:
            copy.wait_recv()
        if len(run["order"]) == 3:
            outs[index][...] = arrived[index][...].astype(F32)
        else:
            value = arrived[index][0].astype(F32)
            for place_x in range(1, 4):
                value = value + arrived[index][place_x].astype(F32)
            outs[index][...] = value
    wires.finish()

    @pl.when(crossed)
    def _():
        for slot in range(2):
            moved(slot).wait_recv()
            moved(slot).wait_send()

    @pl.when(jnp.logical_not(crossed))
    def _():
        for slot in range(2):
            kept(slot).wait()


def sum_gradients(grads, expert_grads):
    scratch_own, scratch_theirs, near1, near2, ends, arrived = [], [], [], [], [], []
    for name, width, order in PARTS:
        kind = F32 if name == "misc" else BF16
        scratch_own.append(pltpu.VMEM((4, 2, 2, 48, width), kind))
        scratch_theirs.append(pltpu.VMEM((4, 2, 2, 48, width), kind))
        if order == "yz":
            near1.append(pltpu.VMEM((3, 2, 2, 48, width), kind))
            near2.append(pltpu.VMEM((4, 64, width), kind))
        elif order == "zy":
            near1.append(pltpu.VMEM((3, 4, 48, width), kind))
            near2.append(pltpu.VMEM((4, 64, width), kind))
        else:
            quarter = width // 4
            near1.append(pltpu.VMEM((3, 4, 2, 2, 48, quarter), kind))
            near2.append(pltpu.VMEM((3, 2, 2, 48, quarter), kind))
        ends.append(pltpu.VMEM((4, 64, width // 4 if len(order) == 3 else 128), kind))
        arrived.append(pltpu.VMEM((16, width) if len(order) == 3 else (4, 16, width), kind))
    copies = 160
    anywhere = pl.BlockSpec(memory_space=pl.ANY)
    return pl.pallas_call(
        sum_kernel,
        out_shape=[jax.ShapeDtypeStruct((16, width), F32) for _, width, _ in PARTS]
        + [jax.ShapeDtypeStruct(grad.shape, grad.dtype) for grad in expert_grads],
        in_specs=[anywhere] * (len(PARTS) + 2),
        out_specs=[pl.BlockSpec(memory_space=pltpu.VMEM)] * len(PARTS) + [anywhere] * 2,
        scratch_shapes=scratch_own
        + scratch_theirs
        + near1
        + near2
        + ends
        + arrived
        + [
            pltpu.SemaphoreType.DMA((copies,)),
            pltpu.SemaphoreType.DMA((copies,)),
            pltpu.SemaphoreType.DMA((48,)),
        ],
        compiler_params=pltpu.CompilerParams(
            collective_id=1, has_side_effects=True, vmem_limit_bytes=56 * 1024 * 1024
        ),
    )(*grads, *expert_grads)


def col_device(col):
    return {"yh": col // 4, "xh": rem(col // 2, 2), "xl": rem(col, 2)}


def col_index():
    return lax.axis_index("yh") * 4 + lax.axis_index("xh") * 2 + lax.axis_index("xl")


def later_kernel(own_ref, marks_ref, out_ref, marks_out, send_sems, recv_sems, local_sem):
    me = col_index()
    rows = own_ref.shape[0]
    tail = marks_ref.shape[0]
    late = pl.ds(rows - tail, tail)
    greet([col_device(rem(me + far, 8)) for far in range(1, 8)])

    def copies(far, first):
        there = col_device(rem(me + far, 8))
        pairs = [(own_ref, out_ref.at[me])]
        if first:
            pairs = [(own_ref.at[late], out_ref.at[0, late]), (marks_ref, marks_out)]
        return [
            pltpu.make_async_remote_copy(
                src_ref=source,
                dst_ref=target,
                send_sem=send_sems.at[far, number],
                recv_sem=recv_sems.at[far, number],
                device_id=there,
                device_id_type=MESH_ID,
            )
            for number, (source, target) in enumerate(pairs)
        ]

    def each(far, first, condition, act):
        @pl.when(condition)
        def _():
            for copy in copies(far, first):
                act(copy)

    for far in range(7, 0, -1):
        each(far, False, (me > 0) & (me + far < 8), lambda copy: copy.start())
        each(far, True, me == 0, lambda copy: copy.start())
    keep = pltpu.make_async_copy(own_ref, out_ref.at[me], local_sem)
    keep.start()

    @pl.when(me == 0)
    def _():
        marks_out[...] = marks_ref[...]

    @pl.when(me > 0)
    def _():
        out_ref[0, : rows - tail] = jnp.zeros((rows - tail, own_ref.shape[1]), own_ref.dtype)

    for far in range(1, 8):

        @pl.when(me + far < 8)
        def _():
            out_ref[me + far] = jnp.zeros(own_ref.shape, own_ref.dtype)

    keep.wait()
    for far in range(1, 8):
        each(far, False, me > far, lambda copy: copy.wait_recv())
        each(far, True, me == far, lambda copy: copy.wait_recv())
        each(far, False, (me > 0) & (me + far < 8), lambda copy: copy.wait_send())
        each(far, True, me == 0, lambda copy: copy.wait_send())


def to_later(rows, marks):
    vmem = pl.BlockSpec(memory_space=pltpu.VMEM)
    return pl.pallas_call(
        later_kernel,
        out_shape=[
            jax.ShapeDtypeStruct((8,) + rows.shape, rows.dtype),
            jax.ShapeDtypeStruct(marks.shape, marks.dtype),
        ],
        in_specs=[vmem, vmem],
        out_specs=[vmem, vmem],
        scratch_shapes=[
            pltpu.SemaphoreType.DMA((8, 2)),
            pltpu.SemaphoreType.DMA((8, 2)),
            pltpu.SemaphoreType.DMA,
        ],
        compiler_params=pltpu.CompilerParams(
            collective_id=2, has_side_effects=True, vmem_limit_bytes=16 * 1024 * 1024
        ),
        cost_estimate=pl.CostEstimate(flops=0, bytes_accessed=70_000_000, transcendentals=0),
    )(rows, marks)


def earlier_kernel(
    tail,
    blocks_ref,
    in_ref,
    down_ref,
    rows_ref,
    out_ref,
    in_out,
    down_out,
    rows_out,
    landed,
    send_sems,
    recv_sems,
    local_sem,
):
    me = col_index()
    spot = place()
    chips = [chip_at(spot, offset) for offset in OFFSETS]
    mine = chip_at(spot, (0, 0, 0))[1]
    rows = out_ref.shape[0]
    late = pl.ds(rows - tail, tail)
    sibling = {"core": 1 - lax.axis_index("core")}
    greet([where for where, _ in chips] + [sibling])

    def remote(source, target, number, where):
        return pltpu.make_async_remote_copy(
            src_ref=source,
            dst_ref=target,
            send_sem=send_sems.at[number],
            recv_sem=recv_sems.at[number],
            device_id=where,
            device_id_type=MESH_ID,
        )

    def copy(far, first):
        block = rem(me + 8 - far, 8)
        there = col_device(block)
        if first:
            return remote(blocks_ref.at[0, late], landed.at[far, late], far, there)
        return remote(blocks_ref.at[block], landed.at[far], far, there)

    def each(far, first, condition, act):
        @pl.when(condition)
        def _():
            act(copy(far, first))

    for far in range(7, 0, -1):
        each(far, False, me > far, lambda moved: moved.start())
        each(far, True, me == far, lambda moved: moved.start())
    halves_sent = [
        remote(in_ref, in_out, 8, sibling),
        remote(down_ref, down_out, 9, sibling),
    ]
    for sent in halves_sent:
        sent.start()
    rows_sent = [
        remote(rows_ref.at[holder], rows_out.at[mine], 10 + number, where)
        for number, (where, holder) in enumerate(chips)
    ]
    for sent in rows_sent:
        sent.start()
    kept = pltpu.make_async_copy(rows_ref.at[mine], rows_out.at[mine], local_sem)
    kept.start()

    @pl.when(me == 0)
    def _():
        for far in range(1, 8):
            landed[far, : rows - tail] = jnp.zeros(
                (rows - tail, landed.shape[2]), landed.dtype
            )

    for far in range(1, 8):

        @pl.when(me + far >= 8)
        def _():
            landed[far] = jnp.zeros(landed.shape[1:], landed.dtype)

    for far in range(1, 8):
        each(far, False, (me > 0) & (me + far < 8), lambda moved: moved.wait_recv())
        each(far, True, me == 0, lambda moved: moved.wait_recv())

    for row in range(0, rows, 16):
        at = pl.ds(row, 16)
        value = blocks_ref[me, at].astype(F32)
        for far in range(1, 8):
            value = value + landed[far, at].astype(F32)
        out_ref[at] = value.astype(out_ref.dtype)
    for far in range(1, 8):
        each(far, False, me > far, lambda moved: moved.wait_send())
        each(far, True, me == far, lambda moved: moved.wait_send())
    for sent in halves_sent + rows_sent:
        sent.wait()
    kept.wait()


def sum_earlier(blocks, tail, expert_in, expert_down, rows):
    vmem = pl.BlockSpec(memory_space=pltpu.VMEM)
    anywhere = pl.BlockSpec(memory_space=pl.ANY)
    return pl.pallas_call(
        functools.partial(earlier_kernel, tail),
        out_shape=[
            jax.ShapeDtypeStruct(blocks.shape[1:], blocks.dtype),
            jax.ShapeDtypeStruct(expert_in.shape, expert_in.dtype),
            jax.ShapeDtypeStruct(expert_down.shape, expert_down.dtype),
            jax.ShapeDtypeStruct(rows.shape, rows.dtype),
        ],
        in_specs=[vmem, anywhere, anywhere, anywhere],
        out_specs=[vmem, anywhere, anywhere, anywhere],
        scratch_shapes=[
            pltpu.VMEM(blocks.shape, blocks.dtype),
            pltpu.SemaphoreType.DMA((73,)),
            pltpu.SemaphoreType.DMA((73,)),
            pltpu.SemaphoreType.DMA,
        ],
        compiler_params=pltpu.CompilerParams(
            collective_id=3, has_side_effects=True, vmem_limit_bytes=16 * 1024 * 1024
        ),
        cost_estimate=pl.CostEstimate(flops=0, bytes_accessed=70_000_000, transcendentals=0),
    )(blocks, expert_in, expert_down, rows)


VMEM_SPEC = pl.BlockSpec(memory_space=pltpu.VMEM)
GROUP = QUERY_HEADS // KEY_VALUE_HEADS
EXTRA = 128


def dot(left, right, left_dim=1, right_dim=0):
    return lax.dot_general(
        left, right, (((left_dim,), (right_dim,)), ((), ())), preferred_element_type=F32
    )


def rounded_parts(value):
    first = value.astype(BF16)
    left = value - first.astype(F32)
    second = left.astype(BF16)
    return [first, second, (left - second.astype(F32)).astype(BF16)]


def lane_column(index):
    return (lax.broadcasted_iota(jnp.int32, (16, 128), 1) == index).astype(BF16)


def gain_row(misc_ref, index):
    return dot(lane_column(index), misc_ref[...], 1, 1)[:1]


def allowed_pairs(marks_ref, segments_ref, rows, keys):
    me = col_index()
    shape = (rows, keys)
    own = segments_ref[:, :1]
    first_length = jnp.where(
        me == 0,
        jnp.sum((own == 0.0).astype(F32), axis=0, keepdims=True),
        marks_ref[:1, :1].astype(F32),
    )
    last_start = (me * rows).astype(F32) + jnp.sum(
        (own < 2.0).astype(F32), axis=0, keepdims=True
    )
    lowest = jnp.where(own == 0.0, 0.0, jnp.where(own == 1.0, first_length, last_start))
    key = lax.broadcasted_iota(jnp.int32, shape, 1)
    query = lax.broadcasted_iota(jnp.int32, shape, 0) + me * rows
    return (key <= query) & (key.astype(F32) >= lowest)


def head_columns(ref, group):
    width = GROUP * HEAD_SIZE
    return jnp.concatenate(
        [
            ref[:, group * width + head * HEAD_SIZE : group * width + (head + 1) * HEAD_SIZE]
            for head in range(GROUP)
        ],
        axis=0,
    )


def head_weights(queries, keys, allowed):
    scores = dot(queries, keys, 1, 1) * (HEAD_SIZE ** (-0.5))
    scores = jnp.where(allowed, scores, -1e30)
    shifted = jnp.exp(scores - jnp.max(scores, axis=1, keepdims=True))
    return shifted / jnp.sum(shifted, axis=1, keepdims=True)


def middle_kernel(
    qkv_ref,
    every_ref,
    marks_ref,
    segments_ref,
    tokens_ref,
    outt_ref,
    misc_ref,
    named_ref,
    slots_ref,
    owner_ref,
    attended_ref,
    residual_ref,
    normed_ref,
    gates_ref,
    outgoing_ref,
):
    rows, features = tokens_ref.shape
    width = KEY_VALUE_HEADS * HEAD_SIZE
    keys_count = 8 * rows
    allowed = allowed_pairs(marks_ref, segments_ref, rows, keys_count)
    allowed = jnp.concatenate([allowed.astype(F32)] * GROUP, axis=0) > 0.5
    for group in range(KEY_VALUE_HEADS):
        queries = head_columns(qkv_ref, group)
        columns = pl.ds(group * HEAD_SIZE, HEAD_SIZE)
        keys = every_ref[:, :, columns].reshape(keys_count, HEAD_SIZE)
        values = every_ref[:, :, pl.ds(width + group * HEAD_SIZE, HEAD_SIZE)].reshape(
            keys_count, HEAD_SIZE
        )
        weights = head_weights(queries, keys, allowed)
        mixed = dot(weights.astype(BF16), values).astype(BF16)
        for head in range(GROUP):
            at = (group * GROUP + head) * HEAD_SIZE
            attended_ref[:, at : at + HEAD_SIZE] = mixed[head * rows : (head + 1) * rows]
    attended = attended_ref[...]
    total = jnp.zeros((rows, 1), F32)
    for left in range(0, features, 512):
        piece = tokens_ref[:, left : left + 512].astype(F32) + dot(
            attended, outt_ref[left : left + 512], 1, 1
        )
        residual_ref[:, left : left + 512] = piece
        total = total + jnp.sum(piece * piece, axis=1, keepdims=True)
    scale = lax.rsqrt(total / features + EPSILON)
    normed_ref[...] = (residual_ref[...] * scale * gain_row(misc_ref, EXPERTS + 1)).astype(BF16)
    normed = normed_ref[...]
    logits = dot(normed, misc_ref[...])
    named = named_ref[...] > 0.5
    chosen = jnp.where(named, logits, -1e30)
    chosen_exp = jnp.where(named, jnp.exp(chosen - jnp.max(chosen, axis=1, keepdims=True)), 0.0)
    gates = chosen_exp / jnp.sum(chosen_exp, axis=1, keepdims=True)
    gates_ref[...] = gates
    parts = jnp.concatenate(rounded_parts(gates), axis=1)

    def send_rows(step, carry):
        at = pl.ds(pl.multiple_of(step * 256, 256), 256)
        slots = slots_ref[at]
        outgoing_ref[at, :features] = dot(slots, normed).astype(BF16)
        gate_parts = dot(slots, parts)
        owner = owner_ref[at].astype(F32)
        lane = lax.broadcasted_iota(jnp.int32, (256, EXTRA), 1)
        extra = jnp.zeros((256, EXTRA), F32)
        for part in range(3):
            column = jnp.sum(
                gate_parts[:, part * 128 : (part + 1) * 128] * owner, axis=1, keepdims=True
            )
            extra = jnp.where(lane == part, column, extra)
        outgoing_ref[at, features:] = extra.astype(BF16)
        return carry

    lax.fori_loop(0, slots_ref.shape[0] // 256, send_rows, 0)


def middle(qkv, every, marks, segments, tokens, outt, misc, named, slots, owner):
    rows, features = tokens.shape
    return pl.pallas_call(
        middle_kernel,
        out_shape=[
            jax.ShapeDtypeStruct((rows, features), BF16),
            jax.ShapeDtypeStruct((rows, features), F32),
            jax.ShapeDtypeStruct((rows, features), BF16),
            jax.ShapeDtypeStruct((rows, 128), F32),
            jax.ShapeDtypeStruct((slots.shape[0], features + EXTRA), BF16),
        ],
        in_specs=[VMEM_SPEC] * 10,
        out_specs=[VMEM_SPEC] * 5,
        compiler_params=pltpu.CompilerParams(vmem_limit_bytes=48 * 1024 * 1024),
        cost_estimate=pl.CostEstimate(
            flops=6_000_000_000, bytes_accessed=20_000_000, transcendentals=2_000_000
        ),
    )(qkv, every, marks, segments, tokens, outt, misc, named, slots, owner)


def expert_kernel(
    arrived_ref, cotangent_ref, weight_ref, down_ref, back_ref, grads_ref, hidden_ref, gated_ref
):
    rows, features = cotangent_ref.shape
    extra = arrived_ref[:, features:].astype(F32)
    gate = extra[:, :1] + extra[:, 1:2] + extra[:, 2:3]
    pre = dot(arrived_ref[:, :features], weight_ref[...])
    grad_hidden = dot(cotangent_ref[...], down_ref[...], 1, 1)
    along = jnp.zeros((rows, 1), F32)
    for part in range(2):
        base = part * 2 * HALF
        gate_pre, up_pre = pre[:, base : base + HALF], pre[:, base + HALF : base + 2 * HALF]
        grad_part = grad_hidden[:, part * HALF : (part + 1) * HALF]
        sigmoid = 1.0 / (1.0 + jnp.exp(-gate_pre))
        silu = gate_pre * sigmoid
        hidden = silu * up_pre
        along = along + jnp.sum(hidden * grad_part, axis=1, keepdims=True)
        gated_grad = grad_part * gate
        grads_ref[:, base : base + HALF] = (
            gated_grad * up_pre * sigmoid * (1.0 + gate_pre * (1.0 - sigmoid))
        ).astype(BF16)
        grads_ref[:, base + HALF : base + 2 * HALF] = (gated_grad * silu).astype(BF16)
        hidden_ref[:, part * HALF : (part + 1) * HALF] = hidden.astype(BF16)
        gated_ref[:, part * HALF : (part + 1) * HALF] = (hidden * gate).astype(BF16)
    back_ref[:, :features] = dot(grads_ref[...], weight_ref[...], 1, 1).astype(BF16)
    lane = lax.broadcasted_iota(jnp.int32, (rows, EXTRA), 1)
    value = jnp.zeros((rows, EXTRA), F32)
    for part, column in enumerate(rounded_parts(along)):
        value = jnp.where(lane == part, column.astype(F32), value)
    back_ref[:, features:] = value.astype(BF16)


def expert(arrived, grad_received, weight, down):
    count, features = grad_received.shape
    tile = 256

    def rows_of(width):
        return pl.BlockSpec((tile, width), lambda step: (step, 0))

    def whole(array):
        return pl.BlockSpec(array.shape, lambda step: (0, 0))

    return pl.pallas_call(
        expert_kernel,
        grid=(count // tile,),
        out_shape=[
            jax.ShapeDtypeStruct((count, features + EXTRA), BF16),
            jax.ShapeDtypeStruct((count, 4 * HALF), BF16),
            jax.ShapeDtypeStruct((count, 2 * HALF), BF16),
            jax.ShapeDtypeStruct((count, 2 * HALF), BF16),
        ],
        in_specs=[rows_of(features + EXTRA), rows_of(features), whole(weight), whole(down)],
        out_specs=[rows_of(features + EXTRA), rows_of(4 * HALF), rows_of(2 * HALF), rows_of(2 * HALF)],
        compiler_params=pltpu.CompilerParams(vmem_limit_bytes=48 * 1024 * 1024),
        cost_estimate=pl.CostEstimate(
            flops=12_000_000_000, bytes_accessed=25_000_000, transcendentals=1_000_000
        ),
    )(arrived, grad_received, weight, down)


def back_kernel(
    grad_back_ref,
    slots_ref,
    owner_ref,
    gates_ref,
    cotangent_ref,
    residual_ref,
    partial_ref,
    misc_ref,
    outt_ref,
    qkv_ref,
    every_ref,
    marks_ref,
    segments_ref,
    grad_residual_ref,
    grad_low_ref,
    grad_logits_ref,
    grad_gain_ref,
    grad_queries_ref,
    partial_keyvals_ref,
    grad_attended,
):
    rows, features = cotangent_ref.shape
    width = KEY_VALUE_HEADS * HEAD_SIZE
    keys_count = 8 * rows
    score_scale = HEAD_SIZE ** (-0.5)
    slots = slots_ref[...]
    extra = grad_back_ref[:, features:].astype(F32)
    owner = owner_ref[...].astype(F32)
    grad_gates = jnp.zeros((rows, 128), F32)
    for part in range(3):
        grad_gates = grad_gates + dot(slots, (owner * extra[:, part : part + 1]).astype(BF16))
    gates = gates_ref[...]
    grad_logits = (
        gates * (grad_gates - jnp.sum(gates * grad_gates, axis=1, keepdims=True))
    ).astype(BF16)
    grad_logits_ref[...] = grad_logits
    gain = gain_row(misc_ref, EXPERTS + 1)
    square, inner = jnp.zeros((rows, 1), F32), jnp.zeros((rows, 1), F32)
    for left in range(0, features, 512):
        columns = pl.ds(left, 512)
        piece = (
            partial_ref[:, columns]
            + dot(slots, grad_back_ref[:, columns])
            + dot(grad_logits, misc_ref[columns], 1, 1)
        )
        grad_residual_ref[:, columns] = piece
        residual = residual_ref[:, columns]
        square = square + jnp.sum(residual * residual, axis=1, keepdims=True)
        inner = inner + jnp.sum(
            piece * gain[:, left : left + 512] * residual, axis=1, keepdims=True
        )
    scale = lax.rsqrt(square / features + EPSILON)
    cubed = scale * scale * scale * (inner / features)
    for left in range(0, features, 512):
        columns = pl.ds(left, 512)
        piece = grad_residual_ref[:, columns]
        residual = residual_ref[:, columns]
        grad_gain_ref[:, columns] = jnp.broadcast_to(
            jnp.sum(piece * residual * scale, axis=0, keepdims=True), (8, 512)
        )
        value = (
            cotangent_ref[:, columns].astype(F32)
            + scale * piece * gain[:, left : left + 512]
            - residual * cubed
        )
        grad_residual_ref[:, columns] = value
        grad_low_ref[:, columns] = value.astype(BF16)
    grad_low = grad_low_ref[...]
    for left in range(0, features, 512):
        columns = pl.ds(left, 512)
        grad_attended[:, columns] = dot(grad_low, outt_ref[:, columns]).astype(BF16)
    allowed = allowed_pairs(marks_ref, segments_ref, rows, keys_count)
    allowed = jnp.concatenate([allowed.astype(F32)] * GROUP, axis=0) > 0.5
    for group in range(KEY_VALUE_HEADS):
        queries = head_columns(qkv_ref, group)
        heads_gradient = head_columns(grad_attended, group)
        key_columns = pl.ds(group * HEAD_SIZE, HEAD_SIZE)
        value_columns = pl.ds(width + group * HEAD_SIZE, HEAD_SIZE)
        keys = every_ref[:, :, key_columns].reshape(keys_count, HEAD_SIZE)
        values = every_ref[:, :, value_columns].reshape(keys_count, HEAD_SIZE)
        weights = head_weights(queries, keys, allowed)
        grad_weights = dot(heads_gradient, values, 1, 1)
        inner_sum = jnp.sum(weights * grad_weights, axis=1, keepdims=True)
        grad_scores = (weights * (grad_weights - inner_sum)).astype(BF16)
        grad_queries = (dot(grad_scores, keys) * score_scale).astype(BF16)
        for head in range(GROUP):
            at = (group * GROUP + head) * HEAD_SIZE
            grad_queries_ref[:, at : at + HEAD_SIZE] = grad_queries[
                head * rows : (head + 1) * rows
            ]
        partial_keyvals_ref[:, :, key_columns] = (
            (dot(grad_scores, queries, 0, 0) * score_scale)
            .astype(BF16)
            .reshape(8, rows, HEAD_SIZE)
        )
        partial_keyvals_ref[:, :, value_columns] = (
            dot(weights.astype(BF16), heads_gradient, 0, 0)
            .astype(BF16)
            .reshape(8, rows, HEAD_SIZE)
        )


def back(
    grad_back,
    slots,
    owner,
    gates,
    cotangent,
    residual1,
    partial,
    misc,
    outt,
    qkv,
    every,
    marks,
    segments,
):
    rows, features = cotangent.shape
    return pl.pallas_call(
        back_kernel,
        out_shape=[
            jax.ShapeDtypeStruct((rows, features), F32),
            jax.ShapeDtypeStruct((rows, features), BF16),
            jax.ShapeDtypeStruct((rows, 128), BF16),
            jax.ShapeDtypeStruct((8, features), F32),
            jax.ShapeDtypeStruct((rows, features), BF16),
            jax.ShapeDtypeStruct(every.shape, BF16),
        ],
        in_specs=[VMEM_SPEC] * 13,
        out_specs=[VMEM_SPEC] * 6,
        scratch_shapes=[pltpu.VMEM((rows, features), BF16)],
        compiler_params=pltpu.CompilerParams(vmem_limit_bytes=48 * 1024 * 1024),
        cost_estimate=pl.CostEstimate(
            flops=10_000_000_000, bytes_accessed=30_000_000, transcendentals=2_000_000
        ),
    )(
        grad_back,
        slots,
        owner,
        gates,
        cotangent,
        residual1,
        partial,
        misc,
        outt,
        qkv,
        every,
        marks,
        segments,
    )


def inverse_rms(residual):
    return lax.rsqrt(jnp.mean(residual * residual, axis=-1, keepdims=True) + EPSILON)


def contract(left_side, right_side, left_dim, right_dim):
    return lax.dot_general(
        left_side,
        right_side,
        (((left_dim,), (right_dim,)), ((), ())),
        preferred_element_type=F32,
    )


def gated_unit(gate_pre, up_pre):
    return jax.nn.silu(gate_pre) * up_pre


def norm_backward(residual, norm_scale, gain_row, grad_normed):
    weighted = grad_normed * gain_row
    inner_sum = jnp.mean(weighted * residual, axis=-1, keepdims=True)
    grad_residual = (
        norm_scale * weighted - residual * norm_scale * norm_scale * norm_scale * inner_sum
    )
    grad_gain = jnp.sum(grad_normed * residual * norm_scale, axis=0)
    return (grad_residual, grad_gain)


def to_experts(rows):
    return lax.all_to_all(rows, EXPERT_AXES, split_axis=0, concat_axis=0, tiled=True)


def shards(
    tokens,
    segments,
    routes,
    norm1_gain,
    w_query,
    key_value_weight,
    w_output,
    norm2_gain,
    w_router,
    w_shgate,
    w_shup,
    w_shdown,
    w_exgate,
    w_exup,
    w_exdown,
    cotangent,
):
    local_rows, feature_count = tokens.shape
    sequence_length = local_rows * 8
    shard = jnp.concatenate(
        [
            w_output.T,
            w_router,
            norm1_gain[:, None],
            norm2_gain[:, None],
            jnp.zeros((12, 62), BF16),
            w_query,
            key_value_weight,
            w_shgate,
            w_shup,
            w_shdown.T,
        ],
        axis=1,
    )
    shard = jnp.concatenate([shard, jnp.zeros((4, TOTAL), BF16)], axis=0)
    *dense, expert_w, expert_down = gather_weights(shard, w_exgate[0], w_exup[0], w_exdown[0])
    outt_w, misc_w, qkv_w, shgu_w, shdt_w = [
        gathered.reshape(feature_count, gathered.shape[-1]) for gathered in dense
    ]
    gain_first = misc_w[:, EXPERTS].astype(F32)

    expert_ids = jnp.arange(128, dtype=jnp.int32)
    named = jnp.any(routes[:, :, None] == expert_ids[None, None, :], axis=1)
    named_low = named.astype(BF16)
    token_ids = jnp.arange(local_rows, dtype=jnp.int32)
    before = (token_ids[None, :] <= token_ids[:, None]).astype(BF16)
    rank = jnp.dot(before, named_low, preferred_element_type=F32) * named.astype(F32)
    slot_count = EXPERTS * CAP
    slot_ids = jnp.arange(slot_count, dtype=jnp.int32)
    holder = slot_ids // CAP
    slot_expert = (holder // 8) * 8 + (holder % 2) * 4 + holder // 2 % 4
    owner = (slot_expert[:, None] == expert_ids[None, :]).astype(BF16)
    rank_wide = contract(rank.astype(BF16), owner, 1, 1)
    slots = (rank_wide == (slot_ids % CAP + 1).astype(F32)[None, :]).astype(BF16)
    slots_down = (
        contract(owner, rank.astype(BF16), 1, 1) == (slot_ids % CAP + 1).astype(F32)[:, None]
    ).astype(BF16)

    def dispatch(rows):
        return rows.reshape(EXPERTS, CAP, rows.shape[-1])

    sent_cotangent = dispatch(jnp.dot(slots_down, cotangent, preferred_element_type=F32).astype(BF16))
    sent_cotangent, qkv_w = lax.optimization_barrier((sent_cotangent, qkv_w))
    grad_received = to_experts(sent_cotangent).reshape(slot_count, feature_count)

    residual0 = tokens.astype(F32)
    scale_first = inverse_rms(residual0)
    first_normed = (residual0 * scale_first * gain_first).astype(BF16)
    qkv_rows = jnp.dot(first_normed, qkv_w, preferred_element_type=F32).astype(BF16)
    own_segments = segments.astype(F32)
    tail = 32
    first_length = jnp.sum((segments == 0).astype(F32)).astype(BF16)
    every, marks = to_later(
        qkv_rows[:, QUERY_HEADS * HEAD_SIZE :], jnp.broadcast_to(first_length, (tail, 128))
    )
    segment_tile = jnp.broadcast_to(own_segments[:, None], (local_rows, 128))
    attended_rows, residual1, second_normed, gates, outgoing = middle(
        qkv_rows,
        every,
        marks,
        segment_tile,
        tokens,
        outt_w,
        misc_w,
        named.astype(F32),
        slots_down,
        owner,
    )
    outgoing, grad_received = lax.optimization_barrier((outgoing, grad_received))
    arrived = to_experts(dispatch(outgoing)).reshape(slot_count, feature_count + EXTRA)

    shared_pre = jnp.dot(second_normed, shgu_w, preferred_element_type=F32)
    shared_gate, shared_up = shared_pre[:, :1024], shared_pre[:, 1024:]
    shared_hidden = gated_unit(shared_gate, shared_up).astype(BF16)
    shared_out = contract(shared_hidden, shdt_w, 1, 1)
    grad_shdt = contract(cotangent, shared_hidden, 0, 0).astype(BF16)
    grad_shared_hidden = jnp.dot(cotangent, shdt_w, preferred_element_type=F32)
    unused_shared, pull_shared = jax.vjp(gated_unit, shared_gate, shared_up)
    grad_shared_gate, grad_shared_up = pull_shared(grad_shared_hidden)
    grad_shared = jnp.concatenate(
        [grad_shared_gate.astype(BF16), grad_shared_up.astype(BF16)], axis=1
    )
    grad_shgu = contract(second_normed, grad_shared, 0, 0).astype(BF16)
    grad_second = contract(grad_shared, shgu_w, 1, 1)

    forward_rows = residual1 + shared_out
    arrived, grad_shdt, grad_shgu, grad_second, forward_rows = lax.optimization_barrier(
        (arrived, grad_shdt, grad_shgu, grad_second, forward_rows)
    )
    grad_rows, grads_pre, hidden, gated_hidden = expert(
        arrived, grad_received, expert_w, expert_down
    )
    grad_back = to_experts(dispatch(grad_rows)).reshape(slot_count, feature_count + EXTRA)
    half_out = jnp.dot(hidden, expert_down, preferred_element_type=F32).astype(BF16)
    received = arrived[:, :feature_count]
    own_in = contract(received, grads_pre[:, : 2 * HALF], 0, 0)
    other_in = contract(received, grads_pre[:, 2 * HALF :], 0, 0).astype(BF16)
    own_down = contract(gated_hidden[:, :HALF], grad_received, 0, 0)
    other_down = contract(gated_hidden[:, HALF:], grad_received, 0, 0).astype(BF16)
    grad_back, half_out, own_in, other_in, own_down, other_down = lax.optimization_barrier(
        (grad_back, half_out, own_in, other_in, own_down, other_down)
    )
    (
        grad_residual1,
        grad_attn_low,
        grad_logits,
        grad_gain_second,
        grad_queries,
        partial_keyvals,
    ) = back(
        grad_back,
        slots,
        owner,
        gates,
        cotangent,
        residual1,
        grad_second,
        misc_w,
        outt_w,
        qkv_rows,
        every,
        marks,
        segment_tile,
    )
    grad_gain_second = grad_gain_second[0]
    grad_router = contract(second_normed, grad_logits, 0, 0)
    grad_outt = contract(grad_attn_low, attended_rows, 0, 0).astype(BF16)
    grad_keyvals, their_in, their_down, returned = sum_earlier(
        partial_keyvals, tail, other_in, other_down, dispatch(half_out)
    )
    returned = returned.reshape(slot_count, feature_count)
    half_in = (own_in + their_in.astype(F32)).astype(BF16)
    half_down = (own_down + their_down.astype(F32)).astype(BF16)
    grad_qkv_rows = jnp.concatenate([grad_queries, grad_keyvals], axis=1)
    grad_qkv = contract(first_normed, grad_qkv_rows, 0, 0).astype(BF16)
    grad_first = contract(grad_qkv_rows, qkv_w, 1, 1)
    grad_norm_first, grad_gain_first = norm_backward(residual0, scale_first, gain_first, grad_first)
    grad_tokens = grad_residual1 + grad_norm_first
    grad_misc = jnp.concatenate(
        [
            grad_router[:, :EXPERTS],
            grad_gain_first[:, None],
            grad_gain_second[:, None],
            jnp.zeros((feature_count, 62), F32),
        ],
        axis=1,
    )
    slot_gates = slots.astype(F32) * jnp.dot(
        gates, owner.T.astype(F32), precision=lax.Precision.HIGHEST, preferred_element_type=F32
    )
    gates_high = lax.reduce_precision(slot_gates, exponent_bits=8, mantissa_bits=7)
    expert_mix = jnp.dot(
        gates_high.astype(BF16), returned, preferred_element_type=F32
    ) + jnp.dot((slot_gates - gates_high).astype(BF16), returned, preferred_element_type=F32)
    block_out = (forward_rows + expert_mix).astype(BF16)
    grad_misc, block_out = lax.optimization_barrier((grad_misc, block_out))
    *summed, half_in, half_down = sum_gradients(
        [
            grad.reshape(4, 2, 2, 2, 48, grad.shape[-1])
            for grad in (grad_outt, grad_misc, grad_qkv, grad_shgu, grad_shdt)
        ],
        [half_in, half_down],
    )
    sum_outt, sum_misc, sum_qkv, sum_shgu, sum_shdt = [piece[:12] for piece in summed]
    return (
        block_out,
        grad_tokens,
        sum_misc[:, EXPERTS],
        sum_qkv[:, :1536],
        sum_qkv[:, 1536:],
        sum_outt.T,
        sum_misc[:, EXPERTS + 1],
        sum_misc[:, :EXPERTS],
        sum_shgu[:, :1024],
        sum_shgu[:, 1024:],
        sum_shdt.T,
        half_in[None, :, :HALF].astype(F32),
        half_in[None, :, HALF:].astype(F32),
        half_down[None].astype(F32),
    )


def solution(mesh):
    fine = Mesh(mesh.devices.reshape(SIZES), AXES)
    rows = P(AXES, None)
    columns = P(None, AXES)
    flat = P(AXES)
    blocks = P(AXES, None, None)
    in_specs = (
        rows,
        flat,
        rows,
        flat,
        rows,
        rows,
        columns,
        flat,
        rows,
        rows,
        rows,
        columns,
        blocks,
        blocks,
        blocks,
        rows,
    )
    out_specs = (
        rows,
        rows,
        flat,
        rows,
        rows,
        columns,
        flat,
        rows,
        rows,
        rows,
        columns,
        blocks,
        blocks,
        blocks,
    )
    return jax.shard_map(shards, mesh=fine, in_specs=in_specs, out_specs=out_specs, check_vma=False)
```

```python
import functools

import jax
import jax.numpy as jnp
from jax import lax
from jax.experimental import pallas as pl
from jax.experimental.pallas import tpu as pltpu
from jax.sharding import Mesh
from jax.sharding import PartitionSpec as P

QUERY_HEADS = 12
KEY_VALUE_HEADS = 4
HEAD_SIZE = 128
EXPERTS = 64
TOPK = 6
CAP = 24
EPSILON = 1e-05

F32 = jnp.float32
BF16 = jnp.bfloat16
MESH_ID = pl.DeviceIdType.MESH
AXES = ("z", "yl", "core", "yh", "xh", "xl")
SIZES = (4, 2, 2, 2, 2, 2)
EXPERT_AXES = ("z", "yl", "yh", "xh", "xl")
COL_AXES = ("yh", "xh", "xl")

PARTS = (
    ("outt", 1536, "yzx", "zy"),
    ("misc", 128, "yz", "yz"),
    ("q", 1536, "yz", "yz"),
    ("kv", 1024, "zy", "yz"),
    ("shg", 1024, "yz", "yz"),
    ("shu", 1024, "zy", "zy"),
    ("shdt", 1024, "zy", "yz"),
)
GATHERED = tuple((name, width, order) for name, width, order, _ in PARTS)
SUMMED = tuple((name, width, order) for name, width, _, order in PARTS)
TOTAL = sum(part[1] for part in PARTS)
HALF = 256
EXPERT_SEM = 200
TOTAL = sum(part[1] for part in PARTS)


def rem(value, size):
    return lax.rem(value, jnp.int32(size))


def place():
    at = {name: lax.axis_index(name) for name in AXES}
    return {
        "x": at["xh"] * 2 + at["xl"],
        "y": at["yh"] * 2 + at["yl"],
        "z": at["z"],
        "core": at["core"],
    }


def device(axis, value):
    if axis == "x":
        return {"xh": value // 2, "xl": rem(value, 2)}
    if axis == "y":
        return {"yh": value // 2, "yl": rem(value, 2)}
    return {axis: value}


def greet(targets):
    barrier = pltpu.get_barrier_semaphore()
    for target in targets:
        pl.semaphore_signal(barrier, inc=1, device_id=target, device_id_type=MESH_ID)
    pl.semaphore_wait(barrier, len(targets))


def ring_neighbours(me):
    near = [device("x", rem(me["x"] + hops, 4)) for hops in (1, 2, 3)]
    near += [device("y", rem(me["y"] + hops, 4)) for hops in (1, 3)]
    near += [device("z", rem(me["z"] + hops, 4)) for hops in (1, 3)]
    return near + [{"core": 1 - me["core"]}]


class Wires:
    def __init__(self, send_sems, recv_sems, local_sems):
        self.send, self.recv, self.local = send_sems, recv_sems, local_sems
        self.used, self.used_local, self.started, self.kept = 0, 0, [], []

    def remote(self, source, target, where):
        copy = pltpu.make_async_remote_copy(
            src_ref=source,
            dst_ref=target,
            send_sem=self.send.at[self.used],
            recv_sem=self.recv.at[self.used],
            device_id=where,
            device_id_type=MESH_ID,
        )
        self.used += 1
        copy.start()
        self.started.append(copy)
        return copy

    def copy(self, source, target):
        copy = pltpu.make_async_copy(source, target, self.local.at[self.used_local])
        self.used_local += 1
        copy.start()
        return copy

    def finish(self):
        for copy in self.started:
            copy.wait_send()


def balanced_offsets():
    left = [(x, y, z) for x in range(4) for y in range(4) for z in range(4) if x + y + z > 0]
    load, order = [0] * 6, []

    def uses(offset):
        used = [0] * 6
        for axis, hops in enumerate(offset):
            used[2 * axis] += hops in (1, 2)
            used[2 * axis + 1] += hops in (2, 3)
        return used

    def cost(offset):
        used = uses(offset)
        after = [a + b for a, b in zip(load, used)]
        mean = sum(after) / 6
        return (max(after), sum((a - mean) ** 2 for a in after), -sum(used))

    while left:
        best = min(left, key=cost)
        load = [a + b for a, b in zip(load, uses(best))]
        left.remove(best)
        order.append(best)
    return order


OFFSETS = balanced_offsets()


def chip_at(me, offset, sign=1):
    x, y, z = [rem(me[axis] + (sign * hops) % 4, 4) for axis, hops in zip("xyz", offset)]
    where = {"z": z, "yh": y // 2, "yl": rem(y, 2), "xh": x // 2, "xl": rem(x, 2)}
    return where, z * 16 + rem(y, 2) * 8 + (y // 2) * 4 + x


def halves(width):
    first = width // 256 * 128 if width > 128 else width
    return first, width - first


def spread_rows(shape, swap):
    dense = lax.broadcasted_iota(jnp.int32, shape, 1 if swap else 0)
    padded = lax.broadcasted_iota(jnp.int32, shape, 0 if swap else 1)
    shift = jnp.zeros(shape, jnp.int32)
    for edge in (12, 24, 36):
        shift = shift + jnp.where(dense >= edge, 4, 0)
    return dense + shift == padded


def block_ref(ref, axes, me, axis, value, columns):
    spot = dict(me)
    spot[axis] = value
    z = slice(None) if "z" in axes else spot["z"]
    yl = slice(None) if "y" in axes else rem(spot["y"], 2)
    yh = slice(None) if "y" in axes else spot["y"] // 2
    return ref.at[z, yl, me["core"], yh, :, columns]


def gather_kernel(shard_ref, gate_ref, up_ref, down_ref, *rest):
    count = len(GATHERED)
    outs = rest[:count]
    expert_in, expert_out, landed = rest[count : count + 3]
    stages = rest[count + 3 : 2 * count + 3]
    send_sems, recv_sems, local_sems = rest[2 * count + 3 :]
    me = place()
    nxt = {axis: rem(me[axis] + 1, 4) for axis in "xyz"}
    opp = {axis: rem(me[axis] + 2, 4) for axis in "xyz"}
    prv = {axis: rem(me[axis] + 3, 4) for axis in "xyz"}
    sibling = {"core": 1 - me["core"]}
    partner = {"core": 1 - me["core"], "xl": 1 - lax.axis_index("xl")}
    crossed = me["core"] != lax.axis_index("xl")
    greet(
        [device("x", nxt["x"]), device("x", opp["x"]), device("x", prv["x"])]
        + [device("y", nxt["y"]), device("y", prv["y"])]
        + [device("z", nxt["z"]), device("z", prv["z"]), sibling, partner]
    )
    wires = Wires(send_sems, recv_sems, local_sems)
    runs, start = [], 0
    for index, (name, width, order) in enumerate(GATHERED):
        last_x = len(order) == 3
        quarter = width // 4 if last_x else width
        run = {
            "out": outs[index],
            "order": order,
            "width": quarter,
            "done": "",
            "stage": stages[index],
            "start": start,
            "landed": landed.at[:, :, pl.ds(start, quarter)],
            "base": me["x"] * quarter if last_x else 0,
            "first": [],
            "shared": [],
        }

        def piece(x):
            if last_x:
                return shard_ref.at[:, pl.ds(pl.multiple_of(start + x * quarter, 128), quarter)]
            return shard_ref.at[:, pl.ds(start, quarter)]

        for where in (nxt, prv, opp):
            run["first"].append(
                wires.remote(piece(where["x"]), run["landed"].at[me["x"]], device("x", where["x"]))
            )
        run["bring"] = wires.copy(piece(me["x"]), run["landed"].at[me["x"]])
        runs.append(run)
        start += width

    whole = [
        (gate_ref, expert_in.at[:, pl.ds(0, HALF)]),
        (up_ref, expert_in.at[:, pl.ds(HALF, HALF)]),
        (down_ref, expert_out.at[pl.ds(0, HALF)]),
    ]

    def moved(slot):
        source, target = whole[slot]
        return pltpu.make_async_remote_copy(
            src_ref=source,
            dst_ref=target,
            send_sem=send_sems.at[EXPERT_SEM + slot],
            recv_sem=recv_sems.at[EXPERT_SEM + slot],
            device_id=partner,
            device_id_type=MESH_ID,
        )

    def kept(slot):
        source, target = whole[slot]
        return pltpu.make_async_copy(source, target, local_sems.at[20 + slot])

    @pl.when(crossed)
    def _():
        for slot in range(3):
            moved(slot).start()

    @pl.when(jnp.logical_not(crossed))
    def _():
        for slot in range(3):
            kept(slot).start()

    def part_columns(run, axis, value, which):
        base = value * run["width"] if axis == "x" else run["base"]
        left, size = 0, run["width"]
        if which is not None:
            first_half, second_half = halves(run["width"])
            left, size = (0, first_half) if which == 0 else (first_half, second_half)
        if isinstance(base, int):
            return pl.ds(base + left, size)
        return pl.ds(pl.multiple_of(base + left, 128), size)

    def blocks(run, axis, value, which=None):
        columns = part_columns(run, axis, value, which)
        return block_ref(run["out"], run["done"], me, axis, value, columns)

    def begin(run, axis, source=None):
        target = blocks(run, axis, me[axis])
        source = target if source is None else source
        run["forth"] = wires.remote(source, target, device(axis, nxt[axis]))
        run["back"] = wires.remote(source, target, device(axis, prv[axis]))

    pick = spread_rows((48, 64), False).astype(BF16)
    for run in runs:
        run["bring"].wait()
        for copy in run["first"]:
            copy.wait_recv()
        for left in range(0, run["width"], 512):
            size = min(512, run["width"] - left)
            left_in = run["start"] + left
            piece_rows = landed[:, :, left_in : left_in + size].reshape(64, size)
            run["stage"][:, left : left + size] = jnp.dot(
                pick, piece_rows, preferred_element_type=F32
            ).astype(BF16)
        axis = run["order"][0]
        begin(run, axis, run["stage"])
        run["own"] = wires.copy(run["stage"], blocks(run, axis, me[axis]))

    def forward(run, axis):
        run["forth"].wait_recv()
        source = blocks(run, axis, prv[axis], 0)
        run["more"] = [wires.remote(source, source, device(axis, nxt[axis]))]
        run["back"].wait_recv()
        if halves(run["width"])[1] > 0:
            source = blocks(run, axis, nxt[axis], 1)
            run["more"].append(wires.remote(source, source, device(axis, prv[axis])))

    def share(run, axis, value):
        source = blocks(run, axis, value)
        run["shared"].append(wires.remote(source, source, sibling))

    def advance(run, step):
        axis = run["order"][step]
        for copy in run["more"]:
            copy.wait_recv()
        if step == len(run["order"]) - 1:
            share(run, axis, opp[axis])
            return
        if step == 0:
            run["own"].wait()
        run["done"] = run["done"] + axis
        following = run["order"][step + 1]
        begin(run, following)
        if step + 1 == len(run["order"]) - 1:
            share(run, following, me[following])

    def last_forward(run):
        axis = run["order"][-1]
        forward(run, axis)
        share(run, axis, prv[axis])
        share(run, axis, nxt[axis])

    threes = [run for run in runs if len(run["order"]) == 3]
    twos = [run for run in runs if len(run["order"]) == 2]
    for run in runs:
        forward(run, run["order"][0])
    for run in runs:
        advance(run, 0)
    for run in threes:
        forward(run, run["order"][1])
    for run in threes:
        advance(run, 1)
    for run in twos:
        last_forward(run)
    for run in threes:
        last_forward(run)

    @pl.when(crossed)
    def _():
        for slot in range(3):
            moved(slot).wait_recv()

    @pl.when(jnp.logical_not(crossed))
    def _():
        for slot in range(3):
            kept(slot).wait()

    handed = [
        wires.remote(
            expert_in.at[:, pl.ds(0, 2 * HALF)], expert_in.at[:, pl.ds(2 * HALF, 2 * HALF)], sibling
        ),
        wires.remote(expert_out.at[pl.ds(0, HALF)], expert_out.at[pl.ds(HALF, HALF)], sibling),
    ]
    for run in twos + threes:
        advance(run, len(run["order"]) - 1)
    for run in runs:
        for copy in run["shared"]:
            copy.wait_recv()
    for copy in handed:
        copy.wait_recv()
    wires.finish()

    @pl.when(crossed)
    def _():
        for slot in range(3):
            moved(slot).wait_send()


def gather_weights(shard, gate_w, up_w, down_w):
    shapes = [jax.ShapeDtypeStruct((4, 2, 2, 2, 48, width), BF16) for _, width, _ in GATHERED]
    shapes += [
        jax.ShapeDtypeStruct((gate_w.shape[0], 4 * HALF), BF16),
        jax.ShapeDtypeStruct((2 * HALF, down_w.shape[1]), BF16),
    ]
    anywhere = pl.BlockSpec(memory_space=pl.ANY)
    return pl.pallas_call(
        gather_kernel,
        out_shape=shapes,
        in_specs=[pl.BlockSpec(memory_space=pltpu.VMEM)] + [anywhere] * 3,
        out_specs=[anywhere] * (len(GATHERED) + 2),
        scratch_shapes=[pltpu.VMEM((4, 16, TOTAL), BF16)]
        + [
            pltpu.VMEM((48, width // 4 if len(order) == 3 else width), BF16)
            for _, width, order in GATHERED
        ]
        + [
            pltpu.SemaphoreType.DMA((EXPERT_SEM + 4,)),
            pltpu.SemaphoreType.DMA((EXPERT_SEM + 4,)),
            pltpu.SemaphoreType.DMA((24,)),
        ],
        compiler_params=pltpu.CompilerParams(
            collective_id=0, has_side_effects=True, vmem_limit_bytes=16 * 1024 * 1024
        ),
        cost_estimate=pl.CostEstimate(flops=0, bytes_accessed=200_000_000, transcendentals=0),
    )(shard, gate_w, up_w, down_w)


class Summing:
    def __init__(self, wires, me, parts, grads, outs, scratch):
        self.wires, self.me = wires, me
        self.next = {axis: rem(me[axis] + 1, 4) for axis in "xyz"}
        self.opposite = {axis: rem(me[axis] + 2, 4) for axis in "xyz"}
        self.previous = {axis: rem(me[axis] + 3, 4) for axis in "xyz"}
        self.sibling = {"core": 1 - me["core"]}
        count = len(parts)
        self.runs = []
        for index, (name, width, order) in enumerate(parts):
            self.runs.append(
                {
                    "order": order[::-1],
                    "width": width // 4 if len(order) == 3 else width,
                    "left": "zy",
                    "turn": 0,
                    "grads": grads[index],
                    "out": outs[index],
                    "own": scratch[index],
                    "theirs": scratch[count + index],
                    "near1": scratch[2 * count + index],
                    "near2": scratch[3 * count + index],
                    "ends": scratch[4 * count + index],
                    "arrived": scratch[5 * count + index],
                }
            )

    def spot(self, left_axes, axis, value, with_core):
        at = dict(self.me)
        if axis is not None:
            at[axis] = value
        whole = [name for name in left_axes if name != axis]
        z = slice(None) if "z" in whole else at["z"]
        yl = slice(None) if "y" in whole else rem(at["y"], 2)
        yh = slice(None) if "y" in whole else at["y"] // 2
        return (z, yl) + (() if with_core is None else (with_core,)) + (yh,)

    def lead(self, left_axes, axis):
        dims = []
        for name in ("z", "y"):
            if name in left_axes and name != axis:
                dims += [4] if name == "z" else [2, 2]
        return dims

    def add_into(self, target, sources, dims):
        total = 1
        for size in dims:
            total *= size

        def body(index):
            for row in range(0, 48, 16):
                at = index + (pl.ds(row, 16),)
                value = target[at].astype(F32)
                for source in sources:
                    value = value + source[at].astype(F32)
                target[at] = value.astype(target.dtype)

        def step(flat, carry):
            index, rest_flat = [], flat
            for size in reversed(dims):
                index.append(rem(rest_flat, size))
                rest_flat = rest_flat // size
            body(tuple(reversed(index)))
            return carry

        if total == 1:
            body(())
        else:
            lax.fori_loop(0, total, step, 0)

    def columns_of(self, run, axis, value, which):
        base = 0
        if len(run["order"]) == 3:
            base = (value if axis == "x" else self.me["x"]) * run["width"]
        left, size = 0, run["width"]
        if which is not None:
            first_half, second_half = halves(run["width"])
            left, size = (0, first_half) if which == 0 else (first_half, second_half)
        if isinstance(base, int):
            return pl.ds(base + left, size)
        return pl.ds(pl.multiple_of(base + left, 128), size)

    def chunk(self, run, axis, value, which=None, ref=None, with_core=None):
        ref = run["own"] if ref is None else ref
        columns = self.columns_of(run, axis, value, which)
        return ref.at[self.spot(run["left"], axis, value, with_core) + (slice(None), columns)]

    def pair(self, run, axis, value):
        core = self.me["core"]
        give = self.wires.remote(
            self.chunk(run, axis, value, None, run["grads"], 1 - core),
            self.chunk(run, axis, value, None, run["theirs"]),
            self.sibling,
        )
        keep = self.wires.copy(
            self.chunk(run, axis, value, None, run["grads"], core), self.chunk(run, axis, value)
        )
        return give, keep

    def join(self, run, axis, value, copies):
        copies[0].wait_recv()
        copies[1].wait()
        self.add_into(
            self.chunk(run, axis, value),
            [self.chunk(run, axis, value, None, run["theirs"])],
            self.lead(run["left"], axis),
        )

    def slots(self, run, axis):
        dims = self.lead(run["left"], axis)
        ref = (run["near1"], run["near2"], run["ends"])[run["turn"]]
        if not dims:
            ref = ref.at[:, pl.ds(0, 48)]
        return ref.at[0], ref.at[1], ref.at[2], dims

    def part(self, ref, run, which, dims):
        first_half, second_half = halves(run["width"])
        columns = pl.ds(0, first_half) if which == 0 else pl.ds(first_half, second_half)
        return ref.at[(slice(None),) * len(dims) + (slice(None), columns)]

    def ring_open(self, run):
        axis = run["order"][run["turn"]]
        _, _, passing, dims = self.slots(run, axis)
        far = self.opposite[axis]
        run["passing"] = [
            self.wires.remote(
                self.chunk(run, axis, far, 0),
                self.part(passing, run, 0, dims),
                device(axis, self.next[axis]),
            )
        ]
        if halves(run["width"])[1]:
            run["passing"].append(
                self.wires.remote(
                    self.chunk(run, axis, far, 1),
                    self.part(passing, run, 1, dims),
                    device(axis, self.previous[axis]),
                )
            )

    def ring_near(self, run):
        axis = run["order"][run["turn"]]
        from_prv, from_nxt, _, dims = self.slots(run, axis)
        nxt, prv = self.next[axis], self.previous[axis]
        run["near"] = []
        if halves(run["width"])[1]:
            run["near"].append(
                self.wires.remote(
                    self.chunk(run, axis, nxt, 1),
                    self.part(from_prv, run, 1, dims),
                    device(axis, nxt),
                )
            )
        run["near"].append(
            self.wires.remote(
                self.chunk(run, axis, prv, 0), self.part(from_nxt, run, 0, dims), device(axis, prv)
            )
        )

    def ring_pass(self, run):
        axis = run["order"][run["turn"]]
        from_prv, from_nxt, passing, dims = self.slots(run, axis)
        nxt, prv = self.next[axis], self.previous[axis]
        run["passing"][0].wait_recv()
        self.add_into(self.chunk(run, axis, nxt, 0), [self.part(passing, run, 0, dims)], dims)
        run["near"].append(
            self.wires.remote(
                self.chunk(run, axis, nxt, 0), self.part(from_prv, run, 0, dims), device(axis, nxt)
            )
        )
        if halves(run["width"])[1]:
            run["passing"][1].wait_recv()
            self.add_into(self.chunk(run, axis, prv, 1), [self.part(passing, run, 1, dims)], dims)
            run["near"].append(
                self.wires.remote(
                    self.chunk(run, axis, prv, 1),
                    self.part(from_nxt, run, 1, dims),
                    device(axis, prv),
                )
            )

    def ring_close(self, run):
        axis = run["order"][run["turn"]]
        from_prv, from_nxt, _, dims = self.slots(run, axis)
        for copy in run["near"]:
            copy.wait_recv()
        self.add_into(self.chunk(run, axis, self.me[axis]), [from_prv, from_nxt], dims)
        run["left"] = run["left"].replace(axis, "")
        run["turn"] += 1

    def turn(self, run):
        self.ring_close(run)
        self.ring_open(run)
        self.ring_near(run)

    def spread(self, run):
        me, width = self.me, run["width"]
        third = len(run["order"]) == 3
        summed = run["own"].at[me["z"], rem(me["y"], 2), me["y"] // 2]
        exact = lax.Precision.HIGHEST if summed.dtype == F32 else None
        pick = spread_rows((64, 48), True).astype(summed.dtype)
        staging = run["ends"].at[3] if third else run["near2"].at[3]
        base = me["x"] * width if third else 0
        for left in range(0, width, 512):
            size = min(512, width - left)
            columns = pl.ds(left, size)
            if third:
                columns = pl.ds(pl.multiple_of(base + left, 128), size)
            staging[:, left : left + size] = jnp.dot(
                pick, summed[:, columns], preferred_element_type=F32, precision=exact
            ).astype(staging.dtype)
        if third:
            lands = run["arrived"].at[:, pl.ds(pl.multiple_of(base, 128), width)]
        else:
            lands = run["arrived"].at[me["x"]]
        run["copies"] = []
        for where in (self.next, self.opposite, self.previous):
            row = pl.ds(pl.multiple_of(where["x"] * 16, 16), 16)
            run["copies"].append(
                self.wires.remote(staging.at[row], lands, device("x", where["x"]))
            )
        row = pl.ds(pl.multiple_of(me["x"] * 16, 16), 16)
        run["keep"] = self.wires.copy(staging.at[row], lands)

    def deliver(self, run):
        run["keep"].wait()
        for copy in run["copies"]:
            copy.wait_recv()
        if len(run["order"]) == 3:
            run["out"][...] = run["arrived"][...].astype(F32)
        else:
            value = run["arrived"][0].astype(F32)
            for place_x in range(1, 4):
                value = value + run["arrived"][place_x].astype(F32)
            run["out"][...] = value

    def stages(self):
        runs = self.runs
        threes = [run for run in runs if len(run["order"]) == 3]
        twos = [run for run in runs if len(run["order"]) == 2]
        begun = []
        for where in (self.opposite, self.next, self.previous, self.me):
            begun.append([self.pair(run, run["order"][0], where[run["order"][0]]) for run in runs])
        yield
        for run, copies in zip(runs, begun[0]):
            axis = run["order"][0]
            self.join(run, axis, self.opposite[axis], copies)
            self.ring_open(run)
        for run, nexts, prevs in zip(runs, begun[1], begun[2]):
            axis = run["order"][0]
            self.join(run, axis, self.next[axis], nexts)
            self.join(run, axis, self.previous[axis], prevs)
            self.ring_near(run)
        yield
        for run in threes:
            self.ring_pass(run)
        for run, copies in zip(runs, begun[3]):
            axis = run["order"][0]
            self.join(run, axis, self.me[axis], copies)
        for run in twos:
            self.ring_pass(run)
        yield
        for run in threes:
            self.turn(run)
        for run in threes:
            self.ring_pass(run)
        for run in twos:
            self.turn(run)
        yield
        for run in threes:
            self.turn(run)
        for run in twos:
            self.ring_pass(run)
        for run in threes:
            self.ring_pass(run)
        yield
        for run in twos:
            self.ring_close(run)
            self.spread(run)
        for run in threes:
            self.ring_close(run)
            self.spread(run)
        yield
        for run in runs:
            self.deliver(run)
        yield


def summing_scratch(parts):
    own, theirs, near1, near2, ends, arrived = [], [], [], [], [], []
    for name, width, order in parts:
        kind = F32 if name == "misc" else BF16
        own.append(pltpu.VMEM((4, 2, 2, 48, width), kind))
        theirs.append(pltpu.VMEM((4, 2, 2, 48, width), kind))
        if len(order) == 3:
            quarter = width // 4
            near1.append(pltpu.VMEM((3, 4, 2, 2, 48, quarter), kind))
            near2.append(pltpu.VMEM((3, 2, 2, 48, quarter), kind))
            ends.append(pltpu.VMEM((4, 64, quarter), kind))
            arrived.append(pltpu.VMEM((16, width), kind))
        else:
            near1.append(pltpu.VMEM((3, 2, 2, 48, width) if order == "yz" else (3, 4, 48, width), kind))
            near2.append(pltpu.VMEM((4, 64, width), kind))
            ends.append(pltpu.VMEM((16, 128), kind))
            arrived.append(pltpu.VMEM((4, 16, width), kind))
    return own + theirs + near1 + near2 + ends + arrived


SHARED_PARTS = [part for part in SUMMED if part[0].startswith("sh")]
LAST_PARTS = [part for part in SUMMED if not part[0].startswith("sh")]

def last_kernel(*refs):
    count = len(LAST_PARTS)
    grads = refs[:count]
    expert_from = refs[count : count + 2]
    outs = refs[count + 2 : 2 * count + 2]
    expert_to = refs[2 * count + 2 : 2 * count + 4]
    scratch = refs[2 * count + 4 : 8 * count + 4]
    swap_send, swap_recv, swap_local, send_sems, recv_sems, local_sems = refs[8 * count + 4 :]
    me = place()
    partner = {"core": 1 - me["core"], "xl": 1 - lax.axis_index("xl")}
    crossed = me["core"] != lax.axis_index("xl")
    greet(ring_neighbours(me) + [partner])

    def moved(slot):
        return pltpu.make_async_remote_copy(
            src_ref=expert_from[slot],
            dst_ref=expert_to[slot],
            send_sem=swap_send.at[slot],
            recv_sem=swap_recv.at[slot],
            device_id=partner,
            device_id_type=MESH_ID,
        )

    def kept(slot):
        return pltpu.make_async_copy(expert_from[slot], expert_to[slot], swap_local.at[slot])

    wires = Wires(send_sems, recv_sems, local_sems)
    stages = Summing(wires, me, LAST_PARTS, grads, outs, scratch).stages()
    next(stages)
    next(stages)

    @pl.when(crossed)
    def _():
        for slot in range(2):
            moved(slot).start()

    @pl.when(jnp.logical_not(crossed))
    def _():
        for slot in range(2):
            kept(slot).start()

    for _ in stages:
        pass
    wires.finish()

    @pl.when(crossed)
    def _():
        for slot in range(2):
            moved(slot).wait_recv()
            moved(slot).wait_send()

    @pl.when(jnp.logical_not(crossed))
    def _():
        for slot in range(2):
            kept(slot).wait()


def sum_last(grads, expert_grads):
    anywhere = pl.BlockSpec(memory_space=pl.ANY)
    vmem = pl.BlockSpec(memory_space=pltpu.VMEM)
    count = len(LAST_PARTS)
    return pl.pallas_call(
        last_kernel,
        out_shape=[jax.ShapeDtypeStruct((16, width), F32) for _, width, _ in LAST_PARTS]
        + [jax.ShapeDtypeStruct(grad.shape, grad.dtype) for grad in expert_grads],
        in_specs=[anywhere] * (count + 2),
        out_specs=[vmem] * count + [anywhere] * 2,
        scratch_shapes=summing_scratch(LAST_PARTS)
        + [
            pltpu.SemaphoreType.DMA((2,)),
            pltpu.SemaphoreType.DMA((2,)),
            pltpu.SemaphoreType.DMA((2,)),
            pltpu.SemaphoreType.DMA((140,)),
            pltpu.SemaphoreType.DMA((140,)),
            pltpu.SemaphoreType.DMA((32,)),
        ],
        compiler_params=pltpu.CompilerParams(
            collective_id=1, has_side_effects=True, vmem_limit_bytes=56 * 1024 * 1024
        ),
        cost_estimate=pl.CostEstimate(
            flops=1_000_000_000, bytes_accessed=200_000_000, transcendentals=0
        ),
    )(*grads, *expert_grads)


def col_device(col):
    return {"yh": col // 4, "xh": rem(col // 2, 2), "xl": rem(col, 2)}


def col_index():
    return lax.axis_index("yh") * 4 + lax.axis_index("xh") * 2 + lax.axis_index("xl")


def later_kernel(own_ref, marks_ref, out_ref, marks_out, send_sems, recv_sems, local_sem):
    me = col_index()
    rows = own_ref.shape[0]
    tail = marks_ref.shape[0]
    late = pl.ds(rows - tail, tail)
    greet([col_device(rem(me + far, 8)) for far in range(1, 8)])

    def copies(far, first):
        there = col_device(rem(me + far, 8))
        pairs = [(own_ref, out_ref.at[me])]
        if first:
            pairs = [(own_ref.at[late], out_ref.at[0, late]), (marks_ref, marks_out)]
        return [
            pltpu.make_async_remote_copy(
                src_ref=source,
                dst_ref=target,
                send_sem=send_sems.at[far, number],
                recv_sem=recv_sems.at[far, number],
                device_id=there,
                device_id_type=MESH_ID,
            )
            for number, (source, target) in enumerate(pairs)
        ]

    def each(far, first, condition, act):
        @pl.when(condition)
        def _():
            for copy in copies(far, first):
                act(copy)

    for far in range(7, 0, -1):
        each(far, False, (me > 0) & (me + far < 8), lambda copy: copy.start())
        each(far, True, me == 0, lambda copy: copy.start())
    keep = pltpu.make_async_copy(own_ref, out_ref.at[me], local_sem)
    keep.start()

    @pl.when(me == 0)
    def _():
        marks_out[...] = marks_ref[...]

    @pl.when(me > 0)
    def _():
        out_ref[0, : rows - tail] = jnp.zeros((rows - tail, own_ref.shape[1]), own_ref.dtype)

    for far in range(1, 8):

        @pl.when(me + far < 8)
        def _():
            out_ref[me + far] = jnp.zeros(own_ref.shape, own_ref.dtype)

    keep.wait()
    for far in range(1, 8):
        each(far, False, me > far, lambda copy: copy.wait_recv())
        each(far, True, me == far, lambda copy: copy.wait_recv())
        each(far, False, (me > 0) & (me + far < 8), lambda copy: copy.wait_send())
        each(far, True, me == 0, lambda copy: copy.wait_send())


def to_later(rows, marks):
    vmem = pl.BlockSpec(memory_space=pltpu.VMEM)
    return pl.pallas_call(
        later_kernel,
        out_shape=[
            jax.ShapeDtypeStruct((8,) + rows.shape, rows.dtype),
            jax.ShapeDtypeStruct(marks.shape, marks.dtype),
        ],
        in_specs=[vmem, vmem],
        out_specs=[vmem, vmem],
        scratch_shapes=[
            pltpu.SemaphoreType.DMA((8, 2)),
            pltpu.SemaphoreType.DMA((8, 2)),
            pltpu.SemaphoreType.DMA,
        ],
        compiler_params=pltpu.CompilerParams(
            collective_id=2, has_side_effects=True, vmem_limit_bytes=16 * 1024 * 1024
        ),
        cost_estimate=pl.CostEstimate(flops=0, bytes_accessed=70_000_000, transcendentals=0),
    )(rows, marks)


VMEM_SPEC = pl.BlockSpec(memory_space=pltpu.VMEM)
GROUP = QUERY_HEADS // KEY_VALUE_HEADS
EXTRA = 128


def dot(left, right, left_dim=1, right_dim=0):
    return lax.dot_general(
        left, right, (((left_dim,), (right_dim,)), ((), ())), preferred_element_type=F32
    )


def rounded_parts(value):
    first = value.astype(BF16)
    left = value - first.astype(F32)
    second = left.astype(BF16)
    return [first, second, (left - second.astype(F32)).astype(BF16)]


def lane_column(index):
    return (lax.broadcasted_iota(jnp.int32, (16, 128), 1) == index).astype(BF16)


def gain_row(misc_ref, index):
    return dot(lane_column(index), misc_ref[...], 1, 1)[:1]


def allowed_pairs(marks_ref, segments_ref, rows, keys):
    me = col_index()
    shape = (rows, keys)
    own = segments_ref[:, :1]
    first_length = jnp.where(
        me == 0,
        jnp.sum((own == 0.0).astype(F32), axis=0, keepdims=True),
        marks_ref[:1, :1].astype(F32),
    )
    last_start = (me * rows).astype(F32) + jnp.sum(
        (own < 2.0).astype(F32), axis=0, keepdims=True
    )
    lowest = jnp.where(own == 0.0, 0.0, jnp.where(own == 1.0, first_length, last_start))
    key = lax.broadcasted_iota(jnp.int32, shape, 1)
    query = lax.broadcasted_iota(jnp.int32, shape, 0) + me * rows
    return (key <= query) & (key.astype(F32) >= lowest)


def head_columns(ref, group):
    width = GROUP * HEAD_SIZE
    return jnp.concatenate(
        [
            ref[:, group * width + head * HEAD_SIZE : group * width + (head + 1) * HEAD_SIZE]
            for head in range(GROUP)
        ],
        axis=0,
    )


def head_weights(queries, keys, allowed):
    scores = dot(queries, keys, 1, 1) * (HEAD_SIZE ** (-0.5))
    scores = jnp.where(allowed, scores, -1e30)
    shifted = jnp.exp(scores - jnp.max(scores, axis=1, keepdims=True))
    return shifted / jnp.sum(shifted, axis=1, keepdims=True)


def middle_kernel(
    qkv_ref,
    every_ref,
    marks_ref,
    segments_ref,
    tokens_ref,
    outt_ref,
    misc_ref,
    named_ref,
    slots_ref,
    owner_ref,
    attended_ref,
    residual_ref,
    normed_ref,
    gates_ref,
    outgoing_ref,
):
    rows, features = tokens_ref.shape
    width = KEY_VALUE_HEADS * HEAD_SIZE
    keys_count = 8 * rows
    allowed = allowed_pairs(marks_ref, segments_ref, rows, keys_count)
    allowed = jnp.concatenate([allowed.astype(F32)] * GROUP, axis=0) > 0.5
    for group in range(KEY_VALUE_HEADS):
        queries = head_columns(qkv_ref, group)
        columns = pl.ds(group * HEAD_SIZE, HEAD_SIZE)
        keys = every_ref[:, :, columns].reshape(keys_count, HEAD_SIZE)
        values = every_ref[:, :, pl.ds(width + group * HEAD_SIZE, HEAD_SIZE)].reshape(
            keys_count, HEAD_SIZE
        )
        weights = head_weights(queries, keys, allowed)
        mixed = dot(weights.astype(BF16), values).astype(BF16)
        for head in range(GROUP):
            at = (group * GROUP + head) * HEAD_SIZE
            attended_ref[:, at : at + HEAD_SIZE] = mixed[head * rows : (head + 1) * rows]
    attended = attended_ref[...]
    total = jnp.zeros((rows, 1), F32)
    for left in range(0, features, 512):
        piece = tokens_ref[:, left : left + 512].astype(F32) + dot(
            attended, outt_ref[left : left + 512], 1, 1
        )
        residual_ref[:, left : left + 512] = piece
        total = total + jnp.sum(piece * piece, axis=1, keepdims=True)
    scale = lax.rsqrt(total / features + EPSILON)
    normed_ref[...] = (residual_ref[...] * scale * gain_row(misc_ref, EXPERTS + 1)).astype(BF16)
    normed = normed_ref[...]
    logits = dot(normed, misc_ref[...])
    named = named_ref[...] > 0.5
    chosen = jnp.where(named, logits, -1e30)
    chosen_exp = jnp.where(named, jnp.exp(chosen - jnp.max(chosen, axis=1, keepdims=True)), 0.0)
    gates = chosen_exp / jnp.sum(chosen_exp, axis=1, keepdims=True)
    gates_ref[...] = gates
    parts = jnp.concatenate(rounded_parts(gates), axis=1)

    def send_rows(step, carry):
        at = pl.ds(pl.multiple_of(step * 256, 256), 256)
        slots = slots_ref[at]
        outgoing_ref[at, :features] = dot(slots, normed).astype(BF16)
        gate_parts = dot(slots, parts)
        owner = owner_ref[at].astype(F32)
        lane = lax.broadcasted_iota(jnp.int32, (256, EXTRA), 1)
        extra = jnp.zeros((256, EXTRA), F32)
        for part in range(3):
            column = jnp.sum(
                gate_parts[:, part * 128 : (part + 1) * 128] * owner, axis=1, keepdims=True
            )
            extra = jnp.where(lane == part, column, extra)
        outgoing_ref[at, features:] = extra.astype(BF16)
        return carry

    lax.fori_loop(0, slots_ref.shape[0] // 256, send_rows, 0)


def middle(qkv, every, marks, segments, tokens, outt, misc, named, slots, owner):
    rows, features = tokens.shape
    return pl.pallas_call(
        middle_kernel,
        out_shape=[
            jax.ShapeDtypeStruct((rows, features), BF16),
            jax.ShapeDtypeStruct((rows, features), F32),
            jax.ShapeDtypeStruct((rows, features), BF16),
            jax.ShapeDtypeStruct((rows, 128), F32),
            jax.ShapeDtypeStruct((slots.shape[0], features + EXTRA), BF16),
        ],
        in_specs=[VMEM_SPEC] * 10,
        out_specs=[VMEM_SPEC] * 5,
        compiler_params=pltpu.CompilerParams(vmem_limit_bytes=48 * 1024 * 1024),
        cost_estimate=pl.CostEstimate(
            flops=6_000_000_000, bytes_accessed=20_000_000, transcendentals=2_000_000
        ),
    )(qkv, every, marks, segments, tokens, outt, misc, named, slots, owner)


GROUP_BLOCKS = 16


def expert_kernel(
    outgoing_ref,
    cotangent_in,
    weight_ref,
    down_ref,
    returned_ref,
    rows_out,
    own_in_ref,
    other_in_ref,
    own_down_ref,
    other_down_ref,
    landed,
    cotangents,
    back,
    grads,
    hiddens,
    gated,
    rows_staged,
    other_in,
    other_down,
    send_sems,
    recv_sems,
    local_sems,
):
    features = cotangent_in.shape[2]
    spot = place()
    chips = [chip_at(spot, offset) for offset in OFFSETS]
    sources = [chip_at(spot, offset, -1) for offset in OFFSETS]
    mine = chip_at(spot, (0, 0, 0))[1]
    greet([where for where, _ in chips])
    wires = Wires(send_sems, recv_sems, local_sems)
    rows_in = [wires.copy(outgoing_ref.at[mine], landed.at[0])]
    for number, (where, holder) in enumerate(chips):
        rows_in.append(wires.remote(outgoing_ref.at[holder], landed.at[number + 1], where))
    holders = [mine] + [holder for _, holder in sources]
    brought = [
        wires.copy(cotangent_in.at[holder], cotangents.at[number])
        for number, holder in enumerate(holders)
    ]
    count = len(holders)
    tile = GROUP_BLOCKS * CAP
    returning = []

    def flat(ref, first, columns):
        blocks = ref[first : first + GROUP_BLOCKS, :, columns].astype(F32)
        return blocks.reshape(tile, blocks.shape[-1]).astype(BF16)

    def blocks_of(value):
        return value.reshape(GROUP_BLOCKS, CAP, value.shape[-1]).astype(BF16)

    for first in range(0, count, GROUP_BLOCKS):
        for number in range(first, first + GROUP_BLOCKS):
            brought[number].wait()
            if number == 0:
                rows_in[number].wait()
            else:
                rows_in[number].wait_recv()
        at = pl.ds(first * CAP, tile)
        extra = flat(landed, first, pl.ds(features, EXTRA)).astype(F32)
        gate = extra[:, :1] + extra[:, 1:2] + extra[:, 2:3]
        everything = pl.ds(0, features)
        pre = dot(flat(landed, first, everything), weight_ref[...])
        grad_hidden = dot(flat(cotangents, first, everything), down_ref[...], 1, 1)
        along = jnp.zeros((tile, 1), F32)
        for part in range(2):
            base = part * 2 * HALF
            gate_pre, up_pre = pre[:, base : base + HALF], pre[:, base + HALF : base + 2 * HALF]
            grad_part = grad_hidden[:, part * HALF : (part + 1) * HALF]
            sigmoid = 1.0 / (1.0 + jnp.exp(-gate_pre))
            silu = gate_pre * sigmoid
            hidden = silu * up_pre
            along = along + jnp.sum(hidden * grad_part, axis=1, keepdims=True)
            gated_grad = grad_part * gate
            grads[at, base : base + HALF] = (
                gated_grad * up_pre * sigmoid * (1.0 + gate_pre * (1.0 - sigmoid))
            ).astype(BF16)
            grads[at, base + HALF : base + 2 * HALF] = (gated_grad * silu).astype(BF16)
            hiddens[at, part * HALF : (part + 1) * HALF] = hidden.astype(BF16)
            gated[at, part * HALF : (part + 1) * HALF] = (hidden * gate).astype(BF16)
        group_grads = grads[at]
        for left in range(0, features, 512):
            back[first : first + GROUP_BLOCKS, :, left : left + 512] = blocks_of(
                dot(group_grads, weight_ref[left : left + 512], 1, 1)
            )
        lane = lax.broadcasted_iota(jnp.int32, (tile, EXTRA), 1)
        value = jnp.zeros((tile, EXTRA), F32)
        for part, column in enumerate(rounded_parts(along)):
            value = jnp.where(lane == part, column.astype(F32), value)
        back[first : first + GROUP_BLOCKS, :, features:] = blocks_of(value)
        for number in range(first, first + GROUP_BLOCKS):
            if number == 0:
                kept = wires.copy(back.at[0], returned_ref.at[mine])
            else:
                returning.append(
                    wires.remote(back.at[number], returned_ref.at[mine], sources[number - 1][0])
                )
    staged = []
    for index, first in enumerate(range(0, count, GROUP_BLOCKS)):
        at = pl.ds(first * CAP, tile)
        group_hidden = hiddens[at]
        slot = index % 2
        if index >= 2:
            for copy in staged[index - 2]:
                copy.wait()
        for left in range(0, features, 512):
            columns = pl.ds(left, 512)
            rows_staged[slot, :, :, left : left + 512] = blocks_of(
                dot(group_hidden, down_ref[:, columns])
            )
        staged.append(
            [
                wires.copy(rows_staged.at[slot, number], rows_out.at[holders[first + number]])
                for number in range(GROUP_BLOCKS)
            ]
        )
        for left in range(0, features, 512):
            columns = pl.ds(left, 512)
            rows = flat(landed, first, columns)
            own = dot(rows, grads[at, : 2 * HALF], 0, 0)
            other = dot(rows, grads[at, 2 * HALF :], 0, 0)
            rows = flat(cotangents, first, columns)
            own_down = dot(gated[at, :HALF], rows, 0, 0)
            other_part = dot(gated[at, HALF:], rows, 0, 0)
            if index > 0:
                own = own + own_in_ref[columns]
                other = other + other_in[columns]
                own_down = own_down + own_down_ref[:, columns]
                other_part = other_part + other_down[:, columns]
            own_in_ref[columns] = own
            own_down_ref[:, columns] = own_down
            if first + GROUP_BLOCKS == count:
                other_in_ref[columns] = other.astype(BF16)
                other_down_ref[:, columns] = other_part.astype(BF16)
            else:
                other_in[columns] = other
                other_down[:, columns] = other_part
    for copies in staged[-2:]:
        for copy in copies:
            copy.wait()
    kept.wait()
    for copy in returning:
        copy.wait_recv()
    wires.finish()


def expert(outgoing, grad_received, weight, down):
    count, cap, features = grad_received.shape
    anywhere = pl.BlockSpec(memory_space=pl.ANY)
    return pl.pallas_call(
        expert_kernel,
        out_shape=[
            jax.ShapeDtypeStruct(outgoing.shape, BF16),
            jax.ShapeDtypeStruct(grad_received.shape, BF16),
            jax.ShapeDtypeStruct((features, 2 * HALF), F32),
            jax.ShapeDtypeStruct((features, 2 * HALF), BF16),
            jax.ShapeDtypeStruct((HALF, features), F32),
            jax.ShapeDtypeStruct((HALF, features), BF16),
        ],
        in_specs=[anywhere, anywhere, VMEM_SPEC, VMEM_SPEC],
        out_specs=[anywhere, anywhere] + [VMEM_SPEC] * 4,
        scratch_shapes=[
            pltpu.VMEM(outgoing.shape, BF16),
            pltpu.VMEM(grad_received.shape, BF16),
            pltpu.VMEM(outgoing.shape, BF16),
            pltpu.VMEM((count * cap, 4 * HALF), BF16),
            pltpu.VMEM((count * cap, 2 * HALF), BF16),
            pltpu.VMEM((count * cap, 2 * HALF), BF16),
            pltpu.VMEM((2, GROUP_BLOCKS, cap, features), BF16),
            pltpu.VMEM((features, 2 * HALF), F32),
            pltpu.VMEM((HALF, features), F32),
            pltpu.SemaphoreType.DMA((128,)),
            pltpu.SemaphoreType.DMA((128,)),
            pltpu.SemaphoreType.DMA((136,)),
        ],
        compiler_params=pltpu.CompilerParams(
            collective_id=4, has_side_effects=True, vmem_limit_bytes=58 * 1024 * 1024
        ),
        cost_estimate=pl.CostEstimate(
            flops=22_000_000_000, bytes_accessed=300_000_000, transcendentals=1_000_000
        ),
    )(outgoing, grad_received, weight, down)


def back_to_residual(
    grad_back_ref,
    slots_ref,
    owner_ref,
    gates_ref,
    cotangent_ref,
    residual_ref,
    partial_ref,
    misc_ref,
    outt_ref,
    grad_residual_ref,
    grad_low_ref,
    grad_logits_ref,
    grad_gain_ref,
    grad_attended,
):
    rows, features = cotangent_ref.shape
    slots = slots_ref[...]
    extra = grad_back_ref[:, features:].astype(F32)
    owner = owner_ref[...].astype(F32)
    grad_gates = jnp.zeros((rows, 128), F32)
    for part in range(3):
        grad_gates = grad_gates + dot(slots, (owner * extra[:, part : part + 1]).astype(BF16))
    gates = gates_ref[...]
    grad_logits = (
        gates * (grad_gates - jnp.sum(gates * grad_gates, axis=1, keepdims=True))
    ).astype(BF16)
    grad_logits_ref[...] = grad_logits
    gain = gain_row(misc_ref, EXPERTS + 1)
    square, inner = jnp.zeros((rows, 1), F32), jnp.zeros((rows, 1), F32)
    for left in range(0, features, 512):
        columns = pl.ds(left, 512)
        piece = (
            partial_ref[:, columns]
            + dot(slots, grad_back_ref[:, columns])
            + dot(grad_logits, misc_ref[columns], 1, 1)
        )
        grad_residual_ref[:, columns] = piece
        residual = residual_ref[:, columns]
        square = square + jnp.sum(residual * residual, axis=1, keepdims=True)
        inner = inner + jnp.sum(
            piece * gain[:, left : left + 512] * residual, axis=1, keepdims=True
        )
    scale = lax.rsqrt(square / features + EPSILON)
    cubed = scale * scale * scale * (inner / features)
    for left in range(0, features, 512):
        columns = pl.ds(left, 512)
        piece = grad_residual_ref[:, columns]
        residual = residual_ref[:, columns]
        grad_gain_ref[:, columns] = jnp.broadcast_to(
            jnp.sum(piece * residual * scale, axis=0, keepdims=True), (8, 512)
        )
        value = (
            cotangent_ref[:, columns].astype(F32)
            + scale * piece * gain[:, left : left + 512]
            - residual * cubed
        )
        grad_residual_ref[:, columns] = value
        grad_low_ref[:, columns] = value.astype(BF16)
    grad_low = grad_low_ref[...]
    for left in range(0, features, 512):
        columns = pl.ds(left, 512)
        grad_attended[:, columns] = dot(grad_low, outt_ref[:, columns]).astype(BF16)


def back_heads(
    group, allowed, qkv_ref, every_ref, grad_attended, grad_queries_ref, partial_keyvals
):
    rows = qkv_ref.shape[0]
    width = KEY_VALUE_HEADS * HEAD_SIZE
    keys_count = 8 * rows
    score_scale = HEAD_SIZE ** (-0.5)
    queries = head_columns(qkv_ref, group)
    heads_gradient = head_columns(grad_attended, group)
    key_columns = pl.ds(group * HEAD_SIZE, HEAD_SIZE)
    value_columns = pl.ds(width + group * HEAD_SIZE, HEAD_SIZE)
    keys = every_ref[:, :, key_columns].reshape(keys_count, HEAD_SIZE)
    values = every_ref[:, :, value_columns].reshape(keys_count, HEAD_SIZE)
    weights = head_weights(queries, keys, allowed)
    grad_weights = dot(heads_gradient, values, 1, 1)
    inner_sum = jnp.sum(weights * grad_weights, axis=1, keepdims=True)
    grad_scores = (weights * (grad_weights - inner_sum)).astype(BF16)
    grad_queries = (dot(grad_scores, keys) * score_scale).astype(BF16)
    for head in range(GROUP):
        at = (group * GROUP + head) * HEAD_SIZE
        grad_queries_ref[:, at : at + HEAD_SIZE] = grad_queries[head * rows : (head + 1) * rows]
    partial_keyvals[:, :, key_columns] = (
        (dot(grad_scores, queries, 0, 0) * score_scale).astype(BF16).reshape(8, rows, HEAD_SIZE)
    )
    partial_keyvals[:, :, value_columns] = (
        dot(weights.astype(BF16), heads_gradient, 0, 0).astype(BF16).reshape(8, rows, HEAD_SIZE)
    )


def rear_kernel(tail, *refs):
    count = len(SHARED_PARTS)
    (
        grad_back_ref,
        slots_ref,
        owner_ref,
        gates_ref,
        cotangent_ref,
        residual_ref,
        partial_ref,
        misc_ref,
        outt_ref,
        qkv_ref,
        every_ref,
        marks_ref,
        segments_ref,
        in_ref,
        down_ref,
    ) = refs[:15]
    grads = refs[15 : 15 + count]
    (
        grad_residual_ref,
        grad_low_ref,
        grad_logits_ref,
        grad_gain_ref,
        grad_queries_ref,
        grad_keyvals_ref,
        in_out,
        down_out,
    ) = refs[15 + count : 23 + count]
    outs = refs[23 + count : 23 + 2 * count]
    scratch = refs[23 + 2 * count : 23 + 8 * count]
    (
        grad_attended,
        blocks_ref,
        landed,
        sequence_send,
        sequence_recv,
        send_sems,
        recv_sems,
        local_sems,
    ) = refs[23 + 8 * count :]
    me = col_index()
    spot = place()
    rows = cotangent_ref.shape[0]
    late = pl.ds(rows - tail, tail)
    sibling = {"core": 1 - spot["core"]}
    distant = [col_device(rem(me + far, 8)) for far in range(1, 8)]
    greet(ring_neighbours(spot) + distant)
    wires = Wires(send_sems, recv_sems, local_sems)
    stages = Summing(wires, spot, SHARED_PARTS, grads, outs, scratch).stages()
    next(stages)
    arriving = [
        wires.remote(in_ref, in_out, sibling),
        wires.remote(down_ref, down_out, sibling),
    ]
    back_to_residual(
        grad_back_ref,
        slots_ref,
        owner_ref,
        gates_ref,
        cotangent_ref,
        residual_ref,
        partial_ref,
        misc_ref,
        outt_ref,
        grad_residual_ref,
        grad_low_ref,
        grad_logits_ref,
        grad_gain_ref,
        grad_attended,
    )
    next(stages)
    allowed = allowed_pairs(marks_ref, segments_ref, rows, 8 * rows)
    allowed = jnp.concatenate([allowed.astype(F32)] * GROUP, axis=0) > 0.5

    def heads(group):
        back_heads(
            group, allowed, qkv_ref, every_ref, grad_attended, grad_queries_ref, blocks_ref
        )

    for group in range(KEY_VALUE_HEADS):
        heads(group)

    def copy(far, first):
        block = rem(me + 8 - far, 8)
        source, target = blocks_ref.at[block], landed.at[far]
        if first:
            source, target = blocks_ref.at[0, late], landed.at[far, late]
        return pltpu.make_async_remote_copy(
            src_ref=source,
            dst_ref=target,
            send_sem=sequence_send.at[far],
            recv_sem=sequence_recv.at[far],
            device_id=col_device(block),
            device_id_type=MESH_ID,
        )

    def each(far, first, condition, act):
        @pl.when(condition)
        def _():
            act(copy(far, first))

    for far in range(7, 0, -1):
        each(far, False, me > far, lambda moved: moved.start())
        each(far, True, me == far, lambda moved: moved.start())

    @pl.when(me == 0)
    def _():
        for far in range(1, 8):
            landed[far, : rows - tail] = jnp.zeros((rows - tail, landed.shape[2]), landed.dtype)

    for far in range(1, 8):

        @pl.when(me + far >= 8)
        def _():
            landed[far] = jnp.zeros(landed.shape[1:], landed.dtype)

    next(stages)
    next(stages)
    for far in range(1, 8):
        each(far, False, (me > 0) & (me + far < 8), lambda moved: moved.wait_recv())
        each(far, True, me == 0, lambda moved: moved.wait_recv())
    for row in range(0, rows, 16):
        at = pl.ds(row, 16)
        value = blocks_ref[me, at].astype(F32)
        for far in range(1, 8):
            value = value + landed[far, at].astype(F32)
        grad_keyvals_ref[at] = value.astype(BF16)
    next(stages)
    next(stages)
    next(stages)
    for far in range(1, 8):
        each(far, False, me > far, lambda moved: moved.wait_send())
        each(far, True, me == far, lambda moved: moved.wait_send())
    for moved in arriving:
        moved.wait_recv()
    wires.finish()


def rear(tail, grad_back, slots, owner, gates, cotangent, residual1, partial, misc, outt, qkv, every,
         marks, segments, expert_in, expert_down, grads):
    rows, features = cotangent.shape
    anywhere = pl.BlockSpec(memory_space=pl.ANY)
    inputs = (grad_back, slots, owner, gates, cotangent, residual1, partial, misc, outt, qkv, every,
              marks, segments)
    return pl.pallas_call(
        functools.partial(rear_kernel, tail),
        out_shape=[
            jax.ShapeDtypeStruct((rows, features), F32),
            jax.ShapeDtypeStruct((rows, features), BF16),
            jax.ShapeDtypeStruct((rows, 128), BF16),
            jax.ShapeDtypeStruct((8, features), F32),
            jax.ShapeDtypeStruct((rows, features), BF16),
            jax.ShapeDtypeStruct(every.shape[1:], BF16),
            jax.ShapeDtypeStruct(expert_in.shape, BF16),
            jax.ShapeDtypeStruct(expert_down.shape, BF16),
        ]
        + [jax.ShapeDtypeStruct((16, width), F32) for _, width, _ in SHARED_PARTS],
        in_specs=[VMEM_SPEC] * 13 + [anywhere] * (2 + len(SHARED_PARTS)),
        out_specs=[VMEM_SPEC] * 6 + [anywhere] * 2 + [VMEM_SPEC] * len(SHARED_PARTS),
        scratch_shapes=summing_scratch(SHARED_PARTS)
        + [
            pltpu.VMEM((rows, features), BF16),
            pltpu.VMEM(every.shape, BF16),
            pltpu.VMEM(every.shape, BF16),
            pltpu.SemaphoreType.DMA((8,)),
            pltpu.SemaphoreType.DMA((8,)),
            pltpu.SemaphoreType.DMA((140,)),
            pltpu.SemaphoreType.DMA((140,)),
            pltpu.SemaphoreType.DMA((32,)),
        ],
        compiler_params=pltpu.CompilerParams(
            collective_id=3, has_side_effects=True, vmem_limit_bytes=56 * 1024 * 1024
        ),
        cost_estimate=pl.CostEstimate(
            flops=10_000_000_000, bytes_accessed=150_000_000, transcendentals=2_000_000
        ),
    )(*inputs, expert_in, expert_down, *grads)


def inverse_rms(residual):
    return lax.rsqrt(jnp.mean(residual * residual, axis=-1, keepdims=True) + EPSILON)


def contract(left_side, right_side, left_dim, right_dim):
    return lax.dot_general(
        left_side,
        right_side,
        (((left_dim,), (right_dim,)), ((), ())),
        preferred_element_type=F32,
    )


def gated_unit(gate_pre, up_pre):
    return jax.nn.silu(gate_pre) * up_pre


def norm_backward(residual, norm_scale, gain_row, grad_normed):
    weighted = grad_normed * gain_row
    inner_sum = jnp.mean(weighted * residual, axis=-1, keepdims=True)
    grad_residual = (
        norm_scale * weighted - residual * norm_scale * norm_scale * norm_scale * inner_sum
    )
    grad_gain = jnp.sum(grad_normed * residual * norm_scale, axis=0)
    return (grad_residual, grad_gain)


def expert_of(holder):
    return (holder // 8) * 8 + (holder % 2) * 4 + holder // 2 % 4


def packed(grad):
    return grad.reshape(4, 2, 2, 2, 48, grad.shape[-1])


def to_experts(rows):
    return lax.all_to_all(rows, EXPERT_AXES, split_axis=0, concat_axis=0, tiled=True)


def shards(
    tokens,
    segments,
    routes,
    norm1_gain,
    w_query,
    key_value_weight,
    w_output,
    norm2_gain,
    w_router,
    w_shgate,
    w_shup,
    w_shdown,
    w_exgate,
    w_exup,
    w_exdown,
    cotangent,
):
    local_rows, feature_count = tokens.shape
    sequence_length = local_rows * 8
    shard = jnp.concatenate(
        [
            w_output.T,
            w_router,
            norm1_gain[:, None],
            norm2_gain[:, None],
            jnp.zeros((12, 62), BF16),
            w_query,
            key_value_weight,
            w_shgate,
            w_shup,
            w_shdown.T,
        ],
        axis=1,
    )
    shard = jnp.concatenate([shard, jnp.zeros((4, TOTAL), BF16)], axis=0)
    *dense, expert_w, expert_down = gather_weights(shard, w_exgate[0], w_exup[0], w_exdown[0])
    outt_w, misc_w, query_w, keyval_w, shgate_w, shup_w, shdt_w = [
        gathered.reshape(feature_count, gathered.shape[-1]) for gathered in dense
    ]
    gain_first = misc_w[:, EXPERTS].astype(F32)

    expert_ids = jnp.arange(128, dtype=jnp.int32)
    named = jnp.any(routes[:, :, None] == expert_ids[None, None, :], axis=1)
    named_low = named.astype(BF16)
    token_ids = jnp.arange(local_rows, dtype=jnp.int32)
    before = (token_ids[None, :] <= token_ids[:, None]).astype(BF16)
    rank = jnp.dot(before, named_low, preferred_element_type=F32) * named.astype(F32)
    slot_count = EXPERTS * CAP
    slot_ids = jnp.arange(slot_count, dtype=jnp.int32)
    holder = slot_ids // CAP
    slot_expert = expert_of(holder)
    owner = (slot_expert[:, None] == expert_ids[None, :]).astype(BF16)
    rank_wide = contract(rank.astype(BF16), owner, 1, 1)
    slots = (rank_wide == (slot_ids % CAP + 1).astype(F32)[None, :]).astype(BF16)
    slots_down = (
        contract(owner, rank.astype(BF16), 1, 1) == (slot_ids % CAP + 1).astype(F32)[:, None]
    ).astype(BF16)

    def dispatch(rows):
        return rows.reshape(EXPERTS, CAP, rows.shape[-1])

    sent_cotangent = dispatch(jnp.dot(slots_down, cotangent, preferred_element_type=F32).astype(BF16))
    residual0 = tokens.astype(F32)
    scale_first = inverse_rms(residual0)
    first_normed = (residual0 * scale_first * gain_first).astype(BF16)
    query_rows = jnp.dot(first_normed, query_w, preferred_element_type=F32).astype(BF16)
    keyval_rows = jnp.dot(first_normed, keyval_w, preferred_element_type=F32).astype(BF16)
    own_segments = segments.astype(F32)
    tail = 32
    first_length = jnp.sum((segments == 0).astype(F32)).astype(BF16)
    every, marks = to_later(
        keyval_rows, jnp.broadcast_to(first_length, (tail, 128))
    )
    sent_cotangent, every = lax.optimization_barrier((sent_cotangent, every))
    grad_received = to_experts(sent_cotangent)
    segment_tile = jnp.broadcast_to(own_segments[:, None], (local_rows, 128))
    attended_rows, residual1, second_normed, gates, outgoing = middle(
        query_rows,
        every,
        marks,
        segment_tile,
        tokens,
        outt_w,
        misc_w,
        named.astype(F32),
        slots_down,
        owner,
    )
    shared_gate = jnp.dot(second_normed, shgate_w, preferred_element_type=F32)
    shared_up = jnp.dot(second_normed, shup_w, preferred_element_type=F32)
    shared_hidden = gated_unit(shared_gate, shared_up).astype(BF16)
    shared_out = contract(shared_hidden, shdt_w, 1, 1)
    grad_shdt = contract(cotangent, shared_hidden, 0, 0).astype(BF16)
    grad_shared_hidden = jnp.dot(cotangent, shdt_w, preferred_element_type=F32)
    unused_shared, pull_shared = jax.vjp(gated_unit, shared_gate, shared_up)
    grad_shared_gate, grad_shared_up = pull_shared(grad_shared_hidden)
    grad_shared_gate = grad_shared_gate.astype(BF16)
    grad_shared_up = grad_shared_up.astype(BF16)
    grad_shgate = contract(second_normed, grad_shared_gate, 0, 0).astype(BF16)
    grad_shup = contract(second_normed, grad_shared_up, 0, 0).astype(BF16)
    grad_second = contract(grad_shared_gate, shgate_w, 1, 1) + contract(
        grad_shared_up, shup_w, 1, 1
    )

    forward_rows = residual1 + shared_out
    slot_gates = slots.astype(F32) * lax.dot_general(
        gates,
        owner.astype(F32),
        (((1,), (1,)), ((), ())),
        precision=lax.Precision.HIGHEST,
        preferred_element_type=F32,
    )
    gates_high = lax.reduce_precision(slot_gates, exponent_bits=8, mantissa_bits=7)
    (
        outgoing,
        grad_shdt,
        grad_shgate,
        grad_shup,
        grad_second,
        forward_rows,
        slot_gates,
        gates_high,
    ) = lax.optimization_barrier(
        (
            outgoing,
            grad_shdt,
            grad_shgate,
            grad_shup,
            grad_second,
            forward_rows,
            slot_gates,
            gates_high,
        )
    )
    grad_back, half_out, own_in, other_in, own_down, other_down = expert(
        dispatch(outgoing), grad_received, expert_w, expert_down
    )
    grad_back = grad_back.reshape(slot_count, feature_count + EXTRA)
    (
        grad_residual1,
        grad_attn_low,
        grad_logits,
        grad_gain_second,
        grad_queries,
        grad_keyvals,
        their_in,
        their_down,
        sum_shgate,
        sum_shup,
        sum_shdt,
    ) = rear(
        tail,
        grad_back,
        slots,
        owner,
        gates,
        cotangent,
        residual1,
        grad_second,
        misc_w,
        outt_w,
        query_rows,
        every,
        marks,
        segment_tile,
        other_in,
        other_down,
        [packed(grad_shgate), packed(grad_shup), packed(grad_shdt)],
    )
    half_out, grad_keyvals = lax.optimization_barrier((half_out, grad_keyvals))
    returned = to_experts(half_out).reshape(slot_count, feature_count)
    grad_gain_second = grad_gain_second[0]
    grad_router = contract(second_normed, grad_logits, 0, 0)
    grad_outt = contract(grad_attn_low, attended_rows, 0, 0).astype(BF16)
    half_in = (own_in + their_in.astype(F32)).astype(BF16)
    half_down = (own_down + their_down.astype(F32)).astype(BF16)
    grad_query = contract(first_normed, grad_queries, 0, 0).astype(BF16)
    grad_keyval = contract(first_normed, grad_keyvals, 0, 0).astype(BF16)
    grad_first = contract(grad_queries, query_w, 1, 1) + contract(grad_keyvals, keyval_w, 1, 1)
    grad_norm_first, grad_gain_first = norm_backward(residual0, scale_first, gain_first, grad_first)
    grad_tokens = grad_residual1 + grad_norm_first
    grad_misc = jnp.concatenate(
        [
            grad_router[:, :EXPERTS],
            grad_gain_first[:, None],
            grad_gain_second[:, None],
            jnp.zeros((feature_count, 62), F32),
        ],
        axis=1,
    )
    expert_mix = jnp.dot(
        gates_high.astype(BF16), returned, preferred_element_type=F32
    ) + jnp.dot((slot_gates - gates_high).astype(BF16), returned, preferred_element_type=F32)
    block_out = (forward_rows + expert_mix).astype(BF16)
    grad_misc, block_out = lax.optimization_barrier((grad_misc, block_out))
    *summed, half_in, half_down = sum_last(
        [packed(grad) for grad in (grad_outt, grad_misc, grad_query, grad_keyval)],
        [half_in, half_down],
    )
    sum_outt, sum_misc, sum_query, sum_keyval, sum_shgate, sum_shup, sum_shdt = [
        piece[:12] for piece in (*summed, sum_shgate, sum_shup, sum_shdt)
    ]
    return (
        block_out,
        grad_tokens,
        sum_misc[:, EXPERTS],
        sum_query,
        sum_keyval,
        sum_outt.T,
        sum_misc[:, EXPERTS + 1],
        sum_misc[:, :EXPERTS],
        sum_shgate,
        sum_shup,
        sum_shdt.T,
        half_in[None, :, :HALF].astype(F32),
        half_in[None, :, HALF:].astype(F32),
        half_down[None].astype(F32),
    )


def solution(mesh):
    fine = Mesh(mesh.devices.reshape(SIZES), AXES)
    rows = P(AXES, None)
    columns = P(None, AXES)
    flat = P(AXES)
    blocks = P(AXES, None, None)
    in_specs = (
        rows,
        flat,
        rows,
        flat,
        rows,
        rows,
        columns,
        flat,
        rows,
        rows,
        rows,
        columns,
        blocks,
        blocks,
        blocks,
        rows,
    )
    out_specs = (
        rows,
        rows,
        flat,
        rows,
        rows,
        columns,
        flat,
        rows,
        rows,
        rows,
        columns,
        blocks,
        blocks,
        blocks,
    )
    return jax.shard_map(shards, mesh=fine, in_specs=in_specs, out_specs=out_specs, check_vma=False)
```

```python
import functools

import jax
import jax.numpy as jnp
from jax import lax
from jax.experimental import pallas as pl
from jax.experimental.pallas import tpu as pltpu
from jax.sharding import Mesh
from jax.sharding import PartitionSpec as P

QUERY_HEADS = 12
KEY_VALUE_HEADS = 4
HEAD_SIZE = 128
EXPERTS = 64
TOPK = 6
CAP = 24
EPSILON = 1e-05

F32 = jnp.float32
BF16 = jnp.bfloat16
MESH_ID = pl.DeviceIdType.MESH
AXES = ("z", "yl", "core", "yh", "xh", "xl")
SIZES = (4, 2, 2, 2, 2, 2)

PARTS = (
    ("outt", 1536, "yzx", "yzx"),
    ("misc", 128, "yz", "yz"),
    ("q", 1536, "yz", "yz"),
    ("kv", 1024, "zy", "zy"),
    ("shg", 1024, "yz", "yz"),
    ("shu", 1024, "zy", "zy"),
    ("shdt", 1024, "zy", "zy"),
)
GATHERED = tuple((name, width, order) for name, width, order, _ in PARTS)
SUMMED = tuple((name, width, order) for name, width, _, order in PARTS)
TOTAL = sum(part[1] for part in PARTS)
HALF = 256
EXPERT_SEM = 200
TOTAL = sum(part[1] for part in PARTS)


def rem(value, size):
    return lax.rem(value, jnp.int32(size))


def place():
    at = {name: lax.axis_index(name) for name in AXES}
    return {
        "x": at["xh"] * 2 + at["xl"],
        "y": at["yh"] * 2 + at["yl"],
        "z": at["z"],
        "core": at["core"],
    }


def device(axis, value):
    if axis == "x":
        return {"xh": value // 2, "xl": rem(value, 2)}
    if axis == "y":
        return {"yh": value // 2, "yl": rem(value, 2)}
    return {axis: value}


def greet(targets):
    barrier = pltpu.get_barrier_semaphore()
    for target in targets:
        pl.semaphore_signal(barrier, inc=1, device_id=target, device_id_type=MESH_ID)
    pl.semaphore_wait(barrier, len(targets))


def ring_neighbours(me):
    near = [device("x", rem(me["x"] + hops, 4)) for hops in (1, 2, 3)]
    near += [device("y", rem(me["y"] + hops, 4)) for hops in (1, 3)]
    near += [device("z", rem(me["z"] + hops, 4)) for hops in (1, 3)]
    return near + [{"core": 1 - me["core"]}]


class Wires:
    def __init__(self, send_sems, recv_sems, local_sems):
        self.send, self.recv, self.local = send_sems, recv_sems, local_sems
        self.used, self.used_local, self.started, self.kept = 0, 0, [], []

    def remote(self, source, target, where):
        copy = pltpu.make_async_remote_copy(
            src_ref=source,
            dst_ref=target,
            send_sem=self.send.at[self.used],
            recv_sem=self.recv.at[self.used],
            device_id=where,
            device_id_type=MESH_ID,
        )
        self.used += 1
        copy.start()
        self.started.append(copy)
        return copy

    def copy(self, source, target):
        copy = pltpu.make_async_copy(source, target, self.local.at[self.used_local])
        self.used_local += 1
        copy.start()
        return copy

    def finish(self):
        for copy in self.started:
            copy.wait_send()


def balanced_offsets():
    left = [(x, y, z) for x in range(4) for y in range(4) for z in range(4) if x + y + z > 0]
    load, order = [0] * 6, []

    def uses(offset):
        used = [0] * 6
        for axis, hops in enumerate(offset):
            used[2 * axis] += hops in (1, 2)
            used[2 * axis + 1] += hops in (2, 3)
        return used

    def cost(offset):
        used = uses(offset)
        after = [a + b for a, b in zip(load, used)]
        mean = sum(after) / 6
        return (max(after), sum((a - mean) ** 2 for a in after), -sum(used))

    while left:
        best = min(left, key=cost)
        load = [a + b for a, b in zip(load, uses(best))]
        left.remove(best)
        order.append(best)
    return order


OFFSETS = balanced_offsets()


def chip_at(me, offset, sign=1):
    x, y, z = [rem(me[axis] + (sign * hops) % 4, 4) for axis, hops in zip("xyz", offset)]
    where = {"z": z, "yh": y // 2, "yl": rem(y, 2), "xh": x // 2, "xl": rem(x, 2)}
    return where, z * 16 + rem(y, 2) * 8 + (y // 2) * 4 + x


def halves(width):
    first = width // 256 * 128 if width > 128 else width
    return first, width - first


def spread_rows(shape, swap):
    dense = lax.broadcasted_iota(jnp.int32, shape, 1 if swap else 0)
    padded = lax.broadcasted_iota(jnp.int32, shape, 0 if swap else 1)
    shift = jnp.zeros(shape, jnp.int32)
    for edge in (12, 24, 36):
        shift = shift + jnp.where(dense >= edge, 4, 0)
    return dense + shift == padded


def block_ref(ref, axes, me, axis, value, columns):
    spot = dict(me)
    spot[axis] = value
    z = slice(None) if "z" in axes else spot["z"]
    yl = slice(None) if "y" in axes else rem(spot["y"], 2)
    yh = slice(None) if "y" in axes else spot["y"] // 2
    return ref.at[z, yl, me["core"], yh, :, columns]


def gather_kernel(shard_ref, gate_ref, up_ref, down_ref, *rest):
    count = len(GATHERED)
    outs = rest[:count]
    expert_in, expert_out, landed = rest[count : count + 3]
    stages = rest[count + 3 : 2 * count + 3]
    send_sems, recv_sems, local_sems = rest[2 * count + 3 :]
    me = place()
    nxt = {axis: rem(me[axis] + 1, 4) for axis in "xyz"}
    opp = {axis: rem(me[axis] + 2, 4) for axis in "xyz"}
    prv = {axis: rem(me[axis] + 3, 4) for axis in "xyz"}
    sibling = {"core": 1 - me["core"]}
    partner = {"core": 1 - me["core"], "xl": 1 - lax.axis_index("xl")}
    crossed = me["core"] != lax.axis_index("xl")
    greet(
        [device("x", nxt["x"]), device("x", opp["x"]), device("x", prv["x"])]
        + [device("y", nxt["y"]), device("y", prv["y"])]
        + [device("z", nxt["z"]), device("z", prv["z"]), sibling, partner]
    )
    wires = Wires(send_sems, recv_sems, local_sems)
    runs, start = [], 0
    for index, (name, width, order) in enumerate(GATHERED):
        last_x = len(order) == 3
        quarter = width // 4 if last_x else width
        run = {
            "out": outs[index],
            "order": order,
            "width": quarter,
            "done": "",
            "stage": stages[index],
            "start": start,
            "landed": landed.at[:, :, pl.ds(start, quarter)],
            "base": me["x"] * quarter if last_x else 0,
            "first": [],
            "shared": [],
        }

        def piece(x):
            if last_x:
                return shard_ref.at[:, pl.ds(pl.multiple_of(start + x * quarter, 128), quarter)]
            return shard_ref.at[:, pl.ds(start, quarter)]

        for where in (nxt, prv, opp):
            run["first"].append(
                wires.remote(piece(where["x"]), run["landed"].at[me["x"]], device("x", where["x"]))
            )
        run["bring"] = wires.copy(piece(me["x"]), run["landed"].at[me["x"]])
        runs.append(run)
        start += width

    whole = [
        (gate_ref, expert_in.at[:, pl.ds(0, HALF)]),
        (up_ref, expert_in.at[:, pl.ds(HALF, HALF)]),
        (down_ref, expert_out.at[pl.ds(0, HALF)]),
    ]

    def moved(slot):
        source, target = whole[slot]
        return pltpu.make_async_remote_copy(
            src_ref=source,
            dst_ref=target,
            send_sem=send_sems.at[EXPERT_SEM + slot],
            recv_sem=recv_sems.at[EXPERT_SEM + slot],
            device_id=partner,
            device_id_type=MESH_ID,
        )

    def kept(slot):
        source, target = whole[slot]
        return pltpu.make_async_copy(source, target, local_sems.at[20 + slot])

    @pl.when(crossed)
    def _():
        for slot in range(3):
            moved(slot).start()

    @pl.when(jnp.logical_not(crossed))
    def _():
        for slot in range(3):
            kept(slot).start()

    def part_columns(run, axis, value, which):
        base = value * run["width"] if axis == "x" else run["base"]
        left, size = 0, run["width"]
        if which is not None:
            first_half, second_half = halves(run["width"])
            left, size = (0, first_half) if which == 0 else (first_half, second_half)
        if isinstance(base, int):
            return pl.ds(base + left, size)
        return pl.ds(pl.multiple_of(base + left, 128), size)

    def blocks(run, axis, value, which=None):
        columns = part_columns(run, axis, value, which)
        return block_ref(run["out"], run["done"], me, axis, value, columns)

    def begin(run, axis, source=None):
        target = blocks(run, axis, me[axis])
        source = target if source is None else source
        run["forth"] = wires.remote(source, target, device(axis, nxt[axis]))
        run["back"] = wires.remote(source, target, device(axis, prv[axis]))

    pick = spread_rows((48, 64), False).astype(BF16)
    for run in runs:
        run["bring"].wait()
        for copy in run["first"]:
            copy.wait_recv()
        for left in range(0, run["width"], 512):
            size = min(512, run["width"] - left)
            left_in = run["start"] + left
            piece_rows = landed[:, :, left_in : left_in + size].reshape(64, size)
            run["stage"][:, left : left + size] = jnp.dot(
                pick, piece_rows, preferred_element_type=F32
            ).astype(BF16)
        axis = run["order"][0]
        begin(run, axis, run["stage"])
        run["own"] = wires.copy(run["stage"], blocks(run, axis, me[axis]))

    def forward(run, axis):
        run["forth"].wait_recv()
        source = blocks(run, axis, prv[axis], 0)
        run["more"] = [wires.remote(source, source, device(axis, nxt[axis]))]
        run["back"].wait_recv()
        if halves(run["width"])[1] > 0:
            source = blocks(run, axis, nxt[axis], 1)
            run["more"].append(wires.remote(source, source, device(axis, prv[axis])))

    def share(run, axis, value):
        source = blocks(run, axis, value)
        run["shared"].append(wires.remote(source, source, sibling))

    def advance(run, step):
        axis = run["order"][step]
        for copy in run["more"]:
            copy.wait_recv()
        if step == len(run["order"]) - 1:
            share(run, axis, opp[axis])
            return
        if step == 0:
            run["own"].wait()
        run["done"] = run["done"] + axis
        following = run["order"][step + 1]
        begin(run, following)
        if step + 1 == len(run["order"]) - 1:
            share(run, following, me[following])

    def last_forward(run):
        axis = run["order"][-1]
        forward(run, axis)
        share(run, axis, prv[axis])
        share(run, axis, nxt[axis])

    threes = [run for run in runs if len(run["order"]) == 3]
    twos = [run for run in runs if len(run["order"]) == 2]
    for run in runs:
        forward(run, run["order"][0])
    for run in runs:
        advance(run, 0)
    for run in threes:
        forward(run, run["order"][1])
    for run in threes:
        advance(run, 1)
    for run in twos:
        last_forward(run)
    for run in threes:
        last_forward(run)

    @pl.when(crossed)
    def _():
        for slot in range(3):
            moved(slot).wait_recv()

    @pl.when(jnp.logical_not(crossed))
    def _():
        for slot in range(3):
            kept(slot).wait()

    handed = [
        wires.remote(
            expert_in.at[:, pl.ds(0, 2 * HALF)], expert_in.at[:, pl.ds(2 * HALF, 2 * HALF)], sibling
        ),
        wires.remote(expert_out.at[pl.ds(0, HALF)], expert_out.at[pl.ds(HALF, HALF)], sibling),
    ]
    for run in twos + threes:
        advance(run, len(run["order"]) - 1)
    for run in runs:
        for copy in run["shared"]:
            copy.wait_recv()
    for copy in handed:
        copy.wait_recv()
    wires.finish()

    @pl.when(crossed)
    def _():
        for slot in range(3):
            moved(slot).wait_send()


def gather_weights(shard, gate_w, up_w, down_w):
    shapes = [jax.ShapeDtypeStruct((4, 2, 2, 2, 48, width), BF16) for _, width, _ in GATHERED]
    shapes += [
        jax.ShapeDtypeStruct((gate_w.shape[0], 4 * HALF), BF16),
        jax.ShapeDtypeStruct((2 * HALF, down_w.shape[1]), BF16),
    ]
    anywhere = pl.BlockSpec(memory_space=pl.ANY)
    return pl.pallas_call(
        gather_kernel,
        out_shape=shapes,
        in_specs=[pl.BlockSpec(memory_space=pltpu.VMEM)] + [anywhere] * 3,
        out_specs=[anywhere] * (len(GATHERED) + 2),
        scratch_shapes=[pltpu.VMEM((4, 16, TOTAL), BF16)]
        + [
            pltpu.VMEM((48, width // 4 if len(order) == 3 else width), BF16)
            for _, width, order in GATHERED
        ]
        + [
            pltpu.SemaphoreType.DMA((EXPERT_SEM + 4,)),
            pltpu.SemaphoreType.DMA((EXPERT_SEM + 4,)),
            pltpu.SemaphoreType.DMA((24,)),
        ],
        compiler_params=pltpu.CompilerParams(
            collective_id=0, has_side_effects=True, vmem_limit_bytes=16 * 1024 * 1024
        ),
        cost_estimate=pl.CostEstimate(flops=0, bytes_accessed=200_000_000, transcendentals=0),
    )(shard, gate_w, up_w, down_w)


class Summing:
    def __init__(self, wires, me, parts, grads, outs, scratch):
        self.wires, self.me = wires, me
        self.next = {axis: rem(me[axis] + 1, 4) for axis in "xyz"}
        self.opposite = {axis: rem(me[axis] + 2, 4) for axis in "xyz"}
        self.previous = {axis: rem(me[axis] + 3, 4) for axis in "xyz"}
        self.sibling = {"core": 1 - me["core"]}
        count = len(parts)
        self.runs = []
        for index, (name, width, order) in enumerate(parts):
            self.runs.append(
                {
                    "order": order[::-1],
                    "width": width // 4 if len(order) == 3 else width,
                    "left": "zy",
                    "turn": 0,
                    "grads": grads[index],
                    "out": outs[index],
                    "own": scratch[index],
                    "theirs": scratch[count + index],
                    "near1": scratch[2 * count + index],
                    "near2": scratch[3 * count + index],
                    "ends": scratch[4 * count + index],
                    "arrived": scratch[5 * count + index],
                }
            )

    def spot(self, left_axes, axis, value, with_core):
        at = dict(self.me)
        if axis is not None:
            at[axis] = value
        whole = [name for name in left_axes if name != axis]
        z = slice(None) if "z" in whole else at["z"]
        yl = slice(None) if "y" in whole else rem(at["y"], 2)
        yh = slice(None) if "y" in whole else at["y"] // 2
        return (z, yl) + (() if with_core is None else (with_core,)) + (yh,)

    def lead(self, left_axes, axis):
        dims = []
        for name in ("z", "y"):
            if name in left_axes and name != axis:
                dims += [4] if name == "z" else [2, 2]
        return dims

    def add_into(self, target, sources, dims):
        total = 1
        for size in dims:
            total *= size

        def body(index):
            for row in range(0, 48, 16):
                at = index + (pl.ds(row, 16),)
                value = target[at].astype(F32)
                for source in sources:
                    value = value + source[at].astype(F32)
                target[at] = value.astype(target.dtype)

        def step(flat, carry):
            index, rest_flat = [], flat
            for size in reversed(dims):
                index.append(rem(rest_flat, size))
                rest_flat = rest_flat // size
            body(tuple(reversed(index)))
            return carry

        if total == 1:
            body(())
        else:
            lax.fori_loop(0, total, step, 0)

    def columns_of(self, run, axis, value, which):
        base = 0
        if len(run["order"]) == 3:
            base = (value if axis == "x" else self.me["x"]) * run["width"]
        left, size = 0, run["width"]
        if which is not None:
            first_half, second_half = halves(run["width"])
            left, size = (0, first_half) if which == 0 else (first_half, second_half)
        if isinstance(base, int):
            return pl.ds(base + left, size)
        return pl.ds(pl.multiple_of(base + left, 128), size)

    def chunk(self, run, axis, value, which=None, ref=None, with_core=None):
        ref = run["own"] if ref is None else ref
        columns = self.columns_of(run, axis, value, which)
        return ref.at[self.spot(run["left"], axis, value, with_core) + (slice(None), columns)]

    def pair(self, run, axis, value):
        core = self.me["core"]
        give = self.wires.remote(
            self.chunk(run, axis, value, None, run["grads"], 1 - core),
            self.chunk(run, axis, value, None, run["theirs"]),
            self.sibling,
        )
        keep = self.wires.copy(
            self.chunk(run, axis, value, None, run["grads"], core), self.chunk(run, axis, value)
        )
        return give, keep

    def join(self, run, axis, value, copies):
        copies[0].wait_recv()
        copies[1].wait()
        self.add_into(
            self.chunk(run, axis, value),
            [self.chunk(run, axis, value, None, run["theirs"])],
            self.lead(run["left"], axis),
        )

    def slots(self, run, axis):
        dims = self.lead(run["left"], axis)
        ref = (run["near1"], run["near2"], run["ends"])[run["turn"]]
        if not dims:
            ref = ref.at[:, pl.ds(0, 48)]
        return ref.at[0], ref.at[1], ref.at[2], dims

    def part(self, ref, run, which, dims):
        first_half, second_half = halves(run["width"])
        columns = pl.ds(0, first_half) if which == 0 else pl.ds(first_half, second_half)
        return ref.at[(slice(None),) * len(dims) + (slice(None), columns)]

    def ring_open(self, run):
        axis = run["order"][run["turn"]]
        _, _, passing, dims = self.slots(run, axis)
        far = self.opposite[axis]
        run["passing"] = [
            self.wires.remote(
                self.chunk(run, axis, far, 0),
                self.part(passing, run, 0, dims),
                device(axis, self.next[axis]),
            )
        ]
        if halves(run["width"])[1]:
            run["passing"].append(
                self.wires.remote(
                    self.chunk(run, axis, far, 1),
                    self.part(passing, run, 1, dims),
                    device(axis, self.previous[axis]),
                )
            )

    def ring_near(self, run):
        axis = run["order"][run["turn"]]
        from_prv, from_nxt, _, dims = self.slots(run, axis)
        nxt, prv = self.next[axis], self.previous[axis]
        run["near"] = []
        if halves(run["width"])[1]:
            run["near"].append(
                self.wires.remote(
                    self.chunk(run, axis, nxt, 1),
                    self.part(from_prv, run, 1, dims),
                    device(axis, nxt),
                )
            )
        run["near"].append(
            self.wires.remote(
                self.chunk(run, axis, prv, 0), self.part(from_nxt, run, 0, dims), device(axis, prv)
            )
        )

    def ring_pass(self, run):
        axis = run["order"][run["turn"]]
        from_prv, from_nxt, passing, dims = self.slots(run, axis)
        nxt, prv = self.next[axis], self.previous[axis]
        run["passing"][0].wait_recv()
        self.add_into(self.chunk(run, axis, nxt, 0), [self.part(passing, run, 0, dims)], dims)
        run["near"].append(
            self.wires.remote(
                self.chunk(run, axis, nxt, 0), self.part(from_prv, run, 0, dims), device(axis, nxt)
            )
        )
        if halves(run["width"])[1]:
            run["passing"][1].wait_recv()
            self.add_into(self.chunk(run, axis, prv, 1), [self.part(passing, run, 1, dims)], dims)
            run["near"].append(
                self.wires.remote(
                    self.chunk(run, axis, prv, 1),
                    self.part(from_nxt, run, 1, dims),
                    device(axis, prv),
                )
            )

    def ring_close(self, run):
        axis = run["order"][run["turn"]]
        from_prv, from_nxt, _, dims = self.slots(run, axis)
        for copy in run["near"]:
            copy.wait_recv()
        self.add_into(self.chunk(run, axis, self.me[axis]), [from_prv, from_nxt], dims)
        run["left"] = run["left"].replace(axis, "")
        run["turn"] += 1

    def turn(self, run):
        self.ring_close(run)
        self.ring_open(run)
        self.ring_near(run)

    def spread(self, run):
        me, width = self.me, run["width"]
        third = len(run["order"]) == 3
        summed = run["own"].at[me["z"], rem(me["y"], 2), me["y"] // 2]
        exact = lax.Precision.HIGHEST if summed.dtype == F32 else None
        pick = spread_rows((64, 48), True).astype(summed.dtype)
        staging = run["ends"].at[3] if third else run["near2"].at[3]
        base = me["x"] * width if third else 0
        for left in range(0, width, 512):
            size = min(512, width - left)
            columns = pl.ds(left, size)
            if third:
                columns = pl.ds(pl.multiple_of(base + left, 128), size)
            staging[:, left : left + size] = jnp.dot(
                pick, summed[:, columns], preferred_element_type=F32, precision=exact
            ).astype(staging.dtype)
        if third:
            lands = run["arrived"].at[:, pl.ds(pl.multiple_of(base, 128), width)]
        else:
            lands = run["arrived"].at[me["x"]]
        run["copies"] = []
        for where in (self.next, self.opposite, self.previous):
            row = pl.ds(pl.multiple_of(where["x"] * 16, 16), 16)
            run["copies"].append(
                self.wires.remote(staging.at[row], lands, device("x", where["x"]))
            )
        row = pl.ds(pl.multiple_of(me["x"] * 16, 16), 16)
        run["keep"] = self.wires.copy(staging.at[row], lands)

    def deliver(self, run):
        run["keep"].wait()
        for copy in run["copies"]:
            copy.wait_recv()
        if len(run["order"]) == 3:
            run["out"][...] = run["arrived"][...].astype(F32)
        else:
            value = run["arrived"][0].astype(F32)
            for place_x in range(1, 4):
                value = value + run["arrived"][place_x].astype(F32)
            run["out"][...] = value

    def stages(self):
        runs = self.runs
        threes = [run for run in runs if len(run["order"]) == 3]
        twos = [run for run in runs if len(run["order"]) == 2]
        begun = []
        for where in (self.opposite, self.next, self.previous, self.me):
            begun.append([self.pair(run, run["order"][0], where[run["order"][0]]) for run in runs])
        yield
        for run, copies in zip(runs, begun[0]):
            axis = run["order"][0]
            self.join(run, axis, self.opposite[axis], copies)
            self.ring_open(run)
        for run, nexts, prevs in zip(runs, begun[1], begun[2]):
            axis = run["order"][0]
            self.join(run, axis, self.next[axis], nexts)
            self.join(run, axis, self.previous[axis], prevs)
            self.ring_near(run)
        yield
        for run in threes:
            self.ring_pass(run)
        for run, copies in zip(runs, begun[3]):
            axis = run["order"][0]
            self.join(run, axis, self.me[axis], copies)
        for run in twos:
            self.ring_pass(run)
        yield
        for run in threes:
            self.turn(run)
        for run in threes:
            self.ring_pass(run)
        for run in twos:
            self.turn(run)
        yield
        for run in threes:
            self.turn(run)
        for run in twos:
            self.ring_pass(run)
        for run in threes:
            self.ring_pass(run)
        yield
        for run in twos:
            self.ring_close(run)
            self.spread(run)
        for run in threes:
            self.ring_close(run)
            self.spread(run)
        yield
        for run in runs:
            self.deliver(run)
        yield


def summing_scratch(parts):
    own, theirs, near1, near2, ends, arrived = [], [], [], [], [], []
    for name, width, order in parts:
        kind = F32 if name == "misc" else BF16
        own.append(pltpu.VMEM((4, 2, 2, 48, width), kind))
        theirs.append(pltpu.VMEM((4, 2, 2, 48, width), kind))
        if len(order) == 3:
            quarter = width // 4
            near1.append(pltpu.VMEM((3, 4, 2, 2, 48, quarter), kind))
            near2.append(pltpu.VMEM((3, 2, 2, 48, quarter), kind))
            ends.append(pltpu.VMEM((4, 64, quarter), kind))
            arrived.append(pltpu.VMEM((16, width), kind))
        else:
            near1.append(pltpu.VMEM((3, 2, 2, 48, width) if order == "yz" else (3, 4, 48, width), kind))
            near2.append(pltpu.VMEM((4, 64, width), kind))
            ends.append(pltpu.VMEM((16, 128), kind))
            arrived.append(pltpu.VMEM((4, 16, width), kind))
    return own + theirs + near1 + near2 + ends + arrived


def last_kernel(*refs):
    count = len(SUMMED)
    grads = refs[:count]
    expert_from = refs[count : count + 2]
    rows_hbm, gates_high_ref, gates_low_ref, forward_ref = refs[count + 2 : count + 6]
    outs = refs[count + 6 : 2 * count + 6]
    expert_to = refs[2 * count + 6 : 2 * count + 8]
    block_ref = refs[2 * count + 8]
    scratch = refs[2 * count + 9 : 8 * count + 9]
    (
        rows_ref,
        swap_send,
        swap_recv,
        swap_local,
        send_sems,
        recv_sems,
        local_sems,
    ) = refs[8 * count + 9 :]
    me = place()
    partner = {"core": 1 - me["core"], "xl": 1 - lax.axis_index("xl")}
    crossed = me["core"] != lax.axis_index("xl")
    greet(ring_neighbours(me) + [partner])

    def moved(slot):
        return pltpu.make_async_remote_copy(
            src_ref=expert_from[slot],
            dst_ref=expert_to[slot],
            send_sem=swap_send.at[slot],
            recv_sem=swap_recv.at[slot],
            device_id=partner,
            device_id_type=MESH_ID,
        )

    def kept(slot):
        return pltpu.make_async_copy(expert_from[slot], expert_to[slot], swap_local.at[slot])

    wires = Wires(send_sems, recv_sems, local_sems)
    stages = Summing(wires, me, SUMMED, grads, outs, scratch).stages()
    next(stages)
    next(stages)

    @pl.when(crossed)
    def _():
        for slot in range(2):
            moved(slot).start()

    @pl.when(jnp.logical_not(crossed))
    def _():
        for slot in range(2):
            kept(slot).start()

    rows_in = wires.copy(rows_hbm, rows_ref)
    next(stages)
    next(stages)
    rows_in.wait()
    features = block_ref.shape[1]
    for left in range(0, features, 512):
        columns = pl.ds(left, 512)

        def mix(step, total):
            blocks = rows_ref[pl.ds(step * 16, 16), :, columns].astype(F32)
            rows = blocks.reshape(16 * CAP, 512).astype(BF16)
            at = pl.ds(pl.multiple_of(step * 16 * CAP, 128), 16 * CAP)
            return total + dot(gates_high_ref[:, at], rows) + dot(gates_low_ref[:, at], rows)

        mixed = lax.fori_loop(0, EXPERTS // 16, mix, forward_ref[:, columns])
        block_ref[:, columns] = mixed.astype(BF16)
    for _ in stages:
        pass
    wires.finish()

    @pl.when(crossed)
    def _():
        for slot in range(2):
            moved(slot).wait_recv()
            moved(slot).wait_send()

    @pl.when(jnp.logical_not(crossed))
    def _():
        for slot in range(2):
            kept(slot).wait()


def sum_last(grads, expert_grads, rows, gates_high, gates_low, forward_rows):
    anywhere = pl.BlockSpec(memory_space=pl.ANY)
    vmem = pl.BlockSpec(memory_space=pltpu.VMEM)
    count = len(SUMMED)
    return pl.pallas_call(
        last_kernel,
        out_shape=[jax.ShapeDtypeStruct((16, width), F32) for _, width, _ in SUMMED]
        + [jax.ShapeDtypeStruct(grad.shape, grad.dtype) for grad in expert_grads]
        + [jax.ShapeDtypeStruct(forward_rows.shape, BF16)],
        in_specs=[anywhere] * (count + 3) + [vmem] * 3,
        out_specs=[vmem] * count + [anywhere] * 2 + [vmem],
        scratch_shapes=summing_scratch(SUMMED)
        + [
            pltpu.VMEM(rows.shape, BF16),
            pltpu.SemaphoreType.DMA((2,)),
            pltpu.SemaphoreType.DMA((2,)),
            pltpu.SemaphoreType.DMA((2,)),
            pltpu.SemaphoreType.DMA((190,)),
            pltpu.SemaphoreType.DMA((190,)),
            pltpu.SemaphoreType.DMA((48,)),
        ],
        compiler_params=pltpu.CompilerParams(
            collective_id=1, has_side_effects=True, vmem_limit_bytes=56 * 1024 * 1024
        ),
        cost_estimate=pl.CostEstimate(
            flops=1_000_000_000, bytes_accessed=200_000_000, transcendentals=0
        ),
    )(*grads, *expert_grads, rows, gates_high, gates_low, forward_rows)


def col_device(col):
    return {"yh": col // 4, "xh": rem(col // 2, 2), "xl": rem(col, 2)}


def col_index():
    return lax.axis_index("yh") * 4 + lax.axis_index("xh") * 2 + lax.axis_index("xl")


VMEM_SPEC = pl.BlockSpec(memory_space=pltpu.VMEM)
GROUP = QUERY_HEADS // KEY_VALUE_HEADS
EXTRA = 128


def dot(left, right, left_dim=1, right_dim=0):
    return lax.dot_general(
        left, right, (((left_dim,), (right_dim,)), ((), ())), preferred_element_type=F32
    )


def rounded_parts(value):
    first = value.astype(BF16)
    left = value - first.astype(F32)
    second = left.astype(BF16)
    return [first, second, (left - second.astype(F32)).astype(BF16)]


def lane_column(index):
    return (lax.broadcasted_iota(jnp.int32, (16, 128), 1) == index).astype(BF16)


def gain_row(misc_ref, index):
    return dot(lane_column(index), misc_ref[...], 1, 1)[:1]


def allowed_pairs(marks_ref, segments_ref, rows, keys):
    me = col_index()
    shape = (rows, keys)
    own = segments_ref[:, :1]
    first_length = jnp.where(
        me == 0,
        jnp.sum((own == 0.0).astype(F32), axis=0, keepdims=True),
        marks_ref[:1, :1].astype(F32),
    )
    last_start = (me * rows).astype(F32) + jnp.sum(
        (own < 2.0).astype(F32), axis=0, keepdims=True
    )
    lowest = jnp.where(own == 0.0, 0.0, jnp.where(own == 1.0, first_length, last_start))
    key = lax.broadcasted_iota(jnp.int32, shape, 1)
    query = lax.broadcasted_iota(jnp.int32, shape, 0) + me * rows
    return (key <= query) & (key.astype(F32) >= lowest)


def head_columns(ref, group):
    width = GROUP * HEAD_SIZE
    return jnp.concatenate(
        [
            ref[:, group * width + head * HEAD_SIZE : group * width + (head + 1) * HEAD_SIZE]
            for head in range(GROUP)
        ],
        axis=0,
    )


def head_weights(queries, keys, allowed):
    scores = dot(queries, keys, 1, 1) * (HEAD_SIZE ** (-0.5))
    scores = jnp.where(allowed, scores, -1e30)
    shifted = jnp.exp(scores - jnp.max(scores, axis=1, keepdims=True))
    return shifted / jnp.sum(shifted, axis=1, keepdims=True)


GROUP_BLOCKS = 16
MIDDLE_MIB = 52


def blocks_of(value):
    return value.reshape(GROUP_BLOCKS, CAP, value.shape[-1]).astype(BF16)


def later_kernel(
    tokens_ref,
    misc_ref,
    marks_ref,
    query_ref,
    keyval_ref,
    slots_ref,
    cotangent_ref,
    out_ref,
    marks_out,
    normed_ref,
    queries_ref,
    rows_out,
    rows_ref,
    own_ref,
    send_sems,
    recv_sems,
    local_sem,
):
    me = col_index()
    rows = own_ref.shape[0]
    tail = marks_ref.shape[0]
    late = pl.ds(rows - tail, tail)
    features = tokens_ref.shape[1]
    gain = gain_row(misc_ref, EXPERTS)
    total = jnp.zeros((rows, 1), F32)
    for left in range(0, features, 512):
        piece = tokens_ref[:, left : left + 512].astype(F32)
        total = total + jnp.sum(piece * piece, axis=1, keepdims=True)
    scale = lax.rsqrt(total / features + EPSILON)
    for left in range(0, features, 512):
        piece = tokens_ref[:, left : left + 512].astype(F32)
        normed_ref[:, left : left + 512] = (piece * scale * gain[:, left : left + 512]).astype(BF16)
    normed = normed_ref[...]
    for left in range(0, own_ref.shape[1], 512):
        own_ref[:, left : left + 512] = dot(normed, keyval_ref[:, left : left + 512]).astype(BF16)
    greet([col_device(rem(me + far, 8)) for far in range(1, 8)])

    def copies(far, first):
        there = col_device(rem(me + far, 8))
        pairs = [(own_ref, out_ref.at[me])]
        if first:
            pairs = [(own_ref.at[late], out_ref.at[0, late]), (marks_ref, marks_out)]
        return [
            pltpu.make_async_remote_copy(
                src_ref=source,
                dst_ref=target,
                send_sem=send_sems.at[far, number],
                recv_sem=recv_sems.at[far, number],
                device_id=there,
                device_id_type=MESH_ID,
            )
            for number, (source, target) in enumerate(pairs)
        ]

    def each(far, first, condition, act):
        @pl.when(condition)
        def _():
            for copy in copies(far, first):
                act(copy)

    for far in range(7, 0, -1):
        each(far, False, (me > 0) & (me + far < 8), lambda copy: copy.start())
        each(far, True, me == 0, lambda copy: copy.start())
    keep = pltpu.make_async_copy(own_ref, out_ref.at[me], local_sem.at[0])
    keep.start()
    for left in range(0, queries_ref.shape[1], 512):
        queries_ref[:, left : left + 512] = dot(normed, query_ref[:, left : left + 512]).astype(
            BF16
        )
    tile = GROUP_BLOCKS * CAP

    def fill(step, carry):
        slots = slots_ref[pl.ds(pl.multiple_of(step * tile, 128), tile)]
        blocks = pl.ds(step * GROUP_BLOCKS, GROUP_BLOCKS)
        for left in range(0, features, 512):
            rows_ref[blocks, :, left : left + 512] = blocks_of(
                dot(slots, cotangent_ref[:, left : left + 512])
            )
        return carry

    lax.fori_loop(0, EXPERTS // GROUP_BLOCKS, fill, 0)
    laid = pltpu.make_async_copy(rows_ref, rows_out, local_sem.at[1])
    laid.start()

    @pl.when(me == 0)
    def _():
        marks_out[...] = marks_ref[...]

    @pl.when(me > 0)
    def _():
        out_ref[0, : rows - tail] = jnp.zeros((rows - tail, own_ref.shape[1]), own_ref.dtype)

    for far in range(1, 8):

        @pl.when(me + far < 8)
        def _():
            out_ref[me + far] = jnp.zeros(own_ref.shape, own_ref.dtype)

    keep.wait()
    for far in range(1, 8):
        each(far, False, me > far, lambda copy: copy.wait_recv())
        each(far, True, me == far, lambda copy: copy.wait_recv())
        each(far, False, (me > 0) & (me + far < 8), lambda copy: copy.wait_send())
        each(far, True, me == 0, lambda copy: copy.wait_send())
    laid.wait()


def to_later(tokens, misc, marks, query_w, keyval_w, slots_down, cotangent):
    vmem = pl.BlockSpec(memory_space=pltpu.VMEM)
    own = (tokens.shape[0], keyval_w.shape[1])
    laid = (EXPERTS, CAP, tokens.shape[1])
    return pl.pallas_call(
        later_kernel,
        out_shape=[
            jax.ShapeDtypeStruct((8,) + own, BF16),
            jax.ShapeDtypeStruct(marks.shape, marks.dtype),
            jax.ShapeDtypeStruct(tokens.shape, BF16),
            jax.ShapeDtypeStruct((tokens.shape[0], query_w.shape[1]), BF16),
            jax.ShapeDtypeStruct(laid, BF16),
        ],
        in_specs=[vmem] * 7,
        out_specs=[vmem] * 4 + [pl.BlockSpec(memory_space=pl.ANY)],
        scratch_shapes=[
            pltpu.VMEM(laid, BF16),
            pltpu.VMEM(own, BF16),
            pltpu.SemaphoreType.DMA((8, 2)),
            pltpu.SemaphoreType.DMA((8, 2)),
            pltpu.SemaphoreType.DMA((2,)),
        ],
        compiler_params=pltpu.CompilerParams(
            collective_id=2, has_side_effects=True, vmem_limit_bytes=28 * 1024 * 1024
        ),
        cost_estimate=pl.CostEstimate(
            flops=1_000_000_000, bytes_accessed=80_000_000, transcendentals=0
        ),
    )(tokens, misc, marks, query_w, keyval_w, slots_down, cotangent)


def middle_kernel(
    queries_ref,
    every_ref,
    marks_ref,
    segments_ref,
    tokens_ref,
    misc_ref,
    named_ref,
    slots_ref,
    slots_down_ref,
    owner_ref,
    cotangent_ref,
    outt_hbm,
    shgate_hbm,
    shup_hbm,
    shdt_hbm,
    cotangent_rows,
    attended_ref,
    residual_ref,
    normed_ref,
    gates_ref,
    gates_high_ref,
    gates_low_ref,
    forward_ref,
    grad_second_ref,
    grad_received,
    outgoing_hbm,
    grad_shgate_hbm,
    grad_shup_hbm,
    grad_shdt_hbm,
    outt_ref,
    shgate_ref,
    shup_ref,
    shdt_ref,
    grad_shgate,
    grad_shup,
    grad_shdt,
    outgoing,
    send_sems,
    recv_sems,
    local_sems,
):
    rows, features = tokens_ref.shape
    width = KEY_VALUE_HEADS * HEAD_SIZE
    keys_count = 8 * rows
    spot = place()
    chips = [chip_at(spot, offset) for offset in OFFSETS]
    mine = chip_at(spot, (0, 0, 0))[1]
    greet([where for where, _ in chips])
    wires = Wires(send_sems, recv_sems, local_sems)
    travelling = [
        wires.remote(cotangent_rows.at[holder], grad_received.at[mine], where)
        for where, holder in chips
    ]
    staying = [wires.copy(cotangent_rows.at[mine], grad_received.at[mine])]
    outt_in = wires.copy(outt_hbm, outt_ref)
    shared_in = [
        wires.copy(shgate_hbm, shgate_ref),
        wires.copy(shup_hbm, shup_ref),
        wires.copy(shdt_hbm, shdt_ref),
    ]
    allowed = allowed_pairs(marks_ref, segments_ref, rows, keys_count)
    allowed = jnp.concatenate([allowed.astype(F32)] * GROUP, axis=0) > 0.5
    for group in range(KEY_VALUE_HEADS):
        queries = head_columns(queries_ref, group)
        columns = pl.ds(group * HEAD_SIZE, HEAD_SIZE)
        keys = every_ref[:, :, columns].reshape(keys_count, HEAD_SIZE)
        values = every_ref[:, :, pl.ds(width + group * HEAD_SIZE, HEAD_SIZE)].reshape(
            keys_count, HEAD_SIZE
        )
        weights = head_weights(queries, keys, allowed)
        mixed = dot(weights.astype(BF16), values).astype(BF16)
        for head in range(GROUP):
            at = (group * GROUP + head) * HEAD_SIZE
            attended_ref[:, at : at + HEAD_SIZE] = mixed[head * rows : (head + 1) * rows]
    attended = attended_ref[...]
    outt_in.wait()
    total = jnp.zeros((rows, 1), F32)
    for left in range(0, features, 512):
        piece = tokens_ref[:, left : left + 512].astype(F32) + dot(
            attended, outt_ref[left : left + 512], 1, 1
        )
        residual_ref[:, left : left + 512] = piece
        total = total + jnp.sum(piece * piece, axis=1, keepdims=True)
    scale = lax.rsqrt(total / features + EPSILON)
    normed_ref[...] = (residual_ref[...] * scale * gain_row(misc_ref, EXPERTS + 1)).astype(BF16)
    normed = normed_ref[...]
    logits = dot(normed, misc_ref[...])
    named = named_ref[...] > 0.5
    chosen = jnp.where(named, logits, -1e30)
    chosen_exp = jnp.where(named, jnp.exp(chosen - jnp.max(chosen, axis=1, keepdims=True)), 0.0)
    gates = chosen_exp / jnp.sum(chosen_exp, axis=1, keepdims=True)
    gates_ref[...] = gates
    parts = jnp.concatenate(rounded_parts(gates), axis=1)
    tile = GROUP_BLOCKS * CAP

    def fill(step, carry):
        at = pl.ds(pl.multiple_of(step * tile, 128), tile)
        blocks = pl.ds(step * GROUP_BLOCKS, GROUP_BLOCKS)
        slots = slots_down_ref[at]
        for left in range(0, features, 512):
            outgoing[blocks, :, left : left + 512] = blocks_of(
                dot(slots, normed_ref[:, left : left + 512])
            )
        gate_parts = dot(slots, parts)
        owner = owner_ref[at].astype(F32)
        lane = lax.broadcasted_iota(jnp.int32, (tile, EXTRA), 1)
        extra = jnp.zeros((tile, EXTRA), F32)
        for part in range(3):
            column = jnp.sum(
                gate_parts[:, part * 128 : (part + 1) * 128] * owner, axis=1, keepdims=True
            )
            extra = jnp.where(lane == part, column, extra)
        outgoing[blocks, :, features:] = blocks_of(extra)
        return carry

    lax.fori_loop(0, EXPERTS // GROUP_BLOCKS, fill, 0)
    staying.append(wires.copy(outgoing, outgoing_hbm))

    slot_gates = jnp.zeros((rows, slots_ref.shape[1]), F32)
    for part in range(3):
        slot_gates = slot_gates + dot(
            parts[:, part * 128 : (part + 1) * 128], owner_ref[...], 1, 1
        )
    slot_gates = slot_gates * slots_ref[...].astype(F32)
    gates_high = slot_gates.astype(BF16)
    gates_high_ref[...] = gates_high
    gates_low_ref[...] = (slot_gates - gates_high.astype(F32)).astype(BF16)

    for copy in shared_in:
        copy.wait()
    cotangent = cotangent_ref[...]
    gate_pre = dot(normed, shgate_ref[...])
    up_pre = dot(normed, shup_ref[...])
    sigmoid = 1.0 / (1.0 + jnp.exp(-gate_pre))
    silu = gate_pre * sigmoid
    hidden = (silu * up_pre).astype(BF16)
    grad_hidden = dot(cotangent, shdt_ref[...])
    grad_gate = (
        grad_hidden * up_pre * sigmoid * (1.0 + gate_pre * (1.0 - sigmoid))
    ).astype(BF16)
    grad_up = (grad_hidden * silu).astype(BF16)
    for left in range(0, features, 512):
        columns = pl.ds(left, 512)
        forward_ref[:, columns] = residual_ref[:, columns] + dot(hidden, shdt_ref[columns], 1, 1)
        grad_second_ref[:, columns] = dot(grad_gate, shgate_ref[columns], 1, 1) + dot(
            grad_up, shup_ref[columns], 1, 1
        )
        grad_shgate[columns] = dot(normed_ref[:, columns], grad_gate, 0, 0).astype(BF16)
        grad_shup[columns] = dot(normed_ref[:, columns], grad_up, 0, 0).astype(BF16)
        grad_shdt[columns] = dot(cotangent_ref[:, columns], hidden, 0, 0).astype(BF16)
    staying += [
        wires.copy(grad_shgate, grad_shgate_hbm),
        wires.copy(grad_shup, grad_shup_hbm),
        wires.copy(grad_shdt, grad_shdt_hbm),
    ]
    for copy in staying:
        copy.wait()
    for copy in travelling:
        copy.wait_recv()
    wires.finish()


def middle(queries, every, marks, segments, tokens, misc, named, slots, slots_down, owner, cotangent,
           cotangent_rows, outt, shgate, shup, shdt):
    rows, features = tokens.shape
    slot_count = slots.shape[1]
    anywhere = pl.BlockSpec(memory_space=pl.ANY)
    inputs = (queries, every, marks, segments, tokens, misc, named, slots, slots_down, owner,
              cotangent, outt, shgate, shup, shdt)
    shared = [shgate.shape, shup.shape, shdt.shape]
    wide = cotangent_rows.shape[:2] + (features + EXTRA,)
    return pl.pallas_call(
        middle_kernel,
        out_shape=[
            jax.ShapeDtypeStruct((rows, features), BF16),
            jax.ShapeDtypeStruct((rows, features), F32),
            jax.ShapeDtypeStruct((rows, features), BF16),
            jax.ShapeDtypeStruct((rows, 128), F32),
            jax.ShapeDtypeStruct((rows, slot_count), BF16),
            jax.ShapeDtypeStruct((rows, slot_count), BF16),
            jax.ShapeDtypeStruct((rows, features), F32),
            jax.ShapeDtypeStruct((rows, features), F32),
            jax.ShapeDtypeStruct(cotangent_rows.shape, BF16),
            jax.ShapeDtypeStruct(wide, BF16),
        ]
        + [jax.ShapeDtypeStruct(shape, BF16) for shape in shared],
        in_specs=[VMEM_SPEC] * 11 + [anywhere] * 5,
        out_specs=[VMEM_SPEC] * 8 + [anywhere] * 5,
        scratch_shapes=[pltpu.VMEM(outt.shape, BF16)]
        + [pltpu.VMEM(shape, BF16) for shape in shared + shared]
        + [
            pltpu.VMEM(wide, BF16),
            pltpu.SemaphoreType.DMA((64,)),
            pltpu.SemaphoreType.DMA((64,)),
            pltpu.SemaphoreType.DMA((10,)),
        ],
        compiler_params=pltpu.CompilerParams(
            collective_id=5, has_side_effects=True, vmem_limit_bytes=MIDDLE_MIB * 1024 * 1024
        ),
        cost_estimate=pl.CostEstimate(
            flops=10_000_000_000, bytes_accessed=250_000_000, transcendentals=2_000_000
        ),
    )(*inputs, cotangent_rows)


def expert_kernel(
    outgoing_ref,
    cotangent_in,
    weight_hbm,
    down_hbm,
    returned_ref,
    rows_out,
    own_in_hbm,
    other_in_hbm,
    own_down_hbm,
    other_down_hbm,
    weight_ref,
    down_ref,
    own_in_ref,
    other_in_ref,
    own_down_ref,
    other_down_ref,
    landed,
    cotangents,
    back,
    grads,
    hiddens,
    gated,
    rows_staged,
    send_sems,
    recv_sems,
    local_sems,
):
    features = cotangent_in.shape[2]
    spot = place()
    chips = [chip_at(spot, offset) for offset in OFFSETS]
    sources = [chip_at(spot, offset, -1) for offset in OFFSETS]
    mine = chip_at(spot, (0, 0, 0))[1]
    holders = [mine] + [holder for _, holder in sources]
    wires = Wires(send_sems, recv_sems, local_sems)
    weights_in = [wires.copy(weight_hbm, weight_ref), wires.copy(down_hbm, down_ref)]
    greet([where for where, _ in chips])
    rows_in = [wires.copy(outgoing_ref.at[mine], landed.at[0])]
    for number, (where, holder) in enumerate(chips):
        rows_in.append(wires.remote(outgoing_ref.at[holder], landed.at[number + 1], where))
    brought = [
        wires.copy(cotangent_in.at[holder], cotangents.at[number])
        for number, holder in enumerate(holders)
    ]
    for copy in weights_in:
        copy.wait()
    count = len(holders)
    tile = GROUP_BLOCKS * CAP
    returning = []

    def flat(ref, first, columns):
        blocks = ref[first : first + GROUP_BLOCKS, :, columns].astype(F32)
        return blocks.reshape(tile, blocks.shape[-1]).astype(BF16)

    for first in range(0, count, GROUP_BLOCKS):
        for number in range(first, first + GROUP_BLOCKS):
            brought[number].wait()
            if number == 0:
                rows_in[number].wait()
            else:
                rows_in[number].wait_recv()
        at = pl.ds(first * CAP, tile)
        extra = flat(landed, first, pl.ds(features, EXTRA)).astype(F32)
        gate = extra[:, :1] + extra[:, 1:2] + extra[:, 2:3]
        everything = pl.ds(0, features)
        pre = dot(flat(landed, first, everything), weight_ref[...])
        grad_hidden = dot(flat(cotangents, first, everything), down_ref[...], 1, 1)
        along = jnp.zeros((tile, 1), F32)
        for part in range(2):
            base = part * 2 * HALF
            gate_pre, up_pre = pre[:, base : base + HALF], pre[:, base + HALF : base + 2 * HALF]
            grad_part = grad_hidden[:, part * HALF : (part + 1) * HALF]
            sigmoid = 1.0 / (1.0 + jnp.exp(-gate_pre))
            silu = gate_pre * sigmoid
            hidden = silu * up_pre
            along = along + jnp.sum(hidden * grad_part, axis=1, keepdims=True)
            gated_grad = grad_part * gate
            grads[at, base : base + HALF] = (
                gated_grad * up_pre * sigmoid * (1.0 + gate_pre * (1.0 - sigmoid))
            ).astype(BF16)
            grads[at, base + HALF : base + 2 * HALF] = (gated_grad * silu).astype(BF16)
            hiddens[at, part * HALF : (part + 1) * HALF] = hidden.astype(BF16)
            gated[at, part * HALF : (part + 1) * HALF] = (hidden * gate).astype(BF16)
        group_grads = grads[at]
        for left in range(0, features, 512):
            back[first : first + GROUP_BLOCKS, :, left : left + 512] = blocks_of(
                dot(group_grads, weight_ref[left : left + 512], 1, 1)
            )
        lane = lax.broadcasted_iota(jnp.int32, (tile, EXTRA), 1)
        value = jnp.zeros((tile, EXTRA), F32)
        for part, column in enumerate(rounded_parts(along)):
            value = jnp.where(lane == part, column.astype(F32), value)
        back[first : first + GROUP_BLOCKS, :, features:] = blocks_of(value)
        for number in range(first, first + GROUP_BLOCKS):
            if number == 0:
                kept = wires.copy(back.at[0], returned_ref.at[mine])
            else:
                returning.append(
                    wires.remote(back.at[number], returned_ref.at[mine], sources[number - 1][0])
                )
    staged = []
    for index, first in enumerate(range(0, count, GROUP_BLOCKS)):
        group_hidden = hiddens[pl.ds(first * CAP, tile)]
        slot = index % 2
        if index >= 2:
            for copy in staged[index - 2]:
                copy.wait()
        for left in range(0, features, 512):
            columns = pl.ds(left, 512)
            rows_staged[slot, :, :, left : left + 512] = blocks_of(
                dot(group_hidden, down_ref[:, columns])
            )
        staged.append(
            [
                wires.copy(rows_staged.at[slot, number], rows_out.at[holders[first + number]])
                for number in range(GROUP_BLOCKS)
            ]
        )

    def every_row(ref, columns):
        return ref[:, :, columns].astype(F32).reshape(count * CAP, 256).astype(BF16)

    def weight_gradients(step, carry):
        columns = pl.ds(pl.multiple_of(step * 256, 256), 256)
        rows = every_row(landed, columns)
        own_in_ref[columns] = dot(rows, grads[:, : 2 * HALF], 0, 0)
        other_in_ref[columns] = dot(rows, grads[:, 2 * HALF :], 0, 0).astype(BF16)
        rows = every_row(cotangents, columns)
        own_down_ref[:, columns] = dot(gated[:, :HALF], rows, 0, 0)
        other_down_ref[:, columns] = dot(gated[:, HALF:], rows, 0, 0).astype(BF16)
        return carry

    lax.fori_loop(0, features // 256, weight_gradients, 0)
    staged.append(
        [
            wires.copy(own_in_ref, own_in_hbm),
            wires.copy(other_in_ref, other_in_hbm),
            wires.copy(own_down_ref, own_down_hbm),
            wires.copy(other_down_ref, other_down_hbm),
        ]
    )
    for copies in staged[-3:]:
        for copy in copies:
            copy.wait()
    kept.wait()
    for copy in returning:
        copy.wait_recv()
    wires.finish()


def expert(outgoing, grad_received, weight, down):
    count, cap, features = grad_received.shape
    anywhere = pl.BlockSpec(memory_space=pl.ANY)
    return pl.pallas_call(
        expert_kernel,
        out_shape=[
            jax.ShapeDtypeStruct(outgoing.shape, BF16),
            jax.ShapeDtypeStruct(grad_received.shape, BF16),
            jax.ShapeDtypeStruct((features, 2 * HALF), F32),
            jax.ShapeDtypeStruct((features, 2 * HALF), BF16),
            jax.ShapeDtypeStruct((HALF, features), F32),
            jax.ShapeDtypeStruct((HALF, features), BF16),
        ],
        in_specs=[anywhere] * 4,
        out_specs=[anywhere] * 6,
        scratch_shapes=[
            pltpu.VMEM(weight.shape, BF16),
            pltpu.VMEM(down.shape, BF16),
            pltpu.VMEM((features, 2 * HALF), F32),
            pltpu.VMEM((features, 2 * HALF), BF16),
            pltpu.VMEM((HALF, features), F32),
            pltpu.VMEM((HALF, features), BF16),
            pltpu.VMEM(outgoing.shape, BF16),
            pltpu.VMEM(grad_received.shape, BF16),
            pltpu.VMEM(outgoing.shape, BF16),
            pltpu.VMEM((count * cap, 4 * HALF), BF16),
            pltpu.VMEM((count * cap, 2 * HALF), BF16),
            pltpu.VMEM((count * cap, 2 * HALF), BF16),
            pltpu.VMEM((2, GROUP_BLOCKS, cap, features), BF16),
            pltpu.SemaphoreType.DMA((128,)),
            pltpu.SemaphoreType.DMA((128,)),
            pltpu.SemaphoreType.DMA((144,)),
        ],
        compiler_params=pltpu.CompilerParams(
            collective_id=4, has_side_effects=True, vmem_limit_bytes=56 * 1024 * 1024
        ),
        cost_estimate=pl.CostEstimate(
            flops=22_000_000_000, bytes_accessed=300_000_000, transcendentals=1_000_000
        ),
    )(outgoing, grad_received, weight, down)


def back_to_residual(
    grad_back_ref,
    slots_ref,
    owner_ref,
    gates_ref,
    cotangent_ref,
    residual_ref,
    partial_ref,
    misc_ref,
    outt_ref,
    grad_residual_ref,
    grad_low_ref,
    grad_logits_ref,
    grad_gain_ref,
    grad_attended,
):
    rows, features = cotangent_ref.shape
    slots = slots_ref[...]
    extra = grad_back_ref[:, features:].astype(F32)
    owner = owner_ref[...].astype(F32)
    grad_gates = jnp.zeros((rows, 128), F32)
    for part in range(3):
        grad_gates = grad_gates + dot(slots, (owner * extra[:, part : part + 1]).astype(BF16))
    gates = gates_ref[...]
    grad_logits = (
        gates * (grad_gates - jnp.sum(gates * grad_gates, axis=1, keepdims=True))
    ).astype(BF16)
    grad_logits_ref[...] = grad_logits
    gain = gain_row(misc_ref, EXPERTS + 1)
    square, inner = jnp.zeros((rows, 1), F32), jnp.zeros((rows, 1), F32)
    for left in range(0, features, 512):
        columns = pl.ds(left, 512)
        piece = (
            partial_ref[:, columns]
            + dot(slots, grad_back_ref[:, columns])
            + dot(grad_logits, misc_ref[columns], 1, 1)
        )
        grad_residual_ref[:, columns] = piece
        residual = residual_ref[:, columns]
        square = square + jnp.sum(residual * residual, axis=1, keepdims=True)
        inner = inner + jnp.sum(
            piece * gain[:, left : left + 512] * residual, axis=1, keepdims=True
        )
    scale = lax.rsqrt(square / features + EPSILON)
    cubed = scale * scale * scale * (inner / features)
    for left in range(0, features, 512):
        columns = pl.ds(left, 512)
        piece = grad_residual_ref[:, columns]
        residual = residual_ref[:, columns]
        grad_gain_ref[:, columns] = jnp.broadcast_to(
            jnp.sum(piece * residual * scale, axis=0, keepdims=True), (8, 512)
        )
        value = (
            cotangent_ref[:, columns].astype(F32)
            + scale * piece * gain[:, left : left + 512]
            - residual * cubed
        )
        grad_residual_ref[:, columns] = value
        grad_low_ref[:, columns] = value.astype(BF16)
    grad_low = grad_low_ref[...]
    for left in range(0, features, 512):
        columns = pl.ds(left, 512)
        grad_attended[:, columns] = dot(grad_low, outt_ref[:, columns]).astype(BF16)


def back_heads(
    group, allowed, qkv_ref, every_ref, grad_attended, grad_queries_ref, partial_keyvals
):
    rows = qkv_ref.shape[0]
    width = KEY_VALUE_HEADS * HEAD_SIZE
    keys_count = 8 * rows
    score_scale = HEAD_SIZE ** (-0.5)
    queries = head_columns(qkv_ref, group)
    heads_gradient = head_columns(grad_attended, group)
    key_columns = pl.ds(group * HEAD_SIZE, HEAD_SIZE)
    value_columns = pl.ds(width + group * HEAD_SIZE, HEAD_SIZE)
    keys = every_ref[:, :, key_columns].reshape(keys_count, HEAD_SIZE)
    values = every_ref[:, :, value_columns].reshape(keys_count, HEAD_SIZE)
    weights = head_weights(queries, keys, allowed)
    grad_weights = dot(heads_gradient, values, 1, 1)
    inner_sum = jnp.sum(weights * grad_weights, axis=1, keepdims=True)
    grad_scores = (weights * (grad_weights - inner_sum)).astype(BF16)
    grad_queries = (dot(grad_scores, keys) * score_scale).astype(BF16)
    for head in range(GROUP):
        at = (group * GROUP + head) * HEAD_SIZE
        grad_queries_ref[:, at : at + HEAD_SIZE] = grad_queries[head * rows : (head + 1) * rows]
    partial_keyvals[:, :, key_columns] = (
        (dot(grad_scores, queries, 0, 0) * score_scale).astype(BF16).reshape(8, rows, HEAD_SIZE)
    )
    partial_keyvals[:, :, value_columns] = (
        dot(weights.astype(BF16), heads_gradient, 0, 0).astype(BF16).reshape(8, rows, HEAD_SIZE)
    )


EARLY_ROWS = 20


def rear_kernel(tail, *refs):
    (
        slots_ref,
        owner_ref,
        gates_ref,
        cotangent_ref,
        residual_ref,
        partial_ref,
        misc_ref,
        qkv_ref,
        marks_ref,
        segments_ref,
        attended_ref,
        normed1_ref,
        normed2_ref,
        tokens_ref,
        grad_back_hbm,
        outt_hbm,
        every_hbm,
        own_in_hbm,
        own_down_hbm,
        query_hbm,
        keyval_hbm,
        in_ref,
        down_ref,
        rows_ref,
    ) = refs[:24]
    (
        grad_tokens_ref,
        grad_outt_hbm,
        grad_query_hbm,
        grad_keyval_hbm,
        grad_misc_hbm,
        half_in_hbm,
        half_down_hbm,
        rows_out,
    ) = refs[24:32]
    (
        grad_back_ref,
        outt_ref,
        every_ref,
        own_in_ref,
        own_down_ref,
        grad_outt_ref,
        grad_query_ref,
        grad_keyval_ref,
        grad_misc_ref,
        grad_residual,
        grad_low,
        grad_logits,
        grad_gain,
        grad_attended,
        grad_queries,
        grad_first,
        blocks_ref,
        landed,
        query_ref,
        keyval_ref,
        their_in,
        their_down,
        sequence_send,
        sequence_recv,
        send_sems,
        recv_sems,
        local_sems,
    ) = refs[32:]
    me = col_index()
    spot = place()
    chips = [chip_at(spot, offset) for offset in OFFSETS]
    mine = chip_at(spot, (0, 0, 0))[1]
    rows, features = tokens_ref.shape
    late = pl.ds(rows - tail, tail)
    sibling = {"core": 1 - spot["core"]}
    greet([where for where, _ in chips] + [sibling])
    wires = Wires(send_sems, recv_sems, local_sems)
    fetched = [
        wires.copy(grad_back_hbm, grad_back_ref),
        wires.copy(outt_hbm, outt_ref),
        wires.copy(every_hbm, every_ref),
        wires.copy(query_hbm, query_ref),
        wires.copy(keyval_hbm, keyval_ref),
        wires.copy(own_in_hbm, own_in_ref),
        wires.copy(own_down_hbm, own_down_ref),
    ]
    halves_in = [
        wires.remote(in_ref, their_in, sibling),
        wires.remote(down_ref, their_down, sibling),
    ]
    kept = wires.copy(rows_ref.at[mine], rows_out.at[mine])
    returning = []

    def send_rows(start, stop):
        for where, holder in chips[start:stop]:
            returning.append(wires.remote(rows_ref.at[holder], rows_out.at[mine], where))

    send_rows(0, EARLY_ROWS)
    for fetch in fetched[:3]:
        fetch.wait()
    back_to_residual(
        grad_back_ref,
        slots_ref,
        owner_ref,
        gates_ref,
        cotangent_ref,
        residual_ref,
        partial_ref,
        misc_ref,
        outt_ref,
        grad_residual,
        grad_low,
        grad_logits,
        grad_gain,
        grad_attended,
    )
    allowed = allowed_pairs(marks_ref, segments_ref, rows, 8 * rows)
    allowed = jnp.concatenate([allowed.astype(F32)] * GROUP, axis=0) > 0.5
    for group in range(KEY_VALUE_HEADS):
        back_heads(
            group, allowed, qkv_ref, every_ref, grad_attended, grad_queries, blocks_ref
        )

    def copy(far, first_block):
        block = rem(me + 8 - far, 8)
        source, target = blocks_ref.at[block], landed.at[far]
        if first_block:
            source, target = blocks_ref.at[0, late], landed.at[far, late]
        return pltpu.make_async_remote_copy(
            src_ref=source,
            dst_ref=target,
            send_sem=sequence_send.at[far],
            recv_sem=sequence_recv.at[far],
            device_id=col_device(block),
            device_id_type=MESH_ID,
        )

    def each(far, first_block, condition, act):
        @pl.when(condition)
        def _():
            act(copy(far, first_block))

    for far in range(7, 0, -1):
        each(far, False, me > far, lambda moved: moved.start())
        each(far, True, me == far, lambda moved: moved.start())
    send_rows(EARLY_ROWS, 63)

    @pl.when(me == 0)
    def _():
        for far in range(1, 8):
            landed[far, : rows - tail] = jnp.zeros((rows - tail, landed.shape[2]), landed.dtype)

    for far in range(1, 8):

        @pl.when(me + far >= 8)
        def _():
            landed[far] = jnp.zeros(landed.shape[1:], landed.dtype)

    low, attended, queries = grad_low[...], attended_ref[...], grad_queries[...]
    for left in range(0, features, 512):
        columns = pl.ds(left, 512)
        grad_outt_ref[columns] = dot(grad_low[:, columns], attended, 0, 0).astype(BF16)
        grad_query_ref[columns] = dot(normed1_ref[:, columns], queries, 0, 0).astype(BF16)
    stored = [
        wires.copy(grad_outt_ref, grad_outt_hbm),
        wires.copy(grad_query_ref, grad_query_hbm),
    ]
    for fetch in fetched[3:]:
        fetch.wait()
    for left in range(0, features, 512):
        columns = pl.ds(left, 512)
        grad_first[:, columns] = dot(queries, query_ref[columns], 1, 1)
    for copy_in in halves_in:
        copy_in.wait_recv()
    for left in range(0, features, 512):
        columns = pl.ds(left, 512)
        their_in[columns] = (own_in_ref[columns] + their_in[columns].astype(F32)).astype(BF16)
        their_down[:, columns] = (
            own_down_ref[:, columns] + their_down[:, columns].astype(F32)
        ).astype(BF16)
    stored += [wires.copy(their_in, half_in_hbm), wires.copy(their_down, half_down_hbm)]
    for far in range(1, 8):
        each(far, False, (me > 0) & (me + far < 8), lambda moved: moved.wait_recv())
        each(far, True, me == 0, lambda moved: moved.wait_recv())
    grad_keyvals = grad_low.at[:, pl.ds(0, keyval_ref.shape[1])]
    for row in range(0, rows, 16):
        at = pl.ds(row, 16)
        value = blocks_ref[me, at].astype(F32)
        for far in range(1, 8):
            value = value + landed[far, at].astype(F32)
        grad_keyvals[at] = value.astype(BF16)
    keyvals = grad_keyvals[...]
    gain = gain_row(misc_ref, EXPERTS)
    square, inner = jnp.zeros((rows, 1), F32), jnp.zeros((rows, 1), F32)
    for left in range(0, features, 512):
        columns = pl.ds(left, 512)
        grad_keyval_ref[columns] = dot(normed1_ref[:, columns], keyvals, 0, 0).astype(BF16)
        piece = grad_first[:, columns] + dot(keyvals, keyval_ref[columns], 1, 1)
        grad_first[:, columns] = piece
        residual = tokens_ref[:, columns].astype(F32)
        square = square + jnp.sum(residual * residual, axis=1, keepdims=True)
        inner = inner + jnp.sum(
            piece * gain[:, left : left + 512] * residual, axis=1, keepdims=True
        )
    stored.append(wires.copy(grad_keyval_ref, grad_keyval_hbm))
    scale = lax.rsqrt(square / features + EPSILON)
    cubed = scale * scale * scale * (inner / features)
    logits = grad_logits[...]
    one_row = (lax.broadcasted_iota(jnp.int32, (16, 128), 0) == 0).astype(F32)
    lane = lax.broadcasted_iota(jnp.int32, (16, 128), 1)
    for left in range(0, features, 512):
        columns = pl.ds(left, 512)
        piece = grad_first[:, columns]
        residual = tokens_ref[:, columns].astype(F32)
        grad_tokens_ref[:, columns] = (
            grad_residual[:, columns]
            + scale * piece * gain[:, left : left + 512]
            - residual * cubed
        )
        total = dot(normed2_ref[:, columns], logits, 0, 0)
        rows1 = jnp.broadcast_to(
            jnp.sum(piece * residual * scale, axis=0, keepdims=True), (16, 512)
        )
        rows2 = jnp.broadcast_to(grad_gain[:1, columns], (16, 512))
        for index, gradient in ((EXPERTS, rows1), (EXPERTS + 1, rows2)):
            spread = (one_row * (lane == index).astype(F32)).astype(BF16)
            for part in rounded_parts(gradient):
                total = total + dot(part, spread, 0, 0)
        grad_misc_ref[columns] = total
    stored.append(wires.copy(grad_misc_ref, grad_misc_hbm))
    for far in range(1, 8):
        each(far, False, me > far, lambda moved: moved.wait_send())
        each(far, True, me == far, lambda moved: moved.wait_send())
    for copy_out in stored:
        copy_out.wait()
    kept.wait()
    for moved in returning:
        moved.wait_recv()
    wires.finish()


def rear(tail, inputs, grad_back, outt, every, own_in, own_down, query_w, keyval_w, expert_in,
         expert_down, rows_back):
    rows, features = inputs[3].shape
    anywhere = pl.BlockSpec(memory_space=pl.ANY)
    return pl.pallas_call(
        functools.partial(rear_kernel, tail),
        out_shape=[
            jax.ShapeDtypeStruct((rows, features), F32),
            jax.ShapeDtypeStruct((features, features), BF16),
            jax.ShapeDtypeStruct(query_w.shape, BF16),
            jax.ShapeDtypeStruct(keyval_w.shape, BF16),
            jax.ShapeDtypeStruct((features, 128), F32),
            jax.ShapeDtypeStruct(expert_in.shape, BF16),
            jax.ShapeDtypeStruct(expert_down.shape, BF16),
            jax.ShapeDtypeStruct(rows_back.shape, BF16),
        ],
        in_specs=[VMEM_SPEC] * 14 + [anywhere] * 10,
        out_specs=[VMEM_SPEC] + [anywhere] * 7,
        scratch_shapes=[
            pltpu.VMEM(grad_back.shape, BF16),
            pltpu.VMEM(outt.shape, BF16),
            pltpu.VMEM(every.shape, BF16),
            pltpu.VMEM(own_in.shape, F32),
            pltpu.VMEM(own_down.shape, F32),
            pltpu.VMEM((features, features), BF16),
            pltpu.VMEM(query_w.shape, BF16),
            pltpu.VMEM(keyval_w.shape, BF16),
            pltpu.VMEM((features, 128), F32),
            pltpu.VMEM((rows, features), F32),
            pltpu.VMEM((rows, features), BF16),
            pltpu.VMEM((rows, 128), BF16),
            pltpu.VMEM((8, features), F32),
            pltpu.VMEM((rows, features), BF16),
            pltpu.VMEM((rows, features), BF16),
            pltpu.VMEM((rows, features), F32),
            pltpu.VMEM(every.shape, BF16),
            pltpu.VMEM(every.shape, BF16),
            pltpu.VMEM(query_w.shape, BF16),
            pltpu.VMEM(keyval_w.shape, BF16),
            pltpu.VMEM(expert_in.shape, BF16),
            pltpu.VMEM(expert_down.shape, BF16),
            pltpu.SemaphoreType.DMA((8,)),
            pltpu.SemaphoreType.DMA((8,)),
            pltpu.SemaphoreType.DMA((66,)),
            pltpu.SemaphoreType.DMA((66,)),
            pltpu.SemaphoreType.DMA((16,)),
        ],
        compiler_params=pltpu.CompilerParams(
            collective_id=3, has_side_effects=True, vmem_limit_bytes=58 * 1024 * 1024
        ),
        cost_estimate=pl.CostEstimate(
            flops=10_000_000_000, bytes_accessed=150_000_000, transcendentals=2_000_000
        ),
    )(
        *inputs,
        grad_back,
        outt,
        every,
        own_in,
        own_down,
        query_w,
        keyval_w,
        expert_in,
        expert_down,
        rows_back,
    )


def contract(left_side, right_side, left_dim, right_dim):
    return lax.dot_general(
        left_side,
        right_side,
        (((left_dim,), (right_dim,)), ((), ())),
        preferred_element_type=F32,
    )


def expert_of(holder):
    return (holder // 8) * 8 + (holder % 2) * 4 + holder // 2 % 4


def packed(grad):
    return grad.reshape(4, 2, 2, 2, 48, grad.shape[-1])


def shards(
    tokens,
    segments,
    routes,
    norm1_gain,
    w_query,
    key_value_weight,
    w_output,
    norm2_gain,
    w_router,
    w_shgate,
    w_shup,
    w_shdown,
    w_exgate,
    w_exup,
    w_exdown,
    cotangent,
):
    local_rows, feature_count = tokens.shape
    sequence_length = local_rows * 8
    shard = jnp.concatenate(
        [
            w_output.T,
            w_router,
            norm1_gain[:, None],
            norm2_gain[:, None],
            jnp.zeros((12, 62), BF16),
            w_query,
            key_value_weight,
            w_shgate,
            w_shup,
            w_shdown.T,
        ],
        axis=1,
    )
    shard = jnp.concatenate([shard, jnp.zeros((4, TOTAL), BF16)], axis=0)
    *dense, expert_w, expert_down = gather_weights(shard, w_exgate[0], w_exup[0], w_exdown[0])
    outt_w, misc_w, query_w, keyval_w, shgate_w, shup_w, shdt_w = [
        gathered.reshape(feature_count, gathered.shape[-1]) for gathered in dense
    ]
    expert_ids = jnp.arange(128, dtype=jnp.int32)
    named = jnp.any(routes[:, :, None] == expert_ids[None, None, :], axis=1)
    named_low = named.astype(BF16)
    token_ids = jnp.arange(local_rows, dtype=jnp.int32)
    before = (token_ids[None, :] <= token_ids[:, None]).astype(BF16)
    rank = jnp.dot(before, named_low, preferred_element_type=F32) * named.astype(F32)
    slot_count = EXPERTS * CAP
    slot_ids = jnp.arange(slot_count, dtype=jnp.int32)
    holder = slot_ids // CAP
    slot_expert = expert_of(holder)
    owner = (slot_expert[:, None] == expert_ids[None, :]).astype(BF16)
    rank_wide = contract(rank.astype(BF16), owner, 1, 1)
    slots = (rank_wide == (slot_ids % CAP + 1).astype(F32)[None, :]).astype(BF16)
    slots_down = (
        contract(owner, rank.astype(BF16), 1, 1) == (slot_ids % CAP + 1).astype(F32)[:, None]
    ).astype(BF16)

    own_segments = segments.astype(F32)
    tail = 32
    first_length = jnp.sum((segments == 0).astype(F32)).astype(BF16)
    every, marks, first_normed, query_rows, sent_cotangent = to_later(
        tokens,
        misc_w,
        jnp.broadcast_to(first_length, (tail, 128)),
        query_w,
        keyval_w,
        slots_down,
        cotangent,
    )
    segment_tile = jnp.broadcast_to(own_segments[:, None], (local_rows, 128))
    (
        attended_rows,
        residual1,
        second_normed,
        gates,
        gates_high,
        gates_low,
        forward_rows,
        grad_second,
        grad_received,
        outgoing,
        grad_shgate,
        grad_shup,
        grad_shdt,
    ) = middle(
        query_rows,
        every,
        marks,
        segment_tile,
        tokens,
        misc_w,
        named.astype(F32),
        slots,
        slots_down,
        owner,
        cotangent,
        sent_cotangent,
        outt_w,
        shgate_w,
        shup_w,
        shdt_w,
    )
    grad_back, half_out, own_in, other_in, own_down, other_down = expert(
        outgoing, grad_received, expert_w, expert_down
    )
    grad_back = grad_back.reshape(slot_count, feature_count + EXTRA)
    (
        grad_tokens,
        grad_outt,
        grad_query,
        grad_keyval,
        grad_misc,
        half_in,
        half_down,
        returned,
    ) = rear(
        tail,
        (
            slots,
            owner,
            gates,
            cotangent,
            residual1,
            grad_second,
            misc_w,
            query_rows,
            marks,
            segment_tile,
            attended_rows,
            first_normed,
            second_normed,
            tokens,
        ),
        grad_back,
        outt_w,
        every,
        own_in,
        own_down,
        query_w,
        keyval_w,
        other_in,
        other_down,
        half_out,
    )
    *summed, half_in, half_down, block_out = sum_last(
        [
            packed(grad)
            for grad in (
                grad_outt,
                grad_misc,
                grad_query,
                grad_keyval,
                grad_shgate,
                grad_shup,
                grad_shdt,
            )
        ],
        [half_in, half_down],
        returned,
        gates_high,
        gates_low,
        forward_rows,
    )
    sum_outt, sum_misc, sum_query, sum_keyval, sum_shgate, sum_shup, sum_shdt = [
        piece[:12] for piece in summed
    ]
    return (
        block_out,
        grad_tokens,
        sum_misc[:, EXPERTS],
        sum_query,
        sum_keyval,
        sum_outt.T,
        sum_misc[:, EXPERTS + 1],
        sum_misc[:, :EXPERTS],
        sum_shgate,
        sum_shup,
        sum_shdt.T,
        half_in[None, :, :HALF].astype(F32),
        half_in[None, :, HALF:].astype(F32),
        half_down[None].astype(F32),
    )


def solution(mesh):
    fine = Mesh(mesh.devices.reshape(SIZES), AXES)
    rows = P(AXES, None)
    columns = P(None, AXES)
    flat = P(AXES)
    blocks = P(AXES, None, None)
    in_specs = (
        rows,
        flat,
        rows,
        flat,
        rows,
        rows,
        columns,
        flat,
        rows,
        rows,
        rows,
        columns,
        blocks,
        blocks,
        blocks,
        rows,
    )
    out_specs = (
        rows,
        rows,
        flat,
        rows,
        rows,
        columns,
        flat,
        rows,
        rows,
        rows,
        columns,
        blocks,
        blocks,
        blocks,
    )
    return jax.shard_map(shards, mesh=fine, in_specs=in_specs, out_specs=out_specs, check_vma=False)
```

```python
import functools

import jax
import jax.numpy as jnp
from jax import lax
from jax.experimental import pallas as pl
from jax.experimental.pallas import tpu as pltpu
from jax.sharding import Mesh
from jax.sharding import PartitionSpec as P

QUERY_HEADS = 12
KEY_VALUE_HEADS = 4
HEAD_SIZE = 128
EXPERTS = 64
TOPK = 6
CAP = 24
EPSILON = 1e-05

F32 = jnp.float32
BF16 = jnp.bfloat16
MESH_ID = pl.DeviceIdType.MESH
AXES = ("z", "yl", "core", "yh", "xh", "xl")
SIZES = (4, 2, 2, 2, 2, 2)

PARTS = (
    ("outt", 1536, "yzx", "yzx"),
    ("misc", 128, "yz", "yz"),
    ("q", 1536, "yz", "yz"),
    ("kv", 1024, "zy", "zy"),
    ("shg", 1024, "yz", "yz"),
    ("shu", 1024, "zy", "zy"),
    ("shdt", 1024, "zy", "zy"),
)
GATHERED = tuple((name, width, order) for name, width, order, _ in PARTS)
SUMMED = tuple((name, width, order) for name, width, _, order in PARTS)
TOTAL = sum(part[1] for part in PARTS)
HALF = 256
EXPERT_SEM = 200
TOTAL = sum(part[1] for part in PARTS)


def rem(value, size):
    return lax.rem(value, jnp.int32(size))


def place():
    at = {name: lax.axis_index(name) for name in AXES}
    return {
        "x": at["xh"] * 2 + at["xl"],
        "y": at["yh"] * 2 + at["yl"],
        "z": at["z"],
        "core": at["core"],
    }


def device(axis, value):
    if axis == "x":
        return {"xh": value // 2, "xl": rem(value, 2)}
    if axis == "y":
        return {"yh": value // 2, "yl": rem(value, 2)}
    return {axis: value}


def greet(targets):
    barrier = pltpu.get_barrier_semaphore()
    for target in targets:
        pl.semaphore_signal(barrier, inc=1, device_id=target, device_id_type=MESH_ID)
    pl.semaphore_wait(barrier, len(targets))


def ring_neighbours(me):
    near = [device("x", rem(me["x"] + hops, 4)) for hops in (1, 2, 3)]
    near += [device("y", rem(me["y"] + hops, 4)) for hops in (1, 3)]
    near += [device("z", rem(me["z"] + hops, 4)) for hops in (1, 3)]
    return near + [{"core": 1 - me["core"]}]


class Wires:
    def __init__(self, send_sems, recv_sems, local_sems):
        self.send, self.recv, self.local = send_sems, recv_sems, local_sems
        self.used, self.used_local, self.started, self.kept = 0, 0, [], []

    def remote(self, source, target, where):
        copy = pltpu.make_async_remote_copy(
            src_ref=source,
            dst_ref=target,
            send_sem=self.send.at[self.used],
            recv_sem=self.recv.at[self.used],
            device_id=where,
            device_id_type=MESH_ID,
        )
        self.used += 1
        copy.start()
        self.started.append(copy)
        return copy

    def copy(self, source, target):
        copy = pltpu.make_async_copy(source, target, self.local.at[self.used_local])
        self.used_local += 1
        copy.start()
        return copy

    def finish(self):
        for copy in self.started:
            copy.wait_send()


def balanced_offsets():
    left = [(x, y, z) for x in range(4) for y in range(4) for z in range(4) if x + y + z > 0]
    load, order = [0] * 6, []

    def uses(offset):
        used = [0] * 6
        for axis, hops in enumerate(offset):
            used[2 * axis] += hops in (1, 2)
            used[2 * axis + 1] += hops in (2, 3)
        return used

    def cost(offset):
        used = uses(offset)
        after = [a + b for a, b in zip(load, used)]
        mean = sum(after) / 6
        return (max(after), sum((a - mean) ** 2 for a in after), -sum(used))

    while left:
        best = min(left, key=cost)
        load = [a + b for a, b in zip(load, uses(best))]
        left.remove(best)
        order.append(best)
    return order


OFFSETS = balanced_offsets()


def chip_at(me, offset, sign=1):
    x, y, z = [rem(me[axis] + (sign * hops) % 4, 4) for axis, hops in zip("xyz", offset)]
    where = {"z": z, "yh": y // 2, "yl": rem(y, 2), "xh": x // 2, "xl": rem(x, 2)}
    return where, z * 16 + rem(y, 2) * 8 + (y // 2) * 4 + x


def halves(width):
    first = width // 256 * 128 if width > 128 else width
    return first, width - first


def spread_rows(shape, swap):
    dense = lax.broadcasted_iota(jnp.int32, shape, 1 if swap else 0)
    padded = lax.broadcasted_iota(jnp.int32, shape, 0 if swap else 1)
    shift = jnp.zeros(shape, jnp.int32)
    for edge in (12, 24, 36):
        shift = shift + jnp.where(dense >= edge, 4, 0)
    return dense + shift == padded


def block_ref(ref, axes, me, axis, value, columns):
    spot = dict(me)
    spot[axis] = value
    z = slice(None) if "z" in axes else spot["z"]
    yl = slice(None) if "y" in axes else rem(spot["y"], 2)
    yh = slice(None) if "y" in axes else spot["y"] // 2
    return ref.at[z, yl, me["core"], yh, :, columns]


class Summing:
    def __init__(self, wires, me, parts, grads, outs, scratch):
        self.wires, self.me = wires, me
        self.next = {axis: rem(me[axis] + 1, 4) for axis in "xyz"}
        self.opposite = {axis: rem(me[axis] + 2, 4) for axis in "xyz"}
        self.previous = {axis: rem(me[axis] + 3, 4) for axis in "xyz"}
        self.sibling = {"core": 1 - me["core"]}
        count = len(parts)
        self.runs = []
        for index, (name, width, order) in enumerate(parts):
            self.runs.append(
                {
                    "order": order[::-1],
                    "width": width // 4 if len(order) == 3 else width,
                    "left": "zy",
                    "turn": 0,
                    "grads": grads[index],
                    "out": outs[index],
                    "own": scratch[index],
                    "theirs": scratch[count + index],
                    "near1": scratch[2 * count + index],
                    "near2": scratch[3 * count + index],
                    "ends": scratch[4 * count + index],
                    "arrived": scratch[5 * count + index],
                }
            )

    def spot(self, left_axes, axis, value, with_core):
        at = dict(self.me)
        if axis is not None:
            at[axis] = value
        whole = [name for name in left_axes if name != axis]
        z = slice(None) if "z" in whole else at["z"]
        yl = slice(None) if "y" in whole else rem(at["y"], 2)
        yh = slice(None) if "y" in whole else at["y"] // 2
        return (z, yl) + (() if with_core is None else (with_core,)) + (yh,)

    def lead(self, left_axes, axis):
        dims = []
        for name in ("z", "y"):
            if name in left_axes and name != axis:
                dims += [4] if name == "z" else [2, 2]
        return dims

    def add_into(self, target, sources, dims):
        total = 1
        for size in dims:
            total *= size

        def body(index):
            for row in range(0, 48, 16):
                at = index + (pl.ds(row, 16),)
                value = target[at].astype(F32)
                for source in sources:
                    value = value + source[at].astype(F32)
                target[at] = value.astype(target.dtype)

        def step(flat, carry):
            index, rest_flat = [], flat
            for size in reversed(dims):
                index.append(rem(rest_flat, size))
                rest_flat = rest_flat // size
            body(tuple(reversed(index)))
            return carry

        if total == 1:
            body(())
        else:
            lax.fori_loop(0, total, step, 0)

    def columns_of(self, run, axis, value, which):
        base = 0
        if len(run["order"]) == 3:
            base = (value if axis == "x" else self.me["x"]) * run["width"]
        left, size = 0, run["width"]
        if which is not None:
            first_half, second_half = halves(run["width"])
            left, size = (0, first_half) if which == 0 else (first_half, second_half)
        if isinstance(base, int):
            return pl.ds(base + left, size)
        return pl.ds(pl.multiple_of(base + left, 128), size)

    def chunk(self, run, axis, value, which=None, ref=None, with_core=None):
        ref = run["own"] if ref is None else ref
        columns = self.columns_of(run, axis, value, which)
        return ref.at[self.spot(run["left"], axis, value, with_core) + (slice(None), columns)]

    def pair(self, run, axis, value):
        core = self.me["core"]
        give = self.wires.remote(
            self.chunk(run, axis, value, None, run["grads"], 1 - core),
            self.chunk(run, axis, value, None, run["theirs"]),
            self.sibling,
        )
        keep = self.wires.copy(
            self.chunk(run, axis, value, None, run["grads"], core), self.chunk(run, axis, value)
        )
        return give, keep

    def join(self, run, axis, value, copies):
        copies[0].wait_recv()
        copies[1].wait()
        self.add_into(
            self.chunk(run, axis, value),
            [self.chunk(run, axis, value, None, run["theirs"])],
            self.lead(run["left"], axis),
        )

    def slots(self, run, axis):
        dims = self.lead(run["left"], axis)
        ref = (run["near1"], run["near2"], run["ends"])[run["turn"]]
        if not dims:
            ref = ref.at[:, pl.ds(0, 48)]
        return ref.at[0], ref.at[1], ref.at[2], dims

    def part(self, ref, run, which, dims):
        first_half, second_half = halves(run["width"])
        columns = pl.ds(0, first_half) if which == 0 else pl.ds(first_half, second_half)
        return ref.at[(slice(None),) * len(dims) + (slice(None), columns)]

    def ring_open(self, run):
        axis = run["order"][run["turn"]]
        _, _, passing, dims = self.slots(run, axis)
        far = self.opposite[axis]
        run["passing"] = [
            self.wires.remote(
                self.chunk(run, axis, far, 0),
                self.part(passing, run, 0, dims),
                device(axis, self.next[axis]),
            )
        ]
        if halves(run["width"])[1]:
            run["passing"].append(
                self.wires.remote(
                    self.chunk(run, axis, far, 1),
                    self.part(passing, run, 1, dims),
                    device(axis, self.previous[axis]),
                )
            )

    def ring_near(self, run):
        axis = run["order"][run["turn"]]
        from_prv, from_nxt, _, dims = self.slots(run, axis)
        nxt, prv = self.next[axis], self.previous[axis]
        run["near"] = []
        if halves(run["width"])[1]:
            run["near"].append(
                self.wires.remote(
                    self.chunk(run, axis, nxt, 1),
                    self.part(from_prv, run, 1, dims),
                    device(axis, nxt),
                )
            )
        run["near"].append(
            self.wires.remote(
                self.chunk(run, axis, prv, 0), self.part(from_nxt, run, 0, dims), device(axis, prv)
            )
        )

    def ring_pass(self, run):
        axis = run["order"][run["turn"]]
        from_prv, from_nxt, passing, dims = self.slots(run, axis)
        nxt, prv = self.next[axis], self.previous[axis]
        run["passing"][0].wait_recv()
        self.add_into(self.chunk(run, axis, nxt, 0), [self.part(passing, run, 0, dims)], dims)
        run["near"].append(
            self.wires.remote(
                self.chunk(run, axis, nxt, 0), self.part(from_prv, run, 0, dims), device(axis, nxt)
            )
        )
        if halves(run["width"])[1]:
            run["passing"][1].wait_recv()
            self.add_into(self.chunk(run, axis, prv, 1), [self.part(passing, run, 1, dims)], dims)
            run["near"].append(
                self.wires.remote(
                    self.chunk(run, axis, prv, 1),
                    self.part(from_nxt, run, 1, dims),
                    device(axis, prv),
                )
            )

    def ring_close(self, run):
        axis = run["order"][run["turn"]]
        from_prv, from_nxt, _, dims = self.slots(run, axis)
        for copy in run["near"]:
            copy.wait_recv()
        self.add_into(self.chunk(run, axis, self.me[axis]), [from_prv, from_nxt], dims)
        run["left"] = run["left"].replace(axis, "")
        run["turn"] += 1

    def turn(self, run):
        self.ring_close(run)
        self.ring_open(run)
        self.ring_near(run)

    def spread(self, run):
        me, width = self.me, run["width"]
        third = len(run["order"]) == 3
        summed = run["own"].at[me["z"], rem(me["y"], 2), me["y"] // 2]
        exact = lax.Precision.HIGHEST if summed.dtype == F32 else None
        pick = spread_rows((64, 48), True).astype(summed.dtype)
        staging = run["ends"].at[3] if third else run["near2"].at[3]
        base = me["x"] * width if third else 0
        for left in range(0, width, 512):
            size = min(512, width - left)
            columns = pl.ds(left, size)
            if third:
                columns = pl.ds(pl.multiple_of(base + left, 128), size)
            staging[:, left : left + size] = jnp.dot(
                pick, summed[:, columns], preferred_element_type=F32, precision=exact
            ).astype(staging.dtype)
        if third:
            lands = run["arrived"].at[:, pl.ds(pl.multiple_of(base, 128), width)]
        else:
            lands = run["arrived"].at[me["x"]]
        run["copies"] = []
        for where in (self.next, self.opposite, self.previous):
            row = pl.ds(pl.multiple_of(where["x"] * 16, 16), 16)
            run["copies"].append(
                self.wires.remote(staging.at[row], lands, device("x", where["x"]))
            )
        row = pl.ds(pl.multiple_of(me["x"] * 16, 16), 16)
        run["keep"] = self.wires.copy(staging.at[row], lands)

    def deliver(self, run):
        run["keep"].wait()
        for copy in run["copies"]:
            copy.wait_recv()
        if len(run["order"]) == 3:
            run["out"][...] = run["arrived"][...].astype(F32)
        else:
            value = run["arrived"][0].astype(F32)
            for place_x in range(1, 4):
                value = value + run["arrived"][place_x].astype(F32)
            run["out"][...] = value

    def stages(self):
        runs = self.runs
        threes = [run for run in runs if len(run["order"]) == 3]
        twos = [run for run in runs if len(run["order"]) == 2]
        begun = []
        for where in (self.opposite, self.next, self.previous, self.me):
            begun.append([self.pair(run, run["order"][0], where[run["order"][0]]) for run in runs])
        yield
        for run, copies in zip(runs, begun[0]):
            axis = run["order"][0]
            self.join(run, axis, self.opposite[axis], copies)
            self.ring_open(run)
        for run, nexts, prevs in zip(runs, begun[1], begun[2]):
            axis = run["order"][0]
            self.join(run, axis, self.next[axis], nexts)
            self.join(run, axis, self.previous[axis], prevs)
            self.ring_near(run)
        yield
        for run in threes:
            self.ring_pass(run)
        for run, copies in zip(runs, begun[3]):
            axis = run["order"][0]
            self.join(run, axis, self.me[axis], copies)
        for run in twos:
            self.ring_pass(run)
        yield
        for run in threes:
            self.turn(run)
        for run in threes:
            self.ring_pass(run)
        for run in twos:
            self.turn(run)
        yield
        for run in threes:
            self.turn(run)
        for run in twos:
            self.ring_pass(run)
        for run in threes:
            self.ring_pass(run)
        yield
        for run in twos:
            self.ring_close(run)
            self.spread(run)
        for run in threes:
            self.ring_close(run)
            self.spread(run)
        yield
        for run in runs:
            self.deliver(run)
        yield


def summing_scratch(parts):
    own, theirs, near1, near2, ends, arrived = [], [], [], [], [], []
    for name, width, order in parts:
        kind = F32 if name == "misc" else BF16
        own.append(pltpu.VMEM((4, 2, 2, 48, width), kind))
        theirs.append(pltpu.VMEM((4, 2, 2, 48, width), kind))
        if len(order) == 3:
            quarter = width // 4
            near1.append(pltpu.VMEM((3, 4, 2, 2, 48, quarter), kind))
            near2.append(pltpu.VMEM((3, 2, 2, 48, quarter), kind))
            ends.append(pltpu.VMEM((4, 64, quarter), kind))
            arrived.append(pltpu.VMEM((16, width), kind))
        else:
            near1.append(pltpu.VMEM((3, 2, 2, 48, width) if order == "yz" else (3, 4, 48, width), kind))
            near2.append(pltpu.VMEM((4, 64, width), kind))
            ends.append(pltpu.VMEM((16, 128), kind))
            arrived.append(pltpu.VMEM((4, 16, width), kind))
    return own + theirs + near1 + near2 + ends + arrived


def last_kernel(*refs):
    count = len(SUMMED)
    grads = refs[:count]
    expert_from = refs[count : count + 2]
    rows_hbm, gates_high_ref, gates_low_ref, forward_ref = refs[count + 2 : count + 6]
    outs = refs[count + 6 : 2 * count + 6]
    expert_to = refs[2 * count + 6 : 2 * count + 8]
    block_ref = refs[2 * count + 8]
    scratch = refs[2 * count + 9 : 8 * count + 9]
    (
        rows_ref,
        swap_send,
        swap_recv,
        swap_local,
        send_sems,
        recv_sems,
        local_sems,
    ) = refs[8 * count + 9 :]
    me = place()
    partner = {"core": 1 - me["core"], "xl": 1 - lax.axis_index("xl")}
    crossed = me["core"] != lax.axis_index("xl")
    greet(ring_neighbours(me) + [partner])

    def moved(slot):
        return pltpu.make_async_remote_copy(
            src_ref=expert_from[slot],
            dst_ref=expert_to[slot],
            send_sem=swap_send.at[slot],
            recv_sem=swap_recv.at[slot],
            device_id=partner,
            device_id_type=MESH_ID,
        )

    def kept(slot):
        return pltpu.make_async_copy(expert_from[slot], expert_to[slot], swap_local.at[slot])

    wires = Wires(send_sems, recv_sems, local_sems)
    stages = Summing(wires, me, SUMMED, grads, outs, scratch).stages()
    next(stages)
    rows_in = wires.copy(rows_hbm, rows_ref)
    next(stages)
    rows_in.wait()
    features = block_ref.shape[1]
    for left in range(0, features, 512):
        columns = pl.ds(left, 512)

        def mix(step, total):
            blocks = rows_ref[pl.ds(step * 16, 16), :, columns].astype(F32)
            rows = blocks.reshape(16 * CAP, 512).astype(BF16)
            at = pl.ds(pl.multiple_of(step * 16 * CAP, 128), 16 * CAP)
            return total + dot(gates_high_ref[:, at], rows) + dot(gates_low_ref[:, at], rows)

        mixed = lax.fori_loop(0, EXPERTS // 16, mix, forward_ref[:, columns])
        block_ref[:, columns] = mixed.astype(BF16)
    next(stages)

    @pl.when(crossed)
    def _():
        for slot in range(2):
            moved(slot).start()

    @pl.when(jnp.logical_not(crossed))
    def _():
        for slot in range(2):
            kept(slot).start()

    for _ in stages:
        pass
    wires.finish()

    @pl.when(crossed)
    def _():
        for slot in range(2):
            moved(slot).wait_recv()
            moved(slot).wait_send()

    @pl.when(jnp.logical_not(crossed))
    def _():
        for slot in range(2):
            kept(slot).wait()


def sum_last(grads, expert_grads, rows, gates_high, gates_low, forward_rows):
    anywhere = pl.BlockSpec(memory_space=pl.ANY)
    vmem = pl.BlockSpec(memory_space=pltpu.VMEM)
    count = len(SUMMED)
    return pl.pallas_call(
        last_kernel,
        out_shape=[jax.ShapeDtypeStruct((16, width), F32) for _, width, _ in SUMMED]
        + [jax.ShapeDtypeStruct(grad.shape, grad.dtype) for grad in expert_grads]
        + [jax.ShapeDtypeStruct(forward_rows.shape, BF16)],
        in_specs=[anywhere] * (count + 3) + [vmem] * 3,
        out_specs=[vmem] * count + [anywhere] * 2 + [vmem],
        scratch_shapes=summing_scratch(SUMMED)
        + [
            pltpu.VMEM(rows.shape, BF16),
            pltpu.SemaphoreType.DMA((2,)),
            pltpu.SemaphoreType.DMA((2,)),
            pltpu.SemaphoreType.DMA((2,)),
            pltpu.SemaphoreType.DMA((190,)),
            pltpu.SemaphoreType.DMA((190,)),
            pltpu.SemaphoreType.DMA((48,)),
        ],
        compiler_params=pltpu.CompilerParams(
            collective_id=1, has_side_effects=True, vmem_limit_bytes=56 * 1024 * 1024
        ),
        cost_estimate=pl.CostEstimate(
            flops=1_000_000_000, bytes_accessed=200_000_000, transcendentals=0
        ),
    )(*grads, *expert_grads, rows, gates_high, gates_low, forward_rows)


def col_device(col):
    return {"yh": col // 4, "xh": rem(col // 2, 2), "xl": rem(col, 2)}


def col_index():
    return lax.axis_index("yh") * 4 + lax.axis_index("xh") * 2 + lax.axis_index("xl")


VMEM_SPEC = pl.BlockSpec(memory_space=pltpu.VMEM)
GROUP = QUERY_HEADS // KEY_VALUE_HEADS
EXTRA = 128


def dot(left, right, left_dim=1, right_dim=0):
    return lax.dot_general(
        left, right, (((left_dim,), (right_dim,)), ((), ())), preferred_element_type=F32
    )


def rounded_parts(value):
    first = value.astype(BF16)
    left = value - first.astype(F32)
    second = left.astype(BF16)
    return [first, second, (left - second.astype(F32)).astype(BF16)]


def lane_column(index):
    return (lax.broadcasted_iota(jnp.int32, (16, 128), 1) == index).astype(BF16)


def gain_row(misc, index):
    return dot(lane_column(index), misc, 1, 1)[:1]


def allowed_pairs(marks_ref, segments_ref, rows, keys):
    me = col_index()
    shape = (rows, keys)
    own = segments_ref[:, :1]
    first_length = jnp.where(
        me == 0,
        jnp.sum((own == 0.0).astype(F32), axis=0, keepdims=True),
        marks_ref[:1, :1].astype(F32),
    )
    last_start = (me * rows).astype(F32) + jnp.sum(
        (own < 2.0).astype(F32), axis=0, keepdims=True
    )
    lowest = jnp.where(own == 0.0, 0.0, jnp.where(own == 1.0, first_length, last_start))
    key = lax.broadcasted_iota(jnp.int32, shape, 1)
    query = lax.broadcasted_iota(jnp.int32, shape, 0) + me * rows
    return (key <= query) & (key.astype(F32) >= lowest)


def head_columns(ref, group):
    width = GROUP * HEAD_SIZE
    return jnp.concatenate(
        [
            ref[:, group * width + head * HEAD_SIZE : group * width + (head + 1) * HEAD_SIZE]
            for head in range(GROUP)
        ],
        axis=0,
    )


def head_weights(queries, keys, allowed):
    scores = dot(queries, keys, 1, 1) * (HEAD_SIZE ** (-0.5))
    scores = jnp.where(allowed, scores, -1e30)
    shifted = jnp.exp(scores - jnp.max(scores, axis=1, keepdims=True))
    return shifted / jnp.sum(shifted, axis=1, keepdims=True)


GROUP_BLOCKS = 16
MIDDLE_MIB = 46


def blocks_of(value):
    return value.reshape(GROUP_BLOCKS, CAP, value.shape[-1]).astype(BF16)


def front_kernel(
    shard_ref, tokens_ref, cotangent_ref, routes_ref, segments_ref, gate_ref, up_ref, down_ref, *rest
):
    count = len(GATHERED)
    results = rest[:count]
    (
        expert_in,
        expert_out,
        every_ref,
        marks_out,
        normed_ref,
        queries_ref,
        rows_out,
        named_ref,
        slots_ref,
        slots_down_ref,
        owner_ref,
        tile_ref,
    ) = rest[count : count + 12]
    rest = rest[count + 12 :]
    outs = rest[:count]
    landed = rest[count]
    stages = rest[count + 1 : 2 * count + 1]
    (
        marks_ref,
        rows_ref,
        own_ref,
        sequence_send,
        sequence_recv,
        send_sems,
        recv_sems,
        local_sems,
    ) = rest[2 * count + 1 :]
    me = place()
    col = col_index()
    rows, features = tokens_ref.shape
    tail = marks_ref.shape[0]
    late = pl.ds(rows - tail, tail)
    nxt = {axis: rem(me[axis] + 1, 4) for axis in "xyz"}
    opp = {axis: rem(me[axis] + 2, 4) for axis in "xyz"}
    prv = {axis: rem(me[axis] + 3, 4) for axis in "xyz"}
    sibling = {"core": 1 - me["core"]}
    partner = {"core": 1 - me["core"], "xl": 1 - lax.axis_index("xl")}
    crossed = me["core"] != lax.axis_index("xl")
    greet(
        [device("x", nxt["x"]), device("x", opp["x"]), device("x", prv["x"])]
        + [device("y", nxt["y"]), device("y", prv["y"])]
        + [device("z", nxt["z"]), device("z", prv["z"]), sibling, partner]
        + [col_device(rem(col + far, 8)) for far in range(1, 8)]
    )
    wires = Wires(send_sems, recv_sems, local_sems)
    runs, start = [], 0
    for index, (name, width, order) in enumerate(GATHERED):
        last_x = len(order) == 3
        quarter = width // 4 if last_x else width
        run = {
            "name": name,
            "out": outs[index],
            "result": results[index],
            "order": order,
            "width": quarter,
            "done": "",
            "stage": stages[index],
            "start": start,
            "landed": landed.at[:, :, pl.ds(start, quarter)],
            "base": me["x"] * quarter if last_x else 0,
            "first": [],
            "shared": [],
        }

        def piece(x):
            if last_x:
                return shard_ref.at[:, pl.ds(pl.multiple_of(start + x * quarter, 128), quarter)]
            return shard_ref.at[:, pl.ds(start, quarter)]

        for where in (nxt, prv, opp):
            run["first"].append(
                wires.remote(piece(where["x"]), run["landed"].at[me["x"]], device("x", where["x"]))
            )
        run["bring"] = wires.copy(piece(me["x"]), run["landed"].at[me["x"]])
        runs.append(run)
        start += width

    whole = [
        (gate_ref, expert_in.at[:, pl.ds(0, HALF)]),
        (up_ref, expert_in.at[:, pl.ds(HALF, HALF)]),
        (down_ref, expert_out.at[pl.ds(0, HALF)]),
    ]

    def moved(slot):
        source, target = whole[slot]
        return pltpu.make_async_remote_copy(
            src_ref=source,
            dst_ref=target,
            send_sem=send_sems.at[EXPERT_SEM + slot],
            recv_sem=recv_sems.at[EXPERT_SEM + slot],
            device_id=partner,
            device_id_type=MESH_ID,
        )

    def kept(slot):
        source, target = whole[slot]
        return pltpu.make_async_copy(source, target, local_sems.at[28 + slot])

    @pl.when(crossed)
    def _():
        for slot in range(3):
            moved(slot).start()

    @pl.when(jnp.logical_not(crossed))
    def _():
        for slot in range(3):
            kept(slot).start()

    def part_columns(run, axis, value, which):
        base = value * run["width"] if axis == "x" else run["base"]
        left, size = 0, run["width"]
        if which is not None:
            first_half, second_half = halves(run["width"])
            left, size = (0, first_half) if which == 0 else (first_half, second_half)
        if isinstance(base, int):
            return pl.ds(base + left, size)
        return pl.ds(pl.multiple_of(base + left, 128), size)

    def blocks(run, axis, value, which=None):
        columns = part_columns(run, axis, value, which)
        return block_ref(run["out"], run["done"], me, axis, value, columns)

    def begin(run, axis, source=None):
        target = blocks(run, axis, me[axis])
        source = target if source is None else source
        run["forth"] = wires.remote(source, target, device(axis, nxt[axis]))
        run["back"] = wires.remote(source, target, device(axis, prv[axis]))

    pick = spread_rows((48, 64), False).astype(BF16)
    for run in runs:
        run["bring"].wait()
        for copy in run["first"]:
            copy.wait_recv()
        for left in range(0, run["width"], 512):
            size = min(512, run["width"] - left)
            left_in = run["start"] + left
            piece_rows = landed[:, :, left_in : left_in + size].reshape(64, size)
            run["stage"][:, left : left + size] = jnp.dot(
                pick, piece_rows, preferred_element_type=F32
            ).astype(BF16)
        axis = run["order"][0]
        begin(run, axis, run["stage"])
        run["own"] = wires.copy(run["stage"], blocks(run, axis, me[axis]))

    def forward(run, axis):
        run["forth"].wait_recv()
        source = blocks(run, axis, prv[axis], 0)
        run["more"] = [wires.remote(source, source, device(axis, nxt[axis]))]
        run["back"].wait_recv()
        if halves(run["width"])[1] > 0:
            source = blocks(run, axis, nxt[axis], 1)
            run["more"].append(wires.remote(source, source, device(axis, prv[axis])))

    def share(run, axis, value):
        source = blocks(run, axis, value)
        run["shared"].append(wires.remote(source, source, sibling))

    def advance(run, step):
        axis = run["order"][step]
        for copy in run["more"]:
            copy.wait_recv()
        if step == len(run["order"]) - 1:
            share(run, axis, opp[axis])
            return
        if step == 0:
            run["own"].wait()
        run["done"] = run["done"] + axis
        following = run["order"][step + 1]
        begin(run, following)
        if step + 1 == len(run["order"]) - 1:
            share(run, following, me[following])

    def last_forward(run):
        axis = run["order"][-1]
        forward(run, axis)
        share(run, axis, prv[axis])
        share(run, axis, nxt[axis])

    lay_out_routes(routes_ref, named_ref, slots_ref, slots_down_ref, owner_ref)
    lay_out_segments(segments_ref, tile_ref, marks_ref)
    threes = [run for run in runs if len(run["order"]) == 3]
    twos = [run for run in runs if len(run["order"]) == 2]
    for run in runs:
        forward(run, run["order"][0])
    for run in runs:
        advance(run, 0)
    for run in threes:
        forward(run, run["order"][1])
    for run in threes:
        advance(run, 1)
    for run in twos:
        last_forward(run)
    for run in threes:
        last_forward(run)

    @pl.when(crossed)
    def _():
        for slot in range(3):
            moved(slot).wait_recv()

    @pl.when(jnp.logical_not(crossed))
    def _():
        for slot in range(3):
            kept(slot).wait()

    handed = [
        wires.remote(
            expert_in.at[:, pl.ds(0, 2 * HALF)], expert_in.at[:, pl.ds(2 * HALF, 2 * HALF)], sibling
        ),
        wires.remote(expert_out.at[pl.ds(0, HALF)], expert_out.at[pl.ds(HALF, HALF)], sibling),
    ]
    for run in twos + threes:
        advance(run, len(run["order"]) - 1)
    stored = []

    def complete(run):
        for copy in run["shared"]:
            copy.wait_recv()
        stored.append(wires.copy(run["out"], run["result"]))

    early = [run for run in runs if run["name"] in ("misc", "q", "kv")]
    for run in early:
        complete(run)
    weights = {run["name"]: run["out"] for run in early}

    def weight_columns(name, columns):
        value = weights[name][:, :, :, :, :, columns]
        return value.reshape(features, value.shape[-1])

    gain = gain_row(weight_columns("misc", pl.ds(0, 128)), EXPERTS)
    total = jnp.zeros((rows, 1), F32)
    for left in range(0, features, 512):
        piece = tokens_ref[:, left : left + 512].astype(F32)
        total = total + jnp.sum(piece * piece, axis=1, keepdims=True)
    scale = lax.rsqrt(total / features + EPSILON)
    for left in range(0, features, 512):
        piece = tokens_ref[:, left : left + 512].astype(F32)
        normed_ref[:, left : left + 512] = (piece * scale * gain[:, left : left + 512]).astype(BF16)
    normed = normed_ref[...]
    for left in range(0, own_ref.shape[1], 512):
        own_ref[:, left : left + 512] = dot(normed, weight_columns("kv", pl.ds(left, 512))).astype(
            BF16
        )

    def copies(far, first):
        there = col_device(rem(col + far, 8))
        pairs = [(own_ref, every_ref.at[col])]
        if first:
            pairs = [(own_ref.at[late], every_ref.at[0, late]), (marks_ref, marks_out)]
        return [
            pltpu.make_async_remote_copy(
                src_ref=source,
                dst_ref=target,
                send_sem=sequence_send.at[far, number],
                recv_sem=sequence_recv.at[far, number],
                device_id=there,
                device_id_type=MESH_ID,
            )
            for number, (source, target) in enumerate(pairs)
        ]

    def each(far, first, condition, act):
        @pl.when(condition)
        def _():
            for copy in copies(far, first):
                act(copy)

    for far in range(7, 0, -1):
        each(far, False, (col > 0) & (col + far < 8), lambda copy: copy.start())
        each(far, True, col == 0, lambda copy: copy.start())
    keep = wires.copy(own_ref, every_ref.at[col])

    @pl.when(col == 0)
    def _():
        marks_out[...] = marks_ref[...]

    @pl.when(col > 0)
    def _():
        every_ref[0, : rows - tail] = jnp.zeros((rows - tail, own_ref.shape[1]), own_ref.dtype)

    for far in range(1, 8):

        @pl.when(col + far < 8)
        def _():
            every_ref[col + far] = jnp.zeros(own_ref.shape, own_ref.dtype)

    for run in runs:
        if run["name"] not in weights:
            complete(run)
    for left in range(0, queries_ref.shape[1], 512):
        queries_ref[:, left : left + 512] = dot(
            normed, weight_columns("q", pl.ds(left, 512))
        ).astype(BF16)
    tile = GROUP_BLOCKS * CAP

    def fill(step, carry):
        slots = slots_down_ref[pl.ds(pl.multiple_of(step * tile, 128), tile)]
        blocks = pl.ds(step * GROUP_BLOCKS, GROUP_BLOCKS)
        for left in range(0, features, 512):
            rows_ref[blocks, :, left : left + 512] = blocks_of(
                dot(slots, cotangent_ref[:, left : left + 512])
            )
        return carry

    lax.fori_loop(0, EXPERTS // GROUP_BLOCKS, fill, 0)
    stored.append(wires.copy(rows_ref, rows_out))
    for copy in handed:
        copy.wait_recv()
    keep.wait()
    for far in range(1, 8):
        each(far, False, col > far, lambda copy: copy.wait_recv())
        each(far, True, col == far, lambda copy: copy.wait_recv())
        each(far, False, (col > 0) & (col + far < 8), lambda copy: copy.wait_send())
        each(far, True, col == 0, lambda copy: copy.wait_send())
    for copy in stored:
        copy.wait()
    wires.finish()

    @pl.when(crossed)
    def _():
        for slot in range(3):
            moved(slot).wait_send()


def lay_out_routes(routes_ref, named_ref, slots_ref, slots_down_ref, owner_ref):
    rows = routes_ref.shape[0]
    count = EXPERTS * CAP
    expert = lax.broadcasted_iota(jnp.int32, (rows, 128), 1)
    named = jnp.zeros((rows, 128), F32)
    for choice in range(TOPK):
        named = named + (routes_ref[:, choice : choice + 1] == expert).astype(F32)
    named_ref[...] = named
    ahead = lax.broadcasted_iota(jnp.int32, (rows, rows), 1) <= lax.broadcasted_iota(
        jnp.int32, (rows, rows), 0
    )
    rank = (dot(ahead.astype(F32).astype(BF16), named.astype(BF16)) * named).astype(BF16)

    def holder_of(slot):
        return ((slot.astype(F32) + 0.5) * (1.0 / CAP)).astype(jnp.int32)

    slot = lax.broadcasted_iota(jnp.int32, (count, 128), 0)
    holder = holder_of(slot)
    owned = (
        (holder & 56) + (holder & 1) * 4 + ((holder & 6) >> 1)
        == lax.broadcasted_iota(jnp.int32, (count, 128), 1)
    )
    owner = owned.astype(F32).astype(BF16)
    owner_ref[...] = owner
    turn = (slot - holder * CAP + 1).astype(F32)
    slots_down_ref[...] = (dot(owner, rank, 1, 1) == turn).astype(F32).astype(BF16)
    slot = lax.broadcasted_iota(jnp.int32, (rows, count), 1)
    turn = (slot - holder_of(slot) * CAP + 1).astype(F32)
    slots_ref[...] = (dot(rank, owner, 1, 1) == turn).astype(F32).astype(BF16)


def lay_out_segments(segments_ref, tile_ref, marks_ref):
    rows = segments_ref.shape[1]
    same = lax.broadcasted_iota(jnp.int32, (rows, rows), 0) == lax.broadcasted_iota(
        jnp.int32, (rows, rows), 1
    )
    numbers = jnp.where(same, segments_ref[...].astype(F32), 0.0).astype(BF16)
    tile = dot(numbers, jnp.ones((rows, 128), BF16))
    tile_ref[...] = tile
    length = jnp.sum((tile == 0.0).astype(F32), axis=0, keepdims=True)
    marks_ref[...] = jnp.broadcast_to(length, marks_ref.shape).astype(BF16)


def front(shard, tokens, cotangent, routes, segments, gate_w, up_w, down_w):
    anywhere = pl.BlockSpec(memory_space=pl.ANY)
    rows, features = tokens.shape
    blocks = [(4, 2, 2, 2, 48, width) for _, width, _ in GATHERED]
    own = (rows, 2 * KEY_VALUE_HEADS * HEAD_SIZE)
    laid = (EXPERTS, CAP, features)
    slots = EXPERTS * CAP
    marks = (32, 128)
    return pl.pallas_call(
        front_kernel,
        out_shape=[jax.ShapeDtypeStruct(shape, BF16) for shape in blocks]
        + [
            jax.ShapeDtypeStruct((features, 4 * HALF), BF16),
            jax.ShapeDtypeStruct((2 * HALF, features), BF16),
            jax.ShapeDtypeStruct((8,) + own, BF16),
            jax.ShapeDtypeStruct(marks, BF16),
            jax.ShapeDtypeStruct(tokens.shape, BF16),
            jax.ShapeDtypeStruct((rows, QUERY_HEADS * HEAD_SIZE), BF16),
            jax.ShapeDtypeStruct(laid, BF16),
            jax.ShapeDtypeStruct((rows, 128), F32),
            jax.ShapeDtypeStruct((rows, slots), BF16),
            jax.ShapeDtypeStruct((slots, 128), BF16),
            jax.ShapeDtypeStruct((slots, 128), BF16),
            jax.ShapeDtypeStruct((rows, 128), F32),
        ],
        in_specs=[VMEM_SPEC] * 5 + [anywhere] * 3,
        out_specs=[anywhere] * (len(GATHERED) + 2)
        + [VMEM_SPEC] * 4
        + [anywhere]
        + [VMEM_SPEC] * 5,
        scratch_shapes=[pltpu.VMEM(shape, BF16) for shape in blocks]
        + [pltpu.VMEM((4, 16, TOTAL), BF16)]
        + [
            pltpu.VMEM((48, width // 4 if len(order) == 3 else width), BF16)
            for _, width, order in GATHERED
        ]
        + [
            pltpu.VMEM(marks, BF16),
            pltpu.VMEM(laid, BF16),
            pltpu.VMEM(own, BF16),
            pltpu.SemaphoreType.DMA((8, 2)),
            pltpu.SemaphoreType.DMA((8, 2)),
            pltpu.SemaphoreType.DMA((EXPERT_SEM + 4,)),
            pltpu.SemaphoreType.DMA((EXPERT_SEM + 4,)),
            pltpu.SemaphoreType.DMA((32,)),
        ],
        compiler_params=pltpu.CompilerParams(
            collective_id=0, has_side_effects=True, vmem_limit_bytes=56 * 1024 * 1024
        ),
        cost_estimate=pl.CostEstimate(
            flops=2_000_000_000, bytes_accessed=250_000_000, transcendentals=0
        ),
    )(shard, tokens, cotangent, routes, segments, gate_w, up_w, down_w)


def middle_kernel(
    queries_ref,
    every_ref,
    marks_ref,
    segments_ref,
    tokens_ref,
    misc_ref,
    named_ref,
    slots_ref,
    slots_down_ref,
    owner_ref,
    cotangent_ref,
    outt_hbm,
    shgate_hbm,
    shup_hbm,
    shdt_hbm,
    cotangent_rows,
    attended_ref,
    residual_ref,
    normed_ref,
    gates_ref,
    gates_high_ref,
    gates_low_ref,
    forward_ref,
    grad_second_ref,
    grad_received,
    outgoing_hbm,
    grad_shgate_hbm,
    grad_shup_hbm,
    grad_shdt_hbm,
    outt_ref,
    shgate_ref,
    shup_ref,
    shdt_ref,
    grad_shgate,
    grad_shup,
    grad_shdt,
    outgoing,
    send_sems,
    recv_sems,
    local_sems,
):
    rows, features = tokens_ref.shape
    width = KEY_VALUE_HEADS * HEAD_SIZE
    keys_count = 8 * rows
    spot = place()
    chips = [chip_at(spot, offset) for offset in OFFSETS]
    mine = chip_at(spot, (0, 0, 0))[1]
    greet([where for where, _ in chips])
    wires = Wires(send_sems, recv_sems, local_sems)
    travelling = [
        wires.remote(cotangent_rows.at[holder], grad_received.at[mine], where)
        for where, holder in chips
    ]
    staying = [wires.copy(cotangent_rows.at[mine], grad_received.at[mine])]
    outt_in = wires.copy(outt_hbm, outt_ref)
    shared_in = [
        wires.copy(shgate_hbm, shgate_ref),
        wires.copy(shup_hbm, shup_ref),
        wires.copy(shdt_hbm, shdt_ref),
    ]
    allowed = allowed_pairs(marks_ref, segments_ref, rows, keys_count)
    allowed = jnp.concatenate([allowed.astype(F32)] * GROUP, axis=0) > 0.5
    for group in range(KEY_VALUE_HEADS):
        queries = head_columns(queries_ref, group)
        columns = pl.ds(group * HEAD_SIZE, HEAD_SIZE)
        keys = every_ref[:, :, columns].reshape(keys_count, HEAD_SIZE)
        values = every_ref[:, :, pl.ds(width + group * HEAD_SIZE, HEAD_SIZE)].reshape(
            keys_count, HEAD_SIZE
        )
        weights = head_weights(queries, keys, allowed)
        mixed = dot(weights.astype(BF16), values).astype(BF16)
        for head in range(GROUP):
            at = (group * GROUP + head) * HEAD_SIZE
            attended_ref[:, at : at + HEAD_SIZE] = mixed[head * rows : (head + 1) * rows]
    attended = attended_ref[...]
    outt_in.wait()
    total = jnp.zeros((rows, 1), F32)
    for left in range(0, features, 512):
        piece = tokens_ref[:, left : left + 512].astype(F32) + dot(
            attended, outt_ref[left : left + 512], 1, 1
        )
        residual_ref[:, left : left + 512] = piece
        total = total + jnp.sum(piece * piece, axis=1, keepdims=True)
    scale = lax.rsqrt(total / features + EPSILON)
    normed_ref[...] = (residual_ref[...] * scale * gain_row(misc_ref[...], EXPERTS + 1)).astype(BF16)
    normed = normed_ref[...]
    logits = dot(normed, misc_ref[...])
    named = named_ref[...] > 0.5
    chosen = jnp.where(named, logits, -1e30)
    chosen_exp = jnp.where(named, jnp.exp(chosen - jnp.max(chosen, axis=1, keepdims=True)), 0.0)
    gates = chosen_exp / jnp.sum(chosen_exp, axis=1, keepdims=True)
    gates_ref[...] = gates
    parts = jnp.concatenate(rounded_parts(gates), axis=1)
    tile = GROUP_BLOCKS * CAP

    def fill(step, carry):
        at = pl.ds(pl.multiple_of(step * tile, 128), tile)
        blocks = pl.ds(step * GROUP_BLOCKS, GROUP_BLOCKS)
        slots = slots_down_ref[at]
        for left in range(0, features, 512):
            outgoing[blocks, :, left : left + 512] = blocks_of(
                dot(slots, normed_ref[:, left : left + 512])
            )
        gate_parts = dot(slots, parts)
        owner = owner_ref[at].astype(F32)
        lane = lax.broadcasted_iota(jnp.int32, (tile, EXTRA), 1)
        extra = jnp.zeros((tile, EXTRA), F32)
        for part in range(3):
            column = jnp.sum(
                gate_parts[:, part * 128 : (part + 1) * 128] * owner, axis=1, keepdims=True
            )
            extra = jnp.where(lane == part, column, extra)
        outgoing[blocks, :, features:] = blocks_of(extra)
        return carry

    lax.fori_loop(0, EXPERTS // GROUP_BLOCKS, fill, 0)
    staying.append(wires.copy(outgoing, outgoing_hbm))

    slot_gates = jnp.zeros((rows, slots_ref.shape[1]), F32)
    for part in range(3):
        slot_gates = slot_gates + dot(
            parts[:, part * 128 : (part + 1) * 128], owner_ref[...], 1, 1
        )
    slot_gates = slot_gates * slots_ref[...].astype(F32)
    gates_high = slot_gates.astype(BF16)
    gates_high_ref[...] = gates_high
    gates_low_ref[...] = (slot_gates - gates_high.astype(F32)).astype(BF16)

    for copy in shared_in:
        copy.wait()
    cotangent = cotangent_ref[...]
    gate_pre = dot(normed, shgate_ref[...])
    up_pre = dot(normed, shup_ref[...])
    sigmoid = 1.0 / (1.0 + jnp.exp(-gate_pre))
    silu = gate_pre * sigmoid
    hidden = (silu * up_pre).astype(BF16)
    grad_hidden = dot(cotangent, shdt_ref[...])
    grad_gate = (
        grad_hidden * up_pre * sigmoid * (1.0 + gate_pre * (1.0 - sigmoid))
    ).astype(BF16)
    grad_up = (grad_hidden * silu).astype(BF16)
    for left in range(0, features, 512):
        columns = pl.ds(left, 512)
        forward_ref[:, columns] = residual_ref[:, columns] + dot(hidden, shdt_ref[columns], 1, 1)
        grad_second_ref[:, columns] = dot(grad_gate, shgate_ref[columns], 1, 1) + dot(
            grad_up, shup_ref[columns], 1, 1
        )
        grad_shgate[columns] = dot(normed_ref[:, columns], grad_gate, 0, 0).astype(BF16)
        grad_shup[columns] = dot(normed_ref[:, columns], grad_up, 0, 0).astype(BF16)
        grad_shdt[columns] = dot(cotangent_ref[:, columns], hidden, 0, 0).astype(BF16)
    staying += [
        wires.copy(grad_shgate, grad_shgate_hbm),
        wires.copy(grad_shup, grad_shup_hbm),
        wires.copy(grad_shdt, grad_shdt_hbm),
    ]
    for copy in staying:
        copy.wait()
    for copy in travelling:
        copy.wait_recv()
    wires.finish()


def middle(queries, every, marks, segments, tokens, misc, named, slots, slots_down, owner, cotangent,
           cotangent_rows, outt, shgate, shup, shdt):
    rows, features = tokens.shape
    slot_count = slots.shape[1]
    anywhere = pl.BlockSpec(memory_space=pl.ANY)
    inputs = (queries, every, marks, segments, tokens, misc, named, slots, slots_down, owner,
              cotangent, outt, shgate, shup, shdt)
    shared = [shgate.shape, shup.shape, shdt.shape]
    wide = cotangent_rows.shape[:2] + (features + EXTRA,)
    return pl.pallas_call(
        middle_kernel,
        out_shape=[
            jax.ShapeDtypeStruct((rows, features), BF16),
            jax.ShapeDtypeStruct((rows, features), F32),
            jax.ShapeDtypeStruct((rows, features), BF16),
            jax.ShapeDtypeStruct((rows, 128), F32),
            jax.ShapeDtypeStruct((rows, slot_count), BF16),
            jax.ShapeDtypeStruct((rows, slot_count), BF16),
            jax.ShapeDtypeStruct((rows, features), F32),
            jax.ShapeDtypeStruct((rows, features), F32),
            jax.ShapeDtypeStruct(cotangent_rows.shape, BF16),
            jax.ShapeDtypeStruct(wide, BF16),
        ]
        + [jax.ShapeDtypeStruct(shape, BF16) for shape in shared],
        in_specs=[VMEM_SPEC] * 11 + [anywhere] * 5,
        out_specs=[VMEM_SPEC] * 8 + [anywhere] * 5,
        scratch_shapes=[pltpu.VMEM(outt.shape, BF16)]
        + [pltpu.VMEM(shape, BF16) for shape in shared + shared]
        + [
            pltpu.VMEM(wide, BF16),
            pltpu.SemaphoreType.DMA((64,)),
            pltpu.SemaphoreType.DMA((64,)),
            pltpu.SemaphoreType.DMA((10,)),
        ],
        compiler_params=pltpu.CompilerParams(
            collective_id=5, has_side_effects=True, vmem_limit_bytes=MIDDLE_MIB * 1024 * 1024
        ),
        cost_estimate=pl.CostEstimate(
            flops=10_000_000_000, bytes_accessed=250_000_000, transcendentals=2_000_000
        ),
    )(*inputs, cotangent_rows)


def expert_kernel(
    outgoing_ref,
    cotangent_in,
    weight_hbm,
    down_hbm,
    returned_ref,
    rows_out,
    own_in_hbm,
    other_in_hbm,
    own_down_hbm,
    other_down_hbm,
    weight_ref,
    down_ref,
    own_in_ref,
    other_in_ref,
    own_down_ref,
    other_down_ref,
    landed,
    cotangents,
    back,
    grads,
    hiddens,
    gated,
    rows_staged,
    send_sems,
    recv_sems,
    local_sems,
):
    features = cotangent_in.shape[2]
    spot = place()
    chips = [chip_at(spot, offset) for offset in OFFSETS]
    sources = [chip_at(spot, offset, -1) for offset in OFFSETS]
    mine = chip_at(spot, (0, 0, 0))[1]
    holders = [mine] + [holder for _, holder in sources]
    wires = Wires(send_sems, recv_sems, local_sems)
    weights_in = [wires.copy(weight_hbm, weight_ref), wires.copy(down_hbm, down_ref)]
    greet([where for where, _ in chips])
    rows_in = [wires.copy(outgoing_ref.at[mine], landed.at[0])]
    for number, (where, holder) in enumerate(chips):
        rows_in.append(wires.remote(outgoing_ref.at[holder], landed.at[number + 1], where))
    brought = [
        wires.copy(cotangent_in.at[holder], cotangents.at[number])
        for number, holder in enumerate(holders)
    ]
    for copy in weights_in:
        copy.wait()
    count = len(holders)
    tile = GROUP_BLOCKS * CAP
    returning = []

    def flat(ref, first, columns):
        blocks = ref[first : first + GROUP_BLOCKS, :, columns].astype(F32)
        return blocks.reshape(tile, blocks.shape[-1]).astype(BF16)

    for first in range(0, count, GROUP_BLOCKS):
        for number in range(first, first + GROUP_BLOCKS):
            brought[number].wait()
            if number == 0:
                rows_in[number].wait()
            else:
                rows_in[number].wait_recv()
        at = pl.ds(first * CAP, tile)
        extra = flat(landed, first, pl.ds(features, EXTRA)).astype(F32)
        gate = extra[:, :1] + extra[:, 1:2] + extra[:, 2:3]
        everything = pl.ds(0, features)
        pre = dot(flat(landed, first, everything), weight_ref[...])
        grad_hidden = dot(flat(cotangents, first, everything), down_ref[...], 1, 1)
        along = jnp.zeros((tile, 1), F32)
        for part in range(2):
            base = part * 2 * HALF
            gate_pre, up_pre = pre[:, base : base + HALF], pre[:, base + HALF : base + 2 * HALF]
            grad_part = grad_hidden[:, part * HALF : (part + 1) * HALF]
            sigmoid = 1.0 / (1.0 + jnp.exp(-gate_pre))
            silu = gate_pre * sigmoid
            hidden = silu * up_pre
            along = along + jnp.sum(hidden * grad_part, axis=1, keepdims=True)
            gated_grad = grad_part * gate
            grads[at, base : base + HALF] = (
                gated_grad * up_pre * sigmoid * (1.0 + gate_pre * (1.0 - sigmoid))
            ).astype(BF16)
            grads[at, base + HALF : base + 2 * HALF] = (gated_grad * silu).astype(BF16)
            hiddens[at, part * HALF : (part + 1) * HALF] = hidden.astype(BF16)
            gated[at, part * HALF : (part + 1) * HALF] = (hidden * gate).astype(BF16)
        group_grads = grads[at]
        for left in range(0, features, 512):
            back[first : first + GROUP_BLOCKS, :, left : left + 512] = blocks_of(
                dot(group_grads, weight_ref[left : left + 512], 1, 1)
            )
        lane = lax.broadcasted_iota(jnp.int32, (tile, EXTRA), 1)
        value = jnp.zeros((tile, EXTRA), F32)
        for part, column in enumerate(rounded_parts(along)):
            value = jnp.where(lane == part, column.astype(F32), value)
        back[first : first + GROUP_BLOCKS, :, features:] = blocks_of(value)
        for number in range(first, first + GROUP_BLOCKS):
            if number == 0:
                kept = wires.copy(back.at[0], returned_ref.at[mine])
            else:
                returning.append(
                    wires.remote(back.at[number], returned_ref.at[mine], sources[number - 1][0])
                )
    staged = []
    for index, first in enumerate(range(0, count, GROUP_BLOCKS)):
        group_hidden = hiddens[pl.ds(first * CAP, tile)]
        slot = index % 2
        if index >= 2:
            for copy in staged[index - 2]:
                copy.wait()
        for left in range(0, features, 512):
            columns = pl.ds(left, 512)
            rows_staged[slot, :, :, left : left + 512] = blocks_of(
                dot(group_hidden, down_ref[:, columns])
            )
        staged.append(
            [
                wires.copy(rows_staged.at[slot, number], rows_out.at[holders[first + number]])
                for number in range(GROUP_BLOCKS)
            ]
        )

    def every_row(ref, columns):
        return ref[:, :, columns].astype(F32).reshape(count * CAP, 256).astype(BF16)

    def weight_gradients(step, carry):
        columns = pl.ds(pl.multiple_of(step * 256, 256), 256)
        rows = every_row(landed, columns)
        own_in_ref[columns] = dot(rows, grads[:, : 2 * HALF], 0, 0)
        other_in_ref[columns] = dot(rows, grads[:, 2 * HALF :], 0, 0).astype(BF16)
        rows = every_row(cotangents, columns)
        own_down_ref[:, columns] = dot(gated[:, :HALF], rows, 0, 0)
        other_down_ref[:, columns] = dot(gated[:, HALF:], rows, 0, 0).astype(BF16)
        return carry

    lax.fori_loop(0, features // 256, weight_gradients, 0)
    staged.append(
        [
            wires.copy(own_in_ref, own_in_hbm),
            wires.copy(other_in_ref, other_in_hbm),
            wires.copy(own_down_ref, own_down_hbm),
            wires.copy(other_down_ref, other_down_hbm),
        ]
    )
    for copies in staged[-3:]:
        for copy in copies:
            copy.wait()
    kept.wait()
    for copy in returning:
        copy.wait_recv()
    wires.finish()


def expert(outgoing, grad_received, weight, down):
    count, cap, features = grad_received.shape
    anywhere = pl.BlockSpec(memory_space=pl.ANY)
    return pl.pallas_call(
        expert_kernel,
        out_shape=[
            jax.ShapeDtypeStruct(outgoing.shape, BF16),
            jax.ShapeDtypeStruct(grad_received.shape, BF16),
            jax.ShapeDtypeStruct((features, 2 * HALF), F32),
            jax.ShapeDtypeStruct((features, 2 * HALF), BF16),
            jax.ShapeDtypeStruct((HALF, features), F32),
            jax.ShapeDtypeStruct((HALF, features), BF16),
        ],
        in_specs=[anywhere] * 4,
        out_specs=[anywhere] * 6,
        scratch_shapes=[
            pltpu.VMEM(weight.shape, BF16),
            pltpu.VMEM(down.shape, BF16),
            pltpu.VMEM((features, 2 * HALF), F32),
            pltpu.VMEM((features, 2 * HALF), BF16),
            pltpu.VMEM((HALF, features), F32),
            pltpu.VMEM((HALF, features), BF16),
            pltpu.VMEM(outgoing.shape, BF16),
            pltpu.VMEM(grad_received.shape, BF16),
            pltpu.VMEM(outgoing.shape, BF16),
            pltpu.VMEM((count * cap, 4 * HALF), BF16),
            pltpu.VMEM((count * cap, 2 * HALF), BF16),
            pltpu.VMEM((count * cap, 2 * HALF), BF16),
            pltpu.VMEM((2, GROUP_BLOCKS, cap, features), BF16),
            pltpu.SemaphoreType.DMA((128,)),
            pltpu.SemaphoreType.DMA((128,)),
            pltpu.SemaphoreType.DMA((144,)),
        ],
        compiler_params=pltpu.CompilerParams(
            collective_id=4, has_side_effects=True, vmem_limit_bytes=48 * 1024 * 1024
        ),
        cost_estimate=pl.CostEstimate(
            flops=22_000_000_000, bytes_accessed=300_000_000, transcendentals=1_000_000
        ),
    )(outgoing, grad_received, weight, down)


def back_to_residual(
    grad_back_ref,
    slots_ref,
    owner_ref,
    gates_ref,
    cotangent_ref,
    residual_ref,
    partial_ref,
    misc_ref,
    outt_ref,
    grad_residual_ref,
    grad_low_ref,
    grad_logits_ref,
    grad_gain_ref,
    grad_attended,
):
    rows, features = cotangent_ref.shape
    slots = slots_ref[...]
    extra = grad_back_ref[:, features:].astype(F32)
    owner = owner_ref[...].astype(F32)
    grad_gates = jnp.zeros((rows, 128), F32)
    for part in range(3):
        grad_gates = grad_gates + dot(slots, (owner * extra[:, part : part + 1]).astype(BF16))
    gates = gates_ref[...]
    grad_logits = (
        gates * (grad_gates - jnp.sum(gates * grad_gates, axis=1, keepdims=True))
    ).astype(BF16)
    grad_logits_ref[...] = grad_logits
    gain = gain_row(misc_ref[...], EXPERTS + 1)
    square, inner = jnp.zeros((rows, 1), F32), jnp.zeros((rows, 1), F32)
    for left in range(0, features, 512):
        columns = pl.ds(left, 512)
        piece = (
            partial_ref[:, columns]
            + dot(slots, grad_back_ref[:, columns])
            + dot(grad_logits, misc_ref[columns], 1, 1)
        )
        grad_residual_ref[:, columns] = piece
        residual = residual_ref[:, columns]
        square = square + jnp.sum(residual * residual, axis=1, keepdims=True)
        inner = inner + jnp.sum(
            piece * gain[:, left : left + 512] * residual, axis=1, keepdims=True
        )
    scale = lax.rsqrt(square / features + EPSILON)
    cubed = scale * scale * scale * (inner / features)
    for left in range(0, features, 512):
        columns = pl.ds(left, 512)
        piece = grad_residual_ref[:, columns]
        residual = residual_ref[:, columns]
        grad_gain_ref[:, columns] = jnp.broadcast_to(
            jnp.sum(piece * residual * scale, axis=0, keepdims=True), (8, 512)
        )
        value = (
            cotangent_ref[:, columns].astype(F32)
            + scale * piece * gain[:, left : left + 512]
            - residual * cubed
        )
        grad_residual_ref[:, columns] = value
        grad_low_ref[:, columns] = value.astype(BF16)
    grad_low = grad_low_ref[...]
    for left in range(0, features, 512):
        columns = pl.ds(left, 512)
        grad_attended[:, columns] = dot(grad_low, outt_ref[:, columns]).astype(BF16)


def back_heads(
    group, allowed, qkv_ref, every_ref, grad_attended, grad_queries_ref, partial_keyvals
):
    rows = qkv_ref.shape[0]
    width = KEY_VALUE_HEADS * HEAD_SIZE
    keys_count = 8 * rows
    score_scale = HEAD_SIZE ** (-0.5)
    queries = head_columns(qkv_ref, group)
    heads_gradient = head_columns(grad_attended, group)
    key_columns = pl.ds(group * HEAD_SIZE, HEAD_SIZE)
    value_columns = pl.ds(width + group * HEAD_SIZE, HEAD_SIZE)
    keys = every_ref[:, :, key_columns].reshape(keys_count, HEAD_SIZE)
    values = every_ref[:, :, value_columns].reshape(keys_count, HEAD_SIZE)
    weights = head_weights(queries, keys, allowed)
    grad_weights = dot(heads_gradient, values, 1, 1)
    inner_sum = jnp.sum(weights * grad_weights, axis=1, keepdims=True)
    grad_scores = (weights * (grad_weights - inner_sum)).astype(BF16)
    grad_queries = (dot(grad_scores, keys) * score_scale).astype(BF16)
    for head in range(GROUP):
        at = (group * GROUP + head) * HEAD_SIZE
        grad_queries_ref[:, at : at + HEAD_SIZE] = grad_queries[head * rows : (head + 1) * rows]
    partial_keyvals[:, :, key_columns] = (
        (dot(grad_scores, queries, 0, 0) * score_scale).astype(BF16).reshape(8, rows, HEAD_SIZE)
    )
    partial_keyvals[:, :, value_columns] = (
        dot(weights.astype(BF16), heads_gradient, 0, 0).astype(BF16).reshape(8, rows, HEAD_SIZE)
    )


EARLY_ROWS = 20


def rear_kernel(tail, *refs):
    (
        slots_ref,
        owner_ref,
        gates_ref,
        cotangent_ref,
        residual_ref,
        partial_ref,
        misc_ref,
        qkv_ref,
        marks_ref,
        segments_ref,
        attended_ref,
        normed1_ref,
        normed2_ref,
        tokens_ref,
        grad_back_hbm,
        outt_hbm,
        every_hbm,
        own_in_hbm,
        own_down_hbm,
        query_hbm,
        keyval_hbm,
        in_ref,
        down_ref,
        rows_ref,
    ) = refs[:24]
    (
        grad_tokens_ref,
        grad_outt_hbm,
        grad_query_hbm,
        grad_keyval_hbm,
        grad_misc_hbm,
        half_in_hbm,
        half_down_hbm,
        rows_out,
    ) = refs[24:32]
    (
        grad_back_ref,
        outt_ref,
        every_ref,
        own_in_ref,
        own_down_ref,
        grad_outt_ref,
        grad_query_ref,
        grad_keyval_ref,
        grad_misc_ref,
        grad_residual,
        grad_low,
        grad_logits,
        grad_gain,
        grad_attended,
        grad_queries,
        grad_first,
        blocks_ref,
        landed,
        query_ref,
        keyval_ref,
        their_in,
        their_down,
        sequence_send,
        sequence_recv,
        send_sems,
        recv_sems,
        local_sems,
    ) = refs[32:]
    me = col_index()
    spot = place()
    chips = [chip_at(spot, offset) for offset in OFFSETS]
    mine = chip_at(spot, (0, 0, 0))[1]
    rows, features = tokens_ref.shape
    late = pl.ds(rows - tail, tail)
    sibling = {"core": 1 - spot["core"]}
    greet([where for where, _ in chips] + [sibling])
    wires = Wires(send_sems, recv_sems, local_sems)
    fetched = [
        wires.copy(grad_back_hbm, grad_back_ref),
        wires.copy(outt_hbm, outt_ref),
        wires.copy(every_hbm, every_ref),
        wires.copy(query_hbm, query_ref),
        wires.copy(keyval_hbm, keyval_ref),
        wires.copy(own_in_hbm, own_in_ref),
        wires.copy(own_down_hbm, own_down_ref),
    ]
    halves_in = [
        wires.remote(in_ref, their_in, sibling),
        wires.remote(down_ref, their_down, sibling),
    ]
    kept = wires.copy(rows_ref.at[mine], rows_out.at[mine])
    returning = []

    def send_rows(start, stop):
        for where, holder in chips[start:stop]:
            returning.append(wires.remote(rows_ref.at[holder], rows_out.at[mine], where))

    send_rows(0, EARLY_ROWS)
    for fetch in fetched[:3]:
        fetch.wait()
    back_to_residual(
        grad_back_ref,
        slots_ref,
        owner_ref,
        gates_ref,
        cotangent_ref,
        residual_ref,
        partial_ref,
        misc_ref,
        outt_ref,
        grad_residual,
        grad_low,
        grad_logits,
        grad_gain,
        grad_attended,
    )
    allowed = allowed_pairs(marks_ref, segments_ref, rows, 8 * rows)
    allowed = jnp.concatenate([allowed.astype(F32)] * GROUP, axis=0) > 0.5
    for group in range(KEY_VALUE_HEADS):
        back_heads(
            group, allowed, qkv_ref, every_ref, grad_attended, grad_queries, blocks_ref
        )

    def copy(far, first_block):
        block = rem(me + 8 - far, 8)
        source, target = blocks_ref.at[block], landed.at[far]
        if first_block:
            source, target = blocks_ref.at[0, late], landed.at[far, late]
        return pltpu.make_async_remote_copy(
            src_ref=source,
            dst_ref=target,
            send_sem=sequence_send.at[far],
            recv_sem=sequence_recv.at[far],
            device_id=col_device(block),
            device_id_type=MESH_ID,
        )

    def each(far, first_block, condition, act):
        @pl.when(condition)
        def _():
            act(copy(far, first_block))

    for far in range(7, 0, -1):
        each(far, False, me > far, lambda moved: moved.start())
        each(far, True, me == far, lambda moved: moved.start())
    send_rows(EARLY_ROWS, 63)

    @pl.when(me == 0)
    def _():
        for far in range(1, 8):
            landed[far, : rows - tail] = jnp.zeros((rows - tail, landed.shape[2]), landed.dtype)

    for far in range(1, 8):

        @pl.when(me + far >= 8)
        def _():
            landed[far] = jnp.zeros(landed.shape[1:], landed.dtype)

    low, attended, queries = grad_low[...], attended_ref[...], grad_queries[...]
    for left in range(0, features, 512):
        columns = pl.ds(left, 512)
        grad_outt_ref[columns] = dot(grad_low[:, columns], attended, 0, 0).astype(BF16)
        grad_query_ref[columns] = dot(normed1_ref[:, columns], queries, 0, 0).astype(BF16)
    stored = [
        wires.copy(grad_outt_ref, grad_outt_hbm),
        wires.copy(grad_query_ref, grad_query_hbm),
    ]
    for fetch in fetched[3:]:
        fetch.wait()
    for left in range(0, features, 512):
        columns = pl.ds(left, 512)
        grad_first[:, columns] = dot(queries, query_ref[columns], 1, 1)
    for copy_in in halves_in:
        copy_in.wait_recv()
    for left in range(0, features, 512):
        columns = pl.ds(left, 512)
        their_in[columns] = (own_in_ref[columns] + their_in[columns].astype(F32)).astype(BF16)
        their_down[:, columns] = (
            own_down_ref[:, columns] + their_down[:, columns].astype(F32)
        ).astype(BF16)
    stored += [wires.copy(their_in, half_in_hbm), wires.copy(their_down, half_down_hbm)]
    for far in range(1, 8):
        each(far, False, (me > 0) & (me + far < 8), lambda moved: moved.wait_recv())
        each(far, True, me == 0, lambda moved: moved.wait_recv())
    grad_keyvals = grad_low.at[:, pl.ds(0, keyval_ref.shape[1])]
    for row in range(0, rows, 16):
        at = pl.ds(row, 16)
        value = blocks_ref[me, at].astype(F32)
        for far in range(1, 8):
            value = value + landed[far, at].astype(F32)
        grad_keyvals[at] = value.astype(BF16)
    keyvals = grad_keyvals[...]
    gain = gain_row(misc_ref[...], EXPERTS)
    square, inner = jnp.zeros((rows, 1), F32), jnp.zeros((rows, 1), F32)
    for left in range(0, features, 512):
        columns = pl.ds(left, 512)
        grad_keyval_ref[columns] = dot(normed1_ref[:, columns], keyvals, 0, 0).astype(BF16)
        piece = grad_first[:, columns] + dot(keyvals, keyval_ref[columns], 1, 1)
        grad_first[:, columns] = piece
        residual = tokens_ref[:, columns].astype(F32)
        square = square + jnp.sum(residual * residual, axis=1, keepdims=True)
        inner = inner + jnp.sum(
            piece * gain[:, left : left + 512] * residual, axis=1, keepdims=True
        )
    stored.append(wires.copy(grad_keyval_ref, grad_keyval_hbm))
    scale = lax.rsqrt(square / features + EPSILON)
    cubed = scale * scale * scale * (inner / features)
    logits = grad_logits[...]
    one_row = (lax.broadcasted_iota(jnp.int32, (16, 128), 0) == 0).astype(F32)
    lane = lax.broadcasted_iota(jnp.int32, (16, 128), 1)
    for left in range(0, features, 512):
        columns = pl.ds(left, 512)
        piece = grad_first[:, columns]
        residual = tokens_ref[:, columns].astype(F32)
        grad_tokens_ref[:, columns] = (
            grad_residual[:, columns]
            + scale * piece * gain[:, left : left + 512]
            - residual * cubed
        )
        total = dot(normed2_ref[:, columns], logits, 0, 0)
        rows1 = jnp.broadcast_to(
            jnp.sum(piece * residual * scale, axis=0, keepdims=True), (16, 512)
        )
        rows2 = jnp.broadcast_to(grad_gain[:1, columns], (16, 512))
        for index, gradient in ((EXPERTS, rows1), (EXPERTS + 1, rows2)):
            spread = (one_row * (lane == index).astype(F32)).astype(BF16)
            for part in rounded_parts(gradient):
                total = total + dot(part, spread, 0, 0)
        grad_misc_ref[columns] = total
    stored.append(wires.copy(grad_misc_ref, grad_misc_hbm))
    for far in range(1, 8):
        each(far, False, me > far, lambda moved: moved.wait_send())
        each(far, True, me == far, lambda moved: moved.wait_send())
    for copy_out in stored:
        copy_out.wait()
    kept.wait()
    for moved in returning:
        moved.wait_recv()
    wires.finish()


def rear(tail, inputs, grad_back, outt, every, own_in, own_down, query_w, keyval_w, expert_in,
         expert_down, rows_back):
    rows, features = inputs[3].shape
    anywhere = pl.BlockSpec(memory_space=pl.ANY)
    return pl.pallas_call(
        functools.partial(rear_kernel, tail),
        out_shape=[
            jax.ShapeDtypeStruct((rows, features), F32),
            jax.ShapeDtypeStruct((features, features), BF16),
            jax.ShapeDtypeStruct(query_w.shape, BF16),
            jax.ShapeDtypeStruct(keyval_w.shape, BF16),
            jax.ShapeDtypeStruct((features, 128), F32),
            jax.ShapeDtypeStruct(expert_in.shape, BF16),
            jax.ShapeDtypeStruct(expert_down.shape, BF16),
            jax.ShapeDtypeStruct(rows_back.shape, BF16),
        ],
        in_specs=[VMEM_SPEC] * 14 + [anywhere] * 10,
        out_specs=[VMEM_SPEC] + [anywhere] * 7,
        scratch_shapes=[
            pltpu.VMEM(grad_back.shape, BF16),
            pltpu.VMEM(outt.shape, BF16),
            pltpu.VMEM(every.shape, BF16),
            pltpu.VMEM(own_in.shape, F32),
            pltpu.VMEM(own_down.shape, F32),
            pltpu.VMEM((features, features), BF16),
            pltpu.VMEM(query_w.shape, BF16),
            pltpu.VMEM(keyval_w.shape, BF16),
            pltpu.VMEM((features, 128), F32),
            pltpu.VMEM((rows, features), F32),
            pltpu.VMEM((rows, features), BF16),
            pltpu.VMEM((rows, 128), BF16),
            pltpu.VMEM((8, features), F32),
            pltpu.VMEM((rows, features), BF16),
            pltpu.VMEM((rows, features), BF16),
            pltpu.VMEM((rows, features), F32),
            pltpu.VMEM(every.shape, BF16),
            pltpu.VMEM(every.shape, BF16),
            pltpu.VMEM(query_w.shape, BF16),
            pltpu.VMEM(keyval_w.shape, BF16),
            pltpu.VMEM(expert_in.shape, BF16),
            pltpu.VMEM(expert_down.shape, BF16),
            pltpu.SemaphoreType.DMA((8,)),
            pltpu.SemaphoreType.DMA((8,)),
            pltpu.SemaphoreType.DMA((66,)),
            pltpu.SemaphoreType.DMA((66,)),
            pltpu.SemaphoreType.DMA((16,)),
        ],
        compiler_params=pltpu.CompilerParams(
            collective_id=3, has_side_effects=True, vmem_limit_bytes=58 * 1024 * 1024
        ),
        cost_estimate=pl.CostEstimate(
            flops=10_000_000_000, bytes_accessed=150_000_000, transcendentals=2_000_000
        ),
    )(
        *inputs,
        grad_back,
        outt,
        every,
        own_in,
        own_down,
        query_w,
        keyval_w,
        expert_in,
        expert_down,
        rows_back,
    )


def contract(left_side, right_side, left_dim, right_dim):
    return lax.dot_general(
        left_side,
        right_side,
        (((left_dim,), (right_dim,)), ((), ())),
        preferred_element_type=F32,
    )


def expert_of(holder):
    return (holder // 8) * 8 + (holder % 2) * 4 + holder // 2 % 4


def packed(grad):
    return grad.reshape(4, 2, 2, 2, 48, grad.shape[-1])


def shards(
    tokens,
    segments,
    routes,
    norm1_gain,
    w_query,
    key_value_weight,
    w_output,
    norm2_gain,
    w_router,
    w_shgate,
    w_shup,
    w_shdown,
    w_exgate,
    w_exup,
    w_exdown,
    cotangent,
):
    local_rows, feature_count = tokens.shape
    sequence_length = local_rows * 8
    shard = jnp.concatenate(
        [
            w_output.T,
            w_router,
            norm1_gain[:, None],
            norm2_gain[:, None],
            jnp.zeros((12, 62), BF16),
            w_query,
            key_value_weight,
            w_shgate,
            w_shup,
            w_shdown.T,
        ],
        axis=1,
    )
    shard = jnp.concatenate([shard, jnp.zeros((4, TOTAL), BF16)], axis=0)
    tail = 32
    (
        outt_w,
        misc_w,
        query_w,
        keyval_w,
        shgate_w,
        shup_w,
        shdt_w,
        expert_w,
        expert_down,
        every,
        marks,
        first_normed,
        query_rows,
        sent_cotangent,
        named,
        slots,
        slots_down,
        owner,
        segment_tile,
    ) = front(
        shard, tokens, cotangent, routes, segments[None, :], w_exgate[0], w_exup[0], w_exdown[0]
    )
    outt_w, misc_w, query_w, keyval_w, shgate_w, shup_w, shdt_w = [
        gathered.reshape(feature_count, gathered.shape[-1])
        for gathered in (outt_w, misc_w, query_w, keyval_w, shgate_w, shup_w, shdt_w)
    ]
    slot_count = EXPERTS * CAP
    (
        attended_rows,
        residual1,
        second_normed,
        gates,
        gates_high,
        gates_low,
        forward_rows,
        grad_second,
        grad_received,
        outgoing,
        grad_shgate,
        grad_shup,
        grad_shdt,
    ) = middle(
        query_rows,
        every,
        marks,
        segment_tile,
        tokens,
        misc_w,
        named,
        slots,
        slots_down,
        owner,
        cotangent,
        sent_cotangent,
        outt_w,
        shgate_w,
        shup_w,
        shdt_w,
    )
    grad_back, half_out, own_in, other_in, own_down, other_down = expert(
        outgoing, grad_received, expert_w, expert_down
    )
    grad_back = grad_back.reshape(slot_count, feature_count + EXTRA)
    (
        grad_tokens,
        grad_outt,
        grad_query,
        grad_keyval,
        grad_misc,
        half_in,
        half_down,
        returned,
    ) = rear(
        tail,
        (
            slots,
            owner,
            gates,
            cotangent,
            residual1,
            grad_second,
            misc_w,
            query_rows,
            marks,
            segment_tile,
            attended_rows,
            first_normed,
            second_normed,
            tokens,
        ),
        grad_back,
        outt_w,
        every,
        own_in,
        own_down,
        query_w,
        keyval_w,
        other_in,
        other_down,
        half_out,
    )
    *summed, half_in, half_down, block_out = sum_last(
        [
            packed(grad)
            for grad in (
                grad_outt,
                grad_misc,
                grad_query,
                grad_keyval,
                grad_shgate,
                grad_shup,
                grad_shdt,
            )
        ],
        [half_in, half_down],
        returned,
        gates_high,
        gates_low,
        forward_rows,
    )
    sum_outt, sum_misc, sum_query, sum_keyval, sum_shgate, sum_shup, sum_shdt = [
        piece[:12] for piece in summed
    ]
    return (
        block_out,
        grad_tokens,
        sum_misc[:, EXPERTS],
        sum_query,
        sum_keyval,
        sum_outt.T,
        sum_misc[:, EXPERTS + 1],
        sum_misc[:, :EXPERTS],
        sum_shgate,
        sum_shup,
        sum_shdt.T,
        half_in[None, :, :HALF].astype(F32),
        half_in[None, :, HALF:].astype(F32),
        half_down[None].astype(F32),
    )


def solution(mesh):
    fine = Mesh(mesh.devices.reshape(SIZES), AXES)
    rows = P(AXES, None)
    columns = P(None, AXES)
    flat = P(AXES)
    blocks = P(AXES, None, None)
    in_specs = (
        rows,
        flat,
        rows,
        flat,
        rows,
        rows,
        columns,
        flat,
        rows,
        rows,
        rows,
        columns,
        blocks,
        blocks,
        blocks,
        rows,
    )
    out_specs = (
        rows,
        rows,
        flat,
        rows,
        rows,
        columns,
        flat,
        rows,
        rows,
        rows,
        columns,
        blocks,
        blocks,
        blocks,
    )
    return jax.shard_map(shards, mesh=fine, in_specs=in_specs, out_specs=out_specs, check_vma=False)
```

```python
import functools

import jax
import jax.numpy as jnp
from jax import lax
from jax.experimental import pallas as pl
from jax.experimental.pallas import tpu as pltpu
from jax.sharding import Mesh
from jax.sharding import PartitionSpec as P

QUERY_HEADS = 12
KEY_VALUE_HEADS = 4
HEAD_SIZE = 128
EXPERTS = 64
TOPK = 6
CAP = 24
EPSILON = 1e-05

F32 = jnp.float32
BF16 = jnp.bfloat16
MESH_ID = pl.DeviceIdType.MESH
AXES = ("z", "yl", "core", "yh", "xh", "xl")
SIZES = (4, 2, 2, 2, 2, 2)

PARTS = (
    ("outt", 1536, "yzx", "yzx"),
    ("misc", 128, "yz", "yz"),
    ("q", 1536, "yz", "yz"),
    ("kv", 1024, "zy", "zy"),
    ("shg", 1024, "yz", "yz"),
    ("shu", 1024, "zy", "zy"),
    ("shdt", 1024, "zy", "zy"),
)
GATHERED = tuple((name, width, order) for name, width, order, _ in PARTS)
SUMMED = tuple((name, width, order) for name, width, _, order in PARTS)
TOTAL = sum(part[1] for part in PARTS)
HALF = 256
EXPERT_SEM = 200
TOTAL = sum(part[1] for part in PARTS)


def rem(value, size):
    return lax.rem(value, jnp.int32(size))


def place():
    at = {name: lax.axis_index(name) for name in AXES}
    return {
        "x": at["xh"] * 2 + at["xl"],
        "y": at["yh"] * 2 + at["yl"],
        "z": at["z"],
        "core": at["core"],
    }


def device(axis, value):
    if axis == "x":
        return {"xh": value // 2, "xl": rem(value, 2)}
    if axis == "y":
        return {"yh": value // 2, "yl": rem(value, 2)}
    return {axis: value}


def greet(targets):
    barrier = pltpu.get_barrier_semaphore()
    for target in targets:
        pl.semaphore_signal(barrier, inc=1, device_id=target, device_id_type=MESH_ID)
    pl.semaphore_wait(barrier, len(targets))


def ring_neighbours(me):
    near = [device("x", rem(me["x"] + hops, 4)) for hops in (1, 2, 3)]
    near += [device("y", rem(me["y"] + hops, 4)) for hops in (1, 3)]
    near += [device("z", rem(me["z"] + hops, 4)) for hops in (1, 3)]
    return near + [{"core": 1 - me["core"]}]


class Wires:
    def __init__(self, send_sems, recv_sems, local_sems):
        self.send, self.recv, self.local = send_sems, recv_sems, local_sems
        self.used, self.used_local, self.started, self.kept = 0, 0, [], []

    def remote(self, source, target, where):
        copy = pltpu.make_async_remote_copy(
            src_ref=source,
            dst_ref=target,
            send_sem=self.send.at[self.used],
            recv_sem=self.recv.at[self.used],
            device_id=where,
            device_id_type=MESH_ID,
        )
        self.used += 1
        copy.start()
        self.started.append(copy)
        return copy

    def copy(self, source, target):
        copy = pltpu.make_async_copy(source, target, self.local.at[self.used_local])
        self.used_local += 1
        copy.start()
        return copy

    def finish(self):
        for copy in self.started:
            copy.wait_send()


def balanced_offsets():
    left = [(x, y, z) for x in range(4) for y in range(4) for z in range(4) if x + y + z > 0]
    load, order = [0] * 6, []

    def uses(offset):
        used = [0] * 6
        for axis, hops in enumerate(offset):
            used[2 * axis] += hops in (1, 2)
            used[2 * axis + 1] += hops in (2, 3)
        return used

    def cost(offset):
        used = uses(offset)
        after = [a + b for a, b in zip(load, used)]
        mean = sum(after) / 6
        return (max(after), sum((a - mean) ** 2 for a in after), -sum(used))

    while left:
        best = min(left, key=cost)
        load = [a + b for a, b in zip(load, uses(best))]
        left.remove(best)
        order.append(best)
    return order


OFFSETS = balanced_offsets()


def chip_at(me, offset, sign=1):
    x, y, z = [rem(me[axis] + (sign * hops) % 4, 4) for axis, hops in zip("xyz", offset)]
    where = {"z": z, "yh": y // 2, "yl": rem(y, 2), "xh": x // 2, "xl": rem(x, 2)}
    return where, z * 16 + rem(y, 2) * 8 + (y // 2) * 4 + x


def halves(width):
    first = width // 256 * 128 if width > 128 else width
    return first, width - first


def spread_rows(shape, swap):
    dense = lax.broadcasted_iota(jnp.int32, shape, 1 if swap else 0)
    padded = lax.broadcasted_iota(jnp.int32, shape, 0 if swap else 1)
    shift = jnp.zeros(shape, jnp.int32)
    for edge in (12, 24, 36):
        shift = shift + jnp.where(dense >= edge, 4, 0)
    return dense + shift == padded


def block_ref(ref, axes, me, axis, value, columns):
    spot = dict(me)
    spot[axis] = value
    z = slice(None) if "z" in axes else spot["z"]
    yl = slice(None) if "y" in axes else rem(spot["y"], 2)
    yh = slice(None) if "y" in axes else spot["y"] // 2
    return ref.at[z, yl, me["core"], yh, :, columns]


class Summing:
    def __init__(self, wires, me, parts, grads, outs, scratch):
        self.wires, self.me = wires, me
        self.next = {axis: rem(me[axis] + 1, 4) for axis in "xyz"}
        self.opposite = {axis: rem(me[axis] + 2, 4) for axis in "xyz"}
        self.previous = {axis: rem(me[axis] + 3, 4) for axis in "xyz"}
        self.sibling = {"core": 1 - me["core"]}
        count = len(parts)
        self.runs = []
        for index, (name, width, order) in enumerate(parts):
            self.runs.append(
                {
                    "order": order[::-1],
                    "width": width // 4 if len(order) == 3 else width,
                    "left": "zy",
                    "turn": 0,
                    "grads": grads[index],
                    "out": outs[index],
                    "own": scratch[index],
                    "theirs": scratch[count + index],
                    "near1": scratch[2 * count + index],
                    "near2": scratch[3 * count + index],
                    "ends": scratch[4 * count + index],
                    "arrived": scratch[5 * count + index],
                }
            )

    def spot(self, left_axes, axis, value, with_core):
        at = dict(self.me)
        if axis is not None:
            at[axis] = value
        whole = [name for name in left_axes if name != axis]
        z = slice(None) if "z" in whole else at["z"]
        yl = slice(None) if "y" in whole else rem(at["y"], 2)
        yh = slice(None) if "y" in whole else at["y"] // 2
        return (z, yl) + (() if with_core is None else (with_core,)) + (yh,)

    def lead(self, left_axes, axis):
        dims = []
        for name in ("z", "y"):
            if name in left_axes and name != axis:
                dims += [4] if name == "z" else [2, 2]
        return dims

    def add_into(self, target, sources, dims):
        total = 1
        for size in dims:
            total *= size

        def body(index):
            for row in range(0, 48, 16):
                at = index + (pl.ds(row, 16),)
                value = target[at].astype(F32)
                for source in sources:
                    value = value + source[at].astype(F32)
                target[at] = value.astype(target.dtype)

        def step(flat, carry):
            index, rest_flat = [], flat
            for size in reversed(dims):
                index.append(rem(rest_flat, size))
                rest_flat = rest_flat // size
            body(tuple(reversed(index)))
            return carry

        if total == 1:
            body(())
        else:
            lax.fori_loop(0, total, step, 0)

    def columns_of(self, run, axis, value, which):
        base = 0
        if len(run["order"]) == 3:
            base = (value if axis == "x" else self.me["x"]) * run["width"]
        left, size = 0, run["width"]
        if which is not None:
            first_half, second_half = halves(run["width"])
            left, size = (0, first_half) if which == 0 else (first_half, second_half)
        if isinstance(base, int):
            return pl.ds(base + left, size)
        return pl.ds(pl.multiple_of(base + left, 128), size)

    def chunk(self, run, axis, value, which=None, ref=None, with_core=None):
        ref = run["own"] if ref is None else ref
        columns = self.columns_of(run, axis, value, which)
        return ref.at[self.spot(run["left"], axis, value, with_core) + (slice(None), columns)]

    def pair(self, run, axis, value):
        core = self.me["core"]
        give = self.wires.remote(
            self.chunk(run, axis, value, None, run["grads"], 1 - core),
            self.chunk(run, axis, value, None, run["theirs"]),
            self.sibling,
        )
        keep = self.wires.copy(
            self.chunk(run, axis, value, None, run["grads"], core), self.chunk(run, axis, value)
        )
        return give, keep

    def join(self, run, axis, value, copies):
        copies[0].wait_recv()
        copies[1].wait()
        self.add_into(
            self.chunk(run, axis, value),
            [self.chunk(run, axis, value, None, run["theirs"])],
            self.lead(run["left"], axis),
        )

    def slots(self, run, axis):
        dims = self.lead(run["left"], axis)
        ref = (run["near1"], run["near2"], run["ends"])[run["turn"]]
        if not dims:
            ref = ref.at[:, pl.ds(0, 48)]
        return ref.at[0], ref.at[1], ref.at[2], dims

    def part(self, ref, run, which, dims):
        first_half, second_half = halves(run["width"])
        columns = pl.ds(0, first_half) if which == 0 else pl.ds(first_half, second_half)
        return ref.at[(slice(None),) * len(dims) + (slice(None), columns)]

    def ring_open(self, run):
        axis = run["order"][run["turn"]]
        _, _, passing, dims = self.slots(run, axis)
        far = self.opposite[axis]
        run["passing"] = [
            self.wires.remote(
                self.chunk(run, axis, far, 0),
                self.part(passing, run, 0, dims),
                device(axis, self.next[axis]),
            )
        ]
        if halves(run["width"])[1]:
            run["passing"].append(
                self.wires.remote(
                    self.chunk(run, axis, far, 1),
                    self.part(passing, run, 1, dims),
                    device(axis, self.previous[axis]),
                )
            )

    def ring_near(self, run):
        axis = run["order"][run["turn"]]
        from_prv, from_nxt, _, dims = self.slots(run, axis)
        nxt, prv = self.next[axis], self.previous[axis]
        run["near"] = []
        if halves(run["width"])[1]:
            run["near"].append(
                self.wires.remote(
                    self.chunk(run, axis, nxt, 1),
                    self.part(from_prv, run, 1, dims),
                    device(axis, nxt),
                )
            )
        run["near"].append(
            self.wires.remote(
                self.chunk(run, axis, prv, 0), self.part(from_nxt, run, 0, dims), device(axis, prv)
            )
        )

    def ring_pass(self, run):
        axis = run["order"][run["turn"]]
        from_prv, from_nxt, passing, dims = self.slots(run, axis)
        nxt, prv = self.next[axis], self.previous[axis]
        run["passing"][0].wait_recv()
        self.add_into(self.chunk(run, axis, nxt, 0), [self.part(passing, run, 0, dims)], dims)
        run["near"].append(
            self.wires.remote(
                self.chunk(run, axis, nxt, 0), self.part(from_prv, run, 0, dims), device(axis, nxt)
            )
        )
        if halves(run["width"])[1]:
            run["passing"][1].wait_recv()
            self.add_into(self.chunk(run, axis, prv, 1), [self.part(passing, run, 1, dims)], dims)
            run["near"].append(
                self.wires.remote(
                    self.chunk(run, axis, prv, 1),
                    self.part(from_nxt, run, 1, dims),
                    device(axis, prv),
                )
            )

    def ring_close(self, run):
        axis = run["order"][run["turn"]]
        from_prv, from_nxt, _, dims = self.slots(run, axis)
        for copy in run["near"]:
            copy.wait_recv()
        self.add_into(self.chunk(run, axis, self.me[axis]), [from_prv, from_nxt], dims)
        run["left"] = run["left"].replace(axis, "")
        run["turn"] += 1

    def turn(self, run):
        self.ring_close(run)
        self.ring_open(run)
        self.ring_near(run)

    def spread(self, run):
        me, width = self.me, run["width"]
        third = len(run["order"]) == 3
        summed = run["own"].at[me["z"], rem(me["y"], 2), me["y"] // 2]
        exact = lax.Precision.HIGHEST if summed.dtype == F32 else None
        pick = spread_rows((64, 48), True).astype(summed.dtype)
        staging = run["ends"].at[3] if third else run["near2"].at[3]
        base = me["x"] * width if third else 0
        for left in range(0, width, 512):
            size = min(512, width - left)
            columns = pl.ds(left, size)
            if third:
                columns = pl.ds(pl.multiple_of(base + left, 128), size)
            staging[:, left : left + size] = jnp.dot(
                pick, summed[:, columns], preferred_element_type=F32, precision=exact
            ).astype(staging.dtype)
        if third:
            lands = run["arrived"].at[:, pl.ds(pl.multiple_of(base, 128), width)]
        else:
            lands = run["arrived"].at[me["x"]]
        run["copies"] = []
        for where in (self.next, self.opposite, self.previous):
            row = pl.ds(pl.multiple_of(where["x"] * 16, 16), 16)
            run["copies"].append(
                self.wires.remote(staging.at[row], lands, device("x", where["x"]))
            )
        row = pl.ds(pl.multiple_of(me["x"] * 16, 16), 16)
        run["keep"] = self.wires.copy(staging.at[row], lands)

    def deliver(self, run):
        run["keep"].wait()
        for copy in run["copies"]:
            copy.wait_recv()
        if len(run["order"]) == 3:
            run["out"][...] = run["arrived"][...].astype(F32)
        else:
            value = run["arrived"][0].astype(F32)
            for place_x in range(1, 4):
                value = value + run["arrived"][place_x].astype(F32)
            run["out"][...] = value

    def stages(self):
        runs = self.runs
        threes = [run for run in runs if len(run["order"]) == 3]
        twos = [run for run in runs if len(run["order"]) == 2]
        begun = []
        for where in (self.opposite, self.next, self.previous, self.me):
            begun.append([self.pair(run, run["order"][0], where[run["order"][0]]) for run in runs])
        yield
        for run, copies in zip(runs, begun[0]):
            axis = run["order"][0]
            self.join(run, axis, self.opposite[axis], copies)
            self.ring_open(run)
        for run, nexts, prevs in zip(runs, begun[1], begun[2]):
            axis = run["order"][0]
            self.join(run, axis, self.next[axis], nexts)
            self.join(run, axis, self.previous[axis], prevs)
            self.ring_near(run)
        yield
        for run in threes:
            self.ring_pass(run)
        for run, copies in zip(runs, begun[3]):
            axis = run["order"][0]
            self.join(run, axis, self.me[axis], copies)
        for run in twos:
            self.ring_pass(run)
        yield
        for run in threes:
            self.turn(run)
        for run in threes:
            self.ring_pass(run)
        for run in twos:
            self.turn(run)
        yield
        for run in threes:
            self.turn(run)
        for run in twos:
            self.ring_pass(run)
        for run in threes:
            self.ring_pass(run)
        yield
        for run in twos:
            self.ring_close(run)
            self.spread(run)
        for run in threes:
            self.ring_close(run)
            self.spread(run)
        yield
        for run in runs:
            self.deliver(run)
        yield


def summing_scratch(parts):
    own, theirs, near1, near2, ends, arrived = [], [], [], [], [], []
    for name, width, order in parts:
        kind = F32 if name == "misc" else BF16
        own.append(pltpu.VMEM((4, 2, 2, 48, width), kind))
        theirs.append(pltpu.VMEM((4, 2, 2, 48, width), kind))
        if len(order) == 3:
            quarter = width // 4
            near1.append(pltpu.VMEM((3, 4, 2, 2, 48, quarter), kind))
            near2.append(pltpu.VMEM((3, 2, 2, 48, quarter), kind))
            ends.append(pltpu.VMEM((4, 64, quarter), kind))
            arrived.append(pltpu.VMEM((16, width), kind))
        else:
            near1.append(pltpu.VMEM((3, 2, 2, 48, width) if order == "yz" else (3, 4, 48, width), kind))
            near2.append(pltpu.VMEM((4, 64, width), kind))
            ends.append(pltpu.VMEM((16, 128), kind))
            arrived.append(pltpu.VMEM((4, 16, width), kind))
    return own + theirs + near1 + near2 + ends + arrived


def last_kernel(*refs):
    count = len(SUMMED)
    grads = refs[:count]
    expert_from = refs[count : count + 2]
    rows_hbm, gates_high_ref, gates_low_ref, forward_ref = refs[count + 2 : count + 6]
    outs = refs[count + 6 : 2 * count + 6]
    expert_to = refs[2 * count + 6 : 2 * count + 8]
    block_ref = refs[2 * count + 8]
    scratch = refs[2 * count + 9 : 8 * count + 9]
    (
        rows_ref,
        swap_send,
        swap_recv,
        swap_local,
        send_sems,
        recv_sems,
        local_sems,
    ) = refs[8 * count + 9 :]
    me = place()
    partner = {"core": 1 - me["core"], "xl": 1 - lax.axis_index("xl")}
    crossed = me["core"] != lax.axis_index("xl")
    greet(ring_neighbours(me) + [partner])

    def moved(slot):
        return pltpu.make_async_remote_copy(
            src_ref=expert_from[slot],
            dst_ref=expert_to[slot],
            send_sem=swap_send.at[slot],
            recv_sem=swap_recv.at[slot],
            device_id=partner,
            device_id_type=MESH_ID,
        )

    def kept(slot):
        return pltpu.make_async_copy(expert_from[slot], expert_to[slot], swap_local.at[slot])

    wires = Wires(send_sems, recv_sems, local_sems)
    stages = Summing(wires, me, SUMMED, grads, outs, scratch).stages()
    next(stages)
    next(stages)

    @pl.when(crossed)
    def _():
        for slot in range(2):
            moved(slot).start()

    @pl.when(jnp.logical_not(crossed))
    def _():
        for slot in range(2):
            kept(slot).start()

    rows_in = wires.copy(rows_hbm, rows_ref)
    next(stages)
    next(stages)
    rows_in.wait()
    features = block_ref.shape[1]
    for left in range(0, features, 512):
        columns = pl.ds(left, 512)

        def mix(step, total):
            blocks = rows_ref[pl.ds(step * 16, 16), :, columns].astype(F32)
            rows = blocks.reshape(16 * CAP, 512).astype(BF16)
            at = pl.ds(pl.multiple_of(step * 16 * CAP, 128), 16 * CAP)
            return total + dot(gates_high_ref[:, at], rows) + dot(gates_low_ref[:, at], rows)

        mixed = lax.fori_loop(0, EXPERTS // 16, mix, forward_ref[:, columns])
        block_ref[:, columns] = mixed.astype(BF16)
    for _ in stages:
        pass
    wires.finish()

    @pl.when(crossed)
    def _():
        for slot in range(2):
            moved(slot).wait_recv()
            moved(slot).wait_send()

    @pl.when(jnp.logical_not(crossed))
    def _():
        for slot in range(2):
            kept(slot).wait()


def sum_last(grads, expert_grads, rows, gates_high, gates_low, forward_rows):
    anywhere = pl.BlockSpec(memory_space=pl.ANY)
    vmem = pl.BlockSpec(memory_space=pltpu.VMEM)
    count = len(SUMMED)
    return pl.pallas_call(
        last_kernel,
        out_shape=[jax.ShapeDtypeStruct((16, width), F32) for _, width, _ in SUMMED]
        + [jax.ShapeDtypeStruct(grad.shape, grad.dtype) for grad in expert_grads]
        + [jax.ShapeDtypeStruct(forward_rows.shape, BF16)],
        in_specs=[anywhere] * (count + 3) + [vmem] * 3,
        out_specs=[vmem] * count + [anywhere] * 2 + [vmem],
        scratch_shapes=summing_scratch(SUMMED)
        + [
            pltpu.VMEM(rows.shape, BF16),
            pltpu.SemaphoreType.DMA((2,)),
            pltpu.SemaphoreType.DMA((2,)),
            pltpu.SemaphoreType.DMA((2,)),
            pltpu.SemaphoreType.DMA((190,)),
            pltpu.SemaphoreType.DMA((190,)),
            pltpu.SemaphoreType.DMA((48,)),
        ],
        compiler_params=pltpu.CompilerParams(
            collective_id=1, has_side_effects=True, vmem_limit_bytes=56 * 1024 * 1024
        ),
        cost_estimate=pl.CostEstimate(
            flops=1_000_000_000, bytes_accessed=200_000_000, transcendentals=0
        ),
    )(*grads, *expert_grads, rows, gates_high, gates_low, forward_rows)


def col_device(col):
    return {"yh": col // 4, "xh": rem(col // 2, 2), "xl": rem(col, 2)}


def col_index():
    return lax.axis_index("yh") * 4 + lax.axis_index("xh") * 2 + lax.axis_index("xl")


VMEM_SPEC = pl.BlockSpec(memory_space=pltpu.VMEM)
GROUP = QUERY_HEADS // KEY_VALUE_HEADS
EXTRA = 128


def dot(left, right, left_dim=1, right_dim=0):
    return lax.dot_general(
        left, right, (((left_dim,), (right_dim,)), ((), ())), preferred_element_type=F32
    )


def rounded_parts(value):
    first = value.astype(BF16)
    left = value - first.astype(F32)
    second = left.astype(BF16)
    return [first, second, (left - second.astype(F32)).astype(BF16)]


def lane_column(index):
    return (lax.broadcasted_iota(jnp.int32, (16, 128), 1) == index).astype(BF16)


def gain_row(misc, index):
    return dot(lane_column(index), misc, 1, 1)[:1]


def allowed_pairs(marks_ref, segments_ref, rows, keys):
    me = col_index()
    shape = (rows, keys)
    own = segments_ref[:, :1]
    first_length = jnp.where(
        me == 0,
        jnp.sum((own == 0.0).astype(F32), axis=0, keepdims=True),
        marks_ref[:1, :1].astype(F32),
    )
    last_start = (me * rows).astype(F32) + jnp.sum(
        (own < 2.0).astype(F32), axis=0, keepdims=True
    )
    lowest = jnp.where(own == 0.0, 0.0, jnp.where(own == 1.0, first_length, last_start))
    key = lax.broadcasted_iota(jnp.int32, shape, 1)
    query = lax.broadcasted_iota(jnp.int32, shape, 0) + me * rows
    return (key <= query) & (key.astype(F32) >= lowest)


def head_columns(ref, group):
    width = GROUP * HEAD_SIZE
    return jnp.concatenate(
        [
            ref[:, group * width + head * HEAD_SIZE : group * width + (head + 1) * HEAD_SIZE]
            for head in range(GROUP)
        ],
        axis=0,
    )


def head_weights(queries, keys, allowed):
    scores = dot(queries, keys, 1, 1) * (HEAD_SIZE ** (-0.5))
    scores = jnp.where(allowed, scores, -1e30)
    shifted = jnp.exp(scores - jnp.max(scores, axis=1, keepdims=True))
    return shifted / jnp.sum(shifted, axis=1, keepdims=True)


GROUP_BLOCKS = 16
MIDDLE_MIB = 52


def blocks_of(value):
    return value.reshape(GROUP_BLOCKS, CAP, value.shape[-1]).astype(BF16)


def front_kernel(
    shard_ref, tokens_ref, cotangent_ref, routes_ref, segments_ref, gate_ref, up_ref, down_ref, *rest
):
    count = len(GATHERED)
    results = rest[:count]
    (
        expert_in,
        expert_out,
        every_ref,
        marks_out,
        normed_ref,
        queries_ref,
        rows_out,
        named_ref,
        slots_ref,
        slots_down_ref,
        owner_ref,
        tile_ref,
    ) = rest[count : count + 12]
    rest = rest[count + 12 :]
    outs = rest[:count]
    landed = rest[count]
    stages = rest[count + 1 : 2 * count + 1]
    (
        marks_ref,
        rows_ref,
        own_ref,
        sequence_send,
        sequence_recv,
        send_sems,
        recv_sems,
        local_sems,
    ) = rest[2 * count + 1 :]
    me = place()
    col = col_index()
    rows, features = tokens_ref.shape
    tail = marks_ref.shape[0]
    late = pl.ds(rows - tail, tail)
    nxt = {axis: rem(me[axis] + 1, 4) for axis in "xyz"}
    opp = {axis: rem(me[axis] + 2, 4) for axis in "xyz"}
    prv = {axis: rem(me[axis] + 3, 4) for axis in "xyz"}
    sibling = {"core": 1 - me["core"]}
    partner = {"core": 1 - me["core"], "xl": 1 - lax.axis_index("xl")}
    crossed = me["core"] != lax.axis_index("xl")
    greet(
        [device("x", nxt["x"]), device("x", opp["x"]), device("x", prv["x"])]
        + [device("y", nxt["y"]), device("y", prv["y"])]
        + [device("z", nxt["z"]), device("z", prv["z"]), sibling, partner]
        + [col_device(rem(col + far, 8)) for far in range(1, 8)]
    )
    wires = Wires(send_sems, recv_sems, local_sems)
    runs, start = [], 0
    for index, (name, width, order) in enumerate(GATHERED):
        last_x = len(order) == 3
        quarter = width // 4 if last_x else width
        run = {
            "name": name,
            "out": outs[index],
            "result": results[index],
            "order": order,
            "width": quarter,
            "done": "",
            "stage": stages[index],
            "start": start,
            "landed": landed.at[:, :, pl.ds(start, quarter)],
            "base": me["x"] * quarter if last_x else 0,
            "first": [],
            "shared": [],
        }

        def piece(x):
            if last_x:
                return shard_ref.at[:, pl.ds(pl.multiple_of(start + x * quarter, 128), quarter)]
            return shard_ref.at[:, pl.ds(start, quarter)]

        for where in (nxt, prv, opp):
            run["first"].append(
                wires.remote(piece(where["x"]), run["landed"].at[me["x"]], device("x", where["x"]))
            )
        run["bring"] = wires.copy(piece(me["x"]), run["landed"].at[me["x"]])
        runs.append(run)
        start += width

    whole = [
        (gate_ref, expert_in.at[:, pl.ds(0, HALF)]),
        (up_ref, expert_in.at[:, pl.ds(HALF, HALF)]),
        (down_ref, expert_out.at[pl.ds(0, HALF)]),
    ]

    def moved(slot):
        source, target = whole[slot]
        return pltpu.make_async_remote_copy(
            src_ref=source,
            dst_ref=target,
            send_sem=send_sems.at[EXPERT_SEM + slot],
            recv_sem=recv_sems.at[EXPERT_SEM + slot],
            device_id=partner,
            device_id_type=MESH_ID,
        )

    def kept(slot):
        source, target = whole[slot]
        return pltpu.make_async_copy(source, target, local_sems.at[28 + slot])

    @pl.when(crossed)
    def _():
        for slot in range(3):
            moved(slot).start()

    @pl.when(jnp.logical_not(crossed))
    def _():
        for slot in range(3):
            kept(slot).start()

    def part_columns(run, axis, value, which):
        base = value * run["width"] if axis == "x" else run["base"]
        left, size = 0, run["width"]
        if which is not None:
            first_half, second_half = halves(run["width"])
            left, size = (0, first_half) if which == 0 else (first_half, second_half)
        if isinstance(base, int):
            return pl.ds(base + left, size)
        return pl.ds(pl.multiple_of(base + left, 128), size)

    def blocks(run, axis, value, which=None):
        columns = part_columns(run, axis, value, which)
        return block_ref(run["out"], run["done"], me, axis, value, columns)

    def begin(run, axis, source=None):
        target = blocks(run, axis, me[axis])
        source = target if source is None else source
        run["forth"] = wires.remote(source, target, device(axis, nxt[axis]))
        run["back"] = wires.remote(source, target, device(axis, prv[axis]))

    pick = spread_rows((48, 64), False).astype(BF16)
    for run in runs:
        run["bring"].wait()
        for copy in run["first"]:
            copy.wait_recv()
        for left in range(0, run["width"], 512):
            size = min(512, run["width"] - left)
            left_in = run["start"] + left
            piece_rows = landed[:, :, left_in : left_in + size].reshape(64, size)
            run["stage"][:, left : left + size] = jnp.dot(
                pick, piece_rows, preferred_element_type=F32
            ).astype(BF16)
        axis = run["order"][0]
        begin(run, axis, run["stage"])
        run["own"] = wires.copy(run["stage"], blocks(run, axis, me[axis]))

    def forward(run, axis):
        run["forth"].wait_recv()
        source = blocks(run, axis, prv[axis], 0)
        run["more"] = [wires.remote(source, source, device(axis, nxt[axis]))]
        run["back"].wait_recv()
        if halves(run["width"])[1] > 0:
            source = blocks(run, axis, nxt[axis], 1)
            run["more"].append(wires.remote(source, source, device(axis, prv[axis])))

    def share(run, axis, value):
        source = blocks(run, axis, value)
        run["shared"].append(wires.remote(source, source, sibling))

    def advance(run, step):
        axis = run["order"][step]
        for copy in run["more"]:
            copy.wait_recv()
        if step == len(run["order"]) - 1:
            share(run, axis, opp[axis])
            return
        if step == 0:
            run["own"].wait()
        run["done"] = run["done"] + axis
        following = run["order"][step + 1]
        begin(run, following)
        if step + 1 == len(run["order"]) - 1:
            share(run, following, me[following])

    def last_forward(run):
        axis = run["order"][-1]
        forward(run, axis)
        share(run, axis, prv[axis])
        share(run, axis, nxt[axis])

    lay_out_routes(routes_ref, named_ref, slots_ref, slots_down_ref, owner_ref)
    lay_out_segments(segments_ref, tile_ref, marks_ref)
    threes = [run for run in runs if len(run["order"]) == 3]
    twos = [run for run in runs if len(run["order"]) == 2]
    for run in runs:
        forward(run, run["order"][0])
    for run in runs:
        advance(run, 0)
    for run in threes:
        forward(run, run["order"][1])
    for run in threes:
        advance(run, 1)
    for run in twos:
        last_forward(run)
    for run in threes:
        last_forward(run)

    @pl.when(crossed)
    def _():
        for slot in range(3):
            moved(slot).wait_recv()

    @pl.when(jnp.logical_not(crossed))
    def _():
        for slot in range(3):
            kept(slot).wait()

    handed = [
        wires.remote(
            expert_in.at[:, pl.ds(0, 2 * HALF)], expert_in.at[:, pl.ds(2 * HALF, 2 * HALF)], sibling
        ),
        wires.remote(expert_out.at[pl.ds(0, HALF)], expert_out.at[pl.ds(HALF, HALF)], sibling),
    ]
    for run in twos + threes:
        advance(run, len(run["order"]) - 1)
    stored = []

    def complete(run):
        for copy in run["shared"]:
            copy.wait_recv()
        stored.append(wires.copy(run["out"], run["result"]))

    early = [run for run in runs if run["name"] in ("misc", "q", "kv")]
    for run in early:
        complete(run)
    weights = {run["name"]: run["out"] for run in early}

    def weight_columns(name, columns):
        value = weights[name][:, :, :, :, :, columns]
        return value.reshape(features, value.shape[-1])

    gain = gain_row(weight_columns("misc", pl.ds(0, 128)), EXPERTS)
    total = jnp.zeros((rows, 1), F32)
    for left in range(0, features, 512):
        piece = tokens_ref[:, left : left + 512].astype(F32)
        total = total + jnp.sum(piece * piece, axis=1, keepdims=True)
    scale = lax.rsqrt(total / features + EPSILON)
    for left in range(0, features, 512):
        piece = tokens_ref[:, left : left + 512].astype(F32)
        normed_ref[:, left : left + 512] = (piece * scale * gain[:, left : left + 512]).astype(BF16)
    normed = normed_ref[...]
    for left in range(0, own_ref.shape[1], 512):
        own_ref[:, left : left + 512] = dot(normed, weight_columns("kv", pl.ds(left, 512))).astype(
            BF16
        )

    def copies(far, first):
        there = col_device(rem(col + far, 8))
        pairs = [(own_ref, every_ref.at[col])]
        if first:
            pairs = [(own_ref.at[late], every_ref.at[0, late]), (marks_ref, marks_out)]
        return [
            pltpu.make_async_remote_copy(
                src_ref=source,
                dst_ref=target,
                send_sem=sequence_send.at[far, number],
                recv_sem=sequence_recv.at[far, number],
                device_id=there,
                device_id_type=MESH_ID,
            )
            for number, (source, target) in enumerate(pairs)
        ]

    def each(far, first, condition, act):
        @pl.when(condition)
        def _():
            for copy in copies(far, first):
                act(copy)

    for far in range(7, 0, -1):
        each(far, False, (col > 0) & (col + far < 8), lambda copy: copy.start())
        each(far, True, col == 0, lambda copy: copy.start())
    keep = wires.copy(own_ref, every_ref.at[col])

    @pl.when(col == 0)
    def _():
        marks_out[...] = marks_ref[...]

    @pl.when(col > 0)
    def _():
        every_ref[0, : rows - tail] = jnp.zeros((rows - tail, own_ref.shape[1]), own_ref.dtype)

    for far in range(1, 8):

        @pl.when(col + far < 8)
        def _():
            every_ref[col + far] = jnp.zeros(own_ref.shape, own_ref.dtype)

    for run in runs:
        if run["name"] not in weights:
            complete(run)
    for left in range(0, queries_ref.shape[1], 512):
        queries_ref[:, left : left + 512] = dot(
            normed, weight_columns("q", pl.ds(left, 512))
        ).astype(BF16)
    tile = GROUP_BLOCKS * CAP

    def fill(step, carry):
        slots = slots_down_ref[pl.ds(pl.multiple_of(step * tile, 128), tile)]
        blocks = pl.ds(step * GROUP_BLOCKS, GROUP_BLOCKS)
        for left in range(0, features, 512):
            rows_ref[blocks, :, left : left + 512] = blocks_of(
                dot(slots, cotangent_ref[:, left : left + 512])
            )
        return carry

    lax.fori_loop(0, EXPERTS // GROUP_BLOCKS, fill, 0)
    stored.append(wires.copy(rows_ref, rows_out))
    for copy in handed:
        copy.wait_recv()
    keep.wait()
    for far in range(1, 8):
        each(far, False, col > far, lambda copy: copy.wait_recv())
        each(far, True, col == far, lambda copy: copy.wait_recv())
        each(far, False, (col > 0) & (col + far < 8), lambda copy: copy.wait_send())
        each(far, True, col == 0, lambda copy: copy.wait_send())
    for copy in stored:
        copy.wait()
    wires.finish()

    @pl.when(crossed)
    def _():
        for slot in range(3):
            moved(slot).wait_send()


def lay_out_routes(routes_ref, named_ref, slots_ref, slots_down_ref, owner_ref):
    rows = routes_ref.shape[0]
    count = EXPERTS * CAP
    expert = lax.broadcasted_iota(jnp.int32, (rows, 128), 1)
    named = jnp.zeros((rows, 128), F32)
    for choice in range(TOPK):
        named = named + (routes_ref[:, choice : choice + 1] == expert).astype(F32)
    named_ref[...] = named
    ahead = lax.broadcasted_iota(jnp.int32, (rows, rows), 1) <= lax.broadcasted_iota(
        jnp.int32, (rows, rows), 0
    )
    rank = (dot(ahead.astype(F32).astype(BF16), named.astype(BF16)) * named).astype(BF16)

    def holder_of(slot):
        return ((slot.astype(F32) + 0.5) * (1.0 / CAP)).astype(jnp.int32)

    slot = lax.broadcasted_iota(jnp.int32, (count, 128), 0)
    holder = holder_of(slot)
    owned = (
        (holder & 56) + (holder & 1) * 4 + ((holder & 6) >> 1)
        == lax.broadcasted_iota(jnp.int32, (count, 128), 1)
    )
    owner = owned.astype(F32).astype(BF16)
    owner_ref[...] = owner
    turn = (slot - holder * CAP + 1).astype(F32)
    slots_down_ref[...] = (dot(owner, rank, 1, 1) == turn).astype(F32).astype(BF16)
    slot = lax.broadcasted_iota(jnp.int32, (rows, count), 1)
    turn = (slot - holder_of(slot) * CAP + 1).astype(F32)
    slots_ref[...] = (dot(rank, owner, 1, 1) == turn).astype(F32).astype(BF16)


def lay_out_segments(segments_ref, tile_ref, marks_ref):
    rows = segments_ref.shape[1]
    same = lax.broadcasted_iota(jnp.int32, (rows, rows), 0) == lax.broadcasted_iota(
        jnp.int32, (rows, rows), 1
    )
    numbers = jnp.where(same, segments_ref[...].astype(F32), 0.0).astype(BF16)
    tile = dot(numbers, jnp.ones((rows, 128), BF16))
    tile_ref[...] = tile
    length = jnp.sum((tile == 0.0).astype(F32), axis=0, keepdims=True)
    marks_ref[...] = jnp.broadcast_to(length, marks_ref.shape).astype(BF16)


def front(shard, tokens, cotangent, routes, segments, gate_w, up_w, down_w):
    anywhere = pl.BlockSpec(memory_space=pl.ANY)
    rows, features = tokens.shape
    blocks = [(4, 2, 2, 2, 48, width) for _, width, _ in GATHERED]
    own = (rows, 2 * KEY_VALUE_HEADS * HEAD_SIZE)
    laid = (EXPERTS, CAP, features)
    slots = EXPERTS * CAP
    marks = (32, 128)
    return pl.pallas_call(
        front_kernel,
        out_shape=[jax.ShapeDtypeStruct(shape, BF16) for shape in blocks]
        + [
            jax.ShapeDtypeStruct((features, 4 * HALF), BF16),
            jax.ShapeDtypeStruct((2 * HALF, features), BF16),
            jax.ShapeDtypeStruct((8,) + own, BF16),
            jax.ShapeDtypeStruct(marks, BF16),
            jax.ShapeDtypeStruct(tokens.shape, BF16),
            jax.ShapeDtypeStruct((rows, QUERY_HEADS * HEAD_SIZE), BF16),
            jax.ShapeDtypeStruct(laid, BF16),
            jax.ShapeDtypeStruct((rows, 128), F32),
            jax.ShapeDtypeStruct((rows, slots), BF16),
            jax.ShapeDtypeStruct((slots, 128), BF16),
            jax.ShapeDtypeStruct((slots, 128), BF16),
            jax.ShapeDtypeStruct((rows, 128), F32),
        ],
        in_specs=[VMEM_SPEC] * 5 + [anywhere] * 3,
        out_specs=[anywhere] * (len(GATHERED) + 2)
        + [VMEM_SPEC] * 4
        + [anywhere]
        + [VMEM_SPEC] * 5,
        scratch_shapes=[pltpu.VMEM(shape, BF16) for shape in blocks]
        + [pltpu.VMEM((4, 16, TOTAL), BF16)]
        + [
            pltpu.VMEM((48, width // 4 if len(order) == 3 else width), BF16)
            for _, width, order in GATHERED
        ]
        + [
            pltpu.VMEM(marks, BF16),
            pltpu.VMEM(laid, BF16),
            pltpu.VMEM(own, BF16),
            pltpu.SemaphoreType.DMA((8, 2)),
            pltpu.SemaphoreType.DMA((8, 2)),
            pltpu.SemaphoreType.DMA((EXPERT_SEM + 4,)),
            pltpu.SemaphoreType.DMA((EXPERT_SEM + 4,)),
            pltpu.SemaphoreType.DMA((32,)),
        ],
        compiler_params=pltpu.CompilerParams(
            collective_id=0, has_side_effects=True, vmem_limit_bytes=56 * 1024 * 1024
        ),
        cost_estimate=pl.CostEstimate(
            flops=2_000_000_000, bytes_accessed=250_000_000, transcendentals=0
        ),
    )(shard, tokens, cotangent, routes, segments, gate_w, up_w, down_w)


def middle_kernel(
    queries_ref,
    every_ref,
    marks_ref,
    segments_ref,
    tokens_ref,
    misc_ref,
    named_ref,
    slots_ref,
    slots_down_ref,
    owner_ref,
    cotangent_ref,
    outt_hbm,
    shgate_hbm,
    shup_hbm,
    shdt_hbm,
    cotangent_rows,
    attended_ref,
    residual_ref,
    normed_ref,
    gates_ref,
    gates_high_ref,
    gates_low_ref,
    forward_ref,
    grad_second_ref,
    grad_received,
    outgoing_hbm,
    grad_shgate_hbm,
    grad_shup_hbm,
    grad_shdt_hbm,
    outt_ref,
    shgate_ref,
    shup_ref,
    shdt_ref,
    grad_shgate,
    grad_shup,
    grad_shdt,
    outgoing,
    send_sems,
    recv_sems,
    local_sems,
):
    rows, features = tokens_ref.shape
    width = KEY_VALUE_HEADS * HEAD_SIZE
    keys_count = 8 * rows
    spot = place()
    chips = [chip_at(spot, offset) for offset in OFFSETS]
    mine = chip_at(spot, (0, 0, 0))[1]
    greet([where for where, _ in chips])
    wires = Wires(send_sems, recv_sems, local_sems)
    travelling = [
        wires.remote(cotangent_rows.at[holder], grad_received.at[mine], where)
        for where, holder in chips
    ]
    staying = [wires.copy(cotangent_rows.at[mine], grad_received.at[mine])]
    outt_in = wires.copy(outt_hbm, outt_ref)
    shared_in = [
        wires.copy(shgate_hbm, shgate_ref),
        wires.copy(shup_hbm, shup_ref),
        wires.copy(shdt_hbm, shdt_ref),
    ]
    allowed = allowed_pairs(marks_ref, segments_ref, rows, keys_count)
    allowed = jnp.concatenate([allowed.astype(F32)] * GROUP, axis=0) > 0.5
    for group in range(KEY_VALUE_HEADS):
        queries = head_columns(queries_ref, group)
        columns = pl.ds(group * HEAD_SIZE, HEAD_SIZE)
        keys = every_ref[:, :, columns].reshape(keys_count, HEAD_SIZE)
        values = every_ref[:, :, pl.ds(width + group * HEAD_SIZE, HEAD_SIZE)].reshape(
            keys_count, HEAD_SIZE
        )
        weights = head_weights(queries, keys, allowed)
        mixed = dot(weights.astype(BF16), values).astype(BF16)
        for head in range(GROUP):
            at = (group * GROUP + head) * HEAD_SIZE
            attended_ref[:, at : at + HEAD_SIZE] = mixed[head * rows : (head + 1) * rows]
    attended = attended_ref[...]
    outt_in.wait()
    total = jnp.zeros((rows, 1), F32)
    for left in range(0, features, 512):
        piece = tokens_ref[:, left : left + 512].astype(F32) + dot(
            attended, outt_ref[left : left + 512], 1, 1
        )
        residual_ref[:, left : left + 512] = piece
        total = total + jnp.sum(piece * piece, axis=1, keepdims=True)
    scale = lax.rsqrt(total / features + EPSILON)
    normed_ref[...] = (residual_ref[...] * scale * gain_row(misc_ref[...], EXPERTS + 1)).astype(BF16)
    normed = normed_ref[...]
    logits = dot(normed, misc_ref[...])
    named = named_ref[...] > 0.5
    chosen = jnp.where(named, logits, -1e30)
    chosen_exp = jnp.where(named, jnp.exp(chosen - jnp.max(chosen, axis=1, keepdims=True)), 0.0)
    gates = chosen_exp / jnp.sum(chosen_exp, axis=1, keepdims=True)
    gates_ref[...] = gates
    parts = jnp.concatenate(rounded_parts(gates), axis=1)
    tile = GROUP_BLOCKS * CAP

    def fill(step, carry):
        at = pl.ds(pl.multiple_of(step * tile, 128), tile)
        blocks = pl.ds(step * GROUP_BLOCKS, GROUP_BLOCKS)
        slots = slots_down_ref[at]
        for left in range(0, features, 512):
            outgoing[blocks, :, left : left + 512] = blocks_of(
                dot(slots, normed_ref[:, left : left + 512])
            )
        gate_parts = dot(slots, parts)
        owner = owner_ref[at].astype(F32)
        lane = lax.broadcasted_iota(jnp.int32, (tile, EXTRA), 1)
        extra = jnp.zeros((tile, EXTRA), F32)
        for part in range(3):
            column = jnp.sum(
                gate_parts[:, part * 128 : (part + 1) * 128] * owner, axis=1, keepdims=True
            )
            extra = jnp.where(lane == part, column, extra)
        outgoing[blocks, :, features:] = blocks_of(extra)
        return carry

    lax.fori_loop(0, EXPERTS // GROUP_BLOCKS, fill, 0)
    staying.append(wires.copy(outgoing, outgoing_hbm))

    slot_gates = jnp.zeros((rows, slots_ref.shape[1]), F32)
    for part in range(3):
        slot_gates = slot_gates + dot(
            parts[:, part * 128 : (part + 1) * 128], owner_ref[...], 1, 1
        )
    slot_gates = slot_gates * slots_ref[...].astype(F32)
    gates_high = slot_gates.astype(BF16)
    gates_high_ref[...] = gates_high
    gates_low_ref[...] = (slot_gates - gates_high.astype(F32)).astype(BF16)

    for copy in shared_in:
        copy.wait()
    cotangent = cotangent_ref[...]
    gate_pre = dot(normed, shgate_ref[...])
    up_pre = dot(normed, shup_ref[...])
    sigmoid = 1.0 / (1.0 + jnp.exp(-gate_pre))
    silu = gate_pre * sigmoid
    hidden = (silu * up_pre).astype(BF16)
    grad_hidden = dot(cotangent, shdt_ref[...])
    grad_gate = (
        grad_hidden * up_pre * sigmoid * (1.0 + gate_pre * (1.0 - sigmoid))
    ).astype(BF16)
    grad_up = (grad_hidden * silu).astype(BF16)
    for left in range(0, features, 512):
        columns = pl.ds(left, 512)
        forward_ref[:, columns] = residual_ref[:, columns] + dot(hidden, shdt_ref[columns], 1, 1)
        grad_second_ref[:, columns] = dot(grad_gate, shgate_ref[columns], 1, 1) + dot(
            grad_up, shup_ref[columns], 1, 1
        )
        grad_shgate[columns] = dot(normed_ref[:, columns], grad_gate, 0, 0).astype(BF16)
        grad_shup[columns] = dot(normed_ref[:, columns], grad_up, 0, 0).astype(BF16)
        grad_shdt[columns] = dot(cotangent_ref[:, columns], hidden, 0, 0).astype(BF16)
    staying += [
        wires.copy(grad_shgate, grad_shgate_hbm),
        wires.copy(grad_shup, grad_shup_hbm),
        wires.copy(grad_shdt, grad_shdt_hbm),
    ]
    for copy in staying:
        copy.wait()
    for copy in travelling:
        copy.wait_recv()
    wires.finish()


def middle(queries, every, marks, segments, tokens, misc, named, slots, slots_down, owner, cotangent,
           cotangent_rows, outt, shgate, shup, shdt):
    rows, features = tokens.shape
    slot_count = slots.shape[1]
    anywhere = pl.BlockSpec(memory_space=pl.ANY)
    inputs = (queries, every, marks, segments, tokens, misc, named, slots, slots_down, owner,
              cotangent, outt, shgate, shup, shdt)
    shared = [shgate.shape, shup.shape, shdt.shape]
    wide = cotangent_rows.shape[:2] + (features + EXTRA,)
    return pl.pallas_call(
        middle_kernel,
        out_shape=[
            jax.ShapeDtypeStruct((rows, features), BF16),
            jax.ShapeDtypeStruct((rows, features), F32),
            jax.ShapeDtypeStruct((rows, features), BF16),
            jax.ShapeDtypeStruct((rows, 128), F32),
            jax.ShapeDtypeStruct((rows, slot_count), BF16),
            jax.ShapeDtypeStruct((rows, slot_count), BF16),
            jax.ShapeDtypeStruct((rows, features), F32),
            jax.ShapeDtypeStruct((rows, features), F32),
            jax.ShapeDtypeStruct(cotangent_rows.shape, BF16),
            jax.ShapeDtypeStruct(wide, BF16),
        ]
        + [jax.ShapeDtypeStruct(shape, BF16) for shape in shared],
        in_specs=[VMEM_SPEC] * 11 + [anywhere] * 5,
        out_specs=[VMEM_SPEC] * 8 + [anywhere] * 5,
        scratch_shapes=[pltpu.VMEM(outt.shape, BF16)]
        + [pltpu.VMEM(shape, BF16) for shape in shared + shared]
        + [
            pltpu.VMEM(wide, BF16),
            pltpu.SemaphoreType.DMA((64,)),
            pltpu.SemaphoreType.DMA((64,)),
            pltpu.SemaphoreType.DMA((10,)),
        ],
        compiler_params=pltpu.CompilerParams(
            collective_id=5, has_side_effects=True, vmem_limit_bytes=MIDDLE_MIB * 1024 * 1024
        ),
        cost_estimate=pl.CostEstimate(
            flops=10_000_000_000, bytes_accessed=250_000_000, transcendentals=2_000_000
        ),
    )(*inputs, cotangent_rows)


def expert_kernel(
    outgoing_ref,
    cotangent_in,
    weight_hbm,
    down_hbm,
    returned_ref,
    rows_out,
    own_in_hbm,
    other_in_hbm,
    own_down_hbm,
    other_down_hbm,
    weight_ref,
    down_ref,
    own_in_ref,
    other_in_ref,
    own_down_ref,
    other_down_ref,
    landed,
    cotangents,
    back,
    grads,
    hiddens,
    gated,
    rows_staged,
    send_sems,
    recv_sems,
    local_sems,
):
    features = cotangent_in.shape[2]
    spot = place()
    chips = [chip_at(spot, offset) for offset in OFFSETS]
    sources = [chip_at(spot, offset, -1) for offset in OFFSETS]
    mine = chip_at(spot, (0, 0, 0))[1]
    holders = [mine] + [holder for _, holder in sources]
    wires = Wires(send_sems, recv_sems, local_sems)
    weights_in = [wires.copy(weight_hbm, weight_ref), wires.copy(down_hbm, down_ref)]
    greet([where for where, _ in chips])
    rows_in = [wires.copy(outgoing_ref.at[mine], landed.at[0])]
    for number, (where, holder) in enumerate(chips):
        rows_in.append(wires.remote(outgoing_ref.at[holder], landed.at[number + 1], where))
    brought = [
        wires.copy(cotangent_in.at[holder], cotangents.at[number])
        for number, holder in enumerate(holders)
    ]
    for copy in weights_in:
        copy.wait()
    count = len(holders)
    tile = GROUP_BLOCKS * CAP
    returning = []

    def flat(ref, first, columns):
        blocks = ref[first : first + GROUP_BLOCKS, :, columns].astype(F32)
        return blocks.reshape(tile, blocks.shape[-1]).astype(BF16)

    for first in range(0, count, GROUP_BLOCKS):
        for number in range(first, first + GROUP_BLOCKS):
            brought[number].wait()
            if number == 0:
                rows_in[number].wait()
            else:
                rows_in[number].wait_recv()
        at = pl.ds(first * CAP, tile)
        extra = flat(landed, first, pl.ds(features, EXTRA)).astype(F32)
        gate = extra[:, :1] + extra[:, 1:2] + extra[:, 2:3]
        everything = pl.ds(0, features)
        pre = dot(flat(landed, first, everything), weight_ref[...])
        grad_hidden = dot(flat(cotangents, first, everything), down_ref[...], 1, 1)
        along = jnp.zeros((tile, 1), F32)
        for part in range(2):
            base = part * 2 * HALF
            gate_pre, up_pre = pre[:, base : base + HALF], pre[:, base + HALF : base + 2 * HALF]
            grad_part = grad_hidden[:, part * HALF : (part + 1) * HALF]
            sigmoid = 1.0 / (1.0 + jnp.exp(-gate_pre))
            silu = gate_pre * sigmoid
            hidden = silu * up_pre
            along = along + jnp.sum(hidden * grad_part, axis=1, keepdims=True)
            gated_grad = grad_part * gate
            grads[at, base : base + HALF] = (
                gated_grad * up_pre * sigmoid * (1.0 + gate_pre * (1.0 - sigmoid))
            ).astype(BF16)
            grads[at, base + HALF : base + 2 * HALF] = (gated_grad * silu).astype(BF16)
            hiddens[at, part * HALF : (part + 1) * HALF] = hidden.astype(BF16)
            gated[at, part * HALF : (part + 1) * HALF] = (hidden * gate).astype(BF16)
        group_grads = grads[at]
        for left in range(0, features, 512):
            back[first : first + GROUP_BLOCKS, :, left : left + 512] = blocks_of(
                dot(group_grads, weight_ref[left : left + 512], 1, 1)
            )
        lane = lax.broadcasted_iota(jnp.int32, (tile, EXTRA), 1)
        value = jnp.zeros((tile, EXTRA), F32)
        for part, column in enumerate(rounded_parts(along)):
            value = jnp.where(lane == part, column.astype(F32), value)
        back[first : first + GROUP_BLOCKS, :, features:] = blocks_of(value)
        for number in range(first, first + GROUP_BLOCKS):
            if number == 0:
                kept = wires.copy(back.at[0], returned_ref.at[mine])
            else:
                returning.append(
                    wires.remote(back.at[number], returned_ref.at[mine], sources[number - 1][0])
                )
    staged = []
    for index, first in enumerate(range(0, count, GROUP_BLOCKS)):
        group_hidden = hiddens[pl.ds(first * CAP, tile)]
        slot = index % 2
        if index >= 2:
            for copy in staged[index - 2]:
                copy.wait()
        for left in range(0, features, 512):
            columns = pl.ds(left, 512)
            rows_staged[slot, :, :, left : left + 512] = blocks_of(
                dot(group_hidden, down_ref[:, columns])
            )
        staged.append(
            [
                wires.copy(rows_staged.at[slot, number], rows_out.at[holders[first + number]])
                for number in range(GROUP_BLOCKS)
            ]
        )

    def every_row(ref, columns):
        return ref[:, :, columns].astype(F32).reshape(count * CAP, 256).astype(BF16)

    def weight_gradients(step, carry):
        columns = pl.ds(pl.multiple_of(step * 256, 256), 256)
        rows = every_row(landed, columns)
        own_in_ref[columns] = dot(rows, grads[:, : 2 * HALF], 0, 0)
        other_in_ref[columns] = dot(rows, grads[:, 2 * HALF :], 0, 0).astype(BF16)
        rows = every_row(cotangents, columns)
        own_down_ref[:, columns] = dot(gated[:, :HALF], rows, 0, 0)
        other_down_ref[:, columns] = dot(gated[:, HALF:], rows, 0, 0).astype(BF16)
        return carry

    lax.fori_loop(0, features // 256, weight_gradients, 0)
    staged.append(
        [
            wires.copy(own_in_ref, own_in_hbm),
            wires.copy(other_in_ref, other_in_hbm),
            wires.copy(own_down_ref, own_down_hbm),
            wires.copy(other_down_ref, other_down_hbm),
        ]
    )
    for copies in staged[-3:]:
        for copy in copies:
            copy.wait()
    kept.wait()
    for copy in returning:
        copy.wait_recv()
    wires.finish()


def expert(outgoing, grad_received, weight, down):
    count, cap, features = grad_received.shape
    anywhere = pl.BlockSpec(memory_space=pl.ANY)
    return pl.pallas_call(
        expert_kernel,
        out_shape=[
            jax.ShapeDtypeStruct(outgoing.shape, BF16),
            jax.ShapeDtypeStruct(grad_received.shape, BF16),
            jax.ShapeDtypeStruct((features, 2 * HALF), F32),
            jax.ShapeDtypeStruct((features, 2 * HALF), BF16),
            jax.ShapeDtypeStruct((HALF, features), F32),
            jax.ShapeDtypeStruct((HALF, features), BF16),
        ],
        in_specs=[anywhere] * 4,
        out_specs=[anywhere] * 6,
        scratch_shapes=[
            pltpu.VMEM(weight.shape, BF16),
            pltpu.VMEM(down.shape, BF16),
            pltpu.VMEM((features, 2 * HALF), F32),
            pltpu.VMEM((features, 2 * HALF), BF16),
            pltpu.VMEM((HALF, features), F32),
            pltpu.VMEM((HALF, features), BF16),
            pltpu.VMEM(outgoing.shape, BF16),
            pltpu.VMEM(grad_received.shape, BF16),
            pltpu.VMEM(outgoing.shape, BF16),
            pltpu.VMEM((count * cap, 4 * HALF), BF16),
            pltpu.VMEM((count * cap, 2 * HALF), BF16),
            pltpu.VMEM((count * cap, 2 * HALF), BF16),
            pltpu.VMEM((2, GROUP_BLOCKS, cap, features), BF16),
            pltpu.SemaphoreType.DMA((128,)),
            pltpu.SemaphoreType.DMA((128,)),
            pltpu.SemaphoreType.DMA((144,)),
        ],
        compiler_params=pltpu.CompilerParams(
            collective_id=4, has_side_effects=True, vmem_limit_bytes=56 * 1024 * 1024
        ),
        cost_estimate=pl.CostEstimate(
            flops=22_000_000_000, bytes_accessed=300_000_000, transcendentals=1_000_000
        ),
    )(outgoing, grad_received, weight, down)


def back_to_residual(
    grad_back_ref,
    slots_ref,
    owner_ref,
    gates_ref,
    cotangent_ref,
    residual_ref,
    partial_ref,
    misc_ref,
    outt_ref,
    grad_residual_ref,
    grad_low_ref,
    grad_logits_ref,
    grad_gain_ref,
    grad_attended,
):
    rows, features = cotangent_ref.shape
    slots = slots_ref[...]
    extra = grad_back_ref[:, features:].astype(F32)
    owner = owner_ref[...].astype(F32)
    grad_gates = jnp.zeros((rows, 128), F32)
    for part in range(3):
        grad_gates = grad_gates + dot(slots, (owner * extra[:, part : part + 1]).astype(BF16))
    gates = gates_ref[...]
    grad_logits = (
        gates * (grad_gates - jnp.sum(gates * grad_gates, axis=1, keepdims=True))
    ).astype(BF16)
    grad_logits_ref[...] = grad_logits
    gain = gain_row(misc_ref[...], EXPERTS + 1)
    square, inner = jnp.zeros((rows, 1), F32), jnp.zeros((rows, 1), F32)
    for left in range(0, features, 512):
        columns = pl.ds(left, 512)
        piece = (
            partial_ref[:, columns]
            + dot(slots, grad_back_ref[:, columns])
            + dot(grad_logits, misc_ref[columns], 1, 1)
        )
        grad_residual_ref[:, columns] = piece
        residual = residual_ref[:, columns]
        square = square + jnp.sum(residual * residual, axis=1, keepdims=True)
        inner = inner + jnp.sum(
            piece * gain[:, left : left + 512] * residual, axis=1, keepdims=True
        )
    scale = lax.rsqrt(square / features + EPSILON)
    cubed = scale * scale * scale * (inner / features)
    for left in range(0, features, 512):
        columns = pl.ds(left, 512)
        piece = grad_residual_ref[:, columns]
        residual = residual_ref[:, columns]
        grad_gain_ref[:, columns] = jnp.broadcast_to(
            jnp.sum(piece * residual * scale, axis=0, keepdims=True), (8, 512)
        )
        value = (
            cotangent_ref[:, columns].astype(F32)
            + scale * piece * gain[:, left : left + 512]
            - residual * cubed
        )
        grad_residual_ref[:, columns] = value
        grad_low_ref[:, columns] = value.astype(BF16)
    grad_low = grad_low_ref[...]
    for left in range(0, features, 512):
        columns = pl.ds(left, 512)
        grad_attended[:, columns] = dot(grad_low, outt_ref[:, columns]).astype(BF16)


def back_heads(
    group, allowed, qkv_ref, every_ref, grad_attended, grad_queries_ref, partial_keyvals
):
    rows = qkv_ref.shape[0]
    width = KEY_VALUE_HEADS * HEAD_SIZE
    keys_count = 8 * rows
    score_scale = HEAD_SIZE ** (-0.5)
    queries = head_columns(qkv_ref, group)
    heads_gradient = head_columns(grad_attended, group)
    key_columns = pl.ds(group * HEAD_SIZE, HEAD_SIZE)
    value_columns = pl.ds(width + group * HEAD_SIZE, HEAD_SIZE)
    keys = every_ref[:, :, key_columns].reshape(keys_count, HEAD_SIZE)
    values = every_ref[:, :, value_columns].reshape(keys_count, HEAD_SIZE)
    weights = head_weights(queries, keys, allowed)
    grad_weights = dot(heads_gradient, values, 1, 1)
    inner_sum = jnp.sum(weights * grad_weights, axis=1, keepdims=True)
    grad_scores = (weights * (grad_weights - inner_sum)).astype(BF16)
    grad_queries = (dot(grad_scores, keys) * score_scale).astype(BF16)
    for head in range(GROUP):
        at = (group * GROUP + head) * HEAD_SIZE
        grad_queries_ref[:, at : at + HEAD_SIZE] = grad_queries[head * rows : (head + 1) * rows]
    partial_keyvals[:, :, key_columns] = (
        (dot(grad_scores, queries, 0, 0) * score_scale).astype(BF16).reshape(8, rows, HEAD_SIZE)
    )
    partial_keyvals[:, :, value_columns] = (
        dot(weights.astype(BF16), heads_gradient, 0, 0).astype(BF16).reshape(8, rows, HEAD_SIZE)
    )


EARLY_ROWS = 20


def rear_kernel(tail, *refs):
    (
        slots_ref,
        owner_ref,
        gates_ref,
        cotangent_ref,
        residual_ref,
        partial_ref,
        misc_ref,
        qkv_ref,
        marks_ref,
        segments_ref,
        attended_ref,
        normed1_ref,
        normed2_ref,
        tokens_ref,
        grad_back_hbm,
        outt_hbm,
        every_hbm,
        own_in_hbm,
        own_down_hbm,
        query_hbm,
        keyval_hbm,
        in_ref,
        down_ref,
        rows_ref,
    ) = refs[:24]
    (
        grad_tokens_ref,
        grad_outt_hbm,
        grad_query_hbm,
        grad_keyval_hbm,
        grad_misc_hbm,
        half_in_hbm,
        half_down_hbm,
        rows_out,
    ) = refs[24:32]
    (
        grad_back_ref,
        outt_ref,
        every_ref,
        own_in_ref,
        own_down_ref,
        grad_outt_ref,
        grad_query_ref,
        grad_keyval_ref,
        grad_misc_ref,
        grad_residual,
        grad_low,
        grad_logits,
        grad_gain,
        grad_attended,
        grad_queries,
        grad_first,
        blocks_ref,
        landed,
        query_ref,
        keyval_ref,
        their_in,
        their_down,
        sequence_send,
        sequence_recv,
        send_sems,
        recv_sems,
        local_sems,
    ) = refs[32:]
    me = col_index()
    spot = place()
    chips = [chip_at(spot, offset) for offset in OFFSETS]
    mine = chip_at(spot, (0, 0, 0))[1]
    rows, features = tokens_ref.shape
    late = pl.ds(rows - tail, tail)
    sibling = {"core": 1 - spot["core"]}
    greet([where for where, _ in chips] + [sibling])
    wires = Wires(send_sems, recv_sems, local_sems)
    fetched = [
        wires.copy(grad_back_hbm, grad_back_ref),
        wires.copy(outt_hbm, outt_ref),
        wires.copy(every_hbm, every_ref),
        wires.copy(query_hbm, query_ref),
        wires.copy(keyval_hbm, keyval_ref),
        wires.copy(own_in_hbm, own_in_ref),
        wires.copy(own_down_hbm, own_down_ref),
    ]
    halves_in = [
        wires.remote(in_ref, their_in, sibling),
        wires.remote(down_ref, their_down, sibling),
    ]
    kept = wires.copy(rows_ref.at[mine], rows_out.at[mine])
    returning = []

    def send_rows(start, stop):
        for where, holder in chips[start:stop]:
            returning.append(wires.remote(rows_ref.at[holder], rows_out.at[mine], where))

    send_rows(0, EARLY_ROWS)
    for fetch in fetched[:3]:
        fetch.wait()
    back_to_residual(
        grad_back_ref,
        slots_ref,
        owner_ref,
        gates_ref,
        cotangent_ref,
        residual_ref,
        partial_ref,
        misc_ref,
        outt_ref,
        grad_residual,
        grad_low,
        grad_logits,
        grad_gain,
        grad_attended,
    )
    allowed = allowed_pairs(marks_ref, segments_ref, rows, 8 * rows)
    allowed = jnp.concatenate([allowed.astype(F32)] * GROUP, axis=0) > 0.5
    for group in range(KEY_VALUE_HEADS):
        back_heads(
            group, allowed, qkv_ref, every_ref, grad_attended, grad_queries, blocks_ref
        )

    def copy(far, first_block):
        block = rem(me + 8 - far, 8)
        source, target = blocks_ref.at[block], landed.at[far]
        if first_block:
            source, target = blocks_ref.at[0, late], landed.at[far, late]
        return pltpu.make_async_remote_copy(
            src_ref=source,
            dst_ref=target,
            send_sem=sequence_send.at[far],
            recv_sem=sequence_recv.at[far],
            device_id=col_device(block),
            device_id_type=MESH_ID,
        )

    def each(far, first_block, condition, act):
        @pl.when(condition)
        def _():
            act(copy(far, first_block))

    for far in range(7, 0, -1):
        each(far, False, me > far, lambda moved: moved.start())
        each(far, True, me == far, lambda moved: moved.start())
    send_rows(EARLY_ROWS, 63)

    @pl.when(me == 0)
    def _():
        for far in range(1, 8):
            landed[far, : rows - tail] = jnp.zeros((rows - tail, landed.shape[2]), landed.dtype)

    for far in range(1, 8):

        @pl.when(me + far >= 8)
        def _():
            landed[far] = jnp.zeros(landed.shape[1:], landed.dtype)

    low, attended, queries = grad_low[...], attended_ref[...], grad_queries[...]
    for left in range(0, features, 512):
        columns = pl.ds(left, 512)
        grad_outt_ref[columns] = dot(grad_low[:, columns], attended, 0, 0).astype(BF16)
        grad_query_ref[columns] = dot(normed1_ref[:, columns], queries, 0, 0).astype(BF16)
    stored = [
        wires.copy(grad_outt_ref, grad_outt_hbm),
        wires.copy(grad_query_ref, grad_query_hbm),
    ]
    for fetch in fetched[3:]:
        fetch.wait()
    for left in range(0, features, 512):
        columns = pl.ds(left, 512)
        grad_first[:, columns] = dot(queries, query_ref[columns], 1, 1)
    for copy_in in halves_in:
        copy_in.wait_recv()
    for left in range(0, features, 512):
        columns = pl.ds(left, 512)
        their_in[columns] = (own_in_ref[columns] + their_in[columns].astype(F32)).astype(BF16)
        their_down[:, columns] = (
            own_down_ref[:, columns] + their_down[:, columns].astype(F32)
        ).astype(BF16)
    stored += [wires.copy(their_in, half_in_hbm), wires.copy(their_down, half_down_hbm)]
    for far in range(1, 8):
        each(far, False, (me > 0) & (me + far < 8), lambda moved: moved.wait_recv())
        each(far, True, me == 0, lambda moved: moved.wait_recv())
    grad_keyvals = grad_low.at[:, pl.ds(0, keyval_ref.shape[1])]
    for row in range(0, rows, 16):
        at = pl.ds(row, 16)
        value = blocks_ref[me, at].astype(F32)
        for far in range(1, 8):
            value = value + landed[far, at].astype(F32)
        grad_keyvals[at] = value.astype(BF16)
    keyvals = grad_keyvals[...]
    gain = gain_row(misc_ref[...], EXPERTS)
    square, inner = jnp.zeros((rows, 1), F32), jnp.zeros((rows, 1), F32)
    for left in range(0, features, 512):
        columns = pl.ds(left, 512)
        grad_keyval_ref[columns] = dot(normed1_ref[:, columns], keyvals, 0, 0).astype(BF16)
        piece = grad_first[:, columns] + dot(keyvals, keyval_ref[columns], 1, 1)
        grad_first[:, columns] = piece
        residual = tokens_ref[:, columns].astype(F32)
        square = square + jnp.sum(residual * residual, axis=1, keepdims=True)
        inner = inner + jnp.sum(
            piece * gain[:, left : left + 512] * residual, axis=1, keepdims=True
        )
    stored.append(wires.copy(grad_keyval_ref, grad_keyval_hbm))
    scale = lax.rsqrt(square / features + EPSILON)
    cubed = scale * scale * scale * (inner / features)
    logits = grad_logits[...]
    one_row = (lax.broadcasted_iota(jnp.int32, (16, 128), 0) == 0).astype(F32)
    lane = lax.broadcasted_iota(jnp.int32, (16, 128), 1)
    for left in range(0, features, 512):
        columns = pl.ds(left, 512)
        piece = grad_first[:, columns]
        residual = tokens_ref[:, columns].astype(F32)
        grad_tokens_ref[:, columns] = (
            grad_residual[:, columns]
            + scale * piece * gain[:, left : left + 512]
            - residual * cubed
        )
        total = dot(normed2_ref[:, columns], logits, 0, 0)
        rows1 = jnp.broadcast_to(
            jnp.sum(piece * residual * scale, axis=0, keepdims=True), (16, 512)
        )
        rows2 = jnp.broadcast_to(grad_gain[:1, columns], (16, 512))
        for index, gradient in ((EXPERTS, rows1), (EXPERTS + 1, rows2)):
            spread = (one_row * (lane == index).astype(F32)).astype(BF16)
            for part in rounded_parts(gradient):
                total = total + dot(part, spread, 0, 0)
        grad_misc_ref[columns] = total
    stored.append(wires.copy(grad_misc_ref, grad_misc_hbm))
    for far in range(1, 8):
        each(far, False, me > far, lambda moved: moved.wait_send())
        each(far, True, me == far, lambda moved: moved.wait_send())
    for copy_out in stored:
        copy_out.wait()
    kept.wait()
    for moved in returning:
        moved.wait_recv()
    wires.finish()


def rear(tail, inputs, grad_back, outt, every, own_in, own_down, query_w, keyval_w, expert_in,
         expert_down, rows_back):
    rows, features = inputs[3].shape
    anywhere = pl.BlockSpec(memory_space=pl.ANY)
    return pl.pallas_call(
        functools.partial(rear_kernel, tail),
        out_shape=[
            jax.ShapeDtypeStruct((rows, features), F32),
            jax.ShapeDtypeStruct((features, features), BF16),
            jax.ShapeDtypeStruct(query_w.shape, BF16),
            jax.ShapeDtypeStruct(keyval_w.shape, BF16),
            jax.ShapeDtypeStruct((features, 128), F32),
            jax.ShapeDtypeStruct(expert_in.shape, BF16),
            jax.ShapeDtypeStruct(expert_down.shape, BF16),
            jax.ShapeDtypeStruct(rows_back.shape, BF16),
        ],
        in_specs=[VMEM_SPEC] * 14 + [anywhere] * 10,
        out_specs=[VMEM_SPEC] + [anywhere] * 7,
        scratch_shapes=[
            pltpu.VMEM(grad_back.shape, BF16),
            pltpu.VMEM(outt.shape, BF16),
            pltpu.VMEM(every.shape, BF16),
            pltpu.VMEM(own_in.shape, F32),
            pltpu.VMEM(own_down.shape, F32),
            pltpu.VMEM((features, features), BF16),
            pltpu.VMEM(query_w.shape, BF16),
            pltpu.VMEM(keyval_w.shape, BF16),
            pltpu.VMEM((features, 128), F32),
            pltpu.VMEM((rows, features), F32),
            pltpu.VMEM((rows, features), BF16),
            pltpu.VMEM((rows, 128), BF16),
            pltpu.VMEM((8, features), F32),
            pltpu.VMEM((rows, features), BF16),
            pltpu.VMEM((rows, features), BF16),
            pltpu.VMEM((rows, features), F32),
            pltpu.VMEM(every.shape, BF16),
            pltpu.VMEM(every.shape, BF16),
            pltpu.VMEM(query_w.shape, BF16),
            pltpu.VMEM(keyval_w.shape, BF16),
            pltpu.VMEM(expert_in.shape, BF16),
            pltpu.VMEM(expert_down.shape, BF16),
            pltpu.SemaphoreType.DMA((8,)),
            pltpu.SemaphoreType.DMA((8,)),
            pltpu.SemaphoreType.DMA((66,)),
            pltpu.SemaphoreType.DMA((66,)),
            pltpu.SemaphoreType.DMA((16,)),
        ],
        compiler_params=pltpu.CompilerParams(
            collective_id=3, has_side_effects=True, vmem_limit_bytes=58 * 1024 * 1024
        ),
        cost_estimate=pl.CostEstimate(
            flops=10_000_000_000, bytes_accessed=150_000_000, transcendentals=2_000_000
        ),
    )(
        *inputs,
        grad_back,
        outt,
        every,
        own_in,
        own_down,
        query_w,
        keyval_w,
        expert_in,
        expert_down,
        rows_back,
    )


def contract(left_side, right_side, left_dim, right_dim):
    return lax.dot_general(
        left_side,
        right_side,
        (((left_dim,), (right_dim,)), ((), ())),
        preferred_element_type=F32,
    )


def expert_of(holder):
    return (holder // 8) * 8 + (holder % 2) * 4 + holder // 2 % 4


def packed(grad):
    return grad.reshape(4, 2, 2, 2, 48, grad.shape[-1])


def shards(
    tokens,
    segments,
    routes,
    norm1_gain,
    w_query,
    key_value_weight,
    w_output,
    norm2_gain,
    w_router,
    w_shgate,
    w_shup,
    w_shdown,
    w_exgate,
    w_exup,
    w_exdown,
    cotangent,
):
    local_rows, feature_count = tokens.shape
    sequence_length = local_rows * 8
    shard = jnp.concatenate(
        [
            w_output.T,
            w_router,
            norm1_gain[:, None],
            norm2_gain[:, None],
            jnp.zeros((12, 62), BF16),
            w_query,
            key_value_weight,
            w_shgate,
            w_shup,
            w_shdown.T,
        ],
        axis=1,
    )
    shard = jnp.concatenate([shard, jnp.zeros((4, TOTAL), BF16)], axis=0)
    tail = 32
    (
        outt_w,
        misc_w,
        query_w,
        keyval_w,
        shgate_w,
        shup_w,
        shdt_w,
        expert_w,
        expert_down,
        every,
        marks,
        first_normed,
        query_rows,
        sent_cotangent,
        named,
        slots,
        slots_down,
        owner,
        segment_tile,
    ) = front(
        shard, tokens, cotangent, routes, segments[None, :], w_exgate[0], w_exup[0], w_exdown[0]
    )
    outt_w, misc_w, query_w, keyval_w, shgate_w, shup_w, shdt_w = [
        gathered.reshape(feature_count, gathered.shape[-1])
        for gathered in (outt_w, misc_w, query_w, keyval_w, shgate_w, shup_w, shdt_w)
    ]
    slot_count = EXPERTS * CAP
    (
        attended_rows,
        residual1,
        second_normed,
        gates,
        gates_high,
        gates_low,
        forward_rows,
        grad_second,
        grad_received,
        outgoing,
        grad_shgate,
        grad_shup,
        grad_shdt,
    ) = middle(
        query_rows,
        every,
        marks,
        segment_tile,
        tokens,
        misc_w,
        named,
        slots,
        slots_down,
        owner,
        cotangent,
        sent_cotangent,
        outt_w,
        shgate_w,
        shup_w,
        shdt_w,
    )
    grad_back, half_out, own_in, other_in, own_down, other_down = expert(
        outgoing, grad_received, expert_w, expert_down
    )
    grad_back = grad_back.reshape(slot_count, feature_count + EXTRA)
    (
        grad_tokens,
        grad_outt,
        grad_query,
        grad_keyval,
        grad_misc,
        half_in,
        half_down,
        returned,
    ) = rear(
        tail,
        (
            slots,
            owner,
            gates,
            cotangent,
            residual1,
            grad_second,
            misc_w,
            query_rows,
            marks,
            segment_tile,
            attended_rows,
            first_normed,
            second_normed,
            tokens,
        ),
        grad_back,
        outt_w,
        every,
        own_in,
        own_down,
        query_w,
        keyval_w,
        other_in,
        other_down,
        half_out,
    )
    *summed, half_in, half_down, block_out = sum_last(
        [
            packed(grad)
            for grad in (
                grad_outt,
                grad_misc,
                grad_query,
                grad_keyval,
                grad_shgate,
                grad_shup,
                grad_shdt,
            )
        ],
        [half_in, half_down],
        returned,
        gates_high,
        gates_low,
        forward_rows,
    )
    sum_outt, sum_misc, sum_query, sum_keyval, sum_shgate, sum_shup, sum_shdt = [
        piece[:12] for piece in summed
    ]
    return (
        block_out,
        grad_tokens,
        sum_misc[:, EXPERTS],
        sum_query,
        sum_keyval,
        sum_outt.T,
        sum_misc[:, EXPERTS + 1],
        sum_misc[:, :EXPERTS],
        sum_shgate,
        sum_shup,
        sum_shdt.T,
        half_in[None, :, :HALF].astype(F32),
        half_in[None, :, HALF:].astype(F32),
        half_down[None].astype(F32),
    )


def solution(mesh):
    fine = Mesh(mesh.devices.reshape(SIZES), AXES)
    rows = P(AXES, None)
    columns = P(None, AXES)
    flat = P(AXES)
    blocks = P(AXES, None, None)
    in_specs = (
        rows,
        flat,
        rows,
        flat,
        rows,
        rows,
        columns,
        flat,
        rows,
        rows,
        rows,
        columns,
        blocks,
        blocks,
        blocks,
        rows,
    )
    out_specs = (
        rows,
        rows,
        flat,
        rows,
        rows,
        columns,
        flat,
        rows,
        rows,
        rows,
        columns,
        blocks,
        blocks,
        blocks,
    )
    return jax.shard_map(shards, mesh=fine, in_specs=in_specs, out_specs=out_specs, check_vma=False)
```

```python
import functools

import jax
import jax.numpy as jnp
from jax import lax
from jax.experimental import pallas as pl
from jax.experimental.pallas import tpu as pltpu
from jax.sharding import Mesh
from jax.sharding import PartitionSpec as P

QUERY_HEADS = 12
KEY_VALUE_HEADS = 4
HEAD_SIZE = 128
EXPERTS = 64
TOPK = 6
CAP = 24
EPSILON = 1e-05

F32 = jnp.float32
BF16 = jnp.bfloat16
MESH_ID = pl.DeviceIdType.MESH
AXES = ("z", "yl", "core", "yh", "xh", "xl")
SIZES = (4, 2, 2, 2, 2, 2)

PARTS = (
    ("outt", 1536, "yzx", "yzx"),
    ("misc", 128, "yz", "yz"),
    ("q", 1536, "yz", "yz"),
    ("kv", 1024, "zy", "zy"),
    ("shg", 1024, "yz", "yz"),
    ("shu", 1024, "zy", "zy"),
    ("shdt", 1024, "zy", "zy"),
)
GATHERED = tuple((name, width, order) for name, width, order, _ in PARTS)
SUMMED = tuple((name, width, order) for name, width, _, order in PARTS)
TOTAL = sum(part[1] for part in PARTS)
HALF = 256
EXPERT_SEM = 200
TOTAL = sum(part[1] for part in PARTS)


def rem(value, size):
    return lax.rem(value, jnp.int32(size))


def place():
    at = {name: lax.axis_index(name) for name in AXES}
    return {
        "x": at["xh"] * 2 + at["xl"],
        "y": at["yh"] * 2 + at["yl"],
        "z": at["z"],
        "core": at["core"],
    }


def device(axis, value):
    if axis == "x":
        return {"xh": value // 2, "xl": rem(value, 2)}
    if axis == "y":
        return {"yh": value // 2, "yl": rem(value, 2)}
    return {axis: value}


def greet(targets):
    barrier = pltpu.get_barrier_semaphore()
    for target in targets:
        pl.semaphore_signal(barrier, inc=1, device_id=target, device_id_type=MESH_ID)
    pl.semaphore_wait(barrier, len(targets))


def ring_neighbours(me):
    near = [device("x", rem(me["x"] + hops, 4)) for hops in (1, 2, 3)]
    near += [device("y", rem(me["y"] + hops, 4)) for hops in (1, 3)]
    near += [device("z", rem(me["z"] + hops, 4)) for hops in (1, 3)]
    return near + [{"core": 1 - me["core"]}]


class Wires:
    def __init__(self, send_sems, recv_sems, local_sems):
        self.send, self.recv, self.local = send_sems, recv_sems, local_sems
        self.used, self.used_local, self.started, self.kept = 0, 0, [], []

    def remote(self, source, target, where):
        copy = pltpu.make_async_remote_copy(
            src_ref=source,
            dst_ref=target,
            send_sem=self.send.at[self.used],
            recv_sem=self.recv.at[self.used],
            device_id=where,
            device_id_type=MESH_ID,
        )
        self.used += 1
        copy.start()
        self.started.append(copy)
        return copy

    def copy(self, source, target):
        copy = pltpu.make_async_copy(source, target, self.local.at[self.used_local])
        self.used_local += 1
        copy.start()
        return copy

    def finish(self):
        for copy in self.started:
            copy.wait_send()


def balanced_offsets():
    left = [(x, y, z) for x in range(4) for y in range(4) for z in range(4) if x + y + z > 0]
    load, order = [0] * 6, []

    def uses(offset):
        used = [0] * 6
        for axis, hops in enumerate(offset):
            used[2 * axis] += hops in (1, 2)
            used[2 * axis + 1] += hops in (2, 3)
        return used

    def cost(offset):
        used = uses(offset)
        after = [a + b for a, b in zip(load, used)]
        mean = sum(after) / 6
        return (max(after), sum((a - mean) ** 2 for a in after), -sum(used))

    while left:
        best = min(left, key=cost)
        load = [a + b for a, b in zip(load, uses(best))]
        left.remove(best)
        order.append(best)
    return order


OFFSETS = balanced_offsets()


def chip_at(me, offset, sign=1):
    x, y, z = [rem(me[axis] + (sign * hops) % 4, 4) for axis, hops in zip("xyz", offset)]
    where = {"z": z, "yh": y // 2, "yl": rem(y, 2), "xh": x // 2, "xl": rem(x, 2)}
    return where, z * 16 + rem(y, 2) * 8 + (y // 2) * 4 + x


def halves(width):
    first = width // 256 * 128 if width > 128 else width
    return first, width - first


def spread_rows(shape, swap):
    dense = lax.broadcasted_iota(jnp.int32, shape, 1 if swap else 0)
    padded = lax.broadcasted_iota(jnp.int32, shape, 0 if swap else 1)
    shift = jnp.zeros(shape, jnp.int32)
    for edge in (12, 24, 36):
        shift = shift + jnp.where(dense >= edge, 4, 0)
    return dense + shift == padded


def block_ref(ref, axes, me, axis, value, columns):
    spot = dict(me)
    spot[axis] = value
    z = slice(None) if "z" in axes else spot["z"]
    yl = slice(None) if "y" in axes else rem(spot["y"], 2)
    yh = slice(None) if "y" in axes else spot["y"] // 2
    return ref.at[z, yl, me["core"], yh, :, columns]


def gather_kernel(shard_ref, gate_ref, up_ref, down_ref, *rest):
    count = len(GATHERED)
    outs = rest[:count]
    expert_in, expert_out, landed = rest[count : count + 3]
    stages = rest[count + 3 : 2 * count + 3]
    send_sems, recv_sems, local_sems = rest[2 * count + 3 :]
    me = place()
    nxt = {axis: rem(me[axis] + 1, 4) for axis in "xyz"}
    opp = {axis: rem(me[axis] + 2, 4) for axis in "xyz"}
    prv = {axis: rem(me[axis] + 3, 4) for axis in "xyz"}
    sibling = {"core": 1 - me["core"]}
    partner = {"core": 1 - me["core"], "xl": 1 - lax.axis_index("xl")}
    crossed = me["core"] != lax.axis_index("xl")
    greet(
        [device("x", nxt["x"]), device("x", opp["x"]), device("x", prv["x"])]
        + [device("y", nxt["y"]), device("y", prv["y"])]
        + [device("z", nxt["z"]), device("z", prv["z"]), sibling, partner]
    )
    wires = Wires(send_sems, recv_sems, local_sems)
    runs, start = [], 0
    for index, (name, width, order) in enumerate(GATHERED):
        last_x = len(order) == 3
        quarter = width // 4 if last_x else width
        run = {
            "out": outs[index],
            "order": order,
            "width": quarter,
            "done": "",
            "stage": stages[index],
            "start": start,
            "landed": landed.at[:, :, pl.ds(start, quarter)],
            "base": me["x"] * quarter if last_x else 0,
            "first": [],
            "shared": [],
        }

        def piece(x):
            if last_x:
                return shard_ref.at[:, pl.ds(pl.multiple_of(start + x * quarter, 128), quarter)]
            return shard_ref.at[:, pl.ds(start, quarter)]

        for where in (nxt, prv, opp):
            run["first"].append(
                wires.remote(piece(where["x"]), run["landed"].at[me["x"]], device("x", where["x"]))
            )
        run["bring"] = wires.copy(piece(me["x"]), run["landed"].at[me["x"]])
        runs.append(run)
        start += width

    whole = [
        (gate_ref, expert_in.at[:, pl.ds(0, HALF)]),
        (up_ref, expert_in.at[:, pl.ds(HALF, HALF)]),
        (down_ref, expert_out.at[pl.ds(0, HALF)]),
    ]

    def moved(slot):
        source, target = whole[slot]
        return pltpu.make_async_remote_copy(
            src_ref=source,
            dst_ref=target,
            send_sem=send_sems.at[EXPERT_SEM + slot],
            recv_sem=recv_sems.at[EXPERT_SEM + slot],
            device_id=partner,
            device_id_type=MESH_ID,
        )

    def kept(slot):
        source, target = whole[slot]
        return pltpu.make_async_copy(source, target, local_sems.at[20 + slot])

    @pl.when(crossed)
    def _():
        for slot in range(3):
            moved(slot).start()

    @pl.when(jnp.logical_not(crossed))
    def _():
        for slot in range(3):
            kept(slot).start()

    def part_columns(run, axis, value, which):
        base = value * run["width"] if axis == "x" else run["base"]
        left, size = 0, run["width"]
        if which is not None:
            first_half, second_half = halves(run["width"])
            left, size = (0, first_half) if which == 0 else (first_half, second_half)
        if isinstance(base, int):
            return pl.ds(base + left, size)
        return pl.ds(pl.multiple_of(base + left, 128), size)

    def blocks(run, axis, value, which=None):
        columns = part_columns(run, axis, value, which)
        return block_ref(run["out"], run["done"], me, axis, value, columns)

    def begin(run, axis, source=None):
        target = blocks(run, axis, me[axis])
        source = target if source is None else source
        run["forth"] = wires.remote(source, target, device(axis, nxt[axis]))
        run["back"] = wires.remote(source, target, device(axis, prv[axis]))

    pick = spread_rows((48, 64), False).astype(BF16)
    for run in runs:
        run["bring"].wait()
        for copy in run["first"]:
            copy.wait_recv()
        for left in range(0, run["width"], 512):
            size = min(512, run["width"] - left)
            left_in = run["start"] + left
            piece_rows = landed[:, :, left_in : left_in + size].reshape(64, size)
            run["stage"][:, left : left + size] = jnp.dot(
                pick, piece_rows, preferred_element_type=F32
            ).astype(BF16)
        axis = run["order"][0]
        begin(run, axis, run["stage"])
        run["own"] = wires.copy(run["stage"], blocks(run, axis, me[axis]))

    def forward(run, axis):
        run["forth"].wait_recv()
        source = blocks(run, axis, prv[axis], 0)
        run["more"] = [wires.remote(source, source, device(axis, nxt[axis]))]
        run["back"].wait_recv()
        if halves(run["width"])[1] > 0:
            source = blocks(run, axis, nxt[axis], 1)
            run["more"].append(wires.remote(source, source, device(axis, prv[axis])))

    def share(run, axis, value):
        source = blocks(run, axis, value)
        run["shared"].append(wires.remote(source, source, sibling))

    def advance(run, step):
        axis = run["order"][step]
        for copy in run["more"]:
            copy.wait_recv()
        if step == len(run["order"]) - 1:
            share(run, axis, opp[axis])
            return
        if step == 0:
            run["own"].wait()
        run["done"] = run["done"] + axis
        following = run["order"][step + 1]
        begin(run, following)
        if step + 1 == len(run["order"]) - 1:
            share(run, following, me[following])

    def last_forward(run):
        axis = run["order"][-1]
        forward(run, axis)
        share(run, axis, prv[axis])
        share(run, axis, nxt[axis])

    threes = [run for run in runs if len(run["order"]) == 3]
    twos = [run for run in runs if len(run["order"]) == 2]
    for run in runs:
        forward(run, run["order"][0])
    for run in runs:
        advance(run, 0)
    for run in threes:
        forward(run, run["order"][1])
    for run in threes:
        advance(run, 1)
    for run in twos:
        last_forward(run)
    for run in threes:
        last_forward(run)

    @pl.when(crossed)
    def _():
        for slot in range(3):
            moved(slot).wait_recv()

    @pl.when(jnp.logical_not(crossed))
    def _():
        for slot in range(3):
            kept(slot).wait()

    handed = [
        wires.remote(
            expert_in.at[:, pl.ds(0, 2 * HALF)], expert_in.at[:, pl.ds(2 * HALF, 2 * HALF)], sibling
        ),
        wires.remote(expert_out.at[pl.ds(0, HALF)], expert_out.at[pl.ds(HALF, HALF)], sibling),
    ]
    for run in twos + threes:
        advance(run, len(run["order"]) - 1)
    for run in runs:
        for copy in run["shared"]:
            copy.wait_recv()
    for copy in handed:
        copy.wait_recv()
    wires.finish()

    @pl.when(crossed)
    def _():
        for slot in range(3):
            moved(slot).wait_send()


def gather_weights(shard, gate_w, up_w, down_w):
    shapes = [jax.ShapeDtypeStruct((4, 2, 2, 2, 48, width), BF16) for _, width, _ in GATHERED]
    shapes += [
        jax.ShapeDtypeStruct((gate_w.shape[0], 4 * HALF), BF16),
        jax.ShapeDtypeStruct((2 * HALF, down_w.shape[1]), BF16),
    ]
    anywhere = pl.BlockSpec(memory_space=pl.ANY)
    return pl.pallas_call(
        gather_kernel,
        out_shape=shapes,
        in_specs=[pl.BlockSpec(memory_space=pltpu.VMEM)] + [anywhere] * 3,
        out_specs=[anywhere] * (len(GATHERED) + 2),
        scratch_shapes=[pltpu.VMEM((4, 16, TOTAL), BF16)]
        + [
            pltpu.VMEM((48, width // 4 if len(order) == 3 else width), BF16)
            for _, width, order in GATHERED
        ]
        + [
            pltpu.SemaphoreType.DMA((EXPERT_SEM + 4,)),
            pltpu.SemaphoreType.DMA((EXPERT_SEM + 4,)),
            pltpu.SemaphoreType.DMA((24,)),
        ],
        compiler_params=pltpu.CompilerParams(
            collective_id=0, has_side_effects=True, vmem_limit_bytes=16 * 1024 * 1024
        ),
        cost_estimate=pl.CostEstimate(flops=0, bytes_accessed=200_000_000, transcendentals=0),
    )(shard, gate_w, up_w, down_w)


class Summing:
    def __init__(self, wires, me, parts, grads, outs, scratch):
        self.wires, self.me = wires, me
        self.next = {axis: rem(me[axis] + 1, 4) for axis in "xyz"}
        self.opposite = {axis: rem(me[axis] + 2, 4) for axis in "xyz"}
        self.previous = {axis: rem(me[axis] + 3, 4) for axis in "xyz"}
        self.sibling = {"core": 1 - me["core"]}
        count = len(parts)
        self.runs = []
        for index, (name, width, order) in enumerate(parts):
            self.runs.append(
                {
                    "order": order[::-1],
                    "width": width // 4 if len(order) == 3 else width,
                    "left": "zy",
                    "turn": 0,
                    "grads": grads[index],
                    "out": outs[index],
                    "own": scratch[index],
                    "theirs": scratch[count + index],
                    "near1": scratch[2 * count + index],
                    "near2": scratch[3 * count + index],
                    "ends": scratch[4 * count + index],
                    "arrived": scratch[5 * count + index],
                }
            )

    def spot(self, left_axes, axis, value, with_core):
        at = dict(self.me)
        if axis is not None:
            at[axis] = value
        whole = [name for name in left_axes if name != axis]
        z = slice(None) if "z" in whole else at["z"]
        yl = slice(None) if "y" in whole else rem(at["y"], 2)
        yh = slice(None) if "y" in whole else at["y"] // 2
        return (z, yl) + (() if with_core is None else (with_core,)) + (yh,)

    def lead(self, left_axes, axis):
        dims = []
        for name in ("z", "y"):
            if name in left_axes and name != axis:
                dims += [4] if name == "z" else [2, 2]
        return dims

    def add_into(self, target, sources, dims):
        total = 1
        for size in dims:
            total *= size

        def body(index):
            for row in range(0, 48, 16):
                at = index + (pl.ds(row, 16),)
                value = target[at].astype(F32)
                for source in sources:
                    value = value + source[at].astype(F32)
                target[at] = value.astype(target.dtype)

        def step(flat, carry):
            index, rest_flat = [], flat
            for size in reversed(dims):
                index.append(rem(rest_flat, size))
                rest_flat = rest_flat // size
            body(tuple(reversed(index)))
            return carry

        if total == 1:
            body(())
        else:
            lax.fori_loop(0, total, step, 0)

    def columns_of(self, run, axis, value, which):
        base = 0
        if len(run["order"]) == 3:
            base = (value if axis == "x" else self.me["x"]) * run["width"]
        left, size = 0, run["width"]
        if which is not None:
            first_half, second_half = halves(run["width"])
            left, size = (0, first_half) if which == 0 else (first_half, second_half)
        if isinstance(base, int):
            return pl.ds(base + left, size)
        return pl.ds(pl.multiple_of(base + left, 128), size)

    def chunk(self, run, axis, value, which=None, ref=None, with_core=None):
        ref = run["own"] if ref is None else ref
        columns = self.columns_of(run, axis, value, which)
        return ref.at[self.spot(run["left"], axis, value, with_core) + (slice(None), columns)]

    def pair(self, run, axis, value):
        core = self.me["core"]
        give = self.wires.remote(
            self.chunk(run, axis, value, None, run["grads"], 1 - core),
            self.chunk(run, axis, value, None, run["theirs"]),
            self.sibling,
        )
        keep = self.wires.copy(
            self.chunk(run, axis, value, None, run["grads"], core), self.chunk(run, axis, value)
        )
        return give, keep

    def join(self, run, axis, value, copies):
        copies[0].wait_recv()
        copies[1].wait()
        self.add_into(
            self.chunk(run, axis, value),
            [self.chunk(run, axis, value, None, run["theirs"])],
            self.lead(run["left"], axis),
        )

    def slots(self, run, axis):
        dims = self.lead(run["left"], axis)
        ref = (run["near1"], run["near2"], run["ends"])[run["turn"]]
        if not dims:
            ref = ref.at[:, pl.ds(0, 48)]
        return ref.at[0], ref.at[1], ref.at[2], dims

    def part(self, ref, run, which, dims):
        first_half, second_half = halves(run["width"])
        columns = pl.ds(0, first_half) if which == 0 else pl.ds(first_half, second_half)
        return ref.at[(slice(None),) * len(dims) + (slice(None), columns)]

    def ring_open(self, run):
        axis = run["order"][run["turn"]]
        _, _, passing, dims = self.slots(run, axis)
        far = self.opposite[axis]
        run["passing"] = [
            self.wires.remote(
                self.chunk(run, axis, far, 0),
                self.part(passing, run, 0, dims),
                device(axis, self.next[axis]),
            )
        ]
        if halves(run["width"])[1]:
            run["passing"].append(
                self.wires.remote(
                    self.chunk(run, axis, far, 1),
                    self.part(passing, run, 1, dims),
                    device(axis, self.previous[axis]),
                )
            )

    def ring_near(self, run):
        axis = run["order"][run["turn"]]
        from_prv, from_nxt, _, dims = self.slots(run, axis)
        nxt, prv = self.next[axis], self.previous[axis]
        run["near"] = []
        if halves(run["width"])[1]:
            run["near"].append(
                self.wires.remote(
                    self.chunk(run, axis, nxt, 1),
                    self.part(from_prv, run, 1, dims),
                    device(axis, nxt),
                )
            )
        run["near"].append(
            self.wires.remote(
                self.chunk(run, axis, prv, 0), self.part(from_nxt, run, 0, dims), device(axis, prv)
            )
        )

    def ring_pass(self, run):
        axis = run["order"][run["turn"]]
        from_prv, from_nxt, passing, dims = self.slots(run, axis)
        nxt, prv = self.next[axis], self.previous[axis]
        run["passing"][0].wait_recv()
        self.add_into(self.chunk(run, axis, nxt, 0), [self.part(passing, run, 0, dims)], dims)
        run["near"].append(
            self.wires.remote(
                self.chunk(run, axis, nxt, 0), self.part(from_prv, run, 0, dims), device(axis, nxt)
            )
        )
        if halves(run["width"])[1]:
            run["passing"][1].wait_recv()
            self.add_into(self.chunk(run, axis, prv, 1), [self.part(passing, run, 1, dims)], dims)
            run["near"].append(
                self.wires.remote(
                    self.chunk(run, axis, prv, 1),
                    self.part(from_nxt, run, 1, dims),
                    device(axis, prv),
                )
            )

    def ring_close(self, run):
        axis = run["order"][run["turn"]]
        from_prv, from_nxt, _, dims = self.slots(run, axis)
        for copy in run["near"]:
            copy.wait_recv()
        self.add_into(self.chunk(run, axis, self.me[axis]), [from_prv, from_nxt], dims)
        run["left"] = run["left"].replace(axis, "")
        run["turn"] += 1

    def turn(self, run):
        self.ring_close(run)
        self.ring_open(run)
        self.ring_near(run)

    def spread(self, run):
        me, width = self.me, run["width"]
        third = len(run["order"]) == 3
        summed = run["own"].at[me["z"], rem(me["y"], 2), me["y"] // 2]
        exact = lax.Precision.HIGHEST if summed.dtype == F32 else None
        pick = spread_rows((64, 48), True).astype(summed.dtype)
        staging = run["ends"].at[3] if third else run["near2"].at[3]
        base = me["x"] * width if third else 0
        for left in range(0, width, 512):
            size = min(512, width - left)
            columns = pl.ds(left, size)
            if third:
                columns = pl.ds(pl.multiple_of(base + left, 128), size)
            staging[:, left : left + size] = jnp.dot(
                pick, summed[:, columns], preferred_element_type=F32, precision=exact
            ).astype(staging.dtype)
        if third:
            lands = run["arrived"].at[:, pl.ds(pl.multiple_of(base, 128), width)]
        else:
            lands = run["arrived"].at[me["x"]]
        run["copies"] = []
        for where in (self.next, self.opposite, self.previous):
            row = pl.ds(pl.multiple_of(where["x"] * 16, 16), 16)
            run["copies"].append(
                self.wires.remote(staging.at[row], lands, device("x", where["x"]))
            )
        row = pl.ds(pl.multiple_of(me["x"] * 16, 16), 16)
        run["keep"] = self.wires.copy(staging.at[row], lands)

    def deliver(self, run):
        run["keep"].wait()
        for copy in run["copies"]:
            copy.wait_recv()
        if len(run["order"]) == 3:
            run["out"][...] = run["arrived"][...].astype(F32)
        else:
            value = run["arrived"][0].astype(F32)
            for place_x in range(1, 4):
                value = value + run["arrived"][place_x].astype(F32)
            run["out"][...] = value

    def stages(self):
        runs = self.runs
        threes = [run for run in runs if len(run["order"]) == 3]
        twos = [run for run in runs if len(run["order"]) == 2]
        begun = []
        for where in (self.opposite, self.next, self.previous, self.me):
            begun.append([self.pair(run, run["order"][0], where[run["order"][0]]) for run in runs])
        yield
        for run, copies in zip(runs, begun[0]):
            axis = run["order"][0]
            self.join(run, axis, self.opposite[axis], copies)
            self.ring_open(run)
        for run, nexts, prevs in zip(runs, begun[1], begun[2]):
            axis = run["order"][0]
            self.join(run, axis, self.next[axis], nexts)
            self.join(run, axis, self.previous[axis], prevs)
            self.ring_near(run)
        yield
        for run in threes:
            self.ring_pass(run)
        for run, copies in zip(runs, begun[3]):
            axis = run["order"][0]
            self.join(run, axis, self.me[axis], copies)
        for run in twos:
            self.ring_pass(run)
        yield
        for run in threes:
            self.turn(run)
        for run in threes:
            self.ring_pass(run)
        for run in twos:
            self.turn(run)
        yield
        for run in threes:
            self.turn(run)
        for run in twos:
            self.ring_pass(run)
        for run in threes:
            self.ring_pass(run)
        yield
        for run in twos:
            self.ring_close(run)
            self.spread(run)
        for run in threes:
            self.ring_close(run)
            self.spread(run)
        yield
        for run in runs:
            self.deliver(run)
        yield


def summing_scratch(parts):
    own, theirs, near1, near2, ends, arrived = [], [], [], [], [], []
    for name, width, order in parts:
        kind = F32 if name == "misc" else BF16
        own.append(pltpu.VMEM((4, 2, 2, 48, width), kind))
        theirs.append(pltpu.VMEM((4, 2, 2, 48, width), kind))
        if len(order) == 3:
            quarter = width // 4
            near1.append(pltpu.VMEM((3, 4, 2, 2, 48, quarter), kind))
            near2.append(pltpu.VMEM((3, 2, 2, 48, quarter), kind))
            ends.append(pltpu.VMEM((4, 64, quarter), kind))
            arrived.append(pltpu.VMEM((16, width), kind))
        else:
            near1.append(pltpu.VMEM((3, 2, 2, 48, width) if order == "yz" else (3, 4, 48, width), kind))
            near2.append(pltpu.VMEM((4, 64, width), kind))
            ends.append(pltpu.VMEM((16, 128), kind))
            arrived.append(pltpu.VMEM((4, 16, width), kind))
    return own + theirs + near1 + near2 + ends + arrived


def last_kernel(*refs):
    count = len(SUMMED)
    grads = refs[:count]
    expert_from = refs[count : count + 2]
    rows_hbm, gates_high_ref, gates_low_ref, forward_ref = refs[count + 2 : count + 6]
    outs = refs[count + 6 : 2 * count + 6]
    expert_to = refs[2 * count + 6 : 2 * count + 8]
    block_ref = refs[2 * count + 8]
    scratch = refs[2 * count + 9 : 8 * count + 9]
    (
        rows_ref,
        swap_send,
        swap_recv,
        swap_local,
        send_sems,
        recv_sems,
        local_sems,
    ) = refs[8 * count + 9 :]
    me = place()
    partner = {"core": 1 - me["core"], "xl": 1 - lax.axis_index("xl")}
    crossed = me["core"] != lax.axis_index("xl")
    greet(ring_neighbours(me) + [partner])

    def moved(slot):
        return pltpu.make_async_remote_copy(
            src_ref=expert_from[slot],
            dst_ref=expert_to[slot],
            send_sem=swap_send.at[slot],
            recv_sem=swap_recv.at[slot],
            device_id=partner,
            device_id_type=MESH_ID,
        )

    def kept(slot):
        return pltpu.make_async_copy(expert_from[slot], expert_to[slot], swap_local.at[slot])

    wires = Wires(send_sems, recv_sems, local_sems)
    stages = Summing(wires, me, SUMMED, grads, outs, scratch).stages()
    next(stages)
    next(stages)

    @pl.when(crossed)
    def _():
        for slot in range(2):
            moved(slot).start()

    @pl.when(jnp.logical_not(crossed))
    def _():
        for slot in range(2):
            kept(slot).start()

    rows_in = wires.copy(rows_hbm, rows_ref)
    next(stages)
    next(stages)
    rows_in.wait()
    features = block_ref.shape[1]
    for left in range(0, features, 512):
        columns = pl.ds(left, 512)

        def mix(step, total):
            blocks = rows_ref[pl.ds(step * 16, 16), :, columns].astype(F32)
            rows = blocks.reshape(16 * CAP, 512).astype(BF16)
            at = pl.ds(pl.multiple_of(step * 16 * CAP, 128), 16 * CAP)
            return total + dot(gates_high_ref[:, at], rows) + dot(gates_low_ref[:, at], rows)

        mixed = lax.fori_loop(0, EXPERTS // 16, mix, forward_ref[:, columns])
        block_ref[:, columns] = mixed.astype(BF16)
    for _ in stages:
        pass
    wires.finish()

    @pl.when(crossed)
    def _():
        for slot in range(2):
            moved(slot).wait_recv()
            moved(slot).wait_send()

    @pl.when(jnp.logical_not(crossed))
    def _():
        for slot in range(2):
            kept(slot).wait()


def sum_last(grads, expert_grads, rows, gates_high, gates_low, forward_rows):
    anywhere = pl.BlockSpec(memory_space=pl.ANY)
    vmem = pl.BlockSpec(memory_space=pltpu.VMEM)
    count = len(SUMMED)
    return pl.pallas_call(
        last_kernel,
        out_shape=[jax.ShapeDtypeStruct((16, width), F32) for _, width, _ in SUMMED]
        + [jax.ShapeDtypeStruct(grad.shape, grad.dtype) for grad in expert_grads]
        + [jax.ShapeDtypeStruct(forward_rows.shape, BF16)],
        in_specs=[anywhere] * (count + 3) + [vmem] * 3,
        out_specs=[vmem] * count + [anywhere] * 2 + [vmem],
        scratch_shapes=summing_scratch(SUMMED)
        + [
            pltpu.VMEM(rows.shape, BF16),
            pltpu.SemaphoreType.DMA((2,)),
            pltpu.SemaphoreType.DMA((2,)),
            pltpu.SemaphoreType.DMA((2,)),
            pltpu.SemaphoreType.DMA((190,)),
            pltpu.SemaphoreType.DMA((190,)),
            pltpu.SemaphoreType.DMA((48,)),
        ],
        compiler_params=pltpu.CompilerParams(
            collective_id=1, has_side_effects=True, vmem_limit_bytes=56 * 1024 * 1024
        ),
        cost_estimate=pl.CostEstimate(
            flops=1_000_000_000, bytes_accessed=200_000_000, transcendentals=0
        ),
    )(*grads, *expert_grads, rows, gates_high, gates_low, forward_rows)


def col_device(col):
    return {"yh": col // 4, "xh": rem(col // 2, 2), "xl": rem(col, 2)}


def col_index():
    return lax.axis_index("yh") * 4 + lax.axis_index("xh") * 2 + lax.axis_index("xl")


VMEM_SPEC = pl.BlockSpec(memory_space=pltpu.VMEM)
GROUP = QUERY_HEADS // KEY_VALUE_HEADS
EXTRA = 128


def dot(left, right, left_dim=1, right_dim=0):
    return lax.dot_general(
        left, right, (((left_dim,), (right_dim,)), ((), ())), preferred_element_type=F32
    )


def rounded_parts(value):
    first = value.astype(BF16)
    left = value - first.astype(F32)
    second = left.astype(BF16)
    return [first, second, (left - second.astype(F32)).astype(BF16)]


def lane_column(index):
    return (lax.broadcasted_iota(jnp.int32, (16, 128), 1) == index).astype(BF16)


def gain_row(misc_ref, index):
    return dot(lane_column(index), misc_ref[...], 1, 1)[:1]


def allowed_pairs(marks_ref, segments_ref, rows, keys):
    me = col_index()
    shape = (rows, keys)
    own = segments_ref[:, :1]
    first_length = jnp.where(
        me == 0,
        jnp.sum((own == 0.0).astype(F32), axis=0, keepdims=True),
        marks_ref[:1, :1].astype(F32),
    )
    last_start = (me * rows).astype(F32) + jnp.sum(
        (own < 2.0).astype(F32), axis=0, keepdims=True
    )
    lowest = jnp.where(own == 0.0, 0.0, jnp.where(own == 1.0, first_length, last_start))
    key = lax.broadcasted_iota(jnp.int32, shape, 1)
    query = lax.broadcasted_iota(jnp.int32, shape, 0) + me * rows
    return (key <= query) & (key.astype(F32) >= lowest)


def head_columns(ref, group):
    width = GROUP * HEAD_SIZE
    return jnp.concatenate(
        [
            ref[:, group * width + head * HEAD_SIZE : group * width + (head + 1) * HEAD_SIZE]
            for head in range(GROUP)
        ],
        axis=0,
    )


def head_weights(queries, keys, allowed):
    scores = dot(queries, keys, 1, 1) * (HEAD_SIZE ** (-0.5))
    scores = jnp.where(allowed, scores, -1e30)
    shifted = jnp.exp(scores - jnp.max(scores, axis=1, keepdims=True))
    return shifted / jnp.sum(shifted, axis=1, keepdims=True)


GROUP_BLOCKS = 16
MIDDLE_MIB = 61


def blocks_of(value):
    return value.reshape(GROUP_BLOCKS, CAP, value.shape[-1]).astype(BF16)


def later_kernel(
    tokens_ref,
    misc_ref,
    marks_ref,
    query_ref,
    keyval_ref,
    slots_ref,
    cotangent_ref,
    out_ref,
    marks_out,
    normed_ref,
    queries_ref,
    rows_out,
    rows_ref,
    own_ref,
    send_sems,
    recv_sems,
    local_sem,
):
    me = col_index()
    rows = own_ref.shape[0]
    tail = marks_ref.shape[0]
    late = pl.ds(rows - tail, tail)
    features = tokens_ref.shape[1]
    gain = gain_row(misc_ref, EXPERTS)
    total = jnp.zeros((rows, 1), F32)
    for left in range(0, features, 512):
        piece = tokens_ref[:, left : left + 512].astype(F32)
        total = total + jnp.sum(piece * piece, axis=1, keepdims=True)
    scale = lax.rsqrt(total / features + EPSILON)
    for left in range(0, features, 512):
        piece = tokens_ref[:, left : left + 512].astype(F32)
        normed_ref[:, left : left + 512] = (piece * scale * gain[:, left : left + 512]).astype(BF16)
    normed = normed_ref[...]
    for left in range(0, own_ref.shape[1], 512):
        own_ref[:, left : left + 512] = dot(normed, keyval_ref[:, left : left + 512]).astype(BF16)
    greet([col_device(rem(me + far, 8)) for far in range(1, 8)])

    def copies(far, first):
        there = col_device(rem(me + far, 8))
        pairs = [(own_ref, out_ref.at[me])]
        if first:
            pairs = [(own_ref.at[late], out_ref.at[0, late]), (marks_ref, marks_out)]
        return [
            pltpu.make_async_remote_copy(
                src_ref=source,
                dst_ref=target,
                send_sem=send_sems.at[far, number],
                recv_sem=recv_sems.at[far, number],
                device_id=there,
                device_id_type=MESH_ID,
            )
            for number, (source, target) in enumerate(pairs)
        ]

    def each(far, first, condition, act):
        @pl.when(condition)
        def _():
            for copy in copies(far, first):
                act(copy)

    for far in range(7, 0, -1):
        each(far, False, (me > 0) & (me + far < 8), lambda copy: copy.start())
        each(far, True, me == 0, lambda copy: copy.start())
    keep = pltpu.make_async_copy(own_ref, out_ref.at[me], local_sem.at[0])
    keep.start()
    for left in range(0, queries_ref.shape[1], 512):
        queries_ref[:, left : left + 512] = dot(normed, query_ref[:, left : left + 512]).astype(
            BF16
        )
    tile = GROUP_BLOCKS * CAP

    def fill(step, carry):
        slots = slots_ref[pl.ds(pl.multiple_of(step * tile, 128), tile)]
        blocks = pl.ds(step * GROUP_BLOCKS, GROUP_BLOCKS)
        for left in range(0, features, 512):
            rows_ref[blocks, :, left : left + 512] = blocks_of(
                dot(slots, cotangent_ref[:, left : left + 512])
            )
        return carry

    lax.fori_loop(0, EXPERTS // GROUP_BLOCKS, fill, 0)
    laid = pltpu.make_async_copy(rows_ref, rows_out, local_sem.at[1])
    laid.start()

    @pl.when(me == 0)
    def _():
        marks_out[...] = marks_ref[...]

    @pl.when(me > 0)
    def _():
        out_ref[0, : rows - tail] = jnp.zeros((rows - tail, own_ref.shape[1]), own_ref.dtype)

    for far in range(1, 8):

        @pl.when(me + far < 8)
        def _():
            out_ref[me + far] = jnp.zeros(own_ref.shape, own_ref.dtype)

    keep.wait()
    for far in range(1, 8):
        each(far, False, me > far, lambda copy: copy.wait_recv())
        each(far, True, me == far, lambda copy: copy.wait_recv())
        each(far, False, (me > 0) & (me + far < 8), lambda copy: copy.wait_send())
        each(far, True, me == 0, lambda copy: copy.wait_send())
    laid.wait()


def to_later(tokens, misc, marks, query_w, keyval_w, slots_down, cotangent):
    vmem = pl.BlockSpec(memory_space=pltpu.VMEM)
    own = (tokens.shape[0], keyval_w.shape[1])
    laid = (EXPERTS, CAP, tokens.shape[1])
    return pl.pallas_call(
        later_kernel,
        out_shape=[
            jax.ShapeDtypeStruct((8,) + own, BF16),
            jax.ShapeDtypeStruct(marks.shape, marks.dtype),
            jax.ShapeDtypeStruct(tokens.shape, BF16),
            jax.ShapeDtypeStruct((tokens.shape[0], query_w.shape[1]), BF16),
            jax.ShapeDtypeStruct(laid, BF16),
        ],
        in_specs=[vmem] * 7,
        out_specs=[vmem] * 4 + [pl.BlockSpec(memory_space=pl.ANY)],
        scratch_shapes=[
            pltpu.VMEM(laid, BF16),
            pltpu.VMEM(own, BF16),
            pltpu.SemaphoreType.DMA((8, 2)),
            pltpu.SemaphoreType.DMA((8, 2)),
            pltpu.SemaphoreType.DMA((2,)),
        ],
        compiler_params=pltpu.CompilerParams(
            collective_id=2, has_side_effects=True, vmem_limit_bytes=28 * 1024 * 1024
        ),
        cost_estimate=pl.CostEstimate(
            flops=1_000_000_000, bytes_accessed=80_000_000, transcendentals=0
        ),
    )(tokens, misc, marks, query_w, keyval_w, slots_down, cotangent)


def middle_kernel(
    queries_ref,
    every_ref,
    marks_ref,
    segments_ref,
    tokens_ref,
    misc_ref,
    named_ref,
    slots_ref,
    slots_down_ref,
    owner_ref,
    cotangent_ref,
    outt_hbm,
    shgate_hbm,
    shup_hbm,
    shdt_hbm,
    cotangent_rows,
    attended_ref,
    residual_ref,
    normed_ref,
    gates_ref,
    gates_high_ref,
    gates_low_ref,
    forward_ref,
    grad_second_ref,
    grad_received,
    outgoing_hbm,
    grad_shgate_hbm,
    grad_shup_hbm,
    grad_shdt_hbm,
    outt_ref,
    shgate_ref,
    shup_ref,
    shdt_ref,
    grad_shgate,
    grad_shup,
    grad_shdt,
    outgoing,
    send_sems,
    recv_sems,
    local_sems,
):
    rows, features = tokens_ref.shape
    width = KEY_VALUE_HEADS * HEAD_SIZE
    keys_count = 8 * rows
    spot = place()
    chips = [chip_at(spot, offset) for offset in OFFSETS]
    mine = chip_at(spot, (0, 0, 0))[1]
    greet([where for where, _ in chips])
    wires = Wires(send_sems, recv_sems, local_sems)
    travelling = [
        wires.remote(cotangent_rows.at[holder], grad_received.at[mine], where)
        for where, holder in chips
    ]
    staying = [wires.copy(cotangent_rows.at[mine], grad_received.at[mine])]
    outt_in = wires.copy(outt_hbm, outt_ref)
    shared_in = [
        wires.copy(shgate_hbm, shgate_ref),
        wires.copy(shup_hbm, shup_ref),
        wires.copy(shdt_hbm, shdt_ref),
    ]
    allowed = allowed_pairs(marks_ref, segments_ref, rows, keys_count)
    allowed = jnp.concatenate([allowed.astype(F32)] * GROUP, axis=0) > 0.5
    for group in range(KEY_VALUE_HEADS):
        queries = head_columns(queries_ref, group)
        columns = pl.ds(group * HEAD_SIZE, HEAD_SIZE)
        keys = every_ref[:, :, columns].reshape(keys_count, HEAD_SIZE)
        values = every_ref[:, :, pl.ds(width + group * HEAD_SIZE, HEAD_SIZE)].reshape(
            keys_count, HEAD_SIZE
        )
        weights = head_weights(queries, keys, allowed)
        mixed = dot(weights.astype(BF16), values).astype(BF16)
        for head in range(GROUP):
            at = (group * GROUP + head) * HEAD_SIZE
            attended_ref[:, at : at + HEAD_SIZE] = mixed[head * rows : (head + 1) * rows]
    attended = attended_ref[...]
    outt_in.wait()
    total = jnp.zeros((rows, 1), F32)
    for left in range(0, features, 512):
        piece = tokens_ref[:, left : left + 512].astype(F32) + dot(
            attended, outt_ref[left : left + 512], 1, 1
        )
        residual_ref[:, left : left + 512] = piece
        total = total + jnp.sum(piece * piece, axis=1, keepdims=True)
    scale = lax.rsqrt(total / features + EPSILON)
    normed_ref[...] = (residual_ref[...] * scale * gain_row(misc_ref, EXPERTS + 1)).astype(BF16)
    normed = normed_ref[...]
    logits = dot(normed, misc_ref[...])
    named = named_ref[...] > 0.5
    chosen = jnp.where(named, logits, -1e30)
    chosen_exp = jnp.where(named, jnp.exp(chosen - jnp.max(chosen, axis=1, keepdims=True)), 0.0)
    gates = chosen_exp / jnp.sum(chosen_exp, axis=1, keepdims=True)
    gates_ref[...] = gates
    parts = jnp.concatenate(rounded_parts(gates), axis=1)
    tile = GROUP_BLOCKS * CAP

    def fill(step, carry):
        at = pl.ds(pl.multiple_of(step * tile, 128), tile)
        blocks = pl.ds(step * GROUP_BLOCKS, GROUP_BLOCKS)
        slots = slots_down_ref[at]
        for left in range(0, features, 512):
            outgoing[blocks, :, left : left + 512] = blocks_of(
                dot(slots, normed_ref[:, left : left + 512])
            )
        gate_parts = dot(slots, parts)
        owner = owner_ref[at].astype(F32)
        lane = lax.broadcasted_iota(jnp.int32, (tile, EXTRA), 1)
        extra = jnp.zeros((tile, EXTRA), F32)
        for part in range(3):
            column = jnp.sum(
                gate_parts[:, part * 128 : (part + 1) * 128] * owner, axis=1, keepdims=True
            )
            extra = jnp.where(lane == part, column, extra)
        outgoing[blocks, :, features:] = blocks_of(extra)
        return carry

    lax.fori_loop(0, EXPERTS // GROUP_BLOCKS, fill, 0)
    staying.append(wires.copy(outgoing, outgoing_hbm))

    slot_gates = jnp.zeros((rows, slots_ref.shape[1]), F32)
    for part in range(3):
        slot_gates = slot_gates + dot(
            parts[:, part * 128 : (part + 1) * 128], owner_ref[...], 1, 1
        )
    slot_gates = slot_gates * slots_ref[...].astype(F32)
    gates_high = slot_gates.astype(BF16)
    gates_high_ref[...] = gates_high
    gates_low_ref[...] = (slot_gates - gates_high.astype(F32)).astype(BF16)

    for copy in shared_in:
        copy.wait()
    cotangent = cotangent_ref[...]
    gate_pre = dot(normed, shgate_ref[...])
    up_pre = dot(normed, shup_ref[...])
    sigmoid = 1.0 / (1.0 + jnp.exp(-gate_pre))
    silu = gate_pre * sigmoid
    hidden = (silu * up_pre).astype(BF16)
    grad_hidden = dot(cotangent, shdt_ref[...])
    grad_gate = (
        grad_hidden * up_pre * sigmoid * (1.0 + gate_pre * (1.0 - sigmoid))
    ).astype(BF16)
    grad_up = (grad_hidden * silu).astype(BF16)
    for left in range(0, features, 512):
        columns = pl.ds(left, 512)
        forward_ref[:, columns] = residual_ref[:, columns] + dot(hidden, shdt_ref[columns], 1, 1)
        grad_second_ref[:, columns] = dot(grad_gate, shgate_ref[columns], 1, 1) + dot(
            grad_up, shup_ref[columns], 1, 1
        )
        grad_shgate[columns] = dot(normed_ref[:, columns], grad_gate, 0, 0).astype(BF16)
        grad_shup[columns] = dot(normed_ref[:, columns], grad_up, 0, 0).astype(BF16)
        grad_shdt[columns] = dot(cotangent_ref[:, columns], hidden, 0, 0).astype(BF16)
    staying += [
        wires.copy(grad_shgate, grad_shgate_hbm),
        wires.copy(grad_shup, grad_shup_hbm),
        wires.copy(grad_shdt, grad_shdt_hbm),
    ]
    for copy in staying:
        copy.wait()
    for copy in travelling:
        copy.wait_recv()
    wires.finish()


def middle(queries, every, marks, segments, tokens, misc, named, slots, slots_down, owner, cotangent,
           cotangent_rows, outt, shgate, shup, shdt):
    rows, features = tokens.shape
    slot_count = slots.shape[1]
    anywhere = pl.BlockSpec(memory_space=pl.ANY)
    inputs = (queries, every, marks, segments, tokens, misc, named, slots, slots_down, owner,
              cotangent, outt, shgate, shup, shdt)
    shared = [shgate.shape, shup.shape, shdt.shape]
    wide = cotangent_rows.shape[:2] + (features + EXTRA,)
    return pl.pallas_call(
        middle_kernel,
        out_shape=[
            jax.ShapeDtypeStruct((rows, features), BF16),
            jax.ShapeDtypeStruct((rows, features), F32),
            jax.ShapeDtypeStruct((rows, features), BF16),
            jax.ShapeDtypeStruct((rows, 128), F32),
            jax.ShapeDtypeStruct((rows, slot_count), BF16),
            jax.ShapeDtypeStruct((rows, slot_count), BF16),
            jax.ShapeDtypeStruct((rows, features), F32),
            jax.ShapeDtypeStruct((rows, features), F32),
            jax.ShapeDtypeStruct(cotangent_rows.shape, BF16),
            jax.ShapeDtypeStruct(wide, BF16),
        ]
        + [jax.ShapeDtypeStruct(shape, BF16) for shape in shared],
        in_specs=[VMEM_SPEC] * 11 + [anywhere] * 5,
        out_specs=[VMEM_SPEC] * 8 + [anywhere] * 5,
        scratch_shapes=[pltpu.VMEM(outt.shape, BF16)]
        + [pltpu.VMEM(shape, BF16) for shape in shared + shared]
        + [
            pltpu.VMEM(wide, BF16),
            pltpu.SemaphoreType.DMA((64,)),
            pltpu.SemaphoreType.DMA((64,)),
            pltpu.SemaphoreType.DMA((10,)),
        ],
        compiler_params=pltpu.CompilerParams(
            collective_id=5, has_side_effects=True, vmem_limit_bytes=MIDDLE_MIB * 1024 * 1024
        ),
        cost_estimate=pl.CostEstimate(
            flops=10_000_000_000, bytes_accessed=250_000_000, transcendentals=2_000_000
        ),
    )(*inputs, cotangent_rows)


def expert_kernel(
    outgoing_ref,
    cotangent_in,
    weight_hbm,
    down_hbm,
    returned_ref,
    rows_out,
    own_in_hbm,
    other_in_hbm,
    own_down_hbm,
    other_down_hbm,
    weight_ref,
    down_ref,
    own_in_ref,
    other_in_ref,
    own_down_ref,
    other_down_ref,
    landed,
    cotangents,
    back,
    grads,
    hiddens,
    gated,
    rows_staged,
    send_sems,
    recv_sems,
    local_sems,
):
    features = cotangent_in.shape[2]
    spot = place()
    chips = [chip_at(spot, offset) for offset in OFFSETS]
    sources = [chip_at(spot, offset, -1) for offset in OFFSETS]
    mine = chip_at(spot, (0, 0, 0))[1]
    holders = [mine] + [holder for _, holder in sources]
    wires = Wires(send_sems, recv_sems, local_sems)
    weights_in = [wires.copy(weight_hbm, weight_ref), wires.copy(down_hbm, down_ref)]
    greet([where for where, _ in chips])
    rows_in = [wires.copy(outgoing_ref.at[mine], landed.at[0])]
    for number, (where, holder) in enumerate(chips):
        rows_in.append(wires.remote(outgoing_ref.at[holder], landed.at[number + 1], where))
    brought = [
        wires.copy(cotangent_in.at[holder], cotangents.at[number])
        for number, holder in enumerate(holders)
    ]
    for copy in weights_in:
        copy.wait()
    count = len(holders)
    tile = GROUP_BLOCKS * CAP
    returning = []

    def flat(ref, first, columns):
        blocks = ref[first : first + GROUP_BLOCKS, :, columns].astype(F32)
        return blocks.reshape(tile, blocks.shape[-1]).astype(BF16)

    for first in range(0, count, GROUP_BLOCKS):
        for number in range(first, first + GROUP_BLOCKS):
            brought[number].wait()
            if number == 0:
                rows_in[number].wait()
            else:
                rows_in[number].wait_recv()
        at = pl.ds(first * CAP, tile)
        extra = flat(landed, first, pl.ds(features, EXTRA)).astype(F32)
        gate = extra[:, :1] + extra[:, 1:2] + extra[:, 2:3]
        everything = pl.ds(0, features)
        pre = dot(flat(landed, first, everything), weight_ref[...])
        grad_hidden = dot(flat(cotangents, first, everything), down_ref[...], 1, 1)
        along = jnp.zeros((tile, 1), F32)
        for part in range(2):
            base = part * 2 * HALF
            gate_pre, up_pre = pre[:, base : base + HALF], pre[:, base + HALF : base + 2 * HALF]
            grad_part = grad_hidden[:, part * HALF : (part + 1) * HALF]
            sigmoid = 1.0 / (1.0 + jnp.exp(-gate_pre))
            silu = gate_pre * sigmoid
            hidden = silu * up_pre
            along = along + jnp.sum(hidden * grad_part, axis=1, keepdims=True)
            gated_grad = grad_part * gate
            grads[at, base : base + HALF] = (
                gated_grad * up_pre * sigmoid * (1.0 + gate_pre * (1.0 - sigmoid))
            ).astype(BF16)
            grads[at, base + HALF : base + 2 * HALF] = (gated_grad * silu).astype(BF16)
            hiddens[at, part * HALF : (part + 1) * HALF] = hidden.astype(BF16)
            gated[at, part * HALF : (part + 1) * HALF] = (hidden * gate).astype(BF16)
        group_grads = grads[at]
        for left in range(0, features, 512):
            back[first : first + GROUP_BLOCKS, :, left : left + 512] = blocks_of(
                dot(group_grads, weight_ref[left : left + 512], 1, 1)
            )
        lane = lax.broadcasted_iota(jnp.int32, (tile, EXTRA), 1)
        value = jnp.zeros((tile, EXTRA), F32)
        for part, column in enumerate(rounded_parts(along)):
            value = jnp.where(lane == part, column.astype(F32), value)
        back[first : first + GROUP_BLOCKS, :, features:] = blocks_of(value)
        for number in range(first, first + GROUP_BLOCKS):
            if number == 0:
                kept = wires.copy(back.at[0], returned_ref.at[mine])
            else:
                returning.append(
                    wires.remote(back.at[number], returned_ref.at[mine], sources[number - 1][0])
                )
    staged = []
    for index, first in enumerate(range(0, count, GROUP_BLOCKS)):
        group_hidden = hiddens[pl.ds(first * CAP, tile)]
        slot = index % 2
        if index >= 2:
            for copy in staged[index - 2]:
                copy.wait()
        for left in range(0, features, 512):
            columns = pl.ds(left, 512)
            rows_staged[slot, :, :, left : left + 512] = blocks_of(
                dot(group_hidden, down_ref[:, columns])
            )
        staged.append(
            [
                wires.copy(rows_staged.at[slot, number], rows_out.at[holders[first + number]])
                for number in range(GROUP_BLOCKS)
            ]
        )

    def every_row(ref, columns):
        return ref[:, :, columns].astype(F32).reshape(count * CAP, 256).astype(BF16)

    def weight_gradients(step, carry):
        columns = pl.ds(pl.multiple_of(step * 256, 256), 256)
        rows = every_row(landed, columns)
        own_in_ref[columns] = dot(rows, grads[:, : 2 * HALF], 0, 0)
        other_in_ref[columns] = dot(rows, grads[:, 2 * HALF :], 0, 0).astype(BF16)
        rows = every_row(cotangents, columns)
        own_down_ref[:, columns] = dot(gated[:, :HALF], rows, 0, 0)
        other_down_ref[:, columns] = dot(gated[:, HALF:], rows, 0, 0).astype(BF16)
        return carry

    lax.fori_loop(0, features // 256, weight_gradients, 0)
    staged.append(
        [
            wires.copy(own_in_ref, own_in_hbm),
            wires.copy(other_in_ref, other_in_hbm),
            wires.copy(own_down_ref, own_down_hbm),
            wires.copy(other_down_ref, other_down_hbm),
        ]
    )
    for copies in staged[-3:]:
        for copy in copies:
            copy.wait()
    kept.wait()
    for copy in returning:
        copy.wait_recv()
    wires.finish()


def expert(outgoing, grad_received, weight, down):
    count, cap, features = grad_received.shape
    anywhere = pl.BlockSpec(memory_space=pl.ANY)
    return pl.pallas_call(
        expert_kernel,
        out_shape=[
            jax.ShapeDtypeStruct(outgoing.shape, BF16),
            jax.ShapeDtypeStruct(grad_received.shape, BF16),
            jax.ShapeDtypeStruct((features, 2 * HALF), F32),
            jax.ShapeDtypeStruct((features, 2 * HALF), BF16),
            jax.ShapeDtypeStruct((HALF, features), F32),
            jax.ShapeDtypeStruct((HALF, features), BF16),
        ],
        in_specs=[anywhere] * 4,
        out_specs=[anywhere] * 6,
        scratch_shapes=[
            pltpu.VMEM(weight.shape, BF16),
            pltpu.VMEM(down.shape, BF16),
            pltpu.VMEM((features, 2 * HALF), F32),
            pltpu.VMEM((features, 2 * HALF), BF16),
            pltpu.VMEM((HALF, features), F32),
            pltpu.VMEM((HALF, features), BF16),
            pltpu.VMEM(outgoing.shape, BF16),
            pltpu.VMEM(grad_received.shape, BF16),
            pltpu.VMEM(outgoing.shape, BF16),
            pltpu.VMEM((count * cap, 4 * HALF), BF16),
            pltpu.VMEM((count * cap, 2 * HALF), BF16),
            pltpu.VMEM((count * cap, 2 * HALF), BF16),
            pltpu.VMEM((2, GROUP_BLOCKS, cap, features), BF16),
            pltpu.SemaphoreType.DMA((128,)),
            pltpu.SemaphoreType.DMA((128,)),
            pltpu.SemaphoreType.DMA((144,)),
        ],
        compiler_params=pltpu.CompilerParams(
            collective_id=4, has_side_effects=True, vmem_limit_bytes=61 * 1024 * 1024
        ),
        cost_estimate=pl.CostEstimate(
            flops=22_000_000_000, bytes_accessed=300_000_000, transcendentals=1_000_000
        ),
    )(outgoing, grad_received, weight, down)


def back_to_residual(
    grad_back_ref,
    slots_ref,
    owner_ref,
    gates_ref,
    cotangent_ref,
    residual_ref,
    partial_ref,
    misc_ref,
    outt_ref,
    grad_residual_ref,
    grad_low_ref,
    grad_logits_ref,
    grad_gain_ref,
    grad_attended,
):
    rows, features = cotangent_ref.shape
    slots = slots_ref[...]
    extra = grad_back_ref[:, features:].astype(F32)
    owner = owner_ref[...].astype(F32)
    grad_gates = jnp.zeros((rows, 128), F32)
    for part in range(3):
        grad_gates = grad_gates + dot(slots, (owner * extra[:, part : part + 1]).astype(BF16))
    gates = gates_ref[...]
    grad_logits = (
        gates * (grad_gates - jnp.sum(gates * grad_gates, axis=1, keepdims=True))
    ).astype(BF16)
    grad_logits_ref[...] = grad_logits
    gain = gain_row(misc_ref, EXPERTS + 1)
    square, inner = jnp.zeros((rows, 1), F32), jnp.zeros((rows, 1), F32)
    for left in range(0, features, 512):
        columns = pl.ds(left, 512)
        piece = (
            partial_ref[:, columns]
            + dot(slots, grad_back_ref[:, columns])
            + dot(grad_logits, misc_ref[columns], 1, 1)
        )
        grad_residual_ref[:, columns] = piece
        residual = residual_ref[:, columns]
        square = square + jnp.sum(residual * residual, axis=1, keepdims=True)
        inner = inner + jnp.sum(
            piece * gain[:, left : left + 512] * residual, axis=1, keepdims=True
        )
    scale = lax.rsqrt(square / features + EPSILON)
    cubed = scale * scale * scale * (inner / features)
    for left in range(0, features, 512):
        columns = pl.ds(left, 512)
        piece = grad_residual_ref[:, columns]
        residual = residual_ref[:, columns]
        grad_gain_ref[:, columns] = jnp.broadcast_to(
            jnp.sum(piece * residual * scale, axis=0, keepdims=True), (8, 512)
        )
        value = (
            cotangent_ref[:, columns].astype(F32)
            + scale * piece * gain[:, left : left + 512]
            - residual * cubed
        )
        grad_residual_ref[:, columns] = value
        grad_low_ref[:, columns] = value.astype(BF16)
    grad_low = grad_low_ref[...]
    for left in range(0, features, 512):
        columns = pl.ds(left, 512)
        grad_attended[:, columns] = dot(grad_low, outt_ref[:, columns]).astype(BF16)


def back_heads(
    group, allowed, qkv_ref, every_ref, grad_attended, grad_queries_ref, partial_keyvals
):
    rows = qkv_ref.shape[0]
    width = KEY_VALUE_HEADS * HEAD_SIZE
    keys_count = 8 * rows
    score_scale = HEAD_SIZE ** (-0.5)
    queries = head_columns(qkv_ref, group)
    heads_gradient = head_columns(grad_attended, group)
    key_columns = pl.ds(group * HEAD_SIZE, HEAD_SIZE)
    value_columns = pl.ds(width + group * HEAD_SIZE, HEAD_SIZE)
    keys = every_ref[:, :, key_columns].reshape(keys_count, HEAD_SIZE)
    values = every_ref[:, :, value_columns].reshape(keys_count, HEAD_SIZE)
    weights = head_weights(queries, keys, allowed)
    grad_weights = dot(heads_gradient, values, 1, 1)
    inner_sum = jnp.sum(weights * grad_weights, axis=1, keepdims=True)
    grad_scores = (weights * (grad_weights - inner_sum)).astype(BF16)
    grad_queries = (dot(grad_scores, keys) * score_scale).astype(BF16)
    for head in range(GROUP):
        at = (group * GROUP + head) * HEAD_SIZE
        grad_queries_ref[:, at : at + HEAD_SIZE] = grad_queries[head * rows : (head + 1) * rows]
    partial_keyvals[:, :, key_columns] = (
        (dot(grad_scores, queries, 0, 0) * score_scale).astype(BF16).reshape(8, rows, HEAD_SIZE)
    )
    partial_keyvals[:, :, value_columns] = (
        dot(weights.astype(BF16), heads_gradient, 0, 0).astype(BF16).reshape(8, rows, HEAD_SIZE)
    )


EARLY_ROWS = 20


def rear_kernel(tail, *refs):
    (
        slots_ref,
        owner_ref,
        gates_ref,
        cotangent_ref,
        residual_ref,
        partial_ref,
        misc_ref,
        qkv_ref,
        marks_ref,
        segments_ref,
        attended_ref,
        normed1_ref,
        normed2_ref,
        tokens_ref,
        grad_back_hbm,
        outt_hbm,
        every_hbm,
        own_in_hbm,
        own_down_hbm,
        query_hbm,
        keyval_hbm,
        in_ref,
        down_ref,
        rows_ref,
    ) = refs[:24]
    (
        grad_tokens_ref,
        grad_outt_hbm,
        grad_query_hbm,
        grad_keyval_hbm,
        grad_misc_hbm,
        half_in_hbm,
        half_down_hbm,
        rows_out,
    ) = refs[24:32]
    (
        grad_back_ref,
        outt_ref,
        every_ref,
        own_in_ref,
        own_down_ref,
        grad_outt_ref,
        grad_query_ref,
        grad_keyval_ref,
        grad_misc_ref,
        grad_residual,
        grad_low,
        grad_logits,
        grad_gain,
        grad_attended,
        grad_queries,
        grad_first,
        blocks_ref,
        landed,
        query_ref,
        keyval_ref,
        their_in,
        their_down,
        sequence_send,
        sequence_recv,
        send_sems,
        recv_sems,
        local_sems,
    ) = refs[32:]
    me = col_index()
    spot = place()
    chips = [chip_at(spot, offset) for offset in OFFSETS]
    mine = chip_at(spot, (0, 0, 0))[1]
    rows, features = tokens_ref.shape
    late = pl.ds(rows - tail, tail)
    sibling = {"core": 1 - spot["core"]}
    greet([where for where, _ in chips] + [sibling])
    wires = Wires(send_sems, recv_sems, local_sems)
    fetched = [
        wires.copy(grad_back_hbm, grad_back_ref),
        wires.copy(outt_hbm, outt_ref),
        wires.copy(every_hbm, every_ref),
        wires.copy(query_hbm, query_ref),
        wires.copy(keyval_hbm, keyval_ref),
        wires.copy(own_in_hbm, own_in_ref),
        wires.copy(own_down_hbm, own_down_ref),
    ]
    halves_in = [
        wires.remote(in_ref, their_in, sibling),
        wires.remote(down_ref, their_down, sibling),
    ]
    kept = wires.copy(rows_ref.at[mine], rows_out.at[mine])
    returning = []

    def send_rows(start, stop):
        for where, holder in chips[start:stop]:
            returning.append(wires.remote(rows_ref.at[holder], rows_out.at[mine], where))

    send_rows(0, EARLY_ROWS)
    for fetch in fetched[:3]:
        fetch.wait()
    back_to_residual(
        grad_back_ref,
        slots_ref,
        owner_ref,
        gates_ref,
        cotangent_ref,
        residual_ref,
        partial_ref,
        misc_ref,
        outt_ref,
        grad_residual,
        grad_low,
        grad_logits,
        grad_gain,
        grad_attended,
    )
    allowed = allowed_pairs(marks_ref, segments_ref, rows, 8 * rows)
    allowed = jnp.concatenate([allowed.astype(F32)] * GROUP, axis=0) > 0.5
    for group in range(KEY_VALUE_HEADS):
        back_heads(
            group, allowed, qkv_ref, every_ref, grad_attended, grad_queries, blocks_ref
        )

    def copy(far, first_block):
        block = rem(me + 8 - far, 8)
        source, target = blocks_ref.at[block], landed.at[far]
        if first_block:
            source, target = blocks_ref.at[0, late], landed.at[far, late]
        return pltpu.make_async_remote_copy(
            src_ref=source,
            dst_ref=target,
            send_sem=sequence_send.at[far],
            recv_sem=sequence_recv.at[far],
            device_id=col_device(block),
            device_id_type=MESH_ID,
        )

    def each(far, first_block, condition, act):
        @pl.when(condition)
        def _():
            act(copy(far, first_block))

    for far in range(7, 0, -1):
        each(far, False, me > far, lambda moved: moved.start())
        each(far, True, me == far, lambda moved: moved.start())
    send_rows(EARLY_ROWS, 63)

    @pl.when(me == 0)
    def _():
        for far in range(1, 8):
            landed[far, : rows - tail] = jnp.zeros((rows - tail, landed.shape[2]), landed.dtype)

    for far in range(1, 8):

        @pl.when(me + far >= 8)
        def _():
            landed[far] = jnp.zeros(landed.shape[1:], landed.dtype)

    low, attended, queries = grad_low[...], attended_ref[...], grad_queries[...]
    for left in range(0, features, 512):
        columns = pl.ds(left, 512)
        grad_outt_ref[columns] = dot(grad_low[:, columns], attended, 0, 0).astype(BF16)
        grad_query_ref[columns] = dot(normed1_ref[:, columns], queries, 0, 0).astype(BF16)
    stored = [
        wires.copy(grad_outt_ref, grad_outt_hbm),
        wires.copy(grad_query_ref, grad_query_hbm),
    ]
    for fetch in fetched[3:]:
        fetch.wait()
    for left in range(0, features, 512):
        columns = pl.ds(left, 512)
        grad_first[:, columns] = dot(queries, query_ref[columns], 1, 1)
    for copy_in in halves_in:
        copy_in.wait_recv()
    for left in range(0, features, 512):
        columns = pl.ds(left, 512)
        their_in[columns] = (own_in_ref[columns] + their_in[columns].astype(F32)).astype(BF16)
        their_down[:, columns] = (
            own_down_ref[:, columns] + their_down[:, columns].astype(F32)
        ).astype(BF16)
    stored += [wires.copy(their_in, half_in_hbm), wires.copy(their_down, half_down_hbm)]
    for far in range(1, 8):
        each(far, False, (me > 0) & (me + far < 8), lambda moved: moved.wait_recv())
        each(far, True, me == 0, lambda moved: moved.wait_recv())
    grad_keyvals = grad_low.at[:, pl.ds(0, keyval_ref.shape[1])]
    for row in range(0, rows, 16):
        at = pl.ds(row, 16)
        value = blocks_ref[me, at].astype(F32)
        for far in range(1, 8):
            value = value + landed[far, at].astype(F32)
        grad_keyvals[at] = value.astype(BF16)
    keyvals = grad_keyvals[...]
    gain = gain_row(misc_ref, EXPERTS)
    square, inner = jnp.zeros((rows, 1), F32), jnp.zeros((rows, 1), F32)
    for left in range(0, features, 512):
        columns = pl.ds(left, 512)
        grad_keyval_ref[columns] = dot(normed1_ref[:, columns], keyvals, 0, 0).astype(BF16)
        piece = grad_first[:, columns] + dot(keyvals, keyval_ref[columns], 1, 1)
        grad_first[:, columns] = piece
        residual = tokens_ref[:, columns].astype(F32)
        square = square + jnp.sum(residual * residual, axis=1, keepdims=True)
        inner = inner + jnp.sum(
            piece * gain[:, left : left + 512] * residual, axis=1, keepdims=True
        )
    stored.append(wires.copy(grad_keyval_ref, grad_keyval_hbm))
    scale = lax.rsqrt(square / features + EPSILON)
    cubed = scale * scale * scale * (inner / features)
    logits = grad_logits[...]
    one_row = (lax.broadcasted_iota(jnp.int32, (16, 128), 0) == 0).astype(F32)
    lane = lax.broadcasted_iota(jnp.int32, (16, 128), 1)
    for left in range(0, features, 512):
        columns = pl.ds(left, 512)
        piece = grad_first[:, columns]
        residual = tokens_ref[:, columns].astype(F32)
        grad_tokens_ref[:, columns] = (
            grad_residual[:, columns]
            + scale * piece * gain[:, left : left + 512]
            - residual * cubed
        )
        total = dot(normed2_ref[:, columns], logits, 0, 0)
        rows1 = jnp.broadcast_to(
            jnp.sum(piece * residual * scale, axis=0, keepdims=True), (16, 512)
        )
        rows2 = jnp.broadcast_to(grad_gain[:1, columns], (16, 512))
        for index, gradient in ((EXPERTS, rows1), (EXPERTS + 1, rows2)):
            spread = (one_row * (lane == index).astype(F32)).astype(BF16)
            for part in rounded_parts(gradient):
                total = total + dot(part, spread, 0, 0)
        grad_misc_ref[columns] = total
    stored.append(wires.copy(grad_misc_ref, grad_misc_hbm))
    for far in range(1, 8):
        each(far, False, me > far, lambda moved: moved.wait_send())
        each(far, True, me == far, lambda moved: moved.wait_send())
    for copy_out in stored:
        copy_out.wait()
    kept.wait()
    for moved in returning:
        moved.wait_recv()
    wires.finish()


def rear(tail, inputs, grad_back, outt, every, own_in, own_down, query_w, keyval_w, expert_in,
         expert_down, rows_back):
    rows, features = inputs[3].shape
    anywhere = pl.BlockSpec(memory_space=pl.ANY)
    return pl.pallas_call(
        functools.partial(rear_kernel, tail),
        out_shape=[
            jax.ShapeDtypeStruct((rows, features), F32),
            jax.ShapeDtypeStruct((features, features), BF16),
            jax.ShapeDtypeStruct(query_w.shape, BF16),
            jax.ShapeDtypeStruct(keyval_w.shape, BF16),
            jax.ShapeDtypeStruct((features, 128), F32),
            jax.ShapeDtypeStruct(expert_in.shape, BF16),
            jax.ShapeDtypeStruct(expert_down.shape, BF16),
            jax.ShapeDtypeStruct(rows_back.shape, BF16),
        ],
        in_specs=[VMEM_SPEC] * 14 + [anywhere] * 10,
        out_specs=[VMEM_SPEC] + [anywhere] * 7,
        scratch_shapes=[
            pltpu.VMEM(grad_back.shape, BF16),
            pltpu.VMEM(outt.shape, BF16),
            pltpu.VMEM(every.shape, BF16),
            pltpu.VMEM(own_in.shape, F32),
            pltpu.VMEM(own_down.shape, F32),
            pltpu.VMEM((features, features), BF16),
            pltpu.VMEM(query_w.shape, BF16),
            pltpu.VMEM(keyval_w.shape, BF16),
            pltpu.VMEM((features, 128), F32),
            pltpu.VMEM((rows, features), F32),
            pltpu.VMEM((rows, features), BF16),
            pltpu.VMEM((rows, 128), BF16),
            pltpu.VMEM((8, features), F32),
            pltpu.VMEM((rows, features), BF16),
            pltpu.VMEM((rows, features), BF16),
            pltpu.VMEM((rows, features), F32),
            pltpu.VMEM(every.shape, BF16),
            pltpu.VMEM(every.shape, BF16),
            pltpu.VMEM(query_w.shape, BF16),
            pltpu.VMEM(keyval_w.shape, BF16),
            pltpu.VMEM(expert_in.shape, BF16),
            pltpu.VMEM(expert_down.shape, BF16),
            pltpu.SemaphoreType.DMA((8,)),
            pltpu.SemaphoreType.DMA((8,)),
            pltpu.SemaphoreType.DMA((66,)),
            pltpu.SemaphoreType.DMA((66,)),
            pltpu.SemaphoreType.DMA((16,)),
        ],
        compiler_params=pltpu.CompilerParams(
            collective_id=3, has_side_effects=True, vmem_limit_bytes=61 * 1024 * 1024
        ),
        cost_estimate=pl.CostEstimate(
            flops=10_000_000_000, bytes_accessed=150_000_000, transcendentals=2_000_000
        ),
    )(
        *inputs,
        grad_back,
        outt,
        every,
        own_in,
        own_down,
        query_w,
        keyval_w,
        expert_in,
        expert_down,
        rows_back,
    )


def contract(left_side, right_side, left_dim, right_dim):
    return lax.dot_general(
        left_side,
        right_side,
        (((left_dim,), (right_dim,)), ((), ())),
        preferred_element_type=F32,
    )


def expert_of(holder):
    return (holder // 8) * 8 + (holder % 2) * 4 + holder // 2 % 4


def packed(grad):
    return grad.reshape(4, 2, 2, 2, 48, grad.shape[-1])


def shards(
    tokens,
    segments,
    routes,
    norm1_gain,
    w_query,
    key_value_weight,
    w_output,
    norm2_gain,
    w_router,
    w_shgate,
    w_shup,
    w_shdown,
    w_exgate,
    w_exup,
    w_exdown,
    cotangent,
):
    local_rows, feature_count = tokens.shape
    sequence_length = local_rows * 8
    shard = jnp.concatenate(
        [
            w_output.T,
            w_router,
            norm1_gain[:, None],
            norm2_gain[:, None],
            jnp.zeros((12, 62), BF16),
            w_query,
            key_value_weight,
            w_shgate,
            w_shup,
            w_shdown.T,
        ],
        axis=1,
    )
    shard = jnp.concatenate([shard, jnp.zeros((4, TOTAL), BF16)], axis=0)
    *dense, expert_w, expert_down = gather_weights(shard, w_exgate[0], w_exup[0], w_exdown[0])
    outt_w, misc_w, query_w, keyval_w, shgate_w, shup_w, shdt_w = [
        gathered.reshape(feature_count, gathered.shape[-1]) for gathered in dense
    ]
    expert_ids = jnp.arange(128, dtype=jnp.int32)
    named = jnp.any(routes[:, :, None] == expert_ids[None, None, :], axis=1)
    named_low = named.astype(BF16)
    token_ids = jnp.arange(local_rows, dtype=jnp.int32)
    before = (token_ids[None, :] <= token_ids[:, None]).astype(BF16)
    rank = jnp.dot(before, named_low, preferred_element_type=F32) * named.astype(F32)
    slot_count = EXPERTS * CAP
    slot_ids = jnp.arange(slot_count, dtype=jnp.int32)
    holder = slot_ids // CAP
    slot_expert = expert_of(holder)
    owner = (slot_expert[:, None] == expert_ids[None, :]).astype(BF16)
    rank_wide = contract(rank.astype(BF16), owner, 1, 1)
    slots = (rank_wide == (slot_ids % CAP + 1).astype(F32)[None, :]).astype(BF16)
    slots_down = (
        contract(owner, rank.astype(BF16), 1, 1) == (slot_ids % CAP + 1).astype(F32)[:, None]
    ).astype(BF16)

    own_segments = segments.astype(F32)
    tail = 32
    first_length = jnp.sum((segments == 0).astype(F32)).astype(BF16)
    every, marks, first_normed, query_rows, sent_cotangent = to_later(
        tokens,
        misc_w,
        jnp.broadcast_to(first_length, (tail, 128)),
        query_w,
        keyval_w,
        slots_down,
        cotangent,
    )
    segment_tile = jnp.broadcast_to(own_segments[:, None], (local_rows, 128))
    (
        attended_rows,
        residual1,
        second_normed,
        gates,
        gates_high,
        gates_low,
        forward_rows,
        grad_second,
        grad_received,
        outgoing,
        grad_shgate,
        grad_shup,
        grad_shdt,
    ) = middle(
        query_rows,
        every,
        marks,
        segment_tile,
        tokens,
        misc_w,
        named.astype(F32),
        slots,
        slots_down,
        owner,
        cotangent,
        sent_cotangent,
        outt_w,
        shgate_w,
        shup_w,
        shdt_w,
    )
    grad_back, half_out, own_in, other_in, own_down, other_down = expert(
        outgoing, grad_received, expert_w, expert_down
    )
    grad_back = grad_back.reshape(slot_count, feature_count + EXTRA)
    (
        grad_tokens,
        grad_outt,
        grad_query,
        grad_keyval,
        grad_misc,
        half_in,
        half_down,
        returned,
    ) = rear(
        tail,
        (
            slots,
            owner,
            gates,
            cotangent,
            residual1,
            grad_second,
            misc_w,
            query_rows,
            marks,
            segment_tile,
            attended_rows,
            first_normed,
            second_normed,
            tokens,
        ),
        grad_back,
        outt_w,
        every,
        own_in,
        own_down,
        query_w,
        keyval_w,
        other_in,
        other_down,
        half_out,
    )
    *summed, half_in, half_down, block_out = sum_last(
        [
            packed(grad)
            for grad in (
                grad_outt,
                grad_misc,
                grad_query,
                grad_keyval,
                grad_shgate,
                grad_shup,
                grad_shdt,
            )
        ],
        [half_in, half_down],
        returned,
        gates_high,
        gates_low,
        forward_rows,
    )
    sum_outt, sum_misc, sum_query, sum_keyval, sum_shgate, sum_shup, sum_shdt = [
        piece[:12] for piece in summed
    ]
    return (
        block_out,
        grad_tokens,
        sum_misc[:, EXPERTS],
        sum_query,
        sum_keyval,
        sum_outt.T,
        sum_misc[:, EXPERTS + 1],
        sum_misc[:, :EXPERTS],
        sum_shgate,
        sum_shup,
        sum_shdt.T,
        half_in[None, :, :HALF].astype(F32),
        half_in[None, :, HALF:].astype(F32),
        half_down[None].astype(F32),
    )


def solution(mesh):
    fine = Mesh(mesh.devices.reshape(SIZES), AXES)
    rows = P(AXES, None)
    columns = P(None, AXES)
    flat = P(AXES)
    blocks = P(AXES, None, None)
    in_specs = (
        rows,
        flat,
        rows,
        flat,
        rows,
        rows,
        columns,
        flat,
        rows,
        rows,
        rows,
        columns,
        blocks,
        blocks,
        blocks,
        rows,
    )
    out_specs = (
        rows,
        rows,
        flat,
        rows,
        rows,
        columns,
        flat,
        rows,
        rows,
        rows,
        columns,
        blocks,
        blocks,
        blocks,
    )
    return jax.shard_map(shards, mesh=fine, in_specs=in_specs, out_specs=out_specs, check_vma=False)
```
